32 devices in a mesh: mode: 4 (over z), ex: 4 (over y, x), ey: 2 (over core).
Axes of the slice: x: 2, y: 2, z: 4, core: 2. Of those that a mesh axis runs over, the one named last changes fastest.
Arguments:
- stream_speed: float32 [12, 12, 16, 4, 256], P(None, None, 'ex', 'ey', 'mode'), may hold values from -9 to 9, as said below
- normal_speed: float32 [12, 12, 16, 4, 256], P(None, None, 'ex', 'ey', 'mode'), may hold values from -9 to 9, as said below
Outputs:
- velocity_modes: float32 [12, 12, 16, 4, 512], P(None, None, 'ex', 'ey', 'mode')
The draws below stay inside these ranges and needn't reach their ends.
Inputs may be any that keep to these rules, and one draw needn't show every extreme that they name: `stream_speed`: continuous across element faces (shared nodes carry equal values), periodic along the streamwise direction and zero on the walls. `normal_speed`: continuous across element faces (shared nodes carry equal values), periodic along the streamwise direction and zero on the walls.
All inputs are finite; a program needn't handle non-finite values.
Results may differ from the reference program's by a relative error of at most 0.00018.
Values sent between devices are 32-bit elements; how exact they have to be, the bound alone decides.
No kernel may reach another device: no remote copies, remote signals or barrier semaphores. Data moves between devices by JAX's collectives and lax.ppermute only.
A program may use at most 128 MiB of HBM per device.

```python
import jax
import jax.numpy as jnp
import numpy as np
from jax import lax

P_SIZE = 11
PL_DEV = 64
SWEEPS = 2
EXT = 16
EYT = 4
PLANES = 256
MODES = 128
N_MODE = 4


def continuous_field(key):
    grid_x = P_SIZE * EXT
    grid_y = P_SIZE * EYT + 1
    values_grid = jnp.clip(jax.random.normal(key, (grid_x, grid_y, PLANES), jnp.float32), -6.0, 6.0)
    height_index = jnp.arange(grid_y, dtype=jnp.int32)
    inside = jnp.where((height_index > 0) & (height_index < grid_y - 1), 1.0, 0.0).astype(jnp.float32)
    values_grid = values_grid * inside[None, :, None]
    index_x = (P_SIZE * np.arange(EXT)[None, :] + np.arange(P_SIZE + 1)[:, None]) % grid_x
    index_y = P_SIZE * np.arange(EYT)[None, :] + np.arange(P_SIZE + 1)[:, None]
    gathered = values_grid[index_x]
    gathered = gathered[:, :, index_y]
    return jnp.transpose(gathered, (0, 2, 1, 3, 4))


def draw_stream_speed(key, part):
    return continuous_field(jax.random.fold_in(key, 11))


def draw_normal_speed(key, part):
    return continuous_field(jax.random.fold_in(key, 23))


def setup_inputs(seed: int = 0) -> dict:
    streams_of = jax.random.split(jax.random.key(seed), 3)
    return {
        "stream_speed": draw_stream_speed(jax.random.fold_in(streams_of[2], 71), 0),
        "normal_speed": draw_normal_speed(jax.random.fold_in(streams_of[2], 71), 0),
    }


element_width = 2.0
shift_base = 10.0
span_rate = 0.0125

def legendre_pair(degree, points):
    before = points * 0.0 + 1.0
    current = points.copy()
    for step in range(1, degree):
        upcoming = ((2 * step + 1) * points * current - step * before) / (step + 1)
        before = current
        current = upcoming
    return (current, before)

def legendre_slope(degree, points):
    current, before = legendre_pair(degree, points)
    return (current, degree * (points * current - before) / (points * points - 1.0))

def lobatto_points(order):
    guesses = -np.cos(np.pi * np.arange(1, order) / order)
    for step in range(60):
        current, slope = legendre_slope(order, guesses)
        second = (2.0 * guesses * slope - order * (order + 1) * current) / (1.0 - guesses * guesses)
        guesses = guesses - slope / second
    return guesses

def gauss_rule(count):
    guesses = -np.cos(np.pi * (np.arange(count) + 0.75) / (count + 0.5))
    for step in range(60):
        current, slope = legendre_slope(count, guesses)
        guesses = guesses - current / slope
    current, slope = legendre_slope(count, guesses)
    return (guesses, 2.0 / ((1.0 - guesses * guesses) * slope * slope))

def jacobi_eigen(matrix):
    size_n = matrix.shape[0]
    work = matrix.copy()
    vectors = np.eye(size_n)
    for sweep_number in range(20):
        for first in range(size_n):
            for second in range(first + 1, size_n):
                coupling = work[first, second]
                if abs(coupling) > 1e-300:
                    theta = (work[second, second] - work[first, first]) / (2.0 * coupling)
                    direction = 1.0 if theta >= 0.0 else -1.0
                    tangent = direction / (abs(theta) + np.sqrt(theta * theta + 1.0))
                    cosine = 1.0 / np.sqrt(tangent * tangent + 1.0)
                    sine = tangent * cosine
                    rotation = np.eye(size_n)
                    rotation[first, first] = cosine
                    rotation[second, second] = cosine
                    rotation[first, second] = sine
                    rotation[second, first] = -sine
                    work = rotation.T @ work @ rotation
                    vectors = vectors @ rotation
    diagonal_index = np.arange(size_n)
    return (work[diagonal_index, diagonal_index], vectors)

def extended_basis(stiffness, weights, left_width, centre_width, right_width):
    node_count = weights.shape[0]
    full_count = 3 * node_count - 2
    stiff_full = np.zeros((full_count, full_count))
    mass_full = np.zeros(full_count)
    for position, span_width in enumerate((left_width, centre_width, right_width)):
        if span_width > 0.0:
            first_node = position * (node_count - 1)
            stiff_full[first_node:first_node + node_count, first_node:first_node + node_count] += stiffness * (2.0 / span_width)
            mass_full[first_node:first_node + node_count] += weights * (span_width / 2.0)
    low_index = node_count - 2
    high_index = low_index + node_count + 2
    stiff_ext = stiff_full[low_index:high_index, low_index:high_index].copy()
    mass_ext = mass_full[low_index:high_index].copy()
    frozen_list = []
    if left_width <= 0.0:
        frozen_list += [0, 1]
    if right_width <= 0.0:
        frozen_list += [node_count, node_count + 1]
    for frozen_index in frozen_list:
        stiff_ext[frozen_index, :] = 0.0
        stiff_ext[:, frozen_index] = 0.0
        stiff_ext[frozen_index, frozen_index] = 1.0
        mass_ext[frozen_index] = 1.0
    inverse_root = 1.0 / np.sqrt(mass_ext)
    lambdas, vectors = jacobi_eigen(inverse_root[:, None] * stiff_ext * inverse_root[None, :])
    return (inverse_root[:, None] * vectors, lambdas)

def spectral_tables(order, rows_total):
    inner_points = lobatto_points(order)
    points = np.concatenate([[-1.0], inner_points, [1.0]])
    values, unused_before = legendre_pair(order, points)
    weights = 2.0 / (order * (order + 1) * values ** 2)
    identity = np.eye(order + 1)
    point_gaps = points[:, None] - points[None, :] + identity
    derivative = values[:, None] / (values[None, :] * point_gaps) * (1.0 - identity)
    derivative[0, 0] = -order * (order + 1) / 4.0
    derivative[order, order] = order * (order + 1) / 4.0
    stiffness = derivative.T @ (weights[:, None] * derivative)
    gauss_points, gauss_weights = gauss_rule(3 * (order + 1) // 2)
    offsets = gauss_points[:, None, None] - points[None, None, :]
    numerators = np.prod(np.where(identity[None, :, :] > 0.5, 1.0, offsets), axis=2)
    denominators = np.prod(np.where(identity > 0.5, 1.0, points[:, None] - points[None, :]), axis=1)
    interp = numerators / denominators[None, :]
    heights = 0.6 + 1.4 * np.sin(np.pi * (np.arange(rows_total) + 0.5) / rows_total)
    basis_x, lambdas_x = extended_basis(stiffness, weights, element_width, element_width, element_width)
    basis_rows = []
    lambda_rows = []
    for row_number in range(rows_total):
        below = heights[row_number - 1] if row_number > 0 else 0.0
        above = heights[row_number + 1] if row_number < rows_total - 1 else 0.0
        basis_one, lambda_one = extended_basis(stiffness, weights, below, heights[row_number], above)
        basis_rows.append(basis_one)
        lambda_rows.append(lambda_one)
    return (derivative, interp, gauss_weights, weights, stiffness, basis_x, lambdas_x, np.stack(basis_rows), np.stack(lambda_rows), heights)

def device_tables(order, rows_total):
    return tuple((jnp.asarray(table_item, jnp.float32) for table_item in spectral_tables(order, rows_total)))

def along_first(matrix, field_data):
    return jnp.tensordot(matrix, field_data, axes=(1, 0), precision=lax.Precision.HIGHEST)

def along_second(matrix, field_data):
    return jnp.einsum('bj,ajefk->abefk', matrix, field_data, precision=lax.Precision.HIGHEST)

def along_second_rows(matrices, field_data):
    return jnp.einsum('fbj,ajefk->abefk', matrices, field_data, precision=lax.Precision.HIGHEST)

def lift_fine(interp, field_data):
    return along_second(interp, along_first(interp, field_data))

def advection(stream_speed, normal_speed, derivative, interp, gauss_weights, heights):
    height_col = heights[None, None, None, :, None]
    fine_stream = lift_fine(interp, stream_speed)
    fine_normal = lift_fine(interp, normal_speed)
    quadrature = (gauss_weights[:, None] * gauss_weights[None, :])[:, :, None, None, None]

    def convect(speed_field):
        slope_x = along_first(derivative, speed_field) * (2.0 / element_width)
        slope_y = along_second(derivative, speed_field) * (2.0 / height_col)
        product = fine_stream * lift_fine(interp, slope_x) + fine_normal * lift_fine(interp, slope_y)
        returned = along_first(interp.T, along_second(interp.T, product * quadrature))
        return -returned * (element_width * height_col / 4.0)
    return (convect(stream_speed), convect(normal_speed))

def mode_shifts(first_mode, columns):
    column_index = jnp.arange(columns, dtype=jnp.int32)
    mode_index = first_mode + column_index // 4
    return shift_base + (span_rate * mode_index.astype(jnp.float32)) ** 2

def wall_masks(first_row, rows_local, rows_total, node_count):
    row_index = first_row + jnp.arange(rows_local + 2, dtype=jnp.int32) - 1
    node_index = jnp.arange(node_count, dtype=jnp.int32)
    bottom = (row_index[None, :] == 0) & (node_index[:, None] == 0)
    top = (row_index[None, :] == rows_total - 1) & (node_index[:, None] == node_count - 1)
    keep = jnp.where(bottom | top, 0.0, 1.0).astype(jnp.float32)
    return (keep[None, :, None, :, None], keep[None, :, None, 1:-1, None])

def local_operator(solution, stiffness, weights, heights, shift_values):
    height_col = heights[None, None, None, :, None]
    across = along_first(stiffness, solution) * (2.0 / element_width) * (weights[None, :, None, None, None] * height_col / 2.0)
    upward = along_second(stiffness, solution) * (2.0 / height_col) * (weights[:, None, None, None, None] * element_width / 2.0)
    masses = (weights[:, None] * weights[None, :])[:, :, None, None, None] * (element_width * height_col / 4.0)
    return across + upward + masses * shift_values[None, None, None, None, :] * solution

def assemble_first(field_data):
    last_node = field_data.shape[0] - 1
    empty = jnp.zeros_like(field_data[:, :, :1])
    from_left = jnp.concatenate([empty, field_data[:, :, :-1]], 2)
    from_right = jnp.concatenate([field_data[:, :, 1:], empty], 2)
    return jnp.concatenate([field_data[:1] + from_left[last_node:], field_data[1:last_node], field_data[last_node:] + from_right[:1]], 0)

def assemble_second(field_data):
    last_node = field_data.shape[1] - 1
    empty = jnp.zeros_like(field_data[:, :, :, :1])
    from_below = jnp.concatenate([empty, field_data[:, :, :, :-1]], 3)
    from_above = jnp.concatenate([field_data[:, :, :, 1:], empty], 3)
    return jnp.concatenate([field_data[:, :1] + from_below[:, last_node:], field_data[:, 1:last_node], field_data[:, last_node:] + from_above[:, :1]], 1)

def extend_points(extended):
    node_count = extended.shape[0]
    across = jnp.concatenate([extended[node_count - 2:node_count - 1, :, :-2], extended[:, :, 1:-1], extended[1:2, :, 2:]], 0)
    return jnp.concatenate([across[:, node_count - 2:node_count - 1, :, :, :][:, :, :, :-2], across[:, :, :, 1:-1], across[:, 1:2, :, 2:]], 1)

def fold_back(extended):
    point_count = extended.shape[0]
    blank = jnp.zeros_like(extended[:point_count - 6, :, 1:-1])
    across = extended[1:point_count - 1, :, 1:-1] + jnp.concatenate([extended[point_count - 2:, :, :-2], blank, extended[:2, :, 2:]], 0)
    blank_y = jnp.zeros_like(across[:, :point_count - 6, :, 1:-1])
    return across[:, 1:point_count - 1, :, 1:-1] + jnp.concatenate([across[:, point_count - 2:, :, :-2], blank_y, across[:, :2, :, 2:]], 1)

def smooth_modes(forcing, shift_values, row_tables, wall_ext, wall_own, extend):
    stiffness, weights, basis_x, lambdas_x, basis_y, lambdas_y, heights = row_tables
    denominator = lambdas_x[:, None, None, None, None] + jnp.transpose(lambdas_y)[None, :, None, :, None] + shift_values[None, None, None, None, :]
    basis_y_t = jnp.transpose(basis_y, (0, 2, 1))
    solution = jnp.zeros_like(forcing)
    for sweep_index in range(SWEEPS):
        if sweep_index == 0:
            residual = forcing
        else:
            residual = forcing - local_operator(solution, stiffness, weights, heights, shift_values)
        extended = assemble_second(assemble_first(extend(residual))) * wall_ext
        spread = extend_points(extended)
        spectral = along_second_rows(basis_y_t, along_first(basis_x.T, spread)) / denominator
        local_fix = along_first(basis_x, along_second_rows(basis_y, spectral))
        solution = solution + fold_back(extend(local_fix)) * wall_own
    return solution

def grow_blocks(block_field):
    widened = jnp.concatenate([block_field[:, :, -1:], block_field, block_field[:, :, :1]], 2)
    blank = jnp.zeros_like(widened[:, :, :, :1])
    return jnp.concatenate([blank, widened, blank], 3)

def reference(stream_speed, normal_speed):
    derivative, interp, gauss_weights, weights, stiffness, basis_x, lambdas_x, basis_y, lambdas_y, heights = device_tables(P_SIZE, EYT)

    def to_blocks(field_data):
        return jnp.moveaxis(field_data.reshape(field_data.shape[:4] + (N_MODE, PL_DEV)), 4, 0)

    def from_blocks(field_data):
        moved = jnp.moveaxis(field_data, 0, 4)
        return moved.reshape(moved.shape[:4] + (moved.shape[4] * moved.shape[5],))

    def advect_block(speed_pair):
        return advection(speed_pair[0], speed_pair[1], derivative, interp, gauss_weights, heights)
    weak_x, weak_y = lax.map(advect_block, (to_blocks(stream_speed), to_blocks(normal_speed)))
    weak_x = from_blocks(weak_x)
    weak_y = from_blocks(weak_y)
    spectra_x = jnp.fft.rfft(weak_x, axis=-1)[..., :MODES] / PLANES
    spectra_y = jnp.fft.rfft(weak_y, axis=-1)[..., :MODES] / PLANES
    cosine_part = jnp.stack([jnp.real(spectra_x), jnp.real(spectra_y)], -1)
    sine_part = jnp.stack([jnp.imag(spectra_x), jnp.imag(spectra_y)], -1)
    spectra = jnp.stack([cosine_part, sine_part], -2)
    spectra = spectra.reshape(spectra.shape[:4] + (4 * MODES,)).astype(jnp.float32)
    columns = 4 * MODES // N_MODE
    blocks = jnp.moveaxis(spectra.reshape(spectra.shape[:4] + (N_MODE, columns)), 4, 0)
    wall_ext, wall_own = wall_masks(0, EYT, EYT, P_SIZE + 1)
    row_tables = (stiffness, weights, basis_x, lambdas_x, basis_y, lambdas_y, heights)

    def solve_block(block_pair):
        shift_values = mode_shifts(block_pair[1] * (columns // 4), columns)
        return smooth_modes(block_pair[0], shift_values, row_tables, wall_ext, wall_own, grow_blocks)
    solved = lax.map(solve_block, (blocks, jnp.arange(N_MODE, dtype=jnp.int32)))
    return from_blocks(solved)
```

```python
import functools
import math

import jax
import jax.numpy as jnp
import ml_dtypes
import numpy as np
from jax import lax
from jax.experimental import pallas as pl
from jax.experimental.pallas import tpu as pltpu
from jax.sharding import PartitionSpec as P

BF16 = ml_dtypes.bfloat16

element_width = 2.0
shift_base = 10.0
span_rate = 0.0125


def legendre_pair(degree, points):
    before = points * 0.0 + 1.0
    current = points.copy()
    for step in range(1, degree):
        upcoming = ((2 * step + 1) * points * current - step * before) / (step + 1)
        before = current
        current = upcoming
    return (current, before)


def legendre_slope(degree, points):
    current, before = legendre_pair(degree, points)
    return (current, degree * (points * current - before) / (points * points - 1.0))


def lobatto_points(order):
    guesses = -np.cos(np.pi * np.arange(1, order) / order)
    for step in range(60):
        current, slope = legendre_slope(order, guesses)
        second = (2.0 * guesses * slope - order * (order + 1) * current) / (1.0 - guesses * guesses)
        guesses = guesses - slope / second
    return guesses


def gauss_rule(count):
    guesses = -np.cos(np.pi * (np.arange(count) + 0.75) / (count + 0.5))
    for step in range(60):
        current, slope = legendre_slope(count, guesses)
        guesses = guesses - current / slope
    current, slope = legendre_slope(count, guesses)
    return (guesses, 2.0 / ((1.0 - guesses * guesses) * slope * slope))


def jacobi_eigen(matrix):
    size_n = matrix.shape[0]
    work = matrix.copy()
    vectors = np.eye(size_n)
    for sweep_number in range(20):
        for first in range(size_n):
            for second in range(first + 1, size_n):
                coupling = work[first, second]
                if abs(coupling) > 1e-300:
                    theta = (work[second, second] - work[first, first]) / (2.0 * coupling)
                    direction = 1.0 if theta >= 0.0 else -1.0
                    tangent = direction / (abs(theta) + np.sqrt(theta * theta + 1.0))
                    cosine = 1.0 / np.sqrt(tangent * tangent + 1.0)
                    sine = tangent * cosine
                    rotation = np.eye(size_n)
                    rotation[first, first] = cosine
                    rotation[second, second] = cosine
                    rotation[first, second] = sine
                    rotation[second, first] = -sine
                    work = rotation.T @ work @ rotation
                    vectors = vectors @ rotation
    diagonal_index = np.arange(size_n)
    return (work[diagonal_index, diagonal_index], vectors)


def extended_basis(stiffness, weights, left_width, centre_width, right_width):
    node_count = weights.shape[0]
    full_count = 3 * node_count - 2
    stiff_full = np.zeros((full_count, full_count))
    mass_full = np.zeros(full_count)
    for position, span_width in enumerate((left_width, centre_width, right_width)):
        if span_width > 0.0:
            first_node = position * (node_count - 1)
            stiff_full[
                first_node : first_node + node_count, first_node : first_node + node_count
            ] += stiffness * (2.0 / span_width)
            mass_full[first_node : first_node + node_count] += weights * (span_width / 2.0)
    low_index = node_count - 2
    high_index = low_index + node_count + 2
    stiff_ext = stiff_full[low_index:high_index, low_index:high_index].copy()
    mass_ext = mass_full[low_index:high_index].copy()
    frozen_list = []
    if left_width <= 0.0:
        frozen_list += [0, 1]
    if right_width <= 0.0:
        frozen_list += [node_count, node_count + 1]
    for frozen_index in frozen_list:
        stiff_ext[frozen_index, :] = 0.0
        stiff_ext[:, frozen_index] = 0.0
        stiff_ext[frozen_index, frozen_index] = 1.0
        mass_ext[frozen_index] = 1.0
    inverse_root = 1.0 / np.sqrt(mass_ext)
    lambdas, vectors = jacobi_eigen(inverse_root[:, None] * stiff_ext * inverse_root[None, :])
    return (inverse_root[:, None] * vectors, lambdas)


def spectral_tables(order, rows_total):
    inner_points = lobatto_points(order)
    points = np.concatenate([[-1.0], inner_points, [1.0]])
    values, unused_before = legendre_pair(order, points)
    weights = 2.0 / (order * (order + 1) * values**2)
    identity = np.eye(order + 1)
    point_gaps = points[:, None] - points[None, :] + identity
    derivative = values[:, None] / (values[None, :] * point_gaps) * (1.0 - identity)
    derivative[0, 0] = -order * (order + 1) / 4.0
    derivative[order, order] = order * (order + 1) / 4.0
    stiffness = derivative.T @ (weights[:, None] * derivative)
    gauss_points, gauss_weights = gauss_rule(3 * (order + 1) // 2)
    offsets = gauss_points[:, None, None] - points[None, None, :]
    numerators = np.prod(np.where(identity[None, :, :] > 0.5, 1.0, offsets), axis=2)
    denominators = np.prod(np.where(identity > 0.5, 1.0, points[:, None] - points[None, :]), axis=1)
    interp = numerators / denominators[None, :]
    heights = 0.6 + 1.4 * np.sin(np.pi * (np.arange(rows_total) + 0.5) / rows_total)
    basis_x, lambdas_x = extended_basis(
        stiffness, weights, element_width, element_width, element_width
    )
    basis_rows = []
    lambda_rows = []
    for row_number in range(rows_total):
        below = heights[row_number - 1] if row_number > 0 else 0.0
        above = heights[row_number + 1] if row_number < rows_total - 1 else 0.0
        basis_one, lambda_one = extended_basis(
            stiffness, weights, below, heights[row_number], above
        )
        basis_rows.append(basis_one)
        lambda_rows.append(lambda_one)
    return (
        derivative,
        interp,
        gauss_weights,
        weights,
        stiffness,
        basis_x,
        lambdas_x,
        np.stack(basis_rows),
        np.stack(lambda_rows),
        heights,
    )


PARTS = 8
LANES = 128


def ceil_to(count, step):
    return -(-count // step) * step


class Sizes:
    def __init__(self, mesh_shape, block_shape):
        self.n_mode, self.n_ex, self.n_ey = (mesh_shape[name] for name in ("mode", "ex", "ey"))
        self.nodes, _, self.elems, self.rows, self.planes = block_shape
        self.order = self.nodes - 1
        self.gauss = 3 * self.nodes // 2
        self.rows_total = self.rows * self.n_ey
        self.elems_total = self.elems * self.n_ex
        self.planes_total = self.planes * self.n_mode
        self.block_x = self.order * self.elems + 1
        full_y = self.order * self.rows + 1
        self.inner = [
            [j for j in range(full_y) if not (p == 0 and j == 0) and not (p == self.n_ey - 1 and j == full_y - 1)]
            for p in range(self.n_ey)
        ]
        self.block_y = max(len(found) for found in self.inner)
        share = -(-(self.block_x * self.block_y + 2) // self.n_mode)
        self.share = ceil_to(share, LANES if share > 64 else 32)
        self.lane_nodes = self.share * self.n_mode
        self.columns = 2 * self.planes
        self.spots = self.n_ex * self.n_ey
        self.own = self.columns // self.spots
        self.folds = self.own // PARTS
        self.fold_width = LANES // self.folds
        self.points = self.nodes + 2
        self.x_nodes = self.n_ex * self.block_x
        self.x_pad = ceil_to(self.x_nodes, 16)
        self.x_eig = self.elems_total * self.points
        self.y_eig = self.rows_total * self.points
        self.fine = ceil_to(self.gauss * self.gauss, 16)
        assert self.own == PARTS * self.folds and self.x_eig % 16 == 0
        assert max(self.y_eig, self.n_ey * self.block_y) <= self.fold_width
        assert 2 * self.planes == LANES


def high_low(table):
    high = np.asarray(table, np.float32).astype(BF16)
    low = (np.asarray(table, np.float64) - high.astype(np.float64)).astype(BF16)
    return high, low


def beside(table):
    high, low = high_low(table)
    return np.concatenate([high, high, low], 1)


def host_tables(sz):
    derivative, interp, gauss_weights, weights, stiffness, basis_x, lam_x, basis_y, lam_y, heights = spectral_tables(
        sz.order, sz.rows_total
    )
    nodes, fine, points = sz.nodes, sz.fine, sz.points
    gauss_count = sz.gauss**2
    lift = np.zeros((3 * fine, nodes * nodes))
    lift[:gauss_count] = np.kron(interp, interp)
    lift[fine : fine + gauss_count] = np.kron(interp @ derivative, interp)
    lift[2 * fine : 2 * fine + gauss_count] = np.kron(interp, interp @ derivative)
    back = np.zeros((sz.n_ey, nodes * sz.block_y, sz.rows * fine))
    weighted = interp.T * gauss_weights[None, :]
    for place in range(sz.n_ey):
        for f in range(sz.rows):
            for jj, j in enumerate(sz.inner[place]):
                b = j - sz.order * f
                if 0 <= b < nodes:
                    back[place, jj :: sz.block_y, f * fine : f * fine + gauss_count] = -np.kron(
                        weighted, weighted[b : b + 1]
                    )
    grid_x, grid_y = sz.order * sz.elems_total, sz.order * sz.rows_total + 1
    to_x, stiff_x, mass_x = np.zeros((sz.x_eig, grid_x)), np.zeros((grid_x, grid_x)), np.zeros(grid_x)
    for e in range(sz.elems_total):
        for t in range(points):
            to_x[e * points : (e + 1) * points, (sz.order * e + t - 1) % grid_x] += basis_x[t]
        index = (sz.order * e + np.arange(nodes)) % grid_x
        stiff_x[np.ix_(index, index)] += stiffness * (2.0 / element_width)
        mass_x[index] += weights * (element_width / 2.0)
    to_y, stiff_y, mass_y = np.zeros((sz.y_eig, grid_y)), np.zeros((grid_y, grid_y)), np.zeros(grid_y)
    for f in range(sz.rows_total):
        for t in range(points):
            y = sz.order * f + t - 1
            if 0 < y < grid_y - 1:
                to_y[f * points : (f + 1) * points, y] = basis_y[f][t]
        index = sz.order * f + np.arange(nodes)
        stiff_y[np.ix_(index, index)] += stiffness * (2.0 / heights[f])
        mass_y[index] += weights * (heights[f] / 2.0)
    stiff_xx, mass_xx = to_x @ stiff_x @ to_x.T, (to_x * mass_x) @ to_x.T
    stiff_yy, mass_yy = to_y @ stiff_y @ to_y.T, (to_y * mass_y) @ to_y.T
    list_x = [(sz.order * sz.elems * p + i) % grid_x for p in range(sz.n_ex) for i in range(sz.block_x)]
    block_x = np.zeros((sz.x_eig, sz.x_pad))
    block_x[:, : sz.x_nodes] = to_x[:, list_x]
    width, folds = sz.fold_width, sz.folds
    block_y = np.zeros((width, width))
    for place in range(sz.n_ey):
        for jj, j in enumerate(sz.inner[place]):
            block_y[place * sz.block_y + jj, : sz.y_eig] = to_y[:, sz.order * sz.rows * place + j]

    def folded(table):
        padded = np.zeros((width, width))
        padded[: table.shape[0], : table.shape[1]] = table
        return np.kron(np.eye(folds), padded)

    def one_dot(table):
        high, low = high_low(folded(table))
        return np.block([[high, low], [high, np.zeros_like(low)]]).astype(BF16)

    mass_pair, stiff_pair = high_low(folded(mass_yy)), high_low(folded(stiff_yy))
    heads = np.concatenate([mass_pair[0], stiff_pair[0]], 1)
    tails = np.concatenate([mass_pair[1], stiff_pair[1]], 1)
    lam_lanes = np.ones((1, folds, width))
    lam_lanes[:, :, : sz.y_eig] = lam_y.reshape(-1)
    planes_total = sz.planes_total
    turns = np.arange(planes_total)[None, :] * np.arange(planes_total // 2)[:, None] % planes_total
    angles = turns * (2.0 * math.pi / planes_total)
    waves = np.stack([np.cos(angles), -np.sin(angles)], 1).reshape(planes_total, planes_total) / planes_total
    return dict(
        heights=np.asarray(heights, np.float32),
        lift=beside(lift),
        back=np.stack([beside(table) for table in back]),
        waves=np.stack(high_low(waves)),
        in_y=one_dot(block_y),
        in_x=beside(block_x),
        pair_y=np.concatenate([heads, heads, tails], 0),
        pair_x=beside(np.concatenate([stiff_xx, mass_xx], 1)),
        out_y=one_dot(block_y.T),
        out_x=beside(block_x.T),
        lam_x=np.asarray(np.tile(lam_x, sz.elems_total)[:, None] * np.ones((1, LANES)), np.float32),
        lam_y=np.asarray(lam_lanes.reshape(1, LANES), np.float32),
    )


def split(value):
    high = value.astype(jnp.bfloat16)
    low = (value - high.astype(jnp.float32)).astype(jnp.bfloat16)
    return high, low


def dot(left, right):
    return lax.dot_general(left, right, (((1,), (0,)), ((), ())), preferred_element_type=jnp.float32)


def below(value):
    high, low = split(value)
    return jnp.concatenate([high, low, high], 0)


def along(value):
    return jnp.concatenate(split(value), 1)


def lane_index(shape):
    return lax.broadcasted_iota(jnp.int32, shape, len(shape) - 1)


def advect_kernel(sz, heights_ref, stream_ref, normal_ref, lift_ref, back_ref, out_ref, total_ref):
    place = lax.axis_index("ey")
    count, fine, rows = sz.nodes * sz.nodes, sz.fine, sz.rows
    spots = sz.elems * rows
    half = lane_index((fine, LANES)) < sz.planes
    column, step = sz.nodes * sz.block_y, sz.order * sz.block_y
    length = sz.block_x * sz.block_y
    total_ref[pl.ds(length // 8 * 8, sz.lane_nodes - length // 8 * 8), :] = jnp.zeros(
        (sz.lane_nodes - length // 8 * 8, LANES), jnp.float32
    )
    carry = None
    for e in range(sz.elems):
        speeds = jnp.concatenate(
            [
                ref[pl.ds(e * rows + f, count, stride=spots), :]
                for f in range(rows)
                for ref in (stream_ref, normal_ref)
            ],
            1,
        )
        values = dot(lift_ref[...], below(speeds))
        highs, lows = [], []
        for f in range(rows):
            height = heights_ref[place * rows + f]
            mine = values[:, f * LANES : (f + 1) * LANES]
            both, slope_x, slope_y = mine[:fine], mine[fine : 2 * fine], mine[2 * fine :]
            turned = pltpu.roll(both, sz.planes, 1)
            stream = jnp.where(half, both, turned)
            normal = jnp.where(half, turned, both)
            high, low = split((stream * (height * 0.5)) * slope_x + (normal * (element_width * 0.5)) * slope_y)
            highs.append(high)
            lows.append(low)
        weak = dot(back_ref[place], jnp.concatenate(highs + lows + highs, 0))
        if carry is not None:
            head = jnp.concatenate([carry, jnp.zeros((column - carry.shape[0], LANES), jnp.float32)], 0)
            weak = weak + head
        if e < sz.elems - 1:
            total_ref[pl.ds(e * step, step), :] = weak[:step]
            carry = weak[step:]
        else:
            total_ref[pl.ds(e * step, column), :] = weak
    for z in range(sz.n_mode):
        out_ref[z] = total_ref[pl.ds(z * sz.share, sz.share), :]


def transform_kernel(sz, weak_ref, waves_ref, out_ref, mixed_ref):
    turned = [weak_ref[z].T for z in range(sz.n_mode)]
    modes = sz.planes_total
    for k in range(2):
        signal = jnp.concatenate([piece[k * sz.planes : (k + 1) * sz.planes] for piece in turned], 0)
        high, low = split(signal)
        part = dot(waves_ref[0], high) + dot(waves_ref[0], low) + dot(waves_ref[1], high)
        for t in range(mixed_ref.shape[0]):
            tile = part[:, t * LANES : (t + 1) * LANES]
            mixed_ref[t, pl.ds(k, modes, stride=2), pl.ds(0, tile.shape[1])] = tile
    for t in range(mixed_ref.shape[0]):
        last = min(LANES, sz.share - t * LANES)
        out_ref[:, pl.ds(t * LANES, last)] = mixed_ref[t, :, pl.ds(0, last)]


def smooth_kernel(
    sz,
    terms_ref,
    in_y_ref,
    in_x_ref,
    pair_y_ref,
    pair_x_ref,
    out_y_ref,
    out_x_ref,
    lam_x_ref,
    lam_y_ref,
    out_ref,
    field_ref,
    first_ref,
    work_ref,
):
    width, folds, strip = sz.fold_width, sz.folds, sz.block_y
    tiles = -(-sz.lane_nodes // LANES)
    lanes = lane_index((PARTS, LANES))
    x_pad, x_eig = sz.x_pad, sz.x_eig
    device = (lax.axis_index("mode") * sz.n_ex + lax.axis_index("ex")) * sz.n_ey + lax.axis_index("ey")
    first_mode = device * (sz.own // 4)

    for c in range(PARTS):
        field_ref[pl.ds(c * x_pad + sz.x_nodes, x_pad - sz.x_nodes), :] = jnp.zeros(
            (x_pad - sz.x_nodes, LANES), jnp.float32
        )
    for p in range(sz.n_ex):
        held = {}
        for q in range(sz.n_ey):
            for fold in range(folds):
                whole = jnp.concatenate(
                    [
                        terms_ref[(z * sz.n_ex + p) * sz.n_ey + q, pl.ds(fold * PARTS, PARTS), :]
                        for z in range(sz.n_mode)
                    ],
                    1,
                )
                held[q, fold] = [whole[:, t * LANES : (t + 1) * LANES] for t in range(tiles)]
        for i in range(sz.block_x):
            start = i * strip
            t, r = start // LANES, start % LANES
            result = jnp.zeros((PARTS, LANES), jnp.float32)
            for fold in range(folds):
                for q in range(sz.n_ey):
                    source = held[q, fold][t]
                    if r + strip > LANES:
                        source = jnp.where(lanes >= r, source, held[q, fold][t + 1])
                    goal = fold * width + q * strip
                    moved = pltpu.roll(source, (goal - r) % LANES, 1) if goal != r else source
                    result = jnp.where((lanes >= goal) & (lanes < goal + strip), moved, result)
            field_ref[pl.ds(p * sz.block_x + i, PARTS, stride=x_pad), :] = result

    parts = dot(along(field_ref[...]), in_y_ref[...])
    field_ref[...] = parts[:, :LANES] + parts[:, LANES:]
    fold_of_lane = lane_index((1, LANES)) // width
    shifts, inverses = [], []
    for group in range(PARTS // 4):
        mode = (first_mode + fold_of_lane * (PARTS // 4) + group).astype(jnp.float32)
        shift = shift_base + (span_rate * mode) ** 2
        shifts.append(shift)
        inverses.append(1.0 / (lam_x_ref[...] + (lam_y_ref[...] + shift)))
    for c in range(0, PARTS, 2):
        pair = jnp.concatenate([field_ref[pl.ds((c + d) * x_pad, x_pad), :] for d in range(2)], 1)
        forced = dot(in_x_ref[...], below(pair))
        for d in range(2):
            mine = forced[:, d * LANES : (d + 1) * LANES]
            first_ref[pl.ds((c + d) * x_eig, x_eig), :] = mine
            work_ref[pl.ds((c + d) * x_eig, x_eig), :] = mine * inverses[(c + d) // 4]
    for c in range(0, PARTS, 2):
        shift = shifts[c // 4]
        masses, stiffs = [], []
        for d in range(2):
            high, low = split(work_ref[pl.ds((c + d) * x_eig, x_eig), :])
            both = dot(jnp.concatenate([high, low, high], 1), pair_y_ref[...])
            masses.append(both[:, :LANES])
            stiffs.append(both[:, LANES:] + shift * both[:, :LANES])
        stacked = jnp.concatenate([jnp.concatenate(masses, 1), jnp.concatenate(stiffs, 1)], 0)
        applied = dot(pair_x_ref[...], below(stacked))
        for d in range(2):
            rows = pl.ds((c + d) * x_eig, x_eig)
            total = (2.0 * first_ref[rows, :] - applied[:, d * LANES : (d + 1) * LANES]) * inverses[c // 4]
            parts = dot(along(total), out_y_ref[...])
            work_ref[rows, :] = parts[:, :LANES] + parts[:, LANES:]
        pair = jnp.concatenate([work_ref[pl.ds((c + d) * x_eig, x_eig), :] for d in range(2)], 1)
        solved = dot(out_x_ref[...], below(pair))
        for d in range(2):
            field_ref[pl.ds((c + d) * x_pad, x_pad), :] = solved[:, d * LANES : (d + 1) * LANES]

    for p in range(sz.n_ex):
        made = {}
        for i in range(sz.block_x):
            source = field_ref[pl.ds(p * sz.block_x + i, PARTS, stride=x_pad), :]
            for q in range(sz.n_ey):
                begin = i * strip + sz.inner[q][0]
                count = len(sz.inner[q])
                t, r = begin // LANES, begin % LANES
                for fold in range(folds):
                    origin = fold * width + q * strip
                    moved = pltpu.roll(source, (r - origin) % LANES, 1) if origin != r else source
                    for tile, low, high in ((t, r, r + count), (t + 1, 0, r + count - LANES)):
                        if high > 0:
                            old = made.get((q, fold, tile))
                            if old is None:
                                old = jnp.zeros((PARTS, LANES), jnp.float32)
                            made[q, fold, tile] = jnp.where((lanes >= low) & (lanes < high), moved, old)
        for (q, fold, tile), value in made.items():
            last = min(LANES, sz.lane_nodes - tile * LANES)
            out_ref[p * sz.n_ey + q, pl.ds(fold * PARTS, PARTS), pl.ds(tile * LANES, last)] = value[:, :last]


def spread_kernel(sz, solved_ref, out_ref, turned_ref):
    place = lax.axis_index("ey")
    turned_ref[...] = solved_ref[...].T
    spots = sz.elems * sz.rows
    for e in range(sz.elems):
        for f in range(sz.rows):
            for a in range(sz.nodes):
                start = sz.block_y * (sz.order * e + a) + sz.order * f
                out_ref[pl.ds(a * sz.nodes * spots + e * sz.rows + f, sz.nodes, stride=spots), :] = turned_ref[
                    pl.ds(start, sz.nodes), :
                ]
    blank = jnp.zeros((sz.elems, LANES), jnp.float32)

    @pl.when(place == 0)
    def _():
        for a in range(sz.nodes):
            out_ref[pl.ds(a * sz.nodes * spots, sz.elems, stride=sz.rows), :] = blank

    @pl.when(place == sz.n_ey - 1)
    def _():
        for a in range(sz.nodes):
            first = ((a + 1) * sz.nodes - 1) * spots + sz.rows - 1
            out_ref[pl.ds(first, sz.elems, stride=sz.rows), :] = blank


def call(kernel, out_shape, operands, scratch=(), scalars=0):
    vmem = pl.BlockSpec(memory_space=pltpu.VMEM)
    smem = pl.BlockSpec(memory_space=pltpu.SMEM)
    return pl.pallas_call(
        kernel,
        out_shape=jax.ShapeDtypeStruct(out_shape, jnp.float32),
        in_specs=[smem] * scalars + [vmem] * (len(operands) - scalars),
        out_specs=vmem,
        scratch_shapes=[pltpu.VMEM(shape, jnp.float32) for shape in scratch],
        compiler_params=pltpu.CompilerParams(vmem_limit_bytes=56 * 2**20),
    )(*operands)


def on_device(sz, tables, stream_speed, normal_speed):
    flat = sz.nodes * sz.nodes * sz.elems * sz.rows
    table = {name: jnp.asarray(value) for name, value in tables.items()}
    weak = call(
        functools.partial(advect_kernel, sz),
        (sz.n_mode, sz.share, LANES),
        [
            table["heights"],
            stream_speed.reshape(flat, sz.planes),
            normal_speed.reshape(flat, sz.planes),
            table["lift"],
            table["back"],
        ],
        [(sz.lane_nodes, LANES)],
        scalars=1,
    )
    weak = lax.all_to_all(weak, "mode", split_axis=0, concat_axis=0, tiled=True)
    spectra = call(
        functools.partial(transform_kernel, sz),
        (2 * sz.planes_total, sz.share),
        [weak, table["waves"]],
        [(-(-sz.share // LANES), 2 * sz.planes_total, LANES)],
    )
    everyone = ("mode", "ex", "ey")
    spectra = spectra.reshape(sz.n_mode * sz.spots, sz.own, sz.share)
    terms = lax.all_to_all(spectra, everyone, split_axis=0, concat_axis=0, tiled=True)
    names = ("in_y", "in_x", "pair_y", "pair_x", "out_y", "out_x", "lam_x", "lam_y")
    solved = call(
        functools.partial(smooth_kernel, sz),
        (sz.spots, sz.own, sz.lane_nodes),
        [terms] + [table[name] for name in names],
        [(PARTS * sz.x_pad, LANES), (PARTS * sz.x_eig, LANES), (PARTS * sz.x_eig, LANES)],
    )
    solved = lax.all_to_all(solved, ("ex", "ey"), split_axis=0, concat_axis=0, tiled=True)
    out = call(
        functools.partial(spread_kernel, sz),
        (flat, LANES),
        [solved.reshape(sz.columns, sz.lane_nodes)],
        [(sz.lane_nodes, LANES)],
    )
    return out.reshape(sz.nodes, sz.nodes, sz.elems, sz.rows, sz.columns)


def solution(mesh):
    spec = P(None, None, "ex", "ey", "mode")

    def whole(stream_speed, normal_speed):
        shape = stream_speed.shape
        counts = mesh.shape
        block = shape[:2] + (shape[2] // counts["ex"], shape[3] // counts["ey"], shape[4] // counts["mode"])
        sz = Sizes(counts, block)
        return jax.shard_map(
            functools.partial(on_device, sz, host_tables(sz)),
            mesh=mesh,
            in_specs=(spec, spec),
            out_specs=spec,
            check_vma=False,
        )(stream_speed, normal_speed)

    return whole
```

```python
import functools
import math

import jax
import jax.numpy as jnp
import ml_dtypes
import numpy as np
from jax import lax
from jax.experimental import pallas as pl
from jax.experimental.pallas import tpu as pltpu
from jax.sharding import PartitionSpec as P

BF16 = ml_dtypes.bfloat16

element_width = 2.0
shift_base = 10.0
span_rate = 0.0125


def legendre_pair(degree, points):
    before = points * 0.0 + 1.0
    current = points.copy()
    for step in range(1, degree):
        upcoming = ((2 * step + 1) * points * current - step * before) / (step + 1)
        before = current
        current = upcoming
    return (current, before)


def legendre_slope(degree, points):
    current, before = legendre_pair(degree, points)
    return (current, degree * (points * current - before) / (points * points - 1.0))


def lobatto_points(order):
    guesses = -np.cos(np.pi * np.arange(1, order) / order)
    for step in range(60):
        current, slope = legendre_slope(order, guesses)
        second = (2.0 * guesses * slope - order * (order + 1) * current) / (1.0 - guesses * guesses)
        guesses = guesses - slope / second
    return guesses


def gauss_rule(count):
    guesses = -np.cos(np.pi * (np.arange(count) + 0.75) / (count + 0.5))
    for step in range(60):
        current, slope = legendre_slope(count, guesses)
        guesses = guesses - current / slope
    current, slope = legendre_slope(count, guesses)
    return (guesses, 2.0 / ((1.0 - guesses * guesses) * slope * slope))


def jacobi_eigen(matrix):
    size_n = matrix.shape[0]
    work = matrix.copy()
    vectors = np.eye(size_n)
    for sweep_number in range(20):
        for first in range(size_n):
            for second in range(first + 1, size_n):
                coupling = work[first, second]
                if abs(coupling) > 1e-300:
                    theta = (work[second, second] - work[first, first]) / (2.0 * coupling)
                    direction = 1.0 if theta >= 0.0 else -1.0
                    tangent = direction / (abs(theta) + np.sqrt(theta * theta + 1.0))
                    cosine = 1.0 / np.sqrt(tangent * tangent + 1.0)
                    sine = tangent * cosine
                    rotation = np.eye(size_n)
                    rotation[first, first] = cosine
                    rotation[second, second] = cosine
                    rotation[first, second] = sine
                    rotation[second, first] = -sine
                    work = rotation.T @ work @ rotation
                    vectors = vectors @ rotation
    diagonal_index = np.arange(size_n)
    return (work[diagonal_index, diagonal_index], vectors)


def extended_basis(stiffness, weights, left_width, centre_width, right_width):
    node_count = weights.shape[0]
    full_count = 3 * node_count - 2
    stiff_full = np.zeros((full_count, full_count))
    mass_full = np.zeros(full_count)
    for position, span_width in enumerate((left_width, centre_width, right_width)):
        if span_width > 0.0:
            first_node = position * (node_count - 1)
            stiff_full[
                first_node : first_node + node_count, first_node : first_node + node_count
            ] += stiffness * (2.0 / span_width)
            mass_full[first_node : first_node + node_count] += weights * (span_width / 2.0)
    low_index = node_count - 2
    high_index = low_index + node_count + 2
    stiff_ext = stiff_full[low_index:high_index, low_index:high_index].copy()
    mass_ext = mass_full[low_index:high_index].copy()
    frozen_list = []
    if left_width <= 0.0:
        frozen_list += [0, 1]
    if right_width <= 0.0:
        frozen_list += [node_count, node_count + 1]
    for frozen_index in frozen_list:
        stiff_ext[frozen_index, :] = 0.0
        stiff_ext[:, frozen_index] = 0.0
        stiff_ext[frozen_index, frozen_index] = 1.0
        mass_ext[frozen_index] = 1.0
    inverse_root = 1.0 / np.sqrt(mass_ext)
    lambdas, vectors = jacobi_eigen(inverse_root[:, None] * stiff_ext * inverse_root[None, :])
    return (inverse_root[:, None] * vectors, lambdas)


def spectral_tables(order, rows_total):
    inner_points = lobatto_points(order)
    points = np.concatenate([[-1.0], inner_points, [1.0]])
    values, unused_before = legendre_pair(order, points)
    weights = 2.0 / (order * (order + 1) * values**2)
    identity = np.eye(order + 1)
    point_gaps = points[:, None] - points[None, :] + identity
    derivative = values[:, None] / (values[None, :] * point_gaps) * (1.0 - identity)
    derivative[0, 0] = -order * (order + 1) / 4.0
    derivative[order, order] = order * (order + 1) / 4.0
    stiffness = derivative.T @ (weights[:, None] * derivative)
    gauss_points, gauss_weights = gauss_rule(3 * (order + 1) // 2)
    offsets = gauss_points[:, None, None] - points[None, None, :]
    numerators = np.prod(np.where(identity[None, :, :] > 0.5, 1.0, offsets), axis=2)
    denominators = np.prod(np.where(identity > 0.5, 1.0, points[:, None] - points[None, :]), axis=1)
    interp = numerators / denominators[None, :]
    heights = 0.6 + 1.4 * np.sin(np.pi * (np.arange(rows_total) + 0.5) / rows_total)
    basis_x, lambdas_x = extended_basis(
        stiffness, weights, element_width, element_width, element_width
    )
    basis_rows = []
    lambda_rows = []
    for row_number in range(rows_total):
        below = heights[row_number - 1] if row_number > 0 else 0.0
        above = heights[row_number + 1] if row_number < rows_total - 1 else 0.0
        basis_one, lambda_one = extended_basis(
            stiffness, weights, below, heights[row_number], above
        )
        basis_rows.append(basis_one)
        lambda_rows.append(lambda_one)
    return (
        derivative,
        interp,
        gauss_weights,
        weights,
        stiffness,
        basis_x,
        lambdas_x,
        np.stack(basis_rows),
        np.stack(lambda_rows),
        heights,
    )


PARTS = 8
LANES = 128


def ceil_to(count, step):
    return -(-count // step) * step


class Sizes:
    def __init__(self, mesh_shape, block_shape):
        self.n_mode, self.n_ex, self.n_ey = (mesh_shape[name] for name in ("mode", "ex", "ey"))
        self.nodes, _, self.elems, self.rows, self.planes = block_shape
        self.order = self.nodes - 1
        self.gauss = 3 * self.nodes // 2
        self.rows_total = self.rows * self.n_ey
        self.elems_total = self.elems * self.n_ex
        self.planes_total = self.planes * self.n_mode
        self.block_x = self.order * self.elems + 1
        full_y = self.order * self.rows + 1
        self.inner = [
            [j for j in range(full_y) if not (p == 0 and j == 0) and not (p == self.n_ey - 1 and j == full_y - 1)]
            for p in range(self.n_ey)
        ]
        self.block_y = max(len(found) for found in self.inner)
        share = -(-(self.block_x * self.block_y + 2) // self.n_mode)
        self.share = ceil_to(share, LANES if share > 64 else 32)
        self.lane_nodes = self.share * self.n_mode
        self.columns = 2 * self.planes
        self.spots = self.n_ex * self.n_ey
        self.own = self.columns // self.spots
        self.folds = self.own // PARTS
        self.fold_width = LANES // self.folds
        self.points = self.nodes + 2
        self.x_nodes = self.n_ex * self.block_x
        self.x_pad = ceil_to(self.x_nodes, 16)
        self.x_eig = self.elems_total * self.points
        self.y_eig = self.rows_total * self.points
        self.fine = ceil_to(self.gauss * self.gauss, 16)
        assert self.own == PARTS * self.folds and self.x_eig % 16 == 0
        assert max(self.y_eig, self.n_ey * self.block_y) <= self.fold_width
        assert 2 * self.planes == LANES


def high_low(table):
    high = np.asarray(table, np.float32).astype(BF16)
    low = (np.asarray(table, np.float64) - high.astype(np.float64)).astype(BF16)
    return high, low


def beside(table):
    high, low = high_low(table)
    return np.concatenate([high, high, low], 1)


def host_tables(sz):
    derivative, interp, gauss_weights, weights, stiffness, basis_x, lam_x, basis_y, lam_y, heights = spectral_tables(
        sz.order, sz.rows_total
    )
    nodes, fine, points = sz.nodes, sz.fine, sz.points
    gauss_count = sz.gauss**2
    lift = np.zeros((3 * fine, nodes * nodes))
    lift[:gauss_count] = np.kron(interp, interp)
    lift[fine : fine + gauss_count] = np.kron(interp @ derivative, interp)
    lift[2 * fine : 2 * fine + gauss_count] = np.kron(interp, interp @ derivative)
    back = np.zeros((sz.n_ey, nodes * sz.block_y, sz.rows * fine))
    weighted = interp.T * gauss_weights[None, :]
    for place in range(sz.n_ey):
        for f in range(sz.rows):
            for jj, j in enumerate(sz.inner[place]):
                b = j - sz.order * f
                if 0 <= b < nodes:
                    back[place, jj :: sz.block_y, f * fine : f * fine + gauss_count] = -np.kron(
                        weighted, weighted[b : b + 1]
                    )
    grid_x, grid_y = sz.order * sz.elems_total, sz.order * sz.rows_total + 1
    to_x, stiff_x, mass_x = np.zeros((sz.x_eig, grid_x)), np.zeros((grid_x, grid_x)), np.zeros(grid_x)
    for e in range(sz.elems_total):
        for t in range(points):
            to_x[e * points : (e + 1) * points, (sz.order * e + t - 1) % grid_x] += basis_x[t]
        index = (sz.order * e + np.arange(nodes)) % grid_x
        stiff_x[np.ix_(index, index)] += stiffness * (2.0 / element_width)
        mass_x[index] += weights * (element_width / 2.0)
    to_y, stiff_y, mass_y = np.zeros((sz.y_eig, grid_y)), np.zeros((grid_y, grid_y)), np.zeros(grid_y)
    for f in range(sz.rows_total):
        for t in range(points):
            y = sz.order * f + t - 1
            if 0 < y < grid_y - 1:
                to_y[f * points : (f + 1) * points, y] = basis_y[f][t]
        index = sz.order * f + np.arange(nodes)
        stiff_y[np.ix_(index, index)] += stiffness * (2.0 / heights[f])
        mass_y[index] += weights * (heights[f] / 2.0)
    stiff_xx, mass_xx = to_x @ stiff_x @ to_x.T, (to_x * mass_x) @ to_x.T
    stiff_yy, mass_yy = to_y @ stiff_y @ to_y.T, (to_y * mass_y) @ to_y.T
    list_x = [(sz.order * sz.elems * p + i) % grid_x for p in range(sz.n_ex) for i in range(sz.block_x)]
    block_x = np.zeros((sz.x_eig, sz.x_pad))
    block_x[:, : sz.x_nodes] = to_x[:, list_x]
    width, folds = sz.fold_width, sz.folds
    block_y = np.zeros((width, width))
    for place in range(sz.n_ey):
        for jj, j in enumerate(sz.inner[place]):
            block_y[place * sz.block_y + jj, : sz.y_eig] = to_y[:, sz.order * sz.rows * place + j]

    def folded(table):
        padded = np.zeros((width, width))
        padded[: table.shape[0], : table.shape[1]] = table
        return np.kron(np.eye(folds), padded)

    def one_dot(table):
        high, low = high_low(folded(table))
        return np.block([[high, low], [high, np.zeros_like(low)]]).astype(BF16)

    mass_pair, stiff_pair = high_low(folded(mass_yy)), high_low(folded(stiff_yy))
    heads = np.concatenate([mass_pair[0], stiff_pair[0]], 1)
    tails = np.concatenate([mass_pair[1], stiff_pair[1]], 1)
    lam_lanes = np.ones((1, folds, width))
    lam_lanes[:, :, : sz.y_eig] = lam_y.reshape(-1)
    planes_total = sz.planes_total
    turns = np.arange(planes_total)[None, :] * np.arange(planes_total // 2)[:, None] % planes_total
    angles = turns * (2.0 * math.pi / planes_total)
    waves = np.stack([np.cos(angles), -np.sin(angles)], 1).reshape(planes_total, planes_total) / planes_total
    return dict(
        heights=np.asarray(heights, np.float32),
        lift=beside(lift),
        back=np.stack([beside(table) for table in back]),
        waves=np.stack(high_low(waves)),
        in_y=one_dot(block_y),
        in_x=beside(block_x),
        pair_y=np.concatenate([heads, heads, tails], 0),
        pair_x=beside(np.concatenate([stiff_xx, mass_xx], 1)),
        out_y=one_dot(block_y.T),
        out_x=beside(block_x.T),
        lam_x=np.asarray(np.tile(lam_x, sz.elems_total)[:, None] * np.ones((1, LANES)), np.float32),
        lam_y=np.asarray(lam_lanes.reshape(1, LANES), np.float32),
    )


def split(value):
    high = value.astype(jnp.bfloat16)
    low = (value - high.astype(jnp.float32)).astype(jnp.bfloat16)
    return high, low


def dot(left, right):
    return lax.dot_general(left, right, (((1,), (0,)), ((), ())), preferred_element_type=jnp.float32)


def below(value):
    high, low = split(value)
    return jnp.concatenate([high, low, high], 0)


def along(value):
    return jnp.concatenate(split(value), 1)


def lane_index(shape):
    return lax.broadcasted_iota(jnp.int32, shape, len(shape) - 1)


def advect_kernel(sz, heights_ref, stream_ref, normal_ref, lift_ref, back_ref, out_ref, total_ref):
    place = lax.axis_index("ey")
    count, fine, rows = sz.nodes * sz.nodes, sz.fine, sz.rows
    spots = sz.elems * rows
    half = lane_index((fine, LANES)) < sz.planes
    column, step = sz.nodes * sz.block_y, sz.order * sz.block_y
    length = sz.block_x * sz.block_y
    total_ref[pl.ds(length // 8 * 8, sz.lane_nodes - length // 8 * 8), :] = jnp.zeros(
        (sz.lane_nodes - length // 8 * 8, LANES), jnp.float32
    )
    carry = None
    for e in range(sz.elems):
        speeds = jnp.concatenate(
            [
                ref[pl.ds(e * rows + f, count, stride=spots), :]
                for f in range(rows)
                for ref in (stream_ref, normal_ref)
            ],
            1,
        )
        values = dot(lift_ref[...], below(speeds))
        highs, lows = [], []
        for f in range(rows):
            height = heights_ref[place * rows + f]
            mine = values[:, f * LANES : (f + 1) * LANES]
            both, slope_x, slope_y = mine[:fine], mine[fine : 2 * fine], mine[2 * fine :]
            turned = pltpu.roll(both, sz.planes, 1)
            stream = jnp.where(half, both, turned)
            normal = jnp.where(half, turned, both)
            high, low = split((stream * (height * 0.5)) * slope_x + (normal * (element_width * 0.5)) * slope_y)
            highs.append(high)
            lows.append(low)
        weak = dot(back_ref[place], jnp.concatenate(highs + lows + highs, 0))
        if carry is not None:
            head = jnp.concatenate([carry, jnp.zeros((column - carry.shape[0], LANES), jnp.float32)], 0)
            weak = weak + head
        if e < sz.elems - 1:
            total_ref[pl.ds(e * step, step), :] = weak[:step]
            carry = weak[step:]
        else:
            total_ref[pl.ds(e * step, column), :] = weak
    for z in range(sz.n_mode):
        out_ref[z] = total_ref[pl.ds(z * sz.share, sz.share), :]


def transform_kernel(sz, weak_ref, waves_ref, out_ref, mixed_ref):
    turned = [weak_ref[z].T for z in range(sz.n_mode)]
    modes = sz.planes_total
    for k in range(2):
        signal = jnp.concatenate([piece[k * sz.planes : (k + 1) * sz.planes] for piece in turned], 0)
        high, low = split(signal)
        part = dot(waves_ref[0], high) + dot(waves_ref[0], low) + dot(waves_ref[1], high)
        for t in range(mixed_ref.shape[0]):
            tile = part[:, t * LANES : (t + 1) * LANES]
            mixed_ref[t, pl.ds(k, modes, stride=2), pl.ds(0, tile.shape[1])] = tile
    for t in range(mixed_ref.shape[0]):
        last = min(LANES, sz.share - t * LANES)
        out_ref[:, pl.ds(t * LANES, last)] = mixed_ref[t, :, pl.ds(0, last)]


def smooth_kernel(
    sz,
    terms_ref,
    in_y_ref,
    in_x_ref,
    pair_y_ref,
    pair_x_ref,
    out_y_ref,
    out_x_ref,
    lam_x_ref,
    lam_y_ref,
    out_ref,
    field_ref,
    first_ref,
    work_ref,
):
    width, folds, strip = sz.fold_width, sz.folds, sz.block_y
    tiles = -(-sz.lane_nodes // LANES)
    lanes = lane_index((PARTS, LANES))
    x_pad, x_eig = sz.x_pad, sz.x_eig
    device = (lax.axis_index("mode") * sz.n_ex + lax.axis_index("ex")) * sz.n_ey + lax.axis_index("ey")
    first_mode = device * (sz.own // 4)

    for c in range(PARTS):
        field_ref[pl.ds(c * x_pad + sz.x_nodes, x_pad - sz.x_nodes), :] = jnp.zeros(
            (x_pad - sz.x_nodes, LANES), jnp.float32
        )
    for p in range(sz.n_ex):
        held = {}
        for q in range(sz.n_ey):
            for fold in range(folds):
                whole = jnp.concatenate(
                    [
                        terms_ref[(z * sz.n_ex + p) * sz.n_ey + q, pl.ds(fold * PARTS, PARTS), :]
                        for z in range(sz.n_mode)
                    ],
                    1,
                )
                held[q, fold] = [whole[:, t * LANES : (t + 1) * LANES] for t in range(tiles)]
        for i in range(sz.block_x):
            start = i * strip
            t, r = start // LANES, start % LANES
            result = jnp.zeros((PARTS, LANES), jnp.float32)
            for fold in range(folds):
                for q in range(sz.n_ey):
                    source = held[q, fold][t]
                    if r + strip > LANES:
                        source = jnp.where(lanes >= r, source, held[q, fold][t + 1])
                    goal = fold * width + q * strip
                    moved = pltpu.roll(source, (goal - r) % LANES, 1) if goal != r else source
                    result = jnp.where((lanes >= goal) & (lanes < goal + strip), moved, result)
            field_ref[pl.ds(p * sz.block_x + i, PARTS, stride=x_pad), :] = result

    parts = dot(along(field_ref[...]), in_y_ref[...])
    field_ref[...] = parts[:, :LANES] + parts[:, LANES:]
    fold_of_lane = lane_index((1, LANES)) // width
    shifts, inverses = [], []
    for group in range(PARTS // 4):
        mode = (first_mode + fold_of_lane * (PARTS // 4) + group).astype(jnp.float32)
        shift = shift_base + (span_rate * mode) ** 2
        shifts.append(shift)
        inverses.append(1.0 / (lam_x_ref[...] + (lam_y_ref[...] + shift)))
    for c in range(0, PARTS, 2):
        pair = jnp.concatenate([field_ref[pl.ds((c + d) * x_pad, x_pad), :] for d in range(2)], 1)
        forced = dot(in_x_ref[...], below(pair))
        for d in range(2):
            mine = forced[:, d * LANES : (d + 1) * LANES]
            first_ref[pl.ds((c + d) * x_eig, x_eig), :] = mine
            work_ref[pl.ds((c + d) * x_eig, x_eig), :] = mine * inverses[(c + d) // 4]
    for c in range(0, PARTS, 2):
        shift = shifts[c // 4]
        masses, stiffs = [], []
        for d in range(2):
            high, low = split(work_ref[pl.ds((c + d) * x_eig, x_eig), :])
            both = dot(jnp.concatenate([high, low, high], 1), pair_y_ref[...])
            masses.append(both[:, :LANES])
            stiffs.append(both[:, LANES:] + shift * both[:, :LANES])
        stacked = jnp.concatenate([jnp.concatenate(masses, 1), jnp.concatenate(stiffs, 1)], 0)
        applied = dot(pair_x_ref[...], below(stacked))
        for d in range(2):
            rows = pl.ds((c + d) * x_eig, x_eig)
            total = (2.0 * first_ref[rows, :] - applied[:, d * LANES : (d + 1) * LANES]) * inverses[c // 4]
            parts = dot(along(total), out_y_ref[...])
            work_ref[rows, :] = parts[:, :LANES] + parts[:, LANES:]
        pair = jnp.concatenate([work_ref[pl.ds((c + d) * x_eig, x_eig), :] for d in range(2)], 1)
        solved = dot(out_x_ref[...], below(pair))
        for d in range(2):
            field_ref[pl.ds((c + d) * x_pad, x_pad), :] = solved[:, d * LANES : (d + 1) * LANES]

    for p in range(sz.n_ex):
        made = {}
        for i in range(sz.block_x):
            source = field_ref[pl.ds(p * sz.block_x + i, PARTS, stride=x_pad), :]
            for q in range(sz.n_ey):
                begin = i * strip + sz.inner[q][0]
                count = len(sz.inner[q])
                t, r = begin // LANES, begin % LANES
                for fold in range(folds):
                    origin = fold * width + q * strip
                    moved = pltpu.roll(source, (r - origin) % LANES, 1) if origin != r else source
                    for tile, low, high in ((t, r, r + count), (t + 1, 0, r + count - LANES)):
                        if high > 0:
                            old = made.get((q, fold, tile))
                            if old is None:
                                old = jnp.zeros((PARTS, LANES), jnp.float32)
                            made[q, fold, tile] = jnp.where((lanes >= low) & (lanes < high), moved, old)
        for (q, fold, tile), value in made.items():
            last = min(LANES, sz.lane_nodes - tile * LANES)
            out_ref[p * sz.n_ey + q, pl.ds(fold * PARTS, PARTS), pl.ds(tile * LANES, last)] = value[:, :last]


def spread_kernel(sz, solved_ref, out_ref, turned_ref):
    place = lax.axis_index("ey")
    turned_ref[...] = solved_ref[...].T
    spots = sz.elems * sz.rows
    for e in range(sz.elems):
        for f in range(sz.rows):
            for a in range(sz.nodes):
                start = sz.block_y * (sz.order * e + a) + sz.order * f
                out_ref[pl.ds(a * sz.nodes * spots + e * sz.rows + f, sz.nodes, stride=spots), :] = turned_ref[
                    pl.ds(start, sz.nodes), :
                ]
    blank = jnp.zeros((sz.elems, LANES), jnp.float32)

    @pl.when(place == 0)
    def _():
        for a in range(sz.nodes):
            out_ref[pl.ds(a * sz.nodes * spots, sz.elems, stride=sz.rows), :] = blank

    @pl.when(place == sz.n_ey - 1)
    def _():
        for a in range(sz.nodes):
            first = ((a + 1) * sz.nodes - 1) * spots + sz.rows - 1
            out_ref[pl.ds(first, sz.elems, stride=sz.rows), :] = blank


def call(kernel, out_shape, operands, scratch=(), scalars=0):
    vmem = pl.BlockSpec(memory_space=pltpu.VMEM)
    smem = pl.BlockSpec(memory_space=pltpu.SMEM)
    return pl.pallas_call(
        kernel,
        out_shape=jax.ShapeDtypeStruct(out_shape, jnp.float32),
        in_specs=[smem] * scalars + [vmem] * (len(operands) - scalars),
        out_specs=vmem,
        scratch_shapes=[pltpu.VMEM(shape, jnp.float32) for shape in scratch],
        compiler_params=pltpu.CompilerParams(vmem_limit_bytes=16 * 2**20),
    )(*operands)


def on_device(sz, tables, stream_speed, normal_speed):
    flat = sz.nodes * sz.nodes * sz.elems * sz.rows
    table = {name: jnp.asarray(value) for name, value in tables.items()}
    weak = call(
        functools.partial(advect_kernel, sz),
        (sz.n_mode, sz.share, LANES),
        [
            table["heights"],
            stream_speed.reshape(flat, sz.planes),
            normal_speed.reshape(flat, sz.planes),
            table["lift"],
            table["back"],
        ],
        [(sz.lane_nodes, LANES)],
        scalars=1,
    )
    weak = lax.all_to_all(weak, "mode", split_axis=0, concat_axis=0, tiled=True)
    spectra = call(
        functools.partial(transform_kernel, sz),
        (2 * sz.planes_total, sz.share),
        [weak, table["waves"]],
        [(-(-sz.share // LANES), 2 * sz.planes_total, LANES)],
    )
    everyone = ("mode", "ex", "ey")
    spectra = spectra.reshape(sz.n_mode * sz.spots, sz.own, sz.share)
    terms = lax.all_to_all(spectra, everyone, split_axis=0, concat_axis=0, tiled=True)
    names = ("in_y", "in_x", "pair_y", "pair_x", "out_y", "out_x", "lam_x", "lam_y")
    solved = call(
        functools.partial(smooth_kernel, sz),
        (sz.spots, sz.own, sz.lane_nodes),
        [terms] + [table[name] for name in names],
        [(PARTS * sz.x_pad, LANES), (PARTS * sz.x_eig, LANES), (PARTS * sz.x_eig, LANES)],
    )
    solved = lax.all_to_all(solved, ("ex", "ey"), split_axis=0, concat_axis=0, tiled=True)
    out = call(
        functools.partial(spread_kernel, sz),
        (flat, LANES),
        [solved.reshape(sz.columns, sz.lane_nodes)],
        [(sz.lane_nodes, LANES)],
    )
    return out.reshape(sz.nodes, sz.nodes, sz.elems, sz.rows, sz.columns)


def solution(mesh):
    spec = P(None, None, "ex", "ey", "mode")

    def whole(stream_speed, normal_speed):
        shape = stream_speed.shape
        counts = mesh.shape
        block = shape[:2] + (shape[2] // counts["ex"], shape[3] // counts["ey"], shape[4] // counts["mode"])
        sz = Sizes(counts, block)
        return jax.shard_map(
            functools.partial(on_device, sz, host_tables(sz)),
            mesh=mesh,
            in_specs=(spec, spec),
            out_specs=spec,
            check_vma=False,
        )(stream_speed, normal_speed)

    return whole
```

```python
import functools
import math

import jax
import jax.numpy as jnp
import ml_dtypes
import numpy as np
from jax import lax
from jax.experimental import pallas as pl
from jax.experimental.pallas import tpu as pltpu
from jax.sharding import PartitionSpec as P

BF16 = ml_dtypes.bfloat16

element_width = 2.0
shift_base = 10.0
span_rate = 0.0125


def legendre_pair(degree, points):
    before = points * 0.0 + 1.0
    current = points.copy()
    for step in range(1, degree):
        upcoming = ((2 * step + 1) * points * current - step * before) / (step + 1)
        before = current
        current = upcoming
    return (current, before)


def legendre_slope(degree, points):
    current, before = legendre_pair(degree, points)
    return (current, degree * (points * current - before) / (points * points - 1.0))


def lobatto_points(order):
    guesses = -np.cos(np.pi * np.arange(1, order) / order)
    for step in range(60):
        current, slope = legendre_slope(order, guesses)
        second = (2.0 * guesses * slope - order * (order + 1) * current) / (1.0 - guesses * guesses)
        guesses = guesses - slope / second
    return guesses


def gauss_rule(count):
    guesses = -np.cos(np.pi * (np.arange(count) + 0.75) / (count + 0.5))
    for step in range(60):
        current, slope = legendre_slope(count, guesses)
        guesses = guesses - current / slope
    current, slope = legendre_slope(count, guesses)
    return (guesses, 2.0 / ((1.0 - guesses * guesses) * slope * slope))


def jacobi_eigen(matrix):
    size_n = matrix.shape[0]
    work = matrix.copy()
    vectors = np.eye(size_n)
    for sweep_number in range(20):
        for first in range(size_n):
            for second in range(first + 1, size_n):
                coupling = work[first, second]
                if abs(coupling) > 1e-300:
                    theta = (work[second, second] - work[first, first]) / (2.0 * coupling)
                    direction = 1.0 if theta >= 0.0 else -1.0
                    tangent = direction / (abs(theta) + np.sqrt(theta * theta + 1.0))
                    cosine = 1.0 / np.sqrt(tangent * tangent + 1.0)
                    sine = tangent * cosine
                    rotation = np.eye(size_n)
                    rotation[first, first] = cosine
                    rotation[second, second] = cosine
                    rotation[first, second] = sine
                    rotation[second, first] = -sine
                    work = rotation.T @ work @ rotation
                    vectors = vectors @ rotation
    diagonal_index = np.arange(size_n)
    return (work[diagonal_index, diagonal_index], vectors)


def extended_basis(stiffness, weights, left_width, centre_width, right_width):
    node_count = weights.shape[0]
    full_count = 3 * node_count - 2
    stiff_full = np.zeros((full_count, full_count))
    mass_full = np.zeros(full_count)
    for position, span_width in enumerate((left_width, centre_width, right_width)):
        if span_width > 0.0:
            first_node = position * (node_count - 1)
            stiff_full[
                first_node : first_node + node_count, first_node : first_node + node_count
            ] += stiffness * (2.0 / span_width)
            mass_full[first_node : first_node + node_count] += weights * (span_width / 2.0)
    low_index = node_count - 2
    high_index = low_index + node_count + 2
    stiff_ext = stiff_full[low_index:high_index, low_index:high_index].copy()
    mass_ext = mass_full[low_index:high_index].copy()
    frozen_list = []
    if left_width <= 0.0:
        frozen_list += [0, 1]
    if right_width <= 0.0:
        frozen_list += [node_count, node_count + 1]
    for frozen_index in frozen_list:
        stiff_ext[frozen_index, :] = 0.0
        stiff_ext[:, frozen_index] = 0.0
        stiff_ext[frozen_index, frozen_index] = 1.0
        mass_ext[frozen_index] = 1.0
    inverse_root = 1.0 / np.sqrt(mass_ext)
    lambdas, vectors = jacobi_eigen(inverse_root[:, None] * stiff_ext * inverse_root[None, :])
    return (inverse_root[:, None] * vectors, lambdas)


def spectral_tables(order, rows_total):
    inner_points = lobatto_points(order)
    points = np.concatenate([[-1.0], inner_points, [1.0]])
    values, unused_before = legendre_pair(order, points)
    weights = 2.0 / (order * (order + 1) * values**2)
    identity = np.eye(order + 1)
    point_gaps = points[:, None] - points[None, :] + identity
    derivative = values[:, None] / (values[None, :] * point_gaps) * (1.0 - identity)
    derivative[0, 0] = -order * (order + 1) / 4.0
    derivative[order, order] = order * (order + 1) / 4.0
    stiffness = derivative.T @ (weights[:, None] * derivative)
    gauss_points, gauss_weights = gauss_rule(3 * (order + 1) // 2)
    offsets = gauss_points[:, None, None] - points[None, None, :]
    numerators = np.prod(np.where(identity[None, :, :] > 0.5, 1.0, offsets), axis=2)
    denominators = np.prod(np.where(identity > 0.5, 1.0, points[:, None] - points[None, :]), axis=1)
    interp = numerators / denominators[None, :]
    heights = 0.6 + 1.4 * np.sin(np.pi * (np.arange(rows_total) + 0.5) / rows_total)
    basis_x, lambdas_x = extended_basis(
        stiffness, weights, element_width, element_width, element_width
    )
    basis_rows = []
    lambda_rows = []
    for row_number in range(rows_total):
        below = heights[row_number - 1] if row_number > 0 else 0.0
        above = heights[row_number + 1] if row_number < rows_total - 1 else 0.0
        basis_one, lambda_one = extended_basis(
            stiffness, weights, below, heights[row_number], above
        )
        basis_rows.append(basis_one)
        lambda_rows.append(lambda_one)
    return (
        derivative,
        interp,
        gauss_weights,
        weights,
        stiffness,
        basis_x,
        lambdas_x,
        np.stack(basis_rows),
        np.stack(lambda_rows),
        heights,
    )


PARTS = 8
LANES = 128


def ceil_to(count, step):
    return -(-count // step) * step


class Sizes:
    def __init__(self, mesh_shape, block_shape):
        self.n_mode, self.n_ex, self.n_ey = (mesh_shape[name] for name in ("mode", "ex", "ey"))
        self.nodes, _, self.elems, self.rows, self.planes = block_shape
        self.order = self.nodes - 1
        self.gauss = 3 * self.nodes // 2
        self.rows_total = self.rows * self.n_ey
        self.elems_total = self.elems * self.n_ex
        self.planes_total = self.planes * self.n_mode
        self.block_x = self.order * self.elems + 1
        full_y = self.order * self.rows + 1
        self.inner = [
            [j for j in range(full_y) if not (p == 0 and j == 0) and not (p == self.n_ey - 1 and j == full_y - 1)]
            for p in range(self.n_ey)
        ]
        self.block_y = max(len(found) for found in self.inner)
        share = -(-(self.block_x * self.block_y + 2) // self.n_mode)
        self.share = ceil_to(share, LANES if share > 64 else 32)
        self.lane_nodes = self.share * self.n_mode
        self.columns = 2 * self.planes
        self.spots = self.n_ex * self.n_ey
        self.own = self.columns // self.spots
        self.folds = self.own // PARTS
        self.fold_width = LANES // self.folds
        self.points = self.nodes + 2
        self.x_nodes = self.n_ex * self.block_x
        self.x_pad = ceil_to(self.x_nodes, 16)
        self.x_eig = self.elems_total * self.points
        self.y_eig = self.rows_total * self.points
        self.fine = ceil_to(self.gauss * self.gauss, 16)
        assert self.own == PARTS * self.folds and self.x_eig % 16 == 0
        assert max(self.y_eig, self.n_ey * self.block_y) <= self.fold_width
        assert 2 * self.planes == LANES and self.n_ey == 2


def high_low(table):
    high = np.asarray(table, np.float32).astype(BF16)
    low = (np.asarray(table, np.float64) - high.astype(np.float64)).astype(BF16)
    return high, low


def beside(table):
    high, low = high_low(table)
    return np.concatenate([high, high, low], 1)


def host_tables(sz):
    derivative, interp, gauss_weights, weights, stiffness, basis_x, lam_x, basis_y, lam_y, heights = spectral_tables(
        sz.order, sz.rows_total
    )
    nodes, fine, points = sz.nodes, sz.fine, sz.points
    gauss_count = sz.gauss**2
    lift = np.zeros((3 * fine, nodes * nodes))
    lift[:gauss_count] = np.kron(interp, interp)
    lift[fine : fine + gauss_count] = np.kron(interp @ derivative, interp)
    lift[2 * fine : 2 * fine + gauss_count] = np.kron(interp, interp @ derivative)
    back = np.zeros((sz.n_ey, nodes * sz.block_y, sz.rows * fine))
    weighted = interp.T * gauss_weights[None, :]
    for place in range(sz.n_ey):
        for f in range(sz.rows):
            for jj, j in enumerate(sz.inner[place]):
                b = j - sz.order * f
                if 0 <= b < nodes:
                    back[place, jj :: sz.block_y, f * fine : f * fine + gauss_count] = -np.kron(
                        weighted, weighted[b : b + 1]
                    )
    grid_x, grid_y = sz.order * sz.elems_total, sz.order * sz.rows_total + 1
    to_x, stiff_x, mass_x = np.zeros((sz.x_eig, grid_x)), np.zeros((grid_x, grid_x)), np.zeros(grid_x)
    for e in range(sz.elems_total):
        for t in range(points):
            to_x[e * points : (e + 1) * points, (sz.order * e + t - 1) % grid_x] += basis_x[t]
        index = (sz.order * e + np.arange(nodes)) % grid_x
        stiff_x[np.ix_(index, index)] += stiffness * (2.0 / element_width)
        mass_x[index] += weights * (element_width / 2.0)
    to_y, stiff_y, mass_y = np.zeros((sz.y_eig, grid_y)), np.zeros((grid_y, grid_y)), np.zeros(grid_y)
    for f in range(sz.rows_total):
        for t in range(points):
            y = sz.order * f + t - 1
            if 0 < y < grid_y - 1:
                to_y[f * points : (f + 1) * points, y] = basis_y[f][t]
        index = sz.order * f + np.arange(nodes)
        stiff_y[np.ix_(index, index)] += stiffness * (2.0 / heights[f])
        mass_y[index] += weights * (heights[f] / 2.0)
    stiff_xx, mass_xx = to_x @ stiff_x @ to_x.T, (to_x * mass_x) @ to_x.T
    stiff_yy, mass_yy = to_y @ stiff_y @ to_y.T, (to_y * mass_y) @ to_y.T
    list_x = [(sz.order * sz.elems * p + i) % grid_x for p in range(sz.n_ex) for i in range(sz.block_x)]
    block_x = np.zeros((sz.x_eig, sz.x_pad))
    block_x[:, : sz.x_nodes] = to_x[:, list_x]
    width, folds = sz.fold_width, sz.folds
    block_y = np.zeros((width, width))
    for place in range(sz.n_ey):
        for jj, j in enumerate(sz.inner[place]):
            block_y[place * sz.block_y + jj, : sz.y_eig] = to_y[:, sz.order * sz.rows * place + j]

    def folded(table):
        padded = np.zeros((width, width))
        padded[: table.shape[0], : table.shape[1]] = table
        return np.kron(np.eye(folds), padded)

    def one_dot(table):
        high, low = high_low(folded(table))
        return np.block([[high, low], [high, np.zeros_like(low)]]).astype(BF16)

    mass_pair, stiff_pair = high_low(folded(mass_yy)), high_low(folded(stiff_yy))
    heads = np.concatenate([mass_pair[0], stiff_pair[0]], 1)
    tails = np.concatenate([mass_pair[1], stiff_pair[1]], 1)
    lam_lanes = np.ones((1, folds, width))
    lam_lanes[:, :, : sz.y_eig] = lam_y.reshape(-1)
    planes_total = sz.planes_total
    turns = np.arange(planes_total)[None, :] * np.arange(planes_total // 2)[:, None] % planes_total
    angles = turns * (2.0 * math.pi / planes_total)
    waves = np.stack([np.cos(angles), -np.sin(angles)], 1).reshape(planes_total, planes_total) / planes_total
    return dict(
        heights=np.asarray(heights, np.float32),
        lift=beside(lift),
        back=np.stack([beside(table) for table in back]),
        waves=np.stack(high_low(waves)),
        in_y=one_dot(block_y),
        in_x=beside(block_x),
        pair_y=np.concatenate([heads, heads, tails], 0),
        pair_x=beside(np.concatenate([stiff_xx, mass_xx], 1)),
        out_y=one_dot(block_y.T),
        out_x=beside(block_x.T),
        lam_x=np.asarray(np.tile(lam_x, sz.elems_total)[:, None] * np.ones((1, LANES)), np.float32),
        lam_y=np.asarray(lam_lanes.reshape(1, LANES), np.float32),
    )


def split(value):
    high = value.astype(jnp.bfloat16)
    low = (value - high.astype(jnp.float32)).astype(jnp.bfloat16)
    return high, low


def dot(left, right):
    return lax.dot_general(left, right, (((1,), (0,)), ((), ())), preferred_element_type=jnp.float32)


def below(value):
    high, low = split(value)
    return jnp.concatenate([high, low, high], 0)


def along(value):
    return jnp.concatenate(split(value), 1)


def lane_index(shape):
    return lax.broadcasted_iota(jnp.int32, shape, len(shape) - 1)


def advect_kernel(
    sz,
    heights_ref,
    stream_hbm,
    normal_hbm,
    lift_hbm,
    back_hbm,
    out_ref,
    total_ref,
    stream_ref,
    normal_ref,
    lift_ref,
    back_ref,
    arrived,
):
    place = lax.axis_index("ey")
    fetched = [
        pltpu.make_async_copy(source, target, arrived.at[i])
        for i, (source, target) in enumerate(
            (
                (stream_hbm, stream_ref),
                (normal_hbm, normal_ref),
                (lift_hbm, lift_ref),
                (back_hbm.at[place], back_ref),
            )
        )
    ]
    for copy in fetched:
        copy.start()
    count, fine, rows = sz.nodes * sz.nodes, sz.fine, sz.rows
    spots = sz.elems * rows
    half = lane_index((fine, LANES)) < sz.planes
    column, step = sz.nodes * sz.block_y, sz.order * sz.block_y
    length = sz.block_x * sz.block_y
    total_ref[pl.ds(length // 8 * 8, sz.lane_nodes - length // 8 * 8), :] = jnp.zeros(
        (sz.lane_nodes - length // 8 * 8, LANES), jnp.float32
    )
    carry = None
    for copy in fetched[:3]:
        copy.wait()
    for e in range(sz.elems):
        speeds = jnp.concatenate(
            [
                ref[pl.ds(e * rows + f, count, stride=spots), :]
                for f in range(rows)
                for ref in (stream_ref, normal_ref)
            ],
            1,
        )
        values = dot(lift_ref[...], below(speeds))
        highs, lows = [], []
        for f in range(rows):
            height = heights_ref[place * rows + f]
            mine = values[:, f * LANES : (f + 1) * LANES]
            both, slope_x, slope_y = mine[:fine], mine[fine : 2 * fine], mine[2 * fine :]
            turned = pltpu.roll(both, sz.planes, 1)
            stream = jnp.where(half, both, turned)
            normal = jnp.where(half, turned, both)
            high, low = split((stream * (height * 0.5)) * slope_x + (normal * (element_width * 0.5)) * slope_y)
            highs.append(high)
            lows.append(low)
        if e == 0:
            fetched[3].wait()
        weak = dot(back_ref[...], jnp.concatenate(highs + lows + highs, 0))
        if carry is not None:
            head = jnp.concatenate([carry, jnp.zeros((column - carry.shape[0], LANES), jnp.float32)], 0)
            weak = weak + head
        if e < sz.elems - 1:
            total_ref[pl.ds(e * step, step), :] = weak[:step]
            carry = weak[step:]
        else:
            total_ref[pl.ds(e * step, column), :] = weak
    for z in range(sz.n_mode):
        out_ref[z] = total_ref[pl.ds(z * sz.share, sz.share), :]


def transform_kernel(sz, weak_ref, waves_ref, out_ref, mixed_ref):
    turned = [weak_ref[z].T for z in range(sz.n_mode)]
    modes = sz.planes_total
    for k in range(2):
        signal = jnp.concatenate([piece[k * sz.planes : (k + 1) * sz.planes] for piece in turned], 0)
        high, low = split(signal)
        part = dot(waves_ref[0], high) + dot(waves_ref[0], low) + dot(waves_ref[1], high)
        for t in range(mixed_ref.shape[0]):
            tile = part[:, t * LANES : (t + 1) * LANES]
            mixed_ref[t, pl.ds(k, modes, stride=2), pl.ds(0, tile.shape[1])] = tile
    for t in range(mixed_ref.shape[0]):
        last = min(LANES, sz.share - t * LANES)
        out_ref[:, pl.ds(t * LANES, last)] = mixed_ref[t, :, pl.ds(0, last)]


def smooth_kernel(
    sz,
    mine_ref,
    other_ref,
    in_y_ref,
    in_x_ref,
    pair_y_ref,
    pair_x_ref,
    out_y_ref,
    out_x_ref,
    lam_x_ref,
    lam_y_ref,
    out_ref,
    field_ref,
    first_ref,
    work_ref,
):
    width, folds, strip = sz.fold_width, sz.folds, sz.block_y
    tiles = -(-sz.lane_nodes // LANES)
    lanes = lane_index((PARTS, LANES))
    x_pad, x_eig = sz.x_pad, sz.x_eig
    place = lax.axis_index("ey")
    device = (lax.axis_index("mode") * sz.n_ex + lax.axis_index("ex")) * sz.n_ey + place
    first_mode = device * (sz.own // 4)

    for c in range(PARTS):
        field_ref[pl.ds(c * x_pad + sz.x_nodes, x_pad - sz.x_nodes), :] = jnp.zeros(
            (x_pad - sz.x_nodes, LANES), jnp.float32
        )
    for p in range(sz.n_ex):
        held = {}
        for q in range(sz.n_ey):
            for fold in range(folds):
                rows = pl.ds(pl.multiple_of(place * sz.own + fold * PARTS, PARTS), PARTS)
                whole = jnp.concatenate(
                    [
                        jnp.where(place == q, mine_ref[z * sz.n_ex + p, rows, :], other_ref[z * sz.n_ex + p, rows, :])
                        for z in range(sz.n_mode)
                    ],
                    1,
                )
                held[q, fold] = [whole[:, t * LANES : (t + 1) * LANES] for t in range(tiles)]
        for i in range(sz.block_x):
            start = i * strip
            t, r = start // LANES, start % LANES
            result = jnp.zeros((PARTS, LANES), jnp.float32)
            for fold in range(folds):
                for q in range(sz.n_ey):
                    source = held[q, fold][t]
                    if r + strip > LANES:
                        source = jnp.where(lanes >= r, source, held[q, fold][t + 1])
                    goal = fold * width + q * strip
                    moved = pltpu.roll(source, (goal - r) % LANES, 1) if goal != r else source
                    result = jnp.where((lanes >= goal) & (lanes < goal + strip), moved, result)
            field_ref[pl.ds(p * sz.block_x + i, PARTS, stride=x_pad), :] = result

    parts = dot(along(field_ref[...]), in_y_ref[...])
    field_ref[...] = parts[:, :LANES] + parts[:, LANES:]
    fold_of_lane = lane_index((1, LANES)) // width
    shifts, inverses = [], []
    for group in range(PARTS // 4):
        mode = (first_mode + fold_of_lane * (PARTS // 4) + group).astype(jnp.float32)
        shift = shift_base + (span_rate * mode) ** 2
        shifts.append(shift)
        inverses.append(1.0 / (lam_x_ref[...] + (lam_y_ref[...] + shift)))
    for c in range(0, PARTS, 2):
        pair = jnp.concatenate([field_ref[pl.ds((c + d) * x_pad, x_pad), :] for d in range(2)], 1)
        forced = dot(in_x_ref[...], below(pair))
        for d in range(2):
            mine = forced[:, d * LANES : (d + 1) * LANES]
            first_ref[pl.ds((c + d) * x_eig, x_eig), :] = mine
            work_ref[pl.ds((c + d) * x_eig, x_eig), :] = mine * inverses[(c + d) // 4]
    for c in range(0, PARTS, 2):
        shift = shifts[c // 4]
        masses, stiffs = [], []
        for d in range(2):
            high, low = split(work_ref[pl.ds((c + d) * x_eig, x_eig), :])
            both = dot(jnp.concatenate([high, low, high], 1), pair_y_ref[...])
            masses.append(both[:, :LANES])
            stiffs.append(both[:, LANES:] + shift * both[:, :LANES])
        stacked = jnp.concatenate([jnp.concatenate(masses, 1), jnp.concatenate(stiffs, 1)], 0)
        applied = dot(pair_x_ref[...], below(stacked))
        for d in range(2):
            rows = pl.ds((c + d) * x_eig, x_eig)
            total = (2.0 * first_ref[rows, :] - applied[:, d * LANES : (d + 1) * LANES]) * inverses[c // 4]
            parts = dot(along(total), out_y_ref[...])
            work_ref[rows, :] = parts[:, :LANES] + parts[:, LANES:]
        pair = jnp.concatenate([work_ref[pl.ds((c + d) * x_eig, x_eig), :] for d in range(2)], 1)
        solved = dot(out_x_ref[...], below(pair))
        for d in range(2):
            field_ref[pl.ds((c + d) * x_pad, x_pad), :] = solved[:, d * LANES : (d + 1) * LANES]

    for p in range(sz.n_ex):
        made = {}
        for i in range(sz.block_x):
            source = field_ref[pl.ds(p * sz.block_x + i, PARTS, stride=x_pad), :]
            for q in range(sz.n_ey):
                begin = i * strip + sz.inner[q][0]
                count = len(sz.inner[q])
                t, r = begin // LANES, begin % LANES
                for fold in range(folds):
                    origin = fold * width + q * strip
                    moved = pltpu.roll(source, (r - origin) % LANES, 1) if origin != r else source
                    for tile, low, high in ((t, r, r + count), (t + 1, 0, r + count - LANES)):
                        if high > 0:
                            old = made.get((q, fold, tile))
                            if old is None:
                                old = jnp.zeros((PARTS, LANES), jnp.float32)
                            made[q, fold, tile] = jnp.where((lanes >= low) & (lanes < high), moved, old)
        for (q, fold, tile), value in made.items():
            last = min(LANES, sz.lane_nodes - tile * LANES)
            out_ref[p, pl.ds(q * sz.own + fold * PARTS, PARTS), pl.ds(tile * LANES, last)] = value[:, :last]


def spread_kernel(sz, mine_ref, other_ref, out_ref, turned_ref):
    place = lax.axis_index("ey")
    rows = pl.ds(pl.multiple_of(place * sz.own, PARTS), sz.own)
    solved = [
        jnp.where(place == q, mine_ref[p, rows, :], other_ref[p, rows, :])
        for p in range(sz.n_ex)
        for q in range(sz.n_ey)
    ]
    turned_ref[...] = jnp.concatenate(solved, 0).T
    spots = sz.elems * sz.rows
    for e in range(sz.elems):
        for f in range(sz.rows):
            for a in range(sz.nodes):
                start = sz.block_y * (sz.order * e + a) + sz.order * f
                out_ref[pl.ds(a * sz.nodes * spots + e * sz.rows + f, sz.nodes, stride=spots), :] = turned_ref[
                    pl.ds(start, sz.nodes), :
                ]
    blank = jnp.zeros((sz.elems, LANES), jnp.float32)

    @pl.when(place == 0)
    def _():
        for a in range(sz.nodes):
            out_ref[pl.ds(a * sz.nodes * spots, sz.elems, stride=sz.rows), :] = blank

    @pl.when(place == sz.n_ey - 1)
    def _():
        for a in range(sz.nodes):
            first = ((a + 1) * sz.nodes - 1) * spots + sz.rows - 1
            out_ref[pl.ds(first, sz.elems, stride=sz.rows), :] = blank


def call(kernel, out_shape, operands, scratch=(), spaces=None):
    spaces = spaces or [pltpu.VMEM] * len(operands)
    return pl.pallas_call(
        kernel,
        out_shape=jax.ShapeDtypeStruct(out_shape, jnp.float32),
        in_specs=[pl.BlockSpec(memory_space=space) for space in spaces],
        out_specs=pl.BlockSpec(memory_space=pltpu.VMEM),
        scratch_shapes=[pltpu.VMEM(each, jnp.float32) if isinstance(each, tuple) else each for each in scratch],
        compiler_params=pltpu.CompilerParams(vmem_limit_bytes=16 * 2**20),
    )(*operands)


def on_device(sz, tables, stream_speed, normal_speed):
    flat = sz.nodes * sz.nodes * sz.elems * sz.rows
    swap = [(q, sz.n_ey - 1 - q) for q in range(sz.n_ey)]
    table = {name: jnp.asarray(value) for name, value in tables.items()}
    weak = call(
        functools.partial(advect_kernel, sz),
        (sz.n_mode, sz.share, LANES),
        [
            table["heights"],
            stream_speed.reshape(flat, sz.planes),
            normal_speed.reshape(flat, sz.planes),
            table["lift"],
            table["back"],
        ],
        [
            (sz.lane_nodes, LANES),
            (flat, sz.planes),
            (flat, sz.planes),
            pltpu.VMEM(tables["lift"].shape, jnp.bfloat16),
            pltpu.VMEM(tables["back"].shape[1:], jnp.bfloat16),
            pltpu.SemaphoreType.DMA((4,)),
        ],
        [pltpu.SMEM] + [pltpu.HBM] * 4,
    )
    weak = lax.all_to_all(weak, "mode", split_axis=0, concat_axis=0, tiled=True)
    spectra = call(
        functools.partial(transform_kernel, sz),
        (2 * sz.planes_total, sz.share),
        [weak, table["waves"]],
        [(-(-sz.share // LANES), 2 * sz.planes_total, LANES)],
    )
    spectra = spectra.reshape(sz.n_mode * sz.n_ex, sz.n_ey * sz.own, sz.share)
    terms = lax.all_to_all(spectra, ("mode", "ex"), split_axis=0, concat_axis=0, tiled=True)
    names = ("in_y", "in_x", "pair_y", "pair_x", "out_y", "out_x", "lam_x", "lam_y")
    solved = call(
        functools.partial(smooth_kernel, sz),
        (sz.n_ex, sz.n_ey * sz.own, sz.lane_nodes),
        [terms, lax.ppermute(terms, "ey", swap)] + [table[name] for name in names],
        [(PARTS * sz.x_pad, LANES), (PARTS * sz.x_eig, LANES), (PARTS * sz.x_eig, LANES)],
    )
    solved = lax.all_to_all(solved, "ex", split_axis=0, concat_axis=0, tiled=True)
    out = call(
        functools.partial(spread_kernel, sz),
        (flat, LANES),
        [solved, lax.ppermute(solved, "ey", swap)],
        [(sz.lane_nodes, LANES)],
    )
    return out.reshape(sz.nodes, sz.nodes, sz.elems, sz.rows, sz.columns)


def solution(mesh):
    spec = P(None, None, "ex", "ey", "mode")

    def whole(stream_speed, normal_speed):
        shape = stream_speed.shape
        counts = mesh.shape
        block = shape[:2] + (shape[2] // counts["ex"], shape[3] // counts["ey"], shape[4] // counts["mode"])
        sz = Sizes(counts, block)
        return jax.shard_map(
            functools.partial(on_device, sz, host_tables(sz)),
            mesh=mesh,
            in_specs=(spec, spec),
            out_specs=spec,
            check_vma=False,
        )(stream_speed, normal_speed)

    return whole
```

```python
import functools
import math

import jax
import jax.numpy as jnp
import ml_dtypes
import numpy as np
from jax import lax
from jax.experimental import pallas as pl
from jax.experimental.pallas import tpu as pltpu
from jax.sharding import PartitionSpec as P

BF16 = ml_dtypes.bfloat16

element_width = 2.0
shift_base = 10.0
span_rate = 0.0125


def legendre_pair(degree, points):
    before = points * 0.0 + 1.0
    current = points.copy()
    for step in range(1, degree):
        upcoming = ((2 * step + 1) * points * current - step * before) / (step + 1)
        before = current
        current = upcoming
    return (current, before)


def legendre_slope(degree, points):
    current, before = legendre_pair(degree, points)
    return (current, degree * (points * current - before) / (points * points - 1.0))


def lobatto_points(order):
    guesses = -np.cos(np.pi * np.arange(1, order) / order)
    for step in range(60):
        current, slope = legendre_slope(order, guesses)
        second = (2.0 * guesses * slope - order * (order + 1) * current) / (1.0 - guesses * guesses)
        guesses = guesses - slope / second
    return guesses


def gauss_rule(count):
    guesses = -np.cos(np.pi * (np.arange(count) + 0.75) / (count + 0.5))
    for step in range(60):
        current, slope = legendre_slope(count, guesses)
        guesses = guesses - current / slope
    current, slope = legendre_slope(count, guesses)
    return (guesses, 2.0 / ((1.0 - guesses * guesses) * slope * slope))


def jacobi_eigen(matrix):
    size_n = matrix.shape[0]
    work = matrix.copy()
    vectors = np.eye(size_n)
    for sweep_number in range(20):
        for first in range(size_n):
            for second in range(first + 1, size_n):
                coupling = work[first, second]
                if abs(coupling) > 1e-300:
                    theta = (work[second, second] - work[first, first]) / (2.0 * coupling)
                    direction = 1.0 if theta >= 0.0 else -1.0
                    tangent = direction / (abs(theta) + np.sqrt(theta * theta + 1.0))
                    cosine = 1.0 / np.sqrt(tangent * tangent + 1.0)
                    sine = tangent * cosine
                    rotation = np.eye(size_n)
                    rotation[first, first] = cosine
                    rotation[second, second] = cosine
                    rotation[first, second] = sine
                    rotation[second, first] = -sine
                    work = rotation.T @ work @ rotation
                    vectors = vectors @ rotation
    diagonal_index = np.arange(size_n)
    return (work[diagonal_index, diagonal_index], vectors)


def extended_basis(stiffness, weights, left_width, centre_width, right_width):
    node_count = weights.shape[0]
    full_count = 3 * node_count - 2
    stiff_full = np.zeros((full_count, full_count))
    mass_full = np.zeros(full_count)
    for position, span_width in enumerate((left_width, centre_width, right_width)):
        if span_width > 0.0:
            first_node = position * (node_count - 1)
            stiff_full[
                first_node : first_node + node_count, first_node : first_node + node_count
            ] += stiffness * (2.0 / span_width)
            mass_full[first_node : first_node + node_count] += weights * (span_width / 2.0)
    low_index = node_count - 2
    high_index = low_index + node_count + 2
    stiff_ext = stiff_full[low_index:high_index, low_index:high_index].copy()
    mass_ext = mass_full[low_index:high_index].copy()
    frozen_list = []
    if left_width <= 0.0:
        frozen_list += [0, 1]
    if right_width <= 0.0:
        frozen_list += [node_count, node_count + 1]
    for frozen_index in frozen_list:
        stiff_ext[frozen_index, :] = 0.0
        stiff_ext[:, frozen_index] = 0.0
        stiff_ext[frozen_index, frozen_index] = 1.0
        mass_ext[frozen_index] = 1.0
    inverse_root = 1.0 / np.sqrt(mass_ext)
    lambdas, vectors = jacobi_eigen(inverse_root[:, None] * stiff_ext * inverse_root[None, :])
    return (inverse_root[:, None] * vectors, lambdas)


def spectral_tables(order, rows_total):
    inner_points = lobatto_points(order)
    points = np.concatenate([[-1.0], inner_points, [1.0]])
    values, unused_before = legendre_pair(order, points)
    weights = 2.0 / (order * (order + 1) * values**2)
    identity = np.eye(order + 1)
    point_gaps = points[:, None] - points[None, :] + identity
    derivative = values[:, None] / (values[None, :] * point_gaps) * (1.0 - identity)
    derivative[0, 0] = -order * (order + 1) / 4.0
    derivative[order, order] = order * (order + 1) / 4.0
    stiffness = derivative.T @ (weights[:, None] * derivative)
    gauss_points, gauss_weights = gauss_rule(3 * (order + 1) // 2)
    offsets = gauss_points[:, None, None] - points[None, None, :]
    numerators = np.prod(np.where(identity[None, :, :] > 0.5, 1.0, offsets), axis=2)
    denominators = np.prod(np.where(identity > 0.5, 1.0, points[:, None] - points[None, :]), axis=1)
    interp = numerators / denominators[None, :]
    heights = 0.6 + 1.4 * np.sin(np.pi * (np.arange(rows_total) + 0.5) / rows_total)
    basis_x, lambdas_x = extended_basis(
        stiffness, weights, element_width, element_width, element_width
    )
    basis_rows = []
    lambda_rows = []
    for row_number in range(rows_total):
        below = heights[row_number - 1] if row_number > 0 else 0.0
        above = heights[row_number + 1] if row_number < rows_total - 1 else 0.0
        basis_one, lambda_one = extended_basis(
            stiffness, weights, below, heights[row_number], above
        )
        basis_rows.append(basis_one)
        lambda_rows.append(lambda_one)
    return (
        derivative,
        interp,
        gauss_weights,
        weights,
        stiffness,
        basis_x,
        lambdas_x,
        np.stack(basis_rows),
        np.stack(lambda_rows),
        heights,
    )


PARTS = 8
LANES = 128


def ceil_to(count, step):
    return -(-count // step) * step


class Sizes:
    def __init__(self, mesh_shape, block_shape):
        self.n_mode, self.n_ex, self.n_ey = (mesh_shape[name] for name in ("mode", "ex", "ey"))
        self.nodes, _, self.elems, self.rows, self.planes = block_shape
        self.order = self.nodes - 1
        self.gauss = 3 * self.nodes // 2
        self.rows_total = self.rows * self.n_ey
        self.elems_total = self.elems * self.n_ex
        self.planes_total = self.planes * self.n_mode
        self.block_x = self.order * self.elems + 1
        full_y = self.order * self.rows + 1
        self.inner = [
            [j for j in range(full_y) if not (p == 0 and j == 0) and not (p == self.n_ey - 1 and j == full_y - 1)]
            for p in range(self.n_ey)
        ]
        self.block_y = max(len(found) for found in self.inner)
        share = -(-(self.block_x * self.block_y + 2) // self.n_mode)
        self.share = ceil_to(share, LANES if share > 64 else 32)
        self.lane_nodes = self.share * self.n_mode
        self.columns = 2 * self.planes
        self.spots = self.n_ex * self.n_ey
        self.own = self.columns // self.spots
        self.folds = self.own // PARTS
        self.fold_width = LANES // self.folds
        self.points = self.nodes + 2
        self.x_nodes = self.n_ex * self.block_x
        self.x_pad = ceil_to(self.x_nodes, 16)
        self.x_eig = self.elems_total * self.points
        self.y_eig = self.rows_total * self.points
        self.fine = ceil_to(self.gauss * self.gauss, 16)
        assert self.own == PARTS * self.folds and self.x_eig % 16 == 0
        assert max(self.y_eig, self.n_ey * self.block_y) <= self.fold_width
        assert 2 * self.planes == LANES


def high_low(table):
    high = np.asarray(table, np.float32).astype(BF16)
    low = (np.asarray(table, np.float64) - high.astype(np.float64)).astype(BF16)
    return high, low


def beside(table):
    high, low = high_low(table)
    return np.concatenate([high, high, low], 1)


def host_tables(sz):
    derivative, interp, gauss_weights, weights, stiffness, basis_x, lam_x, basis_y, lam_y, heights = spectral_tables(
        sz.order, sz.rows_total
    )
    nodes, fine, points = sz.nodes, sz.fine, sz.points
    gauss_count = sz.gauss**2
    lift = np.zeros((3 * fine, nodes * nodes))
    lift[:gauss_count] = np.kron(interp, interp)
    lift[fine : fine + gauss_count] = np.kron(interp @ derivative, interp)
    lift[2 * fine : 2 * fine + gauss_count] = np.kron(interp, interp @ derivative)
    back = np.zeros((sz.n_ey, nodes * sz.block_y, sz.rows * fine))
    weighted = interp.T * gauss_weights[None, :]
    for place in range(sz.n_ey):
        for f in range(sz.rows):
            for jj, j in enumerate(sz.inner[place]):
                b = j - sz.order * f
                if 0 <= b < nodes:
                    back[place, jj :: sz.block_y, f * fine : f * fine + gauss_count] = -np.kron(
                        weighted, weighted[b : b + 1]
                    )
    grid_x, grid_y = sz.order * sz.elems_total, sz.order * sz.rows_total + 1
    to_x, stiff_x, mass_x = np.zeros((sz.x_eig, grid_x)), np.zeros((grid_x, grid_x)), np.zeros(grid_x)
    for e in range(sz.elems_total):
        for t in range(points):
            to_x[e * points : (e + 1) * points, (sz.order * e + t - 1) % grid_x] += basis_x[t]
        index = (sz.order * e + np.arange(nodes)) % grid_x
        stiff_x[np.ix_(index, index)] += stiffness * (2.0 / element_width)
        mass_x[index] += weights * (element_width / 2.0)
    to_y, stiff_y, mass_y = np.zeros((sz.y_eig, grid_y)), np.zeros((grid_y, grid_y)), np.zeros(grid_y)
    for f in range(sz.rows_total):
        for t in range(points):
            y = sz.order * f + t - 1
            if 0 < y < grid_y - 1:
                to_y[f * points : (f + 1) * points, y] = basis_y[f][t]
        index = sz.order * f + np.arange(nodes)
        stiff_y[np.ix_(index, index)] += stiffness * (2.0 / heights[f])
        mass_y[index] += weights * (heights[f] / 2.0)
    stiff_xx, mass_xx = to_x @ stiff_x @ to_x.T, (to_x * mass_x) @ to_x.T
    stiff_yy, mass_yy = to_y @ stiff_y @ to_y.T, (to_y * mass_y) @ to_y.T
    list_x = [(sz.order * sz.elems * p + i) % grid_x for p in range(sz.n_ex) for i in range(sz.block_x)]
    block_x = np.zeros((sz.x_eig, sz.x_pad))
    block_x[:, : sz.x_nodes] = to_x[:, list_x]
    width, folds = sz.fold_width, sz.folds
    block_y = np.zeros((width, width))
    for place in range(sz.n_ey):
        for jj, j in enumerate(sz.inner[place]):
            block_y[place * sz.block_y + jj, : sz.y_eig] = to_y[:, sz.order * sz.rows * place + j]

    def folded(table):
        padded = np.zeros((width, width))
        padded[: table.shape[0], : table.shape[1]] = table
        return np.kron(np.eye(folds), padded)

    def one_dot(table):
        high, low = high_low(folded(table))
        return np.block([[high, low], [high, np.zeros_like(low)]]).astype(BF16)

    mass_pair, stiff_pair = high_low(folded(mass_yy)), high_low(folded(stiff_yy))
    heads = np.concatenate([mass_pair[0], stiff_pair[0]], 1)
    tails = np.concatenate([mass_pair[1], stiff_pair[1]], 1)
    lam_lanes = np.ones((1, folds, width))
    lam_lanes[:, :, : sz.y_eig] = lam_y.reshape(-1)
    planes_total = sz.planes_total
    turns = np.arange(planes_total)[None, :] * np.arange(planes_total // 2)[:, None] % planes_total
    angles = turns * (2.0 * math.pi / planes_total)
    waves = np.stack([np.cos(angles), -np.sin(angles)], 1).reshape(planes_total, planes_total) / planes_total
    return dict(
        heights=np.asarray(heights, np.float32),
        lift=beside(lift),
        back=np.stack([beside(table) for table in back]),
        waves=np.stack(high_low(waves)),
        in_y=one_dot(block_y),
        in_x=beside(block_x),
        pair_y=np.concatenate([heads, heads, tails], 0),
        pair_x=beside(np.concatenate([stiff_xx, mass_xx], 1)),
        out_y=one_dot(block_y.T),
        out_x=beside(block_x.T),
        lam_x=np.asarray(np.tile(lam_x, sz.elems_total)[:, None] * np.ones((1, LANES)), np.float32),
        lam_y=np.asarray(lam_lanes.reshape(1, LANES), np.float32),
    )


def split(value):
    high = value.astype(jnp.bfloat16)
    low = (value - high.astype(jnp.float32)).astype(jnp.bfloat16)
    return high, low


def dot(left, right):
    return lax.dot_general(left, right, (((1,), (0,)), ((), ())), preferred_element_type=jnp.float32)


def below(value):
    high, low = split(value)
    return jnp.concatenate([high, low, high], 0)


def along(value):
    return jnp.concatenate(split(value), 1)


def partner(spot, step, count):
    if count & (count - 1) == 0:
        return spot ^ step
    return (spot + step) % count


def origin(spot, step, count):
    if count & (count - 1) == 0:
        return spot ^ step
    return (spot - step + count) % count


def lane_index(shape):
    return lax.broadcasted_iota(jnp.int32, shape, len(shape) - 1)


def advect_kernel(
    sz,
    heights,
    stream_hbm,
    normal_hbm,
    lift_hbm,
    back_hbm,
    *others,
):
    out_refs, (total_ref, stream_ref, normal_ref, lift_ref, back_ref, arrived) = others[:-6], others[-6:]
    place = lax.axis_index("ey")
    fetched = [
        pltpu.make_async_copy(source, target, arrived.at[i])
        for i, (source, target) in enumerate(
            (
                (stream_hbm, stream_ref),
                (normal_hbm, normal_ref),
                (lift_hbm, lift_ref),
                (back_hbm.at[place], back_ref),
            )
        )
    ]
    for copy in fetched:
        copy.start()
    count, fine, rows = sz.nodes * sz.nodes, sz.fine, sz.rows
    spots = sz.elems * rows
    half = lane_index((fine, LANES)) < sz.planes
    column, step = sz.nodes * sz.block_y, sz.order * sz.block_y
    length = sz.block_x * sz.block_y
    total_ref[pl.ds(length // 8 * 8, sz.lane_nodes - length // 8 * 8), :] = jnp.zeros(
        (sz.lane_nodes - length // 8 * 8, LANES), jnp.float32
    )
    carry = None
    for copy in fetched[:3]:
        copy.wait()
    for e in range(sz.elems):
        speeds = jnp.concatenate(
            [
                ref[pl.ds(e * rows + f, count, stride=spots), :]
                for f in range(rows)
                for ref in (stream_ref, normal_ref)
            ],
            1,
        )
        values = dot(lift_ref[...], below(speeds))
        highs, lows = [], []
        for f in range(rows):
            height = sum(jnp.where(place == q, heights[q * rows + f], 0.0) for q in range(sz.n_ey))
            mine = values[:, f * LANES : (f + 1) * LANES]
            both, slope_x, slope_y = mine[:fine], mine[fine : 2 * fine], mine[2 * fine :]
            turned = pltpu.roll(both, sz.planes, 1)
            stream = jnp.where(half, both, turned)
            normal = jnp.where(half, turned, both)
            high, low = split((stream * (height * 0.5)) * slope_x + (normal * (element_width * 0.5)) * slope_y)
            highs.append(high)
            lows.append(low)
        if e == 0:
            fetched[3].wait()
        weak = dot(back_ref[...], jnp.concatenate(highs + lows + highs, 0))
        if carry is not None:
            head = jnp.concatenate([carry, jnp.zeros((column - carry.shape[0], LANES), jnp.float32)], 0)
            weak = weak + head
        if e < sz.elems - 1:
            total_ref[pl.ds(e * step, step), :] = weak[:step]
            carry = weak[step:]
        else:
            total_ref[pl.ds(e * step, column), :] = weak
    spot = lax.axis_index("mode")
    for step, out_ref in enumerate(out_refs):
        goal = partner(spot, step, sz.n_mode)
        out_ref[...] = total_ref[pl.ds(pl.multiple_of(goal * sz.share, 8), sz.share), :]


def transform_kernel(sz, *refs):
    weak_refs, (waves_ref, out_ref, mixed_ref, signal_ref) = refs[:-4], refs[-4:]
    spot = lax.axis_index("mode")
    for step, weak_ref in enumerate(weak_refs):
        turned = weak_ref[...].T
        first = pl.multiple_of(origin(spot, step, sz.n_mode) * sz.planes, 8)
        for k in range(2):
            signal_ref[k, pl.ds(first, sz.planes), :] = turned[k * sz.planes : (k + 1) * sz.planes]
    modes = sz.planes_total
    for k in range(2):
        high, low = split(signal_ref[k])
        part = dot(waves_ref[0], high) + dot(waves_ref[0], low) + dot(waves_ref[1], high)
        for t in range(mixed_ref.shape[0]):
            tile = part[:, t * LANES : (t + 1) * LANES]
            mixed_ref[t, pl.ds(k, modes, stride=2), pl.ds(0, tile.shape[1])] = tile
    for t in range(mixed_ref.shape[0]):
        last = min(LANES, sz.share - t * LANES)
        out_ref[:, pl.ds(t * LANES, last)] = mixed_ref[t, :, pl.ds(0, last)]


def smooth_kernel(
    sz,
    terms_ref,
    in_y_ref,
    in_x_ref,
    pair_y_ref,
    pair_x_ref,
    out_y_ref,
    out_x_ref,
    lam_x_ref,
    lam_y_ref,
    *others,
):
    out_refs, (field_ref, first_ref, work_ref) = others[:-3], others[-3:]
    width, folds, strip = sz.fold_width, sz.folds, sz.block_y
    tiles = -(-sz.lane_nodes // LANES)
    lanes = lane_index((PARTS, LANES))
    x_pad, x_eig = sz.x_pad, sz.x_eig
    place, spot = lax.axis_index("ey"), lax.axis_index("ex")
    device = (lax.axis_index("mode") * sz.n_ex + spot) * sz.n_ey + place
    first_mode = device * (sz.own // 4)

    for c in range(PARTS):
        field_ref[pl.ds(c * x_pad + sz.x_nodes, x_pad - sz.x_nodes), :] = jnp.zeros(
            (x_pad - sz.x_nodes, LANES), jnp.float32
        )
    for p in range(sz.n_ex):
        block = (spot + p) % sz.n_ex
        held = {}
        for q in range(sz.n_ey):
            for fold in range(folds):
                whole = jnp.concatenate(
                    [
                        terms_ref[(z * sz.n_ex + block) * sz.n_ey + q, pl.ds(fold * PARTS, PARTS), :]
                        for z in range(sz.n_mode)
                    ],
                    1,
                )
                held[q, fold] = [whole[:, t * LANES : (t + 1) * LANES] for t in range(tiles)]
        for i in range(sz.block_x):
            start = i * strip
            t, r = start // LANES, start % LANES
            result = jnp.zeros((PARTS, LANES), jnp.float32)
            for fold in range(folds):
                for q in range(sz.n_ey):
                    source = held[q, fold][t]
                    if r + strip > LANES:
                        source = jnp.where(lanes >= r, source, held[q, fold][t + 1])
                    goal = fold * width + q * strip
                    moved = pltpu.roll(source, (goal - r) % LANES, 1) if goal != r else source
                    result = jnp.where((lanes >= goal) & (lanes < goal + strip), moved, result)
            field_ref[pl.ds(p * sz.block_x + i, PARTS, stride=x_pad), :] = result

    parts = dot(along(field_ref[...]), in_y_ref[...])
    field_ref[...] = parts[:, :LANES] + parts[:, LANES:]
    fold_of_lane = lane_index((1, LANES)) // width
    shifts, inverses = [], []
    for group in range(PARTS // 4):
        mode = (first_mode + fold_of_lane * (PARTS // 4) + group).astype(jnp.float32)
        shift = shift_base + (span_rate * mode) ** 2
        shifts.append(shift)
        inverses.append(1.0 / (lam_x_ref[...] + (lam_y_ref[...] + shift)))
    for c in range(0, PARTS, 2):
        pair = jnp.concatenate([field_ref[pl.ds((c + d) * x_pad, x_pad), :] for d in range(2)], 1)
        forced = dot(in_x_ref[...], below(pair))
        for d in range(2):
            mine = forced[:, d * LANES : (d + 1) * LANES]
            first_ref[pl.ds((c + d) * x_eig, x_eig), :] = mine
            work_ref[pl.ds((c + d) * x_eig, x_eig), :] = mine * inverses[(c + d) // 4]
    for c in range(0, PARTS, 2):
        shift = shifts[c // 4]
        masses, stiffs = [], []
        for d in range(2):
            high, low = split(work_ref[pl.ds((c + d) * x_eig, x_eig), :])
            both = dot(jnp.concatenate([high, low, high], 1), pair_y_ref[...])
            masses.append(both[:, :LANES])
            stiffs.append(both[:, LANES:] + shift * both[:, :LANES])
        stacked = jnp.concatenate([jnp.concatenate(masses, 1), jnp.concatenate(stiffs, 1)], 0)
        applied = dot(pair_x_ref[...], below(stacked))
        for d in range(2):
            rows = pl.ds((c + d) * x_eig, x_eig)
            total = (2.0 * first_ref[rows, :] - applied[:, d * LANES : (d + 1) * LANES]) * inverses[c // 4]
            parts = dot(along(total), out_y_ref[...])
            work_ref[rows, :] = parts[:, :LANES] + parts[:, LANES:]
        pair = jnp.concatenate([work_ref[pl.ds((c + d) * x_eig, x_eig), :] for d in range(2)], 1)
        solved = dot(out_x_ref[...], below(pair))
        for d in range(2):
            field_ref[pl.ds((c + d) * x_pad, x_pad), :] = solved[:, d * LANES : (d + 1) * LANES]

    for p in range(sz.n_ex):
        made = {}
        for i in range(sz.block_x):
            source = field_ref[pl.ds(p * sz.block_x + i, PARTS, stride=x_pad), :]
            for q in range(sz.n_ey):
                begin = i * strip + sz.inner[q][0]
                count = len(sz.inner[q])
                t, r = begin // LANES, begin % LANES
                for fold in range(folds):
                    origin = fold * width + q * strip
                    moved = pltpu.roll(source, (r - origin) % LANES, 1) if origin != r else source
                    for tile, low, high in ((t, r, r + count), (t + 1, 0, r + count - LANES)):
                        if high > 0:
                            old = made.get((q, fold, tile))
                            if old is None:
                                old = jnp.zeros((PARTS, LANES), jnp.float32)
                            made[q, fold, tile] = jnp.where((lanes >= low) & (lanes < high), moved, old)
        for (q, fold, tile), value in made.items():
            last = min(LANES, sz.lane_nodes - tile * LANES)
            where = (pl.ds(fold * PARTS, PARTS), pl.ds(tile * LANES, last))
            for turn in range(sz.n_ey):

                @pl.when((place + turn) % sz.n_ey == q)
                def _(out_ref=out_refs[p * sz.n_ey + turn], value=value[:, :last], where=where):
                    out_ref[where] = value


def spread_kernel(sz, *refs):
    solved_refs, (out_ref, stacked_ref, turned_ref) = refs[:-3], refs[-3:]
    place, spot = lax.axis_index("ey"), lax.axis_index("ex")
    for step, solved_ref in enumerate(solved_refs):
        shift, turn = step // sz.n_ey, step % sz.n_ey
        source = (spot - shift + sz.n_ex) % sz.n_ex * sz.n_ey + (place - turn + sz.n_ey) % sz.n_ey
        stacked_ref[pl.ds(pl.multiple_of(source * sz.own, PARTS), sz.own), :] = solved_ref[...]
    turned_ref[...] = stacked_ref[...].T
    spots = sz.elems * sz.rows
    for e in range(sz.elems):
        for f in range(sz.rows):
            for a in range(sz.nodes):
                start = sz.block_y * (sz.order * e + a) + sz.order * f
                out_ref[pl.ds(a * sz.nodes * spots + e * sz.rows + f, sz.nodes, stride=spots), :] = turned_ref[
                    pl.ds(start, sz.nodes), :
                ]
    blank = jnp.zeros((sz.elems, LANES), jnp.float32)

    @pl.when(place == 0)
    def _():
        for a in range(sz.nodes):
            out_ref[pl.ds(a * sz.nodes * spots, sz.elems, stride=sz.rows), :] = blank

    @pl.when(place == sz.n_ey - 1)
    def _():
        for a in range(sz.nodes):
            first = ((a + 1) * sz.nodes - 1) * spots + sz.rows - 1
            out_ref[pl.ds(first, sz.elems, stride=sz.rows), :] = blank


def call(kernel, shapes, operands, scratch=(), space=pltpu.VMEM, limit=16):
    made = pl.pallas_call(
        kernel,
        out_shape=[jax.ShapeDtypeStruct(shape, jnp.float32) for shape in shapes],
        in_specs=[pl.BlockSpec(memory_space=space) for _ in operands],
        out_specs=[pl.BlockSpec(memory_space=pltpu.VMEM) for _ in shapes],
        scratch_shapes=[pltpu.VMEM(each, jnp.float32) if isinstance(each, tuple) else each for each in scratch],
        compiler_params=pltpu.CompilerParams(vmem_limit_bytes=limit * 2**20),
    )(*operands)
    return list(made)


def on_device(sz, tables, stream_speed, normal_speed):
    flat = sz.nodes * sz.nodes * sz.elems * sz.rows
    table = {name: jnp.asarray(value) for name, value in tables.items() if name != "heights"}
    heights = [float(height) for height in tables["heights"]]
    weak = call(
        functools.partial(advect_kernel, sz, heights),
        [(sz.share, LANES)] * sz.n_mode,
        [
            stream_speed.reshape(flat, sz.planes),
            normal_speed.reshape(flat, sz.planes),
            table["lift"],
            table["back"],
        ],
        [
            (sz.lane_nodes, LANES),
            (flat, sz.planes),
            (flat, sz.planes),
            pltpu.VMEM(tables["lift"].shape, jnp.bfloat16),
            pltpu.VMEM(tables["back"].shape[1:], jnp.bfloat16),
            pltpu.SemaphoreType.DMA((4,)),
        ],
        pltpu.HBM,
        60,
    )
    for step in sorted(range(1, sz.n_mode), key=lambda each: (each & -each, each), reverse=True):
        pairs = [(z, partner(z, step, sz.n_mode)) for z in range(sz.n_mode)]
        weak[step] = lax.ppermute(weak[step], "mode", pairs)
    (spectra,) = call(
        functools.partial(transform_kernel, sz),
        [(2 * sz.planes_total, sz.share)],
        [*weak, table["waves"]],
        [(-(-sz.share // LANES), 2 * sz.planes_total, LANES), (2, sz.planes_total, sz.share)],
    )
    spectra = spectra.reshape(sz.n_mode * sz.spots, sz.own, sz.share)
    terms = lax.all_to_all(spectra, ("mode", "ex", "ey"), split_axis=0, concat_axis=0, tiled=True)
    names = ("in_y", "in_x", "pair_y", "pair_x", "out_y", "out_x", "lam_x", "lam_y")
    solved = call(
        functools.partial(smooth_kernel, sz),
        [(sz.own, sz.lane_nodes)] * sz.spots,
        [terms] + [table[name] for name in names],
        [(PARTS * sz.x_pad, LANES), (PARTS * sz.x_eig, LANES), (PARTS * sz.x_eig, LANES)],
    )
    for step in range(1, sz.spots):
        shift, turn = step // sz.n_ey, step % sz.n_ey
        pairs = [
            (p * sz.n_ey + q, (p + shift) % sz.n_ex * sz.n_ey + (q + turn) % sz.n_ey)
            for p in range(sz.n_ex)
            for q in range(sz.n_ey)
        ]
        solved[step] = lax.ppermute(solved[step], ("ex", "ey"), pairs)
    (out,) = call(
        functools.partial(spread_kernel, sz),
        [(flat, LANES)],
        solved,
        [(sz.columns, sz.lane_nodes), (sz.lane_nodes, LANES)],
    )
    return out.reshape(sz.nodes, sz.nodes, sz.elems, sz.rows, sz.columns)


def solution(mesh):
    spec = P(None, None, "ex", "ey", "mode")

    def whole(stream_speed, normal_speed):
        shape = stream_speed.shape
        counts = mesh.shape
        block = shape[:2] + (shape[2] // counts["ex"], shape[3] // counts["ey"], shape[4] // counts["mode"])
        sz = Sizes(counts, block)
        return jax.shard_map(
            functools.partial(on_device, sz, host_tables(sz)),
            mesh=mesh,
            in_specs=(spec, spec),
            out_specs=spec,
            check_vma=False,
        )(stream_speed, normal_speed)

    return whole
```

```python
import functools
import math

import jax
import jax.numpy as jnp
import ml_dtypes
import numpy as np
from jax import lax
from jax.experimental import pallas as pl
from jax.experimental.pallas import tpu as pltpu
from jax.sharding import PartitionSpec as P

BF16 = ml_dtypes.bfloat16

element_width = 2.0
shift_base = 10.0
span_rate = 0.0125


def legendre_pair(degree, points):
    before = points * 0.0 + 1.0
    current = points.copy()
    for step in range(1, degree):
        upcoming = ((2 * step + 1) * points * current - step * before) / (step + 1)
        before = current
        current = upcoming
    return (current, before)


def legendre_slope(degree, points):
    current, before = legendre_pair(degree, points)
    return (current, degree * (points * current - before) / (points * points - 1.0))


def lobatto_points(order):
    guesses = -np.cos(np.pi * np.arange(1, order) / order)
    for step in range(60):
        current, slope = legendre_slope(order, guesses)
        second = (2.0 * guesses * slope - order * (order + 1) * current) / (1.0 - guesses * guesses)
        guesses = guesses - slope / second
    return guesses


def gauss_rule(count):
    guesses = -np.cos(np.pi * (np.arange(count) + 0.75) / (count + 0.5))
    for step in range(60):
        current, slope = legendre_slope(count, guesses)
        guesses = guesses - current / slope
    current, slope = legendre_slope(count, guesses)
    return (guesses, 2.0 / ((1.0 - guesses * guesses) * slope * slope))


def jacobi_eigen(matrix):
    size_n = matrix.shape[0]
    work = matrix.copy()
    vectors = np.eye(size_n)
    for sweep_number in range(20):
        for first in range(size_n):
            for second in range(first + 1, size_n):
                coupling = work[first, second]
                if abs(coupling) > 1e-300:
                    theta = (work[second, second] - work[first, first]) / (2.0 * coupling)
                    direction = 1.0 if theta >= 0.0 else -1.0
                    tangent = direction / (abs(theta) + np.sqrt(theta * theta + 1.0))
                    cosine = 1.0 / np.sqrt(tangent * tangent + 1.0)
                    sine = tangent * cosine
                    rotation = np.eye(size_n)
                    rotation[first, first] = cosine
                    rotation[second, second] = cosine
                    rotation[first, second] = sine
                    rotation[second, first] = -sine
                    work = rotation.T @ work @ rotation
                    vectors = vectors @ rotation
    diagonal_index = np.arange(size_n)
    return (work[diagonal_index, diagonal_index], vectors)


def extended_basis(stiffness, weights, left_width, centre_width, right_width):
    node_count = weights.shape[0]
    full_count = 3 * node_count - 2
    stiff_full = np.zeros((full_count, full_count))
    mass_full = np.zeros(full_count)
    for position, span_width in enumerate((left_width, centre_width, right_width)):
        if span_width > 0.0:
            first_node = position * (node_count - 1)
            stiff_full[
                first_node : first_node + node_count, first_node : first_node + node_count
            ] += stiffness * (2.0 / span_width)
            mass_full[first_node : first_node + node_count] += weights * (span_width / 2.0)
    low_index = node_count - 2
    high_index = low_index + node_count + 2
    stiff_ext = stiff_full[low_index:high_index, low_index:high_index].copy()
    mass_ext = mass_full[low_index:high_index].copy()
    frozen_list = []
    if left_width <= 0.0:
        frozen_list += [0, 1]
    if right_width <= 0.0:
        frozen_list += [node_count, node_count + 1]
    for frozen_index in frozen_list:
        stiff_ext[frozen_index, :] = 0.0
        stiff_ext[:, frozen_index] = 0.0
        stiff_ext[frozen_index, frozen_index] = 1.0
        mass_ext[frozen_index] = 1.0
    inverse_root = 1.0 / np.sqrt(mass_ext)
    lambdas, vectors = jacobi_eigen(inverse_root[:, None] * stiff_ext * inverse_root[None, :])
    return (inverse_root[:, None] * vectors, lambdas)


def spectral_tables(order, rows_total):
    inner_points = lobatto_points(order)
    points = np.concatenate([[-1.0], inner_points, [1.0]])
    values, unused_before = legendre_pair(order, points)
    weights = 2.0 / (order * (order + 1) * values**2)
    identity = np.eye(order + 1)
    point_gaps = points[:, None] - points[None, :] + identity
    derivative = values[:, None] / (values[None, :] * point_gaps) * (1.0 - identity)
    derivative[0, 0] = -order * (order + 1) / 4.0
    derivative[order, order] = order * (order + 1) / 4.0
    stiffness = derivative.T @ (weights[:, None] * derivative)
    gauss_points, gauss_weights = gauss_rule(3 * (order + 1) // 2)
    offsets = gauss_points[:, None, None] - points[None, None, :]
    numerators = np.prod(np.where(identity[None, :, :] > 0.5, 1.0, offsets), axis=2)
    denominators = np.prod(np.where(identity > 0.5, 1.0, points[:, None] - points[None, :]), axis=1)
    interp = numerators / denominators[None, :]
    heights = 0.6 + 1.4 * np.sin(np.pi * (np.arange(rows_total) + 0.5) / rows_total)
    basis_x, lambdas_x = extended_basis(
        stiffness, weights, element_width, element_width, element_width
    )
    basis_rows = []
    lambda_rows = []
    for row_number in range(rows_total):
        below = heights[row_number - 1] if row_number > 0 else 0.0
        above = heights[row_number + 1] if row_number < rows_total - 1 else 0.0
        basis_one, lambda_one = extended_basis(
            stiffness, weights, below, heights[row_number], above
        )
        basis_rows.append(basis_one)
        lambda_rows.append(lambda_one)
    return (
        derivative,
        interp,
        gauss_weights,
        weights,
        stiffness,
        basis_x,
        lambdas_x,
        np.stack(basis_rows),
        np.stack(lambda_rows),
        heights,
    )


PARTS = 8
LANES = 128


def ceil_to(count, step):
    return -(-count // step) * step


class Sizes:
    def __init__(self, mesh_shape, block_shape):
        self.n_mode, self.n_ex, self.n_ey = (mesh_shape[name] for name in ("mode", "ex", "ey"))
        self.nodes, _, self.elems, self.rows, self.planes = block_shape
        self.order = self.nodes - 1
        self.gauss = 3 * self.nodes // 2
        self.rows_total = self.rows * self.n_ey
        self.elems_total = self.elems * self.n_ex
        self.planes_total = self.planes * self.n_mode
        self.block_x = self.order * self.elems + 1
        full_y = self.order * self.rows + 1
        self.inner = [
            [j for j in range(full_y) if not (p == 0 and j == 0) and not (p == self.n_ey - 1 and j == full_y - 1)]
            for p in range(self.n_ey)
        ]
        self.block_y = max(len(found) for found in self.inner)
        self.cuts = 2 if self.elems % 2 == 0 else 1
        self.cut_elems = self.elems // self.cuts
        self.cut_x = self.order * self.cut_elems + 1
        share = -(-self.cut_x * self.block_y // self.n_mode)
        self.share = ceil_to(share, LANES if share > 64 else 16)
        self.cut_nodes = self.share * self.n_mode
        self.lane_nodes = ceil_to(self.block_x * self.block_y + 2, LANES)
        self.columns = 2 * self.planes
        self.spots = self.n_ex * self.n_ey
        self.own = self.columns // self.spots
        self.folds = self.own // PARTS
        self.fold_width = LANES // self.folds
        self.points = self.nodes + 2
        self.x_cuts = self.n_ex * self.cuts * self.cut_x
        self.x_pad = ceil_to(max(self.x_cuts, self.n_ex * self.block_x), 16)
        self.x_eig = self.elems_total * self.points
        self.y_eig = self.rows_total * self.points
        self.fine = ceil_to(self.gauss * self.gauss, 16)
        assert self.own == PARTS * self.folds and self.x_eig % 16 == 0
        assert max(self.y_eig, self.n_ey * self.block_y) <= self.fold_width
        assert 2 * self.planes == LANES


def high_low(table):
    high = np.asarray(table, np.float32).astype(BF16)
    low = (np.asarray(table, np.float64) - high.astype(np.float64)).astype(BF16)
    return high, low


def beside(table):
    high, low = high_low(table)
    return np.concatenate([high, high, low], 1)


def host_tables(sz):
    derivative, interp, gauss_weights, weights, stiffness, basis_x, lam_x, basis_y, lam_y, heights = spectral_tables(
        sz.order, sz.rows_total
    )
    nodes, fine, points = sz.nodes, sz.fine, sz.points
    gauss_count = sz.gauss**2
    lift = np.zeros((3 * fine, nodes * nodes))
    lift[:gauss_count] = np.kron(interp, interp)
    lift[fine : fine + gauss_count] = np.kron(interp @ derivative, interp)
    lift[2 * fine : 2 * fine + gauss_count] = np.kron(interp, interp @ derivative)
    back = np.zeros((sz.n_ey, nodes * sz.block_y, sz.rows * fine))
    weighted = interp.T * gauss_weights[None, :]
    for place in range(sz.n_ey):
        for f in range(sz.rows):
            for jj, j in enumerate(sz.inner[place]):
                b = j - sz.order * f
                if 0 <= b < nodes:
                    back[place, jj :: sz.block_y, f * fine : f * fine + gauss_count] = -np.kron(
                        weighted, weighted[b : b + 1]
                    )
    grid_x, grid_y = sz.order * sz.elems_total, sz.order * sz.rows_total + 1
    to_x, stiff_x, mass_x = np.zeros((sz.x_eig, grid_x)), np.zeros((grid_x, grid_x)), np.zeros(grid_x)
    for e in range(sz.elems_total):
        for t in range(points):
            to_x[e * points : (e + 1) * points, (sz.order * e + t - 1) % grid_x] += basis_x[t]
        index = (sz.order * e + np.arange(nodes)) % grid_x
        stiff_x[np.ix_(index, index)] += stiffness * (2.0 / element_width)
        mass_x[index] += weights * (element_width / 2.0)
    to_y, stiff_y, mass_y = np.zeros((sz.y_eig, grid_y)), np.zeros((grid_y, grid_y)), np.zeros(grid_y)
    for f in range(sz.rows_total):
        for t in range(points):
            y = sz.order * f + t - 1
            if 0 < y < grid_y - 1:
                to_y[f * points : (f + 1) * points, y] = basis_y[f][t]
        index = sz.order * f + np.arange(nodes)
        stiff_y[np.ix_(index, index)] += stiffness * (2.0 / heights[f])
        mass_y[index] += weights * (heights[f] / 2.0)
    stiff_xx, mass_xx = to_x @ stiff_x @ to_x.T, (to_x * mass_x) @ to_x.T
    stiff_yy, mass_yy = to_y @ stiff_y @ to_y.T, (to_y * mass_y) @ to_y.T
    def block_x(blocks, elems):
        length = sz.order * elems + 1
        nodes_of = [(sz.order * elems * p + i) % grid_x for p in range(blocks) for i in range(length)]
        table = np.zeros((sz.x_eig, sz.x_pad))
        table[:, : len(nodes_of)] = to_x[:, nodes_of]
        return table

    width, folds = sz.fold_width, sz.folds
    block_y = np.zeros((width, width))
    for place in range(sz.n_ey):
        for jj, j in enumerate(sz.inner[place]):
            block_y[place * sz.block_y + jj, : sz.y_eig] = to_y[:, sz.order * sz.rows * place + j]

    def folded(table):
        padded = np.zeros((width, width))
        padded[: table.shape[0], : table.shape[1]] = table
        return np.kron(np.eye(folds), padded)

    def one_dot(table):
        high, low = high_low(folded(table))
        return np.block([[high, low], [high, np.zeros_like(low)]]).astype(BF16)

    mass_pair, stiff_pair = high_low(folded(mass_yy)), high_low(folded(stiff_yy))
    heads = np.concatenate([mass_pair[0], stiff_pair[0]], 1)
    tails = np.concatenate([mass_pair[1], stiff_pair[1]], 1)
    lam_lanes = np.ones((1, folds, width))
    lam_lanes[:, :, : sz.y_eig] = lam_y.reshape(-1)
    planes_total = sz.planes_total
    turns = np.arange(planes_total)[None, :] * np.arange(planes_total // 2)[:, None] % planes_total
    angles = turns * (2.0 * math.pi / planes_total)
    waves = np.stack([np.cos(angles), -np.sin(angles)], 1).reshape(planes_total, planes_total) / planes_total
    return dict(
        heights=np.asarray(heights, np.float32),
        lift=beside(lift),
        back=np.stack([beside(table) for table in back]),
        waves=np.stack(high_low(waves)),
        in_y=one_dot(block_y),
        in_x=beside(block_x(sz.n_ex * sz.cuts, sz.cut_elems)),
        pair_y=np.concatenate([heads, heads, tails], 0),
        pair_x=beside(np.concatenate([stiff_xx, mass_xx], 1)),
        out_y=one_dot(block_y.T),
        out_x=beside(block_x(sz.n_ex, sz.elems).T),
        lam_x=np.asarray(np.tile(lam_x, sz.elems_total)[:, None] * np.ones((1, LANES)), np.float32),
        lam_y=np.asarray(lam_lanes.reshape(1, LANES), np.float32),
    )


def split(value):
    high = value.astype(jnp.bfloat16)
    low = (value - high.astype(jnp.float32)).astype(jnp.bfloat16)
    return high, low


def dot(left, right):
    return lax.dot_general(left, right, (((1,), (0,)), ((), ())), preferred_element_type=jnp.float32)


def below(value):
    high, low = split(value)
    return jnp.concatenate([high, low, high], 0)


def along(value):
    return jnp.concatenate(split(value), 1)


def partner(spot, step, count):
    if count & (count - 1) == 0:
        return spot ^ step
    return (spot + step) % count


def origin(spot, step, count):
    if count & (count - 1) == 0:
        return spot ^ step
    return (spot - step + count) % count


def lane_index(shape):
    return lax.broadcasted_iota(jnp.int32, shape, len(shape) - 1)


def advect_kernel(
    sz,
    heights,
    cut,
    stream_hbm,
    normal_hbm,
    lift_hbm,
    back_hbm,
    *others,
):
    out_refs, (total_ref, stream_ref, normal_ref, lift_ref, back_ref, arrived) = others[:-6], others[-6:]
    place = lax.axis_index("ey")
    fetched = [
        pltpu.make_async_copy(source, target, arrived.at[i])
        for i, (source, target) in enumerate(
            (
                (stream_hbm, stream_ref),
                (normal_hbm, normal_ref),
                (lift_hbm, lift_ref),
                (back_hbm.at[place], back_ref),
            )
        )
    ]
    for copy in fetched:
        copy.start()
    count, fine, rows = sz.nodes * sz.nodes, sz.fine, sz.rows
    spots = sz.elems * rows
    half = lane_index((fine, LANES)) < sz.planes
    column, step = sz.nodes * sz.block_y, sz.order * sz.block_y
    full = sz.cut_x * sz.block_y // 8 * 8
    total_ref[pl.ds(full, sz.cut_nodes - full), :] = jnp.zeros((sz.cut_nodes - full, LANES), jnp.float32)
    carry = None
    for copy in fetched[:3]:
        copy.wait()
    for e in range(sz.cut_elems):
        speeds = jnp.concatenate(
            [
                ref[pl.ds((cut * sz.cut_elems + e) * rows + f, count, stride=spots), :]
                for f in range(rows)
                for ref in (stream_ref, normal_ref)
            ],
            1,
        )
        values = dot(lift_ref[...], below(speeds))
        highs, lows = [], []
        for f in range(rows):
            height = sum(jnp.where(place == q, heights[q * rows + f], 0.0) for q in range(sz.n_ey))
            mine = values[:, f * LANES : (f + 1) * LANES]
            both, slope_x, slope_y = mine[:fine], mine[fine : 2 * fine], mine[2 * fine :]
            turned = pltpu.roll(both, sz.planes, 1)
            stream = jnp.where(half, both, turned)
            normal = jnp.where(half, turned, both)
            high, low = split((stream * (height * 0.5)) * slope_x + (normal * (element_width * 0.5)) * slope_y)
            highs.append(high)
            lows.append(low)
        if e == 0:
            fetched[3].wait()
        weak = dot(back_ref[...], jnp.concatenate(highs + lows + highs, 0))
        if carry is not None:
            head = jnp.concatenate([carry, jnp.zeros((column - carry.shape[0], LANES), jnp.float32)], 0)
            weak = weak + head
        if e < sz.cut_elems - 1:
            total_ref[pl.ds(e * step, step), :] = weak[:step]
            carry = weak[step:]
        else:
            total_ref[pl.ds(e * step, column), :] = weak
    spot = lax.axis_index("mode")
    for step, out_ref in enumerate(out_refs):
        goal = partner(spot, step, sz.n_mode)
        out_ref[...] = total_ref[pl.ds(pl.multiple_of(goal * sz.share, 8), sz.share), :]


def transform_kernel(sz, *refs):
    weak_refs, (waves_ref, out_ref, mixed_ref, signal_ref) = refs[: sz.n_mode], refs[-4:]
    spot = lax.axis_index("mode")
    for step, weak_ref in enumerate(weak_refs):
        turned = weak_ref[...].T
        first = pl.multiple_of(origin(spot, step, sz.n_mode) * sz.planes, 8)
        for k in range(2):
            signal_ref[k, pl.ds(first, sz.planes), :] = turned[k * sz.planes : (k + 1) * sz.planes]
    modes = sz.planes_total
    for k in range(2):
        high, low = split(signal_ref[k])
        part = dot(waves_ref[0], high) + dot(waves_ref[0], low) + dot(waves_ref[1], high)
        for t in range(mixed_ref.shape[0]):
            tile = part[:, t * LANES : (t + 1) * LANES]
            mixed_ref[t, pl.ds(k, modes, stride=2), pl.ds(0, tile.shape[1])] = tile
    for t in range(mixed_ref.shape[0]):
        last = min(LANES, sz.share - t * LANES)
        out_ref[:, pl.ds(t * LANES, last)] = mixed_ref[t, :, pl.ds(0, last)]


def smooth_kernel(
    sz,
    *refs,
):
    terms_refs, out_refs, (field_ref, first_ref, work_ref) = refs[: sz.cuts], refs[sz.cuts + 8 : -3], refs[-3:]
    in_y_ref, in_x_ref, pair_y_ref, pair_x_ref, out_y_ref, out_x_ref, lam_x_ref, lam_y_ref = refs[
        sz.cuts : sz.cuts + 8
    ]
    width, folds, strip = sz.fold_width, sz.folds, sz.block_y
    tiles = -(-sz.cut_nodes // LANES)
    lanes = lane_index((PARTS, LANES))
    x_pad, x_eig = sz.x_pad, sz.x_eig
    place, spot = lax.axis_index("ey"), lax.axis_index("ex")
    device = (lax.axis_index("mode") * sz.n_ex + spot) * sz.n_ey + place
    first_mode = device * (sz.own // 4)

    for c in range(PARTS):
        field_ref[pl.ds(c * x_pad + sz.x_cuts, x_pad - sz.x_cuts), :] = jnp.zeros(
            (x_pad - sz.x_cuts, LANES), jnp.float32
        )
    for p, cut in [(p, cut) for p in range(sz.n_ex) for cut in range(sz.cuts)]:
        block = (spot + p) % sz.n_ex
        held = {}
        for q in range(sz.n_ey):
            for fold in range(folds):
                whole = jnp.concatenate(
                    [
                        terms_refs[cut][(z * sz.n_ex + block) * sz.n_ey + q, pl.ds(fold * PARTS, PARTS), :]
                        for z in range(sz.n_mode)
                    ],
                    1,
                )
                held[q, fold] = [whole[:, t * LANES : (t + 1) * LANES] for t in range(tiles)]
        for i in range(sz.cut_x):
            start = i * strip
            t, r = start // LANES, start % LANES
            result = jnp.zeros((PARTS, LANES), jnp.float32)
            for fold in range(folds):
                for q in range(sz.n_ey):
                    source = held[q, fold][t]
                    if r + strip > LANES:
                        source = jnp.where(lanes >= r, source, held[q, fold][t + 1])
                    goal = fold * width + q * strip
                    moved = pltpu.roll(source, (goal - r) % LANES, 1) if goal != r else source
                    result = jnp.where((lanes >= goal) & (lanes < goal + strip), moved, result)
            field_ref[pl.ds((p * sz.cuts + cut) * sz.cut_x + i, PARTS, stride=x_pad), :] = result

    parts = dot(along(field_ref[...]), in_y_ref[...])
    field_ref[...] = parts[:, :LANES] + parts[:, LANES:]
    fold_of_lane = lane_index((1, LANES)) // width
    shifts, inverses = [], []
    for group in range(PARTS // 4):
        mode = (first_mode + fold_of_lane * (PARTS // 4) + group).astype(jnp.float32)
        shift = shift_base + (span_rate * mode) ** 2
        shifts.append(shift)
        inverses.append(1.0 / (lam_x_ref[...] + (lam_y_ref[...] + shift)))
    for c in range(0, PARTS, 2):
        pair = jnp.concatenate([field_ref[pl.ds((c + d) * x_pad, x_pad), :] for d in range(2)], 1)
        forced = dot(in_x_ref[...], below(pair))
        for d in range(2):
            mine = forced[:, d * LANES : (d + 1) * LANES]
            first_ref[pl.ds((c + d) * x_eig, x_eig), :] = mine
            work_ref[pl.ds((c + d) * x_eig, x_eig), :] = mine * inverses[(c + d) // 4]
    for c in range(0, PARTS, 2):
        shift = shifts[c // 4]
        masses, stiffs = [], []
        for d in range(2):
            high, low = split(work_ref[pl.ds((c + d) * x_eig, x_eig), :])
            both = dot(jnp.concatenate([high, low, high], 1), pair_y_ref[...])
            masses.append(both[:, :LANES])
            stiffs.append(both[:, LANES:] + shift * both[:, :LANES])
        stacked = jnp.concatenate([jnp.concatenate(masses, 1), jnp.concatenate(stiffs, 1)], 0)
        applied = dot(pair_x_ref[...], below(stacked))
        for d in range(2):
            rows = pl.ds((c + d) * x_eig, x_eig)
            total = (2.0 * first_ref[rows, :] - applied[:, d * LANES : (d + 1) * LANES]) * inverses[c // 4]
            parts = dot(along(total), out_y_ref[...])
            work_ref[rows, :] = parts[:, :LANES] + parts[:, LANES:]
        pair = jnp.concatenate([work_ref[pl.ds((c + d) * x_eig, x_eig), :] for d in range(2)], 1)
        solved = dot(out_x_ref[...], below(pair))
        for d in range(2):
            field_ref[pl.ds((c + d) * x_pad, x_pad), :] = solved[:, d * LANES : (d + 1) * LANES]

    for p in range(sz.n_ex):
        made = {}
        for i in range(sz.block_x):
            source = field_ref[pl.ds(p * sz.block_x + i, PARTS, stride=x_pad), :]
            for q in range(sz.n_ey):
                begin = i * strip + sz.inner[q][0]
                count = len(sz.inner[q])
                t, r = begin // LANES, begin % LANES
                for fold in range(folds):
                    origin = fold * width + q * strip
                    moved = pltpu.roll(source, (r - origin) % LANES, 1) if origin != r else source
                    for tile, low, high in ((t, r, r + count), (t + 1, 0, r + count - LANES)):
                        if high > 0:
                            old = made.get((q, fold, tile))
                            if old is None:
                                old = jnp.zeros((PARTS, LANES), jnp.float32)
                            made[q, fold, tile] = jnp.where((lanes >= low) & (lanes < high), moved, old)
        for fold in range(folds):
            for tile in range(sz.lane_nodes // LANES):
                for turn in range(sz.n_ey):
                    chosen = jnp.zeros((PARTS, LANES), jnp.float32)
                    for q in range(sz.n_ey):
                        if (q, fold, tile) in made:
                            chosen = jnp.where((place + turn) % sz.n_ey == q, made[q, fold, tile], chosen)
                    out_refs[p * sz.n_ey + turn][pl.ds(fold * PARTS, PARTS), pl.ds(tile * LANES, LANES)] = chosen


def spread_kernel(sz, *refs):
    solved_refs, (out_ref, stacked_ref, turned_ref) = refs[:-3], refs[-3:]
    place, spot = lax.axis_index("ey"), lax.axis_index("ex")
    for step, solved_ref in enumerate(solved_refs):
        shift, turn = step // sz.n_ey, step % sz.n_ey
        source = (spot - shift + sz.n_ex) % sz.n_ex * sz.n_ey + (place - turn + sz.n_ey) % sz.n_ey
        stacked_ref[pl.ds(pl.multiple_of(source * sz.own, PARTS), sz.own), :] = solved_ref[...]
    turned_ref[...] = stacked_ref[...].T
    spots = sz.elems * sz.rows
    for e in range(sz.elems):
        for f in range(sz.rows):
            for a in range(sz.nodes):
                start = sz.block_y * (sz.order * e + a) + sz.order * f
                out_ref[pl.ds(a * sz.nodes * spots + e * sz.rows + f, sz.nodes, stride=spots), :] = turned_ref[
                    pl.ds(start, sz.nodes), :
                ]
    blank = jnp.zeros((sz.elems, LANES), jnp.float32)

    @pl.when(place == 0)
    def _():
        for a in range(sz.nodes):
            out_ref[pl.ds(a * sz.nodes * spots, sz.elems, stride=sz.rows), :] = blank

    @pl.when(place == sz.n_ey - 1)
    def _():
        for a in range(sz.nodes):
            first = ((a + 1) * sz.nodes - 1) * spots + sz.rows - 1
            out_ref[pl.ds(first, sz.elems, stride=sz.rows), :] = blank


def call(kernel, shapes, operands, scratch=(), spaces=pltpu.VMEM, limit=16):
    if not isinstance(spaces, list):
        spaces = [spaces] * len(operands)
    made = pl.pallas_call(
        kernel,
        out_shape=[jax.ShapeDtypeStruct(shape, jnp.float32) for shape in shapes],
        in_specs=[pl.BlockSpec(memory_space=space) for space in spaces],
        out_specs=[pl.BlockSpec(memory_space=pltpu.VMEM) for _ in shapes],
        scratch_shapes=[pltpu.VMEM(each, jnp.float32) if isinstance(each, tuple) else each for each in scratch],
        compiler_params=pltpu.CompilerParams(vmem_limit_bytes=limit * 2**20),
    )(*operands)
    return list(made)


def on_device(sz, tables, stream_speed, normal_speed):
    flat = sz.nodes * sz.nodes * sz.elems * sz.rows
    table = {name: jnp.asarray(value) for name, value in tables.items() if name != "heights"}
    heights = [float(height) for height in tables["heights"]]
    weak, made = [], []
    for cut in range(sz.cuts):
        weak.append(
            call(
                functools.partial(advect_kernel, sz, heights, cut),
                [(sz.share, LANES)] * sz.n_mode,
                [
                    stream_speed.reshape(flat, sz.planes),
                    normal_speed.reshape(flat, sz.planes),
                    table["lift"],
                    table["back"],
                ],
                [
                    (sz.cut_nodes, LANES),
                    (flat, sz.planes),
                    (flat, sz.planes),
                    pltpu.VMEM(tables["lift"].shape, jnp.bfloat16),
                    pltpu.VMEM(tables["back"].shape[1:], jnp.bfloat16),
                    pltpu.SemaphoreType.DMA((4,)),
                ],
                pltpu.HBM,
                60,
            )
        )
        made.append(weak[cut][0])
        for step in sorted(range(1, sz.n_mode), key=lambda each: (each & -each, each), reverse=True):
            pairs = [(z, partner(z, step, sz.n_mode)) for z in range(sz.n_mode)]
            weak[cut][step] = lax.ppermute(weak[cut][step], "mode", pairs)
    terms, ahead = [], made[-1]
    for cut in range(sz.cuts):
        (spectra,) = call(
            functools.partial(transform_kernel, sz),
            [(2 * sz.planes_total, sz.share)],
            [*weak[cut], ahead, table["waves"]],
            [(-(-sz.share // LANES), 2 * sz.planes_total, LANES), (2, sz.planes_total, sz.share)],
            [pltpu.VMEM] * sz.n_mode + [pl.ANY, pltpu.VMEM],
        )
        spectra = spectra.reshape(sz.n_mode * sz.spots, sz.own, sz.share)
        terms.append(lax.all_to_all(spectra, ("mode", "ex", "ey"), split_axis=0, concat_axis=0, tiled=True))
        ahead = terms[cut]
    names = ("in_y", "in_x", "pair_y", "pair_x", "out_y", "out_x", "lam_x", "lam_y")
    solved = call(
        functools.partial(smooth_kernel, sz),
        [(sz.own, sz.lane_nodes)] * sz.spots,
        terms + [table[name] for name in names],
        [(PARTS * sz.x_pad, LANES), (PARTS * sz.x_eig, LANES), (PARTS * sz.x_eig, LANES)],
    )
    for step in range(1, sz.spots):
        shift, turn = step // sz.n_ey, step % sz.n_ey
        pairs = [
            (p * sz.n_ey + q, (p + shift) % sz.n_ex * sz.n_ey + (q + turn) % sz.n_ey)
            for p in range(sz.n_ex)
            for q in range(sz.n_ey)
        ]
        solved[step] = lax.ppermute(solved[step], ("ex", "ey"), pairs)
    (out,) = call(
        functools.partial(spread_kernel, sz),
        [(flat, LANES)],
        solved,
        [(sz.columns, sz.lane_nodes), (sz.lane_nodes, LANES)],
    )
    return out.reshape(sz.nodes, sz.nodes, sz.elems, sz.rows, sz.columns)


def solution(mesh):
    spec = P(None, None, "ex", "ey", "mode")

    def whole(stream_speed, normal_speed):
        shape = stream_speed.shape
        counts = mesh.shape
        block = shape[:2] + (shape[2] // counts["ex"], shape[3] // counts["ey"], shape[4] // counts["mode"])
        sz = Sizes(counts, block)
        return jax.shard_map(
            functools.partial(on_device, sz, host_tables(sz)),
            mesh=mesh,
            in_specs=(spec, spec),
            out_specs=spec,
            check_vma=False,
        )(stream_speed, normal_speed)

    return whole
```

```python
import functools
import math

import jax
import jax.numpy as jnp
import ml_dtypes
import numpy as np
from jax import lax
from jax.experimental import pallas as pl
from jax.experimental.pallas import tpu as pltpu
from jax.sharding import PartitionSpec as P

BF16 = ml_dtypes.bfloat16

element_width = 2.0
shift_base = 10.0
span_rate = 0.0125


def legendre_pair(degree, points):
    before = points * 0.0 + 1.0
    current = points.copy()
    for step in range(1, degree):
        upcoming = ((2 * step + 1) * points * current - step * before) / (step + 1)
        before = current
        current = upcoming
    return (current, before)


def legendre_slope(degree, points):
    current, before = legendre_pair(degree, points)
    return (current, degree * (points * current - before) / (points * points - 1.0))


def lobatto_points(order):
    guesses = -np.cos(np.pi * np.arange(1, order) / order)
    for step in range(60):
        current, slope = legendre_slope(order, guesses)
        second = (2.0 * guesses * slope - order * (order + 1) * current) / (1.0 - guesses * guesses)
        guesses = guesses - slope / second
    return guesses


def gauss_rule(count):
    guesses = -np.cos(np.pi * (np.arange(count) + 0.75) / (count + 0.5))
    for step in range(60):
        current, slope = legendre_slope(count, guesses)
        guesses = guesses - current / slope
    current, slope = legendre_slope(count, guesses)
    return (guesses, 2.0 / ((1.0 - guesses * guesses) * slope * slope))


def jacobi_eigen(matrix):
    size_n = matrix.shape[0]
    work = matrix.copy()
    vectors = np.eye(size_n)
    for sweep_number in range(20):
        for first in range(size_n):
            for second in range(first + 1, size_n):
                coupling = work[first, second]
                if abs(coupling) > 1e-300:
                    theta = (work[second, second] - work[first, first]) / (2.0 * coupling)
                    direction = 1.0 if theta >= 0.0 else -1.0
                    tangent = direction / (abs(theta) + np.sqrt(theta * theta + 1.0))
                    cosine = 1.0 / np.sqrt(tangent * tangent + 1.0)
                    sine = tangent * cosine
                    rotation = np.eye(size_n)
                    rotation[first, first] = cosine
                    rotation[second, second] = cosine
                    rotation[first, second] = sine
                    rotation[second, first] = -sine
                    work = rotation.T @ work @ rotation
                    vectors = vectors @ rotation
    diagonal_index = np.arange(size_n)
    return (work[diagonal_index, diagonal_index], vectors)


def extended_basis(stiffness, weights, left_width, centre_width, right_width):
    node_count = weights.shape[0]
    full_count = 3 * node_count - 2
    stiff_full = np.zeros((full_count, full_count))
    mass_full = np.zeros(full_count)
    for position, span_width in enumerate((left_width, centre_width, right_width)):
        if span_width > 0.0:
            first_node = position * (node_count - 1)
            stiff_full[
                first_node : first_node + node_count, first_node : first_node + node_count
            ] += stiffness * (2.0 / span_width)
            mass_full[first_node : first_node + node_count] += weights * (span_width / 2.0)
    low_index = node_count - 2
    high_index = low_index + node_count + 2
    stiff_ext = stiff_full[low_index:high_index, low_index:high_index].copy()
    mass_ext = mass_full[low_index:high_index].copy()
    frozen_list = []
    if left_width <= 0.0:
        frozen_list += [0, 1]
    if right_width <= 0.0:
        frozen_list += [node_count, node_count + 1]
    for frozen_index in frozen_list:
        stiff_ext[frozen_index, :] = 0.0
        stiff_ext[:, frozen_index] = 0.0
        stiff_ext[frozen_index, frozen_index] = 1.0
        mass_ext[frozen_index] = 1.0
    inverse_root = 1.0 / np.sqrt(mass_ext)
    lambdas, vectors = jacobi_eigen(inverse_root[:, None] * stiff_ext * inverse_root[None, :])
    return (inverse_root[:, None] * vectors, lambdas)


def spectral_tables(order, rows_total):
    inner_points = lobatto_points(order)
    points = np.concatenate([[-1.0], inner_points, [1.0]])
    values, unused_before = legendre_pair(order, points)
    weights = 2.0 / (order * (order + 1) * values**2)
    identity = np.eye(order + 1)
    point_gaps = points[:, None] - points[None, :] + identity
    derivative = values[:, None] / (values[None, :] * point_gaps) * (1.0 - identity)
    derivative[0, 0] = -order * (order + 1) / 4.0
    derivative[order, order] = order * (order + 1) / 4.0
    stiffness = derivative.T @ (weights[:, None] * derivative)
    gauss_points, gauss_weights = gauss_rule(3 * (order + 1) // 2)
    offsets = gauss_points[:, None, None] - points[None, None, :]
    numerators = np.prod(np.where(identity[None, :, :] > 0.5, 1.0, offsets), axis=2)
    denominators = np.prod(np.where(identity > 0.5, 1.0, points[:, None] - points[None, :]), axis=1)
    interp = numerators / denominators[None, :]
    heights = 0.6 + 1.4 * np.sin(np.pi * (np.arange(rows_total) + 0.5) / rows_total)
    basis_x, lambdas_x = extended_basis(
        stiffness, weights, element_width, element_width, element_width
    )
    basis_rows = []
    lambda_rows = []
    for row_number in range(rows_total):
        below = heights[row_number - 1] if row_number > 0 else 0.0
        above = heights[row_number + 1] if row_number < rows_total - 1 else 0.0
        basis_one, lambda_one = extended_basis(
            stiffness, weights, below, heights[row_number], above
        )
        basis_rows.append(basis_one)
        lambda_rows.append(lambda_one)
    return (
        derivative,
        interp,
        gauss_weights,
        weights,
        stiffness,
        basis_x,
        lambdas_x,
        np.stack(basis_rows),
        np.stack(lambda_rows),
        heights,
    )


PARTS = 8
LANES = 128


def ceil_to(count, step):
    return -(-count // step) * step


class Sizes:
    def __init__(self, mesh_shape, block_shape):
        self.n_mode, self.n_ex, self.n_ey = (mesh_shape[name] for name in ("mode", "ex", "ey"))
        self.nodes, _, self.elems, self.rows, self.planes = block_shape
        self.order = self.nodes - 1
        self.gauss = 3 * self.nodes // 2
        self.rows_total = self.rows * self.n_ey
        self.elems_total = self.elems * self.n_ex
        self.planes_total = self.planes * self.n_mode
        self.block_x = self.order * self.elems + 1
        full_y = self.order * self.rows + 1
        self.inner = [
            [j for j in range(full_y) if not (p == 0 and j == 0) and not (p == self.n_ey - 1 and j == full_y - 1)]
            for p in range(self.n_ey)
        ]
        self.block_y = max(len(found) for found in self.inner)
        self.cuts = 2 if self.elems % 2 == 0 else 1
        self.cut_elems = self.elems // self.cuts
        self.cut_x = self.order * self.cut_elems + 1
        share = -(-self.cut_x * self.block_y // self.n_mode)
        self.share = ceil_to(share, LANES if share > 64 else 16)
        self.cut_nodes = self.share * self.n_mode
        self.lane_nodes = ceil_to(self.block_x * self.block_y + 2, LANES)
        self.columns = 2 * self.planes
        self.spots = self.n_ex * self.n_ey
        self.own = self.columns // self.spots
        self.folds = self.own // PARTS
        self.fold_width = LANES // self.folds
        self.points = self.nodes + 2
        self.x_cuts = self.n_ex * self.cuts * self.cut_x
        self.x_pad = ceil_to(max(self.x_cuts, self.n_ex * self.block_x), 16)
        self.x_eig = self.elems_total * self.points
        self.y_eig = self.rows_total * self.points
        self.fine = ceil_to(self.gauss * self.gauss, 16)
        assert self.own == PARTS * self.folds and self.x_eig % 16 == 0
        assert max(self.y_eig, self.n_ey * self.block_y) <= self.fold_width
        assert 2 * self.planes == LANES


def high_low(table):
    high = np.asarray(table, np.float32).astype(BF16)
    low = (np.asarray(table, np.float64) - high.astype(np.float64)).astype(BF16)
    return high, low


def beside(table):
    high, low = high_low(table)
    return np.concatenate([high, high, low], 1)


def host_tables(sz):
    derivative, interp, gauss_weights, weights, stiffness, basis_x, lam_x, basis_y, lam_y, heights = spectral_tables(
        sz.order, sz.rows_total
    )
    nodes, fine, points = sz.nodes, sz.fine, sz.points
    gauss_count = sz.gauss**2
    lift = np.zeros((3 * fine, nodes * nodes))
    lift[:gauss_count] = np.kron(interp, interp)
    lift[fine : fine + gauss_count] = np.kron(interp @ derivative, interp)
    lift[2 * fine : 2 * fine + gauss_count] = np.kron(interp, interp @ derivative)
    back = np.zeros((sz.n_ey, nodes * sz.block_y, sz.rows * fine))
    weighted = interp.T * gauss_weights[None, :]
    for place in range(sz.n_ey):
        for f in range(sz.rows):
            for jj, j in enumerate(sz.inner[place]):
                b = j - sz.order * f
                if 0 <= b < nodes:
                    back[place, jj :: sz.block_y, f * fine : f * fine + gauss_count] = -np.kron(
                        weighted, weighted[b : b + 1]
                    )
    grid_x, grid_y = sz.order * sz.elems_total, sz.order * sz.rows_total + 1
    to_x, stiff_x, mass_x = np.zeros((sz.x_eig, grid_x)), np.zeros((grid_x, grid_x)), np.zeros(grid_x)
    for e in range(sz.elems_total):
        for t in range(points):
            to_x[e * points : (e + 1) * points, (sz.order * e + t - 1) % grid_x] += basis_x[t]
        index = (sz.order * e + np.arange(nodes)) % grid_x
        stiff_x[np.ix_(index, index)] += stiffness * (2.0 / element_width)
        mass_x[index] += weights * (element_width / 2.0)
    to_y, stiff_y, mass_y = np.zeros((sz.y_eig, grid_y)), np.zeros((grid_y, grid_y)), np.zeros(grid_y)
    for f in range(sz.rows_total):
        for t in range(points):
            y = sz.order * f + t - 1
            if 0 < y < grid_y - 1:
                to_y[f * points : (f + 1) * points, y] = basis_y[f][t]
        index = sz.order * f + np.arange(nodes)
        stiff_y[np.ix_(index, index)] += stiffness * (2.0 / heights[f])
        mass_y[index] += weights * (heights[f] / 2.0)
    stiff_xx, mass_xx = to_x @ stiff_x @ to_x.T, (to_x * mass_x) @ to_x.T
    stiff_yy, mass_yy = to_y @ stiff_y @ to_y.T, (to_y * mass_y) @ to_y.T
    def block_x(blocks, elems):
        length = sz.order * elems + 1
        nodes_of = [(sz.order * elems * p + i) % grid_x for p in range(blocks) for i in range(length)]
        table = np.zeros((sz.x_eig, sz.x_pad))
        table[:, : len(nodes_of)] = to_x[:, nodes_of]
        return table

    width, folds = sz.fold_width, sz.folds
    block_y = np.zeros((width, width))
    for place in range(sz.n_ey):
        for jj, j in enumerate(sz.inner[place]):
            block_y[place * sz.block_y + jj, : sz.y_eig] = to_y[:, sz.order * sz.rows * place + j]

    def folded(table):
        padded = np.zeros((width, width))
        padded[: table.shape[0], : table.shape[1]] = table
        return np.kron(np.eye(folds), padded)

    def one_dot(table):
        high, low = high_low(folded(table))
        return np.block([[high, low], [high, np.zeros_like(low)]]).astype(BF16)

    mass_pair, stiff_pair = high_low(folded(mass_yy)), high_low(folded(stiff_yy))
    heads = np.concatenate([mass_pair[0], stiff_pair[0]], 1)
    tails = np.concatenate([mass_pair[1], stiff_pair[1]], 1)
    lam_lanes = np.ones((1, folds, width))
    lam_lanes[:, :, : sz.y_eig] = lam_y.reshape(-1)
    planes_total = sz.planes_total
    turns = np.arange(planes_total)[None, :] * np.arange(planes_total // 2)[:, None] % planes_total
    angles = turns * (2.0 * math.pi / planes_total)
    waves = np.stack([np.cos(angles), -np.sin(angles)], 1).reshape(planes_total, planes_total) / planes_total
    return dict(
        heights=np.asarray(heights, np.float32),
        lift=beside(lift),
        back=np.stack([beside(table) for table in back]),
        waves=np.stack(high_low(waves)),
        in_y=one_dot(block_y),
        in_x=beside(block_x(sz.n_ex * sz.cuts, sz.cut_elems)),
        pair_y=np.concatenate([heads, heads, tails], 0),
        pair_x=beside(np.concatenate([stiff_xx, mass_xx], 1)),
        out_y=one_dot(block_y.T),
        out_x=beside(block_x(sz.n_ex, sz.elems).T),
        lam_x=np.asarray(np.tile(lam_x, sz.elems_total)[:, None] * np.ones((1, LANES)), np.float32),
        lam_y=np.asarray(lam_lanes.reshape(1, LANES), np.float32),
    )


def split(value):
    high = value.astype(jnp.bfloat16)
    low = (value - high.astype(jnp.float32)).astype(jnp.bfloat16)
    return high, low


def dot(left, right):
    return lax.dot_general(left, right, (((1,), (0,)), ((), ())), preferred_element_type=jnp.float32)


def below(value):
    high, low = split(value)
    return jnp.concatenate([high, low, high], 0)


def along(value):
    return jnp.concatenate(split(value), 1)


def partner(spot, step, count):
    if count & (count - 1) == 0:
        return spot ^ step
    return (spot + step) % count


def origin(spot, step, count):
    if count & (count - 1) == 0:
        return spot ^ step
    return (spot - step + count) % count


def lane_index(shape):
    return lax.broadcasted_iota(jnp.int32, shape, len(shape) - 1)


def advect_kernel(sz, heights, stream_hbm, normal_hbm, lift_hbm, back_hbm, *others):
    out_refs, (total_ref, stream_ref, normal_ref, lift_ref, back_ref, arrived) = others[:-6], others[-6:]
    place = lax.axis_index("ey")
    fetched = [
        pltpu.make_async_copy(source, target, arrived.at[i])
        for i, (source, target) in enumerate(
            (
                (stream_hbm, stream_ref),
                (normal_hbm, normal_ref),
                (lift_hbm, lift_ref),
                (back_hbm.at[place], back_ref),
            )
        )
    ]
    for copy in fetched:
        copy.start()
    count, fine, rows = sz.nodes * sz.nodes, sz.fine, sz.rows
    spots = sz.elems * rows
    half = lane_index((fine, LANES)) < sz.planes
    column, step = sz.nodes * sz.block_y, sz.order * sz.block_y
    factors = [
        sum(jnp.where(place == q, heights[q * rows + f] * 0.5, 0.0) for q in range(sz.n_ey)) for f in range(rows)
    ]
    full = sz.cut_x * sz.block_y // 8 * 8
    total_ref[pl.ds(full, sz.cut_nodes - full), :] = jnp.zeros((sz.cut_nodes - full, LANES), jnp.float32)
    spot = lax.axis_index("mode")
    for copy in fetched[:3]:
        copy.wait()
    for cut in range(sz.cuts):
        products = []
        for e in range(cut * sz.cut_elems, (cut + 1) * sz.cut_elems):
            speeds = jnp.concatenate(
                [
                    ref[pl.ds(e * rows + f, count, stride=spots), :]
                    for f in range(rows)
                    for ref in (stream_ref, normal_ref)
                ],
                1,
            )
            values = dot(lift_ref[...], below(speeds))
            highs, lows = [], []
            for f in range(rows):
                mine = values[:, f * LANES : (f + 1) * LANES]
                both, slope_x, slope_y = mine[:fine], mine[fine : 2 * fine], mine[2 * fine :]
                turned = pltpu.roll(both, sz.planes, 1)
                stream = jnp.where(half, both, turned)
                normal = jnp.where(half, turned, both)
                high, low = split((stream * factors[f]) * slope_x + (normal * (element_width * 0.5)) * slope_y)
                highs.append(high)
                lows.append(low)
            products.append(jnp.concatenate(highs + lows + highs, 0))
        if cut == 0:
            fetched[3].wait()
        weak = dot(back_ref[...], jnp.concatenate(products, 1))
        carry = None
        for e in range(sz.cut_elems):
            mine = weak[:, e * LANES : (e + 1) * LANES]
            if carry is not None:
                gap = jnp.zeros((column - carry.shape[0], LANES), jnp.float32)
                mine = mine + jnp.concatenate([carry, gap], 0)
            length = step if e < sz.cut_elems - 1 else column
            total_ref[pl.ds(e * step, length), :] = mine[:length]
            carry = mine[length:]
        for turn in range(sz.n_mode):
            goal = partner(spot, turn, sz.n_mode)
            out_refs[cut * sz.n_mode + turn][...] = total_ref[pl.ds(pl.multiple_of(goal * sz.share, 8), sz.share), :]


def transform_kernel(sz, *refs):
    weak_refs, (waves_ref, out_ref, mixed_ref, signal_ref) = refs[: sz.n_mode], refs[-4:]
    spot = lax.axis_index("mode")
    for step, weak_ref in enumerate(weak_refs):
        turned = weak_ref[...].T
        first = pl.multiple_of(origin(spot, step, sz.n_mode) * sz.planes, 8)
        for k in range(2):
            signal_ref[k, pl.ds(first, sz.planes), :] = turned[k * sz.planes : (k + 1) * sz.planes]
    modes = sz.planes_total
    for k in range(2):
        high, low = split(signal_ref[k])
        part = dot(waves_ref[0], high) + dot(waves_ref[0], low) + dot(waves_ref[1], high)
        for t in range(mixed_ref.shape[0]):
            tile = part[:, t * LANES : (t + 1) * LANES]
            mixed_ref[t, pl.ds(k, modes, stride=2), pl.ds(0, tile.shape[1])] = tile
    for t in range(mixed_ref.shape[0]):
        last = min(LANES, sz.share - t * LANES)
        out_ref[:, pl.ds(t * LANES, last)] = mixed_ref[t, :, pl.ds(0, last)]


def smooth_kernel(
    sz,
    *refs,
):
    terms_refs, out_refs, (field_ref, first_ref, work_ref) = refs[: sz.cuts], refs[sz.cuts + 8 : -3], refs[-3:]
    in_y_ref, in_x_ref, pair_y_ref, pair_x_ref, out_y_ref, out_x_ref, lam_x_ref, lam_y_ref = refs[
        sz.cuts : sz.cuts + 8
    ]
    width, folds, strip = sz.fold_width, sz.folds, sz.block_y
    tiles = -(-sz.cut_nodes // LANES)
    lanes = lane_index((PARTS, LANES))
    x_pad, x_eig = sz.x_pad, sz.x_eig
    place, spot = lax.axis_index("ey"), lax.axis_index("ex")
    device = (lax.axis_index("mode") * sz.n_ex + spot) * sz.n_ey + place
    first_mode = device * (sz.own // 4)

    for c in range(PARTS):
        field_ref[pl.ds(c * x_pad + sz.x_cuts, x_pad - sz.x_cuts), :] = jnp.zeros(
            (x_pad - sz.x_cuts, LANES), jnp.float32
        )
    for p, cut in [(p, cut) for p in range(sz.n_ex) for cut in range(sz.cuts)]:
        block = (spot + p) % sz.n_ex
        held = {}
        for q in range(sz.n_ey):
            for fold in range(folds):
                whole = jnp.concatenate(
                    [
                        terms_refs[cut][(z * sz.n_ex + block) * sz.n_ey + q, pl.ds(fold * PARTS, PARTS), :]
                        for z in range(sz.n_mode)
                    ],
                    1,
                )
                held[q, fold] = [whole[:, t * LANES : (t + 1) * LANES] for t in range(tiles)]
        for i in range(sz.cut_x):
            start = i * strip
            t, r = start // LANES, start % LANES
            result = jnp.zeros((PARTS, LANES), jnp.float32)
            for fold in range(folds):
                for q in range(sz.n_ey):
                    source = held[q, fold][t]
                    if r + strip > LANES:
                        source = jnp.where(lanes >= r, source, held[q, fold][t + 1])
                    goal = fold * width + q * strip
                    moved = pltpu.roll(source, (goal - r) % LANES, 1) if goal != r else source
                    result = jnp.where((lanes >= goal) & (lanes < goal + strip), moved, result)
            field_ref[pl.ds((p * sz.cuts + cut) * sz.cut_x + i, PARTS, stride=x_pad), :] = result

    parts = dot(along(field_ref[...]), in_y_ref[...])
    field_ref[...] = parts[:, :LANES] + parts[:, LANES:]
    fold_of_lane = lane_index((1, LANES)) // width
    shifts, inverses = [], []
    for group in range(PARTS // 4):
        mode = (first_mode + fold_of_lane * (PARTS // 4) + group).astype(jnp.float32)
        shift = shift_base + (span_rate * mode) ** 2
        shifts.append(shift)
        inverses.append(1.0 / (lam_x_ref[...] + (lam_y_ref[...] + shift)))
    for c in range(0, PARTS, 2):
        pair = jnp.concatenate([field_ref[pl.ds((c + d) * x_pad, x_pad), :] for d in range(2)], 1)
        forced = dot(in_x_ref[...], below(pair))
        for d in range(2):
            mine = forced[:, d * LANES : (d + 1) * LANES]
            first_ref[pl.ds((c + d) * x_eig, x_eig), :] = mine
            work_ref[pl.ds((c + d) * x_eig, x_eig), :] = mine * inverses[(c + d) // 4]
    for c in range(0, PARTS, 2):
        shift = shifts[c // 4]
        masses, stiffs = [], []
        for d in range(2):
            high, low = split(work_ref[pl.ds((c + d) * x_eig, x_eig), :])
            both = dot(jnp.concatenate([high, low, high], 1), pair_y_ref[...])
            masses.append(both[:, :LANES])
            stiffs.append(both[:, LANES:] + shift * both[:, :LANES])
        stacked = jnp.concatenate([jnp.concatenate(masses, 1), jnp.concatenate(stiffs, 1)], 0)
        applied = dot(pair_x_ref[...], below(stacked))
        for d in range(2):
            rows = pl.ds((c + d) * x_eig, x_eig)
            total = (2.0 * first_ref[rows, :] - applied[:, d * LANES : (d + 1) * LANES]) * inverses[c // 4]
            parts = dot(along(total), out_y_ref[...])
            work_ref[rows, :] = parts[:, :LANES] + parts[:, LANES:]
        pair = jnp.concatenate([work_ref[pl.ds((c + d) * x_eig, x_eig), :] for d in range(2)], 1)
        solved = dot(out_x_ref[...], below(pair))
        for d in range(2):
            field_ref[pl.ds((c + d) * x_pad, x_pad), :] = solved[:, d * LANES : (d + 1) * LANES]

    for p in range(sz.n_ex):
        made = {}
        for i in range(sz.block_x):
            source = field_ref[pl.ds(p * sz.block_x + i, PARTS, stride=x_pad), :]
            for q in range(sz.n_ey):
                begin = i * strip + sz.inner[q][0]
                count = len(sz.inner[q])
                t, r = begin // LANES, begin % LANES
                for fold in range(folds):
                    origin = fold * width + q * strip
                    moved = pltpu.roll(source, (r - origin) % LANES, 1) if origin != r else source
                    for tile, low, high in ((t, r, r + count), (t + 1, 0, r + count - LANES)):
                        if high > 0:
                            old = made.get((q, fold, tile))
                            if old is None:
                                old = jnp.zeros((PARTS, LANES), jnp.float32)
                            made[q, fold, tile] = jnp.where((lanes >= low) & (lanes < high), moved, old)
        for fold in range(folds):
            for tile in range(sz.lane_nodes // LANES):
                for turn in range(sz.n_ey):
                    chosen = jnp.zeros((PARTS, LANES), jnp.float32)
                    for q in range(sz.n_ey):
                        if (q, fold, tile) in made:
                            chosen = jnp.where((place + turn) % sz.n_ey == q, made[q, fold, tile], chosen)
                    out_refs[p * sz.n_ey + turn][pl.ds(fold * PARTS, PARTS), pl.ds(tile * LANES, LANES)] = chosen


def spread_kernel(sz, *refs):
    solved_refs, (out_ref, stacked_ref, turned_ref) = refs[:-3], refs[-3:]
    place, spot = lax.axis_index("ey"), lax.axis_index("ex")
    for step, solved_ref in enumerate(solved_refs):
        shift, turn = step // sz.n_ey, step % sz.n_ey
        source = (spot - shift + sz.n_ex) % sz.n_ex * sz.n_ey + (place - turn + sz.n_ey) % sz.n_ey
        stacked_ref[pl.ds(pl.multiple_of(source * sz.own, PARTS), sz.own), :] = solved_ref[...]
    turned_ref[...] = stacked_ref[...].T
    spots = sz.elems * sz.rows
    for e in range(sz.elems):
        for f in range(sz.rows):
            for a in range(sz.nodes):
                start = sz.block_y * (sz.order * e + a) + sz.order * f
                out_ref[pl.ds(a * sz.nodes * spots + e * sz.rows + f, sz.nodes, stride=spots), :] = turned_ref[
                    pl.ds(start, sz.nodes), :
                ]
    blank = jnp.zeros((sz.elems, LANES), jnp.float32)

    @pl.when(place == 0)
    def _():
        for a in range(sz.nodes):
            out_ref[pl.ds(a * sz.nodes * spots, sz.elems, stride=sz.rows), :] = blank

    @pl.when(place == sz.n_ey - 1)
    def _():
        for a in range(sz.nodes):
            first = ((a + 1) * sz.nodes - 1) * spots + sz.rows - 1
            out_ref[pl.ds(first, sz.elems, stride=sz.rows), :] = blank


def call(kernel, shapes, operands, scratch=(), spaces=pltpu.VMEM, limit=16, flops=10**9):
    if not isinstance(spaces, list):
        spaces = [spaces] * len(operands)
    made = pl.pallas_call(
        kernel,
        out_shape=[jax.ShapeDtypeStruct(shape, jnp.float32) for shape in shapes],
        in_specs=[pl.BlockSpec(memory_space=space) for space in spaces],
        out_specs=[pl.BlockSpec(memory_space=pltpu.VMEM) for _ in shapes],
        scratch_shapes=[pltpu.VMEM(each, jnp.float32) if isinstance(each, tuple) else each for each in scratch],
        compiler_params=pltpu.CompilerParams(vmem_limit_bytes=limit * 2**20),
        cost_estimate=pl.CostEstimate(flops=flops, bytes_accessed=10**6, transcendentals=0),
    )(*operands)
    return list(made)


def on_device(sz, tables, stream_speed, normal_speed):
    flat = sz.nodes * sz.nodes * sz.elems * sz.rows
    table = {name: jnp.asarray(value) for name, value in tables.items() if name != "heights"}
    heights = [float(height) for height in tables["heights"]]
    pieces = call(
        functools.partial(advect_kernel, sz, heights),
        [(sz.share, LANES)] * (sz.n_mode * sz.cuts),
        [
            stream_speed.reshape(flat, sz.planes),
            normal_speed.reshape(flat, sz.planes),
            table["lift"],
            table["back"],
        ],
        [
            (sz.cut_nodes, LANES),
            (flat, sz.planes),
            (flat, sz.planes),
            pltpu.VMEM(tables["lift"].shape, jnp.bfloat16),
            pltpu.VMEM(tables["back"].shape[1:], jnp.bfloat16),
            pltpu.SemaphoreType.DMA((4,)),
        ],
        pltpu.HBM,
        60,
    )
    weak = [pieces[cut * sz.n_mode : (cut + 1) * sz.n_mode] for cut in range(sz.cuts)]
    for cut in range(sz.cuts):
        for step in sorted(range(1, sz.n_mode), key=lambda each: (each & -each, each), reverse=True):
            pairs = [(z, partner(z, step, sz.n_mode)) for z in range(sz.n_mode)]
            weak[cut][step] = lax.ppermute(weak[cut][step], "mode", pairs)
    terms, ahead = [], []
    for cut in range(sz.cuts):
        (spectra,) = call(
            functools.partial(transform_kernel, sz),
            [(2 * sz.planes_total, sz.share)],
            [*weak[cut], *ahead, table["waves"]],
            [(-(-sz.share // LANES), 2 * sz.planes_total, LANES), (2, sz.planes_total, sz.share)],
            [pltpu.VMEM] * sz.n_mode + [pl.ANY] * len(ahead) + [pltpu.VMEM],
            flops=10**11 if cut == sz.cuts - 1 else 10**8,
        )
        spectra = spectra.reshape(sz.n_mode * sz.spots, sz.own, sz.share)
        terms.append(lax.all_to_all(spectra, ("mode", "ex", "ey"), split_axis=0, concat_axis=0, tiled=True))
        ahead = [spectra]
    names = ("in_y", "in_x", "pair_y", "pair_x", "out_y", "out_x", "lam_x", "lam_y")
    solved = call(
        functools.partial(smooth_kernel, sz),
        [(sz.own, sz.lane_nodes)] * sz.spots,
        terms + [table[name] for name in names],
        [(PARTS * sz.x_pad, LANES), (PARTS * sz.x_eig, LANES), (PARTS * sz.x_eig, LANES)],
    )
    for step in range(1, sz.spots):
        shift, turn = step // sz.n_ey, step % sz.n_ey
        pairs = [
            (p * sz.n_ey + q, (p + shift) % sz.n_ex * sz.n_ey + (q + turn) % sz.n_ey)
            for p in range(sz.n_ex)
            for q in range(sz.n_ey)
        ]
        solved[step] = lax.ppermute(solved[step], ("ex", "ey"), pairs)
    (out,) = call(
        functools.partial(spread_kernel, sz),
        [(flat, LANES)],
        solved,
        [(sz.columns, sz.lane_nodes), (sz.lane_nodes, LANES)],
    )
    return out.reshape(sz.nodes, sz.nodes, sz.elems, sz.rows, sz.columns)


def solution(mesh):
    spec = P(None, None, "ex", "ey", "mode")

    def whole(stream_speed, normal_speed):
        shape = stream_speed.shape
        counts = mesh.shape
        block = shape[:2] + (shape[2] // counts["ex"], shape[3] // counts["ey"], shape[4] // counts["mode"])
        sz = Sizes(counts, block)
        return jax.shard_map(
            functools.partial(on_device, sz, host_tables(sz)),
            mesh=mesh,
            in_specs=(spec, spec),
            out_specs=spec,
            check_vma=False,
        )(stream_speed, normal_speed)

    return whole
```

```python
import functools
import math

import jax
import jax.numpy as jnp
import ml_dtypes
import numpy as np
from jax import lax
from jax.experimental import pallas as pl
from jax.experimental.pallas import tpu as pltpu
from jax.sharding import PartitionSpec as P

BF16 = ml_dtypes.bfloat16

element_width = 2.0
shift_base = 10.0
span_rate = 0.0125


def legendre_pair(degree, points):
    before = points * 0.0 + 1.0
    current = points.copy()
    for step in range(1, degree):
        upcoming = ((2 * step + 1) * points * current - step * before) / (step + 1)
        before = current
        current = upcoming
    return (current, before)


def legendre_slope(degree, points):
    current, before = legendre_pair(degree, points)
    return (current, degree * (points * current - before) / (points * points - 1.0))


def lobatto_points(order):
    guesses = -np.cos(np.pi * np.arange(1, order) / order)
    for step in range(60):
        current, slope = legendre_slope(order, guesses)
        second = (2.0 * guesses * slope - order * (order + 1) * current) / (1.0 - guesses * guesses)
        guesses = guesses - slope / second
    return guesses


def gauss_rule(count):
    guesses = -np.cos(np.pi * (np.arange(count) + 0.75) / (count + 0.5))
    for step in range(60):
        current, slope = legendre_slope(count, guesses)
        guesses = guesses - current / slope
    current, slope = legendre_slope(count, guesses)
    return (guesses, 2.0 / ((1.0 - guesses * guesses) * slope * slope))


def jacobi_eigen(matrix):
    size_n = matrix.shape[0]
    work = matrix.copy()
    vectors = np.eye(size_n)
    for sweep_number in range(20):
        for first in range(size_n):
            for second in range(first + 1, size_n):
                coupling = work[first, second]
                if abs(coupling) > 1e-300:
                    theta = (work[second, second] - work[first, first]) / (2.0 * coupling)
                    direction = 1.0 if theta >= 0.0 else -1.0
                    tangent = direction / (abs(theta) + np.sqrt(theta * theta + 1.0))
                    cosine = 1.0 / np.sqrt(tangent * tangent + 1.0)
                    sine = tangent * cosine
                    rotation = np.eye(size_n)
                    rotation[first, first] = cosine
                    rotation[second, second] = cosine
                    rotation[first, second] = sine
                    rotation[second, first] = -sine
                    work = rotation.T @ work @ rotation
                    vectors = vectors @ rotation
    diagonal_index = np.arange(size_n)
    return (work[diagonal_index, diagonal_index], vectors)


def extended_basis(stiffness, weights, left_width, centre_width, right_width):
    node_count = weights.shape[0]
    full_count = 3 * node_count - 2
    stiff_full = np.zeros((full_count, full_count))
    mass_full = np.zeros(full_count)
    for position, span_width in enumerate((left_width, centre_width, right_width)):
        if span_width > 0.0:
            first_node = position * (node_count - 1)
            stiff_full[
                first_node : first_node + node_count, first_node : first_node + node_count
            ] += stiffness * (2.0 / span_width)
            mass_full[first_node : first_node + node_count] += weights * (span_width / 2.0)
    low_index = node_count - 2
    high_index = low_index + node_count + 2
    stiff_ext = stiff_full[low_index:high_index, low_index:high_index].copy()
    mass_ext = mass_full[low_index:high_index].copy()
    frozen_list = []
    if left_width <= 0.0:
        frozen_list += [0, 1]
    if right_width <= 0.0:
        frozen_list += [node_count, node_count + 1]
    for frozen_index in frozen_list:
        stiff_ext[frozen_index, :] = 0.0
        stiff_ext[:, frozen_index] = 0.0
        stiff_ext[frozen_index, frozen_index] = 1.0
        mass_ext[frozen_index] = 1.0
    inverse_root = 1.0 / np.sqrt(mass_ext)
    lambdas, vectors = jacobi_eigen(inverse_root[:, None] * stiff_ext * inverse_root[None, :])
    return (inverse_root[:, None] * vectors, lambdas)


def spectral_tables(order, rows_total):
    inner_points = lobatto_points(order)
    points = np.concatenate([[-1.0], inner_points, [1.0]])
    values, unused_before = legendre_pair(order, points)
    weights = 2.0 / (order * (order + 1) * values**2)
    identity = np.eye(order + 1)
    point_gaps = points[:, None] - points[None, :] + identity
    derivative = values[:, None] / (values[None, :] * point_gaps) * (1.0 - identity)
    derivative[0, 0] = -order * (order + 1) / 4.0
    derivative[order, order] = order * (order + 1) / 4.0
    stiffness = derivative.T @ (weights[:, None] * derivative)
    gauss_points, gauss_weights = gauss_rule(3 * (order + 1) // 2)
    offsets = gauss_points[:, None, None] - points[None, None, :]
    numerators = np.prod(np.where(identity[None, :, :] > 0.5, 1.0, offsets), axis=2)
    denominators = np.prod(np.where(identity > 0.5, 1.0, points[:, None] - points[None, :]), axis=1)
    interp = numerators / denominators[None, :]
    heights = 0.6 + 1.4 * np.sin(np.pi * (np.arange(rows_total) + 0.5) / rows_total)
    basis_x, lambdas_x = extended_basis(
        stiffness, weights, element_width, element_width, element_width
    )
    basis_rows = []
    lambda_rows = []
    for row_number in range(rows_total):
        below = heights[row_number - 1] if row_number > 0 else 0.0
        above = heights[row_number + 1] if row_number < rows_total - 1 else 0.0
        basis_one, lambda_one = extended_basis(
            stiffness, weights, below, heights[row_number], above
        )
        basis_rows.append(basis_one)
        lambda_rows.append(lambda_one)
    return (
        derivative,
        interp,
        gauss_weights,
        weights,
        stiffness,
        basis_x,
        lambdas_x,
        np.stack(basis_rows),
        np.stack(lambda_rows),
        heights,
    )


PARTS = 8
LANES = 128


def ceil_to(count, step):
    return -(-count // step) * step


class Sizes:
    def __init__(self, mesh_shape, block_shape):
        self.n_mode, self.n_ex, self.n_ey = (mesh_shape[name] for name in ("mode", "ex", "ey"))
        self.nodes, _, self.elems, self.rows, self.planes = block_shape
        self.order = self.nodes - 1
        self.gauss = 3 * self.nodes // 2
        self.rows_total = self.rows * self.n_ey
        self.elems_total = self.elems * self.n_ex
        self.planes_total = self.planes * self.n_mode
        self.block_x = self.order * self.elems + 1
        full_y = self.order * self.rows + 1
        self.inner = [
            [j for j in range(full_y) if not (p == 0 and j == 0) and not (p == self.n_ey - 1 and j == full_y - 1)]
            for p in range(self.n_ey)
        ]
        self.block_y = max(len(found) for found in self.inner)
        self.cuts = 1
        self.cut_elems = self.elems // self.cuts
        self.cut_x = self.order * self.cut_elems + 1
        share = -(-self.cut_x * self.block_y // self.n_mode)
        self.share = ceil_to(share, LANES if share > 64 else 16)
        self.cut_nodes = self.share * self.n_mode
        self.lane_nodes = ceil_to(self.block_x * self.block_y + 2, LANES)
        self.columns = 2 * self.planes
        self.spots = self.n_ex * self.n_ey
        self.own = self.columns // self.spots
        self.folds = self.own // PARTS
        self.fold_width = LANES // self.folds
        self.points = self.nodes + 2
        self.x_cuts = self.n_ex * self.cuts * self.cut_x
        self.x_pad = ceil_to(max(self.x_cuts, self.n_ex * self.block_x), 16)
        self.x_eig = self.elems_total * self.points
        self.y_eig = self.rows_total * self.points
        self.fine = ceil_to(self.gauss * self.gauss, 16)
        assert self.own == PARTS * self.folds and self.x_eig % 16 == 0
        assert max(self.y_eig, self.n_ey * self.block_y) <= self.fold_width
        assert 2 * self.planes == LANES


def high_low(table):
    high = np.asarray(table, np.float32).astype(BF16)
    low = (np.asarray(table, np.float64) - high.astype(np.float64)).astype(BF16)
    return high, low


def beside(table):
    high, low = high_low(table)
    return np.concatenate([high, high, low], 1)


def host_tables(sz):
    derivative, interp, gauss_weights, weights, stiffness, basis_x, lam_x, basis_y, lam_y, heights = spectral_tables(
        sz.order, sz.rows_total
    )
    nodes, fine, points = sz.nodes, sz.fine, sz.points
    gauss_count = sz.gauss**2
    lift = np.zeros((3 * fine, nodes * nodes))
    lift[:gauss_count] = np.kron(interp, interp)
    lift[fine : fine + gauss_count] = np.kron(interp @ derivative, interp)
    lift[2 * fine : 2 * fine + gauss_count] = np.kron(interp, interp @ derivative)
    back = np.zeros((sz.n_ey, nodes * sz.block_y, sz.rows * fine))
    weighted = interp.T * gauss_weights[None, :]
    for place in range(sz.n_ey):
        for f in range(sz.rows):
            for jj, j in enumerate(sz.inner[place]):
                b = j - sz.order * f
                if 0 <= b < nodes:
                    back[place, jj :: sz.block_y, f * fine : f * fine + gauss_count] = -np.kron(
                        weighted, weighted[b : b + 1]
                    )
    grid_x, grid_y = sz.order * sz.elems_total, sz.order * sz.rows_total + 1
    to_x, stiff_x, mass_x = np.zeros((sz.x_eig, grid_x)), np.zeros((grid_x, grid_x)), np.zeros(grid_x)
    for e in range(sz.elems_total):
        for t in range(points):
            to_x[e * points : (e + 1) * points, (sz.order * e + t - 1) % grid_x] += basis_x[t]
        index = (sz.order * e + np.arange(nodes)) % grid_x
        stiff_x[np.ix_(index, index)] += stiffness * (2.0 / element_width)
        mass_x[index] += weights * (element_width / 2.0)
    to_y, stiff_y, mass_y = np.zeros((sz.y_eig, grid_y)), np.zeros((grid_y, grid_y)), np.zeros(grid_y)
    for f in range(sz.rows_total):
        for t in range(points):
            y = sz.order * f + t - 1
            if 0 < y < grid_y - 1:
                to_y[f * points : (f + 1) * points, y] = basis_y[f][t]
        index = sz.order * f + np.arange(nodes)
        stiff_y[np.ix_(index, index)] += stiffness * (2.0 / heights[f])
        mass_y[index] += weights * (heights[f] / 2.0)
    stiff_xx, mass_xx = to_x @ stiff_x @ to_x.T, (to_x * mass_x) @ to_x.T
    stiff_yy, mass_yy = to_y @ stiff_y @ to_y.T, (to_y * mass_y) @ to_y.T
    def block_x(blocks, elems):
        length = sz.order * elems + 1
        nodes_of = [(sz.order * elems * p + i) % grid_x for p in range(blocks) for i in range(length)]
        table = np.zeros((sz.x_eig, sz.x_pad))
        table[:, : len(nodes_of)] = to_x[:, nodes_of]
        return table

    width, folds = sz.fold_width, sz.folds
    block_y = np.zeros((width, width))
    for place in range(sz.n_ey):
        for jj, j in enumerate(sz.inner[place]):
            block_y[place * sz.block_y + jj, : sz.y_eig] = to_y[:, sz.order * sz.rows * place + j]

    def folded(table):
        padded = np.zeros((width, width))
        padded[: table.shape[0], : table.shape[1]] = table
        return np.kron(np.eye(folds), padded)

    def one_dot(table):
        high, low = high_low(folded(table))
        return np.block([[high, low], [high, np.zeros_like(low)]]).astype(BF16)

    mass_pair, stiff_pair = high_low(folded(mass_yy)), high_low(folded(stiff_yy))
    heads = np.concatenate([mass_pair[0], stiff_pair[0]], 1)
    tails = np.concatenate([mass_pair[1], stiff_pair[1]], 1)
    lam_lanes = np.ones((1, folds, width))
    lam_lanes[:, :, : sz.y_eig] = lam_y.reshape(-1)
    planes_total = sz.planes_total
    turns = np.arange(planes_total)[None, :] * np.arange(planes_total // 2)[:, None] % planes_total
    angles = turns * (2.0 * math.pi / planes_total)
    waves = np.stack([np.cos(angles), -np.sin(angles)], 1).reshape(planes_total, planes_total) / planes_total
    return dict(
        heights=np.asarray(heights, np.float32),
        lift=beside(lift),
        back=np.stack([beside(table) for table in back]),
        waves=np.stack(high_low(waves)),
        in_y=one_dot(block_y),
        in_x=beside(block_x(sz.n_ex * sz.cuts, sz.cut_elems)),
        pair_y=np.concatenate([heads, heads, tails], 0),
        pair_x=beside(np.concatenate([stiff_xx, mass_xx], 1)),
        out_y=one_dot(block_y.T),
        out_x=beside(block_x(sz.n_ex, sz.elems).T),
        lam_x=np.asarray(np.tile(lam_x, sz.elems_total)[:, None] * np.ones((1, LANES)), np.float32),
        lam_y=np.asarray(lam_lanes.reshape(1, LANES), np.float32),
    )


def split(value):
    high = value.astype(jnp.bfloat16)
    low = (value - high.astype(jnp.float32)).astype(jnp.bfloat16)
    return high, low


def dot(left, right):
    return lax.dot_general(left, right, (((1,), (0,)), ((), ())), preferred_element_type=jnp.float32)


def below(value):
    high, low = split(value)
    return jnp.concatenate([high, low, high], 0)


def along(value):
    return jnp.concatenate(split(value), 1)


def partner(spot, step, count):
    if count & (count - 1) == 0:
        return spot ^ step
    return (spot + step) % count


def origin(spot, step, count):
    if count & (count - 1) == 0:
        return spot ^ step
    return (spot - step + count) % count


def lane_index(shape):
    return lax.broadcasted_iota(jnp.int32, shape, len(shape) - 1)


def advect_kernel(sz, heights, stream_hbm, normal_hbm, lift_hbm, back_hbm, *others):
    out_refs, (total_ref, stream_ref, normal_ref, lift_ref, back_ref, arrived) = others[:-6], others[-6:]
    place = lax.axis_index("ey")
    fetched = [
        pltpu.make_async_copy(source, target, arrived.at[i])
        for i, (source, target) in enumerate(
            (
                (stream_hbm, stream_ref),
                (normal_hbm, normal_ref),
                (lift_hbm, lift_ref),
                (back_hbm.at[place], back_ref),
            )
        )
    ]
    for copy in fetched:
        copy.start()
    count, fine, rows = sz.nodes * sz.nodes, sz.fine, sz.rows
    spots = sz.elems * rows
    half = lane_index((fine, LANES)) < sz.planes
    column, step = sz.nodes * sz.block_y, sz.order * sz.block_y
    factors = [
        sum(jnp.where(place == q, heights[q * rows + f] * 0.5, 0.0) for q in range(sz.n_ey)) for f in range(rows)
    ]
    full = sz.cut_x * sz.block_y // 8 * 8
    total_ref[pl.ds(full, sz.cut_nodes - full), :] = jnp.zeros((sz.cut_nodes - full, LANES), jnp.float32)
    spot = lax.axis_index("mode")
    for copy in fetched[:3]:
        copy.wait()
    for cut in range(sz.cuts):
        products = []
        for e in range(cut * sz.cut_elems, (cut + 1) * sz.cut_elems):
            speeds = jnp.concatenate(
                [
                    ref[pl.ds(e * rows + f, count, stride=spots), :]
                    for f in range(rows)
                    for ref in (stream_ref, normal_ref)
                ],
                1,
            )
            values = dot(lift_ref[...], below(speeds))
            highs, lows = [], []
            for f in range(rows):
                mine = values[:, f * LANES : (f + 1) * LANES]
                both, slope_x, slope_y = mine[:fine], mine[fine : 2 * fine], mine[2 * fine :]
                turned = pltpu.roll(both, sz.planes, 1)
                stream = jnp.where(half, both, turned)
                normal = jnp.where(half, turned, both)
                high, low = split((stream * factors[f]) * slope_x + (normal * (element_width * 0.5)) * slope_y)
                highs.append(high)
                lows.append(low)
            products.append(jnp.concatenate(highs + lows + highs, 0))
        if cut == 0:
            fetched[3].wait()
        weak = dot(back_ref[...], jnp.concatenate(products, 1))
        carry = None
        for e in range(sz.cut_elems):
            mine = weak[:, e * LANES : (e + 1) * LANES]
            if carry is not None:
                gap = jnp.zeros((column - carry.shape[0], LANES), jnp.float32)
                mine = mine + jnp.concatenate([carry, gap], 0)
            length = step if e < sz.cut_elems - 1 else column
            total_ref[pl.ds(e * step, length), :] = mine[:length]
            carry = mine[length:]
        for turn in range(sz.n_mode):
            goal = partner(spot, turn, sz.n_mode)
            out_refs[cut * sz.n_mode + turn][...] = total_ref[pl.ds(pl.multiple_of(goal * sz.share, 8), sz.share), :]


def transform_kernel(sz, *refs):
    weak_refs, (waves_ref, out_ref, mixed_ref, signal_ref) = refs[: sz.n_mode], refs[-4:]
    spot = lax.axis_index("mode")
    for step, weak_ref in enumerate(weak_refs):
        turned = weak_ref[...].T
        first = pl.multiple_of(origin(spot, step, sz.n_mode) * sz.planes, 8)
        for k in range(2):
            signal_ref[k, pl.ds(first, sz.planes), :] = turned[k * sz.planes : (k + 1) * sz.planes]
    modes = sz.planes_total
    for k in range(2):
        high, low = split(signal_ref[k])
        part = dot(waves_ref[0], high) + dot(waves_ref[0], low) + dot(waves_ref[1], high)
        for t in range(mixed_ref.shape[0]):
            tile = part[:, t * LANES : (t + 1) * LANES]
            mixed_ref[t, pl.ds(k, modes, stride=2), pl.ds(0, tile.shape[1])] = tile
    for t in range(mixed_ref.shape[0]):
        last = min(LANES, sz.share - t * LANES)
        out_ref[:, pl.ds(t * LANES, last)] = mixed_ref[t, :, pl.ds(0, last)]


def smooth_kernel(
    sz,
    *refs,
):
    terms_refs, out_refs, (field_ref, first_ref, work_ref) = refs[: sz.cuts], refs[sz.cuts + 8 : -3], refs[-3:]
    in_y_ref, in_x_ref, pair_y_ref, pair_x_ref, out_y_ref, out_x_ref, lam_x_ref, lam_y_ref = refs[
        sz.cuts : sz.cuts + 8
    ]
    width, folds, strip = sz.fold_width, sz.folds, sz.block_y
    tiles = -(-sz.cut_nodes // LANES)
    lanes = lane_index((PARTS, LANES))
    x_pad, x_eig = sz.x_pad, sz.x_eig
    place, spot = lax.axis_index("ey"), lax.axis_index("ex")
    device = (lax.axis_index("mode") * sz.n_ex + spot) * sz.n_ey + place
    first_mode = device * (sz.own // 4)

    for c in range(PARTS):
        field_ref[pl.ds(c * x_pad + sz.x_cuts, x_pad - sz.x_cuts), :] = jnp.zeros(
            (x_pad - sz.x_cuts, LANES), jnp.float32
        )
    for p, cut in [(p, cut) for p in range(sz.n_ex) for cut in range(sz.cuts)]:
        block = (spot + p) % sz.n_ex
        held = {}
        for q in range(sz.n_ey):
            for fold in range(folds):
                whole = jnp.concatenate(
                    [
                        terms_refs[cut][(z * sz.n_ex + block) * sz.n_ey + q, pl.ds(fold * PARTS, PARTS), :]
                        for z in range(sz.n_mode)
                    ],
                    1,
                )
                held[q, fold] = [whole[:, t * LANES : (t + 1) * LANES] for t in range(tiles)]
        for i in range(sz.cut_x):
            start = i * strip
            t, r = start // LANES, start % LANES
            result = jnp.zeros((PARTS, LANES), jnp.float32)
            for fold in range(folds):
                for q in range(sz.n_ey):
                    source = held[q, fold][t]
                    if r + strip > LANES:
                        source = jnp.where(lanes >= r, source, held[q, fold][t + 1])
                    goal = fold * width + q * strip
                    moved = pltpu.roll(source, (goal - r) % LANES, 1) if goal != r else source
                    result = jnp.where((lanes >= goal) & (lanes < goal + strip), moved, result)
            field_ref[pl.ds((p * sz.cuts + cut) * sz.cut_x + i, PARTS, stride=x_pad), :] = result

    parts = dot(along(field_ref[...]), in_y_ref[...])
    field_ref[...] = parts[:, :LANES] + parts[:, LANES:]
    fold_of_lane = lane_index((1, LANES)) // width
    shifts, inverses = [], []
    for group in range(PARTS // 4):
        mode = (first_mode + fold_of_lane * (PARTS // 4) + group).astype(jnp.float32)
        shift = shift_base + (span_rate * mode) ** 2
        shifts.append(shift)
        inverses.append(1.0 / (lam_x_ref[...] + (lam_y_ref[...] + shift)))
    for c in range(0, PARTS, 2):
        pair = jnp.concatenate([field_ref[pl.ds((c + d) * x_pad, x_pad), :] for d in range(2)], 1)
        forced = dot(in_x_ref[...], below(pair))
        for d in range(2):
            mine = forced[:, d * LANES : (d + 1) * LANES]
            first_ref[pl.ds((c + d) * x_eig, x_eig), :] = mine
            work_ref[pl.ds((c + d) * x_eig, x_eig), :] = mine * inverses[(c + d) // 4]
    for c in range(0, PARTS, 2):
        shift = shifts[c // 4]
        masses, stiffs = [], []
        for d in range(2):
            high, low = split(work_ref[pl.ds((c + d) * x_eig, x_eig), :])
            both = dot(jnp.concatenate([high, low, high], 1), pair_y_ref[...])
            masses.append(both[:, :LANES])
            stiffs.append(both[:, LANES:] + shift * both[:, :LANES])
        stacked = jnp.concatenate([jnp.concatenate(masses, 1), jnp.concatenate(stiffs, 1)], 0)
        applied = dot(pair_x_ref[...], below(stacked))
        for d in range(2):
            rows = pl.ds((c + d) * x_eig, x_eig)
            total = (2.0 * first_ref[rows, :] - applied[:, d * LANES : (d + 1) * LANES]) * inverses[c // 4]
            parts = dot(along(total), out_y_ref[...])
            work_ref[rows, :] = parts[:, :LANES] + parts[:, LANES:]
        pair = jnp.concatenate([work_ref[pl.ds((c + d) * x_eig, x_eig), :] for d in range(2)], 1)
        solved = dot(out_x_ref[...], below(pair))
        for d in range(2):
            field_ref[pl.ds((c + d) * x_pad, x_pad), :] = solved[:, d * LANES : (d + 1) * LANES]

    for p in range(sz.n_ex):
        made = {}
        for i in range(sz.block_x):
            source = field_ref[pl.ds(p * sz.block_x + i, PARTS, stride=x_pad), :]
            for q in range(sz.n_ey):
                begin = i * strip + sz.inner[q][0]
                count = len(sz.inner[q])
                t, r = begin // LANES, begin % LANES
                for fold in range(folds):
                    origin = fold * width + q * strip
                    moved = pltpu.roll(source, (r - origin) % LANES, 1) if origin != r else source
                    for tile, low, high in ((t, r, r + count), (t + 1, 0, r + count - LANES)):
                        if high > 0:
                            old = made.get((q, fold, tile))
                            if old is None:
                                old = jnp.zeros((PARTS, LANES), jnp.float32)
                            made[q, fold, tile] = jnp.where((lanes >= low) & (lanes < high), moved, old)
        for fold in range(folds):
            for tile in range(sz.lane_nodes // LANES):
                for turn in range(sz.n_ey):
                    chosen = jnp.zeros((PARTS, LANES), jnp.float32)
                    for q in range(sz.n_ey):
                        if (q, fold, tile) in made:
                            chosen = jnp.where((place + turn) % sz.n_ey == q, made[q, fold, tile], chosen)
                    out_refs[p * sz.n_ey + turn][pl.ds(fold * PARTS, PARTS), pl.ds(tile * LANES, LANES)] = chosen


def spread_kernel(sz, *refs):
    solved_refs, (out_ref, stacked_ref, turned_ref) = refs[:-3], refs[-3:]
    place, spot = lax.axis_index("ey"), lax.axis_index("ex")
    for step, solved_ref in enumerate(solved_refs):
        shift, turn = step // sz.n_ey, step % sz.n_ey
        source = (spot - shift + sz.n_ex) % sz.n_ex * sz.n_ey + (place - turn + sz.n_ey) % sz.n_ey
        stacked_ref[pl.ds(pl.multiple_of(source * sz.own, PARTS), sz.own), :] = solved_ref[...]
    turned_ref[...] = stacked_ref[...].T
    spots = sz.elems * sz.rows
    for e in range(sz.elems):
        for f in range(sz.rows):
            for a in range(sz.nodes):
                start = sz.block_y * (sz.order * e + a) + sz.order * f
                out_ref[pl.ds(a * sz.nodes * spots + e * sz.rows + f, sz.nodes, stride=spots), :] = turned_ref[
                    pl.ds(start, sz.nodes), :
                ]
    blank = jnp.zeros((sz.elems, LANES), jnp.float32)

    @pl.when(place == 0)
    def _():
        for a in range(sz.nodes):
            out_ref[pl.ds(a * sz.nodes * spots, sz.elems, stride=sz.rows), :] = blank

    @pl.when(place == sz.n_ey - 1)
    def _():
        for a in range(sz.nodes):
            first = ((a + 1) * sz.nodes - 1) * spots + sz.rows - 1
            out_ref[pl.ds(first, sz.elems, stride=sz.rows), :] = blank


def call(kernel, shapes, operands, scratch=(), spaces=pltpu.VMEM, limit=16, flops=10**9):
    if not isinstance(spaces, list):
        spaces = [spaces] * len(operands)
    made = pl.pallas_call(
        kernel,
        out_shape=[jax.ShapeDtypeStruct(shape, jnp.float32) for shape in shapes],
        in_specs=[pl.BlockSpec(memory_space=space) for space in spaces],
        out_specs=[pl.BlockSpec(memory_space=pltpu.VMEM) for _ in shapes],
        scratch_shapes=[pltpu.VMEM(each, jnp.float32) if isinstance(each, tuple) else each for each in scratch],
        compiler_params=pltpu.CompilerParams(vmem_limit_bytes=limit * 2**20),
        cost_estimate=pl.CostEstimate(flops=flops, bytes_accessed=10**6, transcendentals=0),
    )(*operands)
    return list(made)


def on_device(sz, tables, stream_speed, normal_speed):
    flat = sz.nodes * sz.nodes * sz.elems * sz.rows
    table = {name: jnp.asarray(value) for name, value in tables.items() if name != "heights"}
    heights = [float(height) for height in tables["heights"]]
    pieces = call(
        functools.partial(advect_kernel, sz, heights),
        [(sz.share, LANES)] * (sz.n_mode * sz.cuts),
        [
            pltpu.with_memory_space_constraint(each, pltpu.HBM)
            for each in (
                stream_speed.reshape(flat, sz.planes),
                normal_speed.reshape(flat, sz.planes),
                table["lift"],
                table["back"],
            )
        ],
        [
            (sz.cut_nodes, LANES),
            (flat, sz.planes),
            (flat, sz.planes),
            pltpu.VMEM(tables["lift"].shape, jnp.bfloat16),
            pltpu.VMEM(tables["back"].shape[1:], jnp.bfloat16),
            pltpu.SemaphoreType.DMA((4,)),
        ],
        pltpu.HBM,
    )
    weak = [pieces[cut * sz.n_mode : (cut + 1) * sz.n_mode] for cut in range(sz.cuts)]
    for cut in range(sz.cuts):
        for step in sorted(range(1, sz.n_mode), key=lambda each: (each & -each, each), reverse=True):
            pairs = [(z, partner(z, step, sz.n_mode)) for z in range(sz.n_mode)]
            weak[cut][step] = lax.ppermute(weak[cut][step], "mode", pairs)
    terms, ahead = [], []
    for cut in range(sz.cuts):
        (spectra,) = call(
            functools.partial(transform_kernel, sz),
            [(2 * sz.planes_total, sz.share)],
            [*weak[cut], *ahead, table["waves"]],
            [(-(-sz.share // LANES), 2 * sz.planes_total, LANES), (2, sz.planes_total, sz.share)],
            [pltpu.VMEM] * sz.n_mode + [pl.ANY] * len(ahead) + [pltpu.VMEM],
            flops=10**11 if cut == sz.cuts - 1 else 10**8,
        )
        spectra = spectra.reshape(sz.n_mode * sz.spots, sz.own, sz.share)
        terms.append(lax.all_to_all(spectra, ("mode", "ex", "ey"), split_axis=0, concat_axis=0, tiled=True))
        ahead = [spectra]
    names = ("in_y", "in_x", "pair_y", "pair_x", "out_y", "out_x", "lam_x", "lam_y")
    solved = call(
        functools.partial(smooth_kernel, sz),
        [(sz.own, sz.lane_nodes)] * sz.spots,
        terms + [table[name] for name in names],
        [(PARTS * sz.x_pad, LANES), (PARTS * sz.x_eig, LANES), (PARTS * sz.x_eig, LANES)],
    )
    for step in sorted(range(1, sz.spots), key=lambda each: each // sz.n_ey == 0):
        shift, turn = step // sz.n_ey, step % sz.n_ey
        pairs = [
            (p * sz.n_ey + q, (p + shift) % sz.n_ex * sz.n_ey + (q + turn) % sz.n_ey)
            for p in range(sz.n_ex)
            for q in range(sz.n_ey)
        ]
        solved[step] = lax.ppermute(solved[step], ("ex", "ey"), pairs)
    (out,) = call(
        functools.partial(spread_kernel, sz),
        [(flat, LANES)],
        solved,
        [(sz.columns, sz.lane_nodes), (sz.lane_nodes, LANES)],
    )
    return out.reshape(sz.nodes, sz.nodes, sz.elems, sz.rows, sz.columns)


def solution(mesh):
    spec = P(None, None, "ex", "ey", "mode")

    def whole(stream_speed, normal_speed):
        shape = stream_speed.shape
        counts = mesh.shape
        block = shape[:2] + (shape[2] // counts["ex"], shape[3] // counts["ey"], shape[4] // counts["mode"])
        sz = Sizes(counts, block)
        return jax.shard_map(
            functools.partial(on_device, sz, host_tables(sz)),
            mesh=mesh,
            in_specs=(spec, spec),
            out_specs=spec,
            check_vma=False,
        )(stream_speed, normal_speed)

    return whole
```

```python
import functools
import math

import jax
import jax.numpy as jnp
import ml_dtypes
import numpy as np
from jax import lax
from jax.experimental import pallas as pl
from jax.experimental.pallas import tpu as pltpu
from jax.sharding import PartitionSpec as P

BF16 = ml_dtypes.bfloat16

element_width = 2.0
shift_base = 10.0
span_rate = 0.0125


def legendre_pair(degree, points):
    before = points * 0.0 + 1.0
    current = points.copy()
    for step in range(1, degree):
        upcoming = ((2 * step + 1) * points * current - step * before) / (step + 1)
        before = current
        current = upcoming
    return (current, before)


def legendre_slope(degree, points):
    current, before = legendre_pair(degree, points)
    return (current, degree * (points * current - before) / (points * points - 1.0))


def lobatto_points(order):
    guesses = -np.cos(np.pi * np.arange(1, order) / order)
    for step in range(60):
        current, slope = legendre_slope(order, guesses)
        second = (2.0 * guesses * slope - order * (order + 1) * current) / (1.0 - guesses * guesses)
        guesses = guesses - slope / second
    return guesses


def gauss_rule(count):
    guesses = -np.cos(np.pi * (np.arange(count) + 0.75) / (count + 0.5))
    for step in range(60):
        current, slope = legendre_slope(count, guesses)
        guesses = guesses - current / slope
    current, slope = legendre_slope(count, guesses)
    return (guesses, 2.0 / ((1.0 - guesses * guesses) * slope * slope))


def jacobi_eigen(matrix):
    size_n = matrix.shape[0]
    work = matrix.copy()
    vectors = np.eye(size_n)
    for sweep_number in range(20):
        for first in range(size_n):
            for second in range(first + 1, size_n):
                coupling = work[first, second]
                if abs(coupling) > 1e-300:
                    theta = (work[second, second] - work[first, first]) / (2.0 * coupling)
                    direction = 1.0 if theta >= 0.0 else -1.0
                    tangent = direction / (abs(theta) + np.sqrt(theta * theta + 1.0))
                    cosine = 1.0 / np.sqrt(tangent * tangent + 1.0)
                    sine = tangent * cosine
                    rotation = np.eye(size_n)
                    rotation[first, first] = cosine
                    rotation[second, second] = cosine
                    rotation[first, second] = sine
                    rotation[second, first] = -sine
                    work = rotation.T @ work @ rotation
                    vectors = vectors @ rotation
    diagonal_index = np.arange(size_n)
    return (work[diagonal_index, diagonal_index], vectors)


def extended_basis(stiffness, weights, left_width, centre_width, right_width):
    node_count = weights.shape[0]
    full_count = 3 * node_count - 2
    stiff_full = np.zeros((full_count, full_count))
    mass_full = np.zeros(full_count)
    for position, span_width in enumerate((left_width, centre_width, right_width)):
        if span_width > 0.0:
            first_node = position * (node_count - 1)
            stiff_full[
                first_node : first_node + node_count, first_node : first_node + node_count
            ] += stiffness * (2.0 / span_width)
            mass_full[first_node : first_node + node_count] += weights * (span_width / 2.0)
    low_index = node_count - 2
    high_index = low_index + node_count + 2
    stiff_ext = stiff_full[low_index:high_index, low_index:high_index].copy()
    mass_ext = mass_full[low_index:high_index].copy()
    frozen_list = []
    if left_width <= 0.0:
        frozen_list += [0, 1]
    if right_width <= 0.0:
        frozen_list += [node_count, node_count + 1]
    for frozen_index in frozen_list:
        stiff_ext[frozen_index, :] = 0.0
        stiff_ext[:, frozen_index] = 0.0
        stiff_ext[frozen_index, frozen_index] = 1.0
        mass_ext[frozen_index] = 1.0
    inverse_root = 1.0 / np.sqrt(mass_ext)
    lambdas, vectors = jacobi_eigen(inverse_root[:, None] * stiff_ext * inverse_root[None, :])
    return (inverse_root[:, None] * vectors, lambdas)


def spectral_tables(order, rows_total):
    inner_points = lobatto_points(order)
    points = np.concatenate([[-1.0], inner_points, [1.0]])
    values, unused_before = legendre_pair(order, points)
    weights = 2.0 / (order * (order + 1) * values**2)
    identity = np.eye(order + 1)
    point_gaps = points[:, None] - points[None, :] + identity
    derivative = values[:, None] / (values[None, :] * point_gaps) * (1.0 - identity)
    derivative[0, 0] = -order * (order + 1) / 4.0
    derivative[order, order] = order * (order + 1) / 4.0
    stiffness = derivative.T @ (weights[:, None] * derivative)
    gauss_points, gauss_weights = gauss_rule(3 * (order + 1) // 2)
    offsets = gauss_points[:, None, None] - points[None, None, :]
    numerators = np.prod(np.where(identity[None, :, :] > 0.5, 1.0, offsets), axis=2)
    denominators = np.prod(np.where(identity > 0.5, 1.0, points[:, None] - points[None, :]), axis=1)
    interp = numerators / denominators[None, :]
    heights = 0.6 + 1.4 * np.sin(np.pi * (np.arange(rows_total) + 0.5) / rows_total)
    basis_x, lambdas_x = extended_basis(
        stiffness, weights, element_width, element_width, element_width
    )
    basis_rows = []
    lambda_rows = []
    for row_number in range(rows_total):
        below = heights[row_number - 1] if row_number > 0 else 0.0
        above = heights[row_number + 1] if row_number < rows_total - 1 else 0.0
        basis_one, lambda_one = extended_basis(
            stiffness, weights, below, heights[row_number], above
        )
        basis_rows.append(basis_one)
        lambda_rows.append(lambda_one)
    return (
        derivative,
        interp,
        gauss_weights,
        weights,
        stiffness,
        basis_x,
        lambdas_x,
        np.stack(basis_rows),
        np.stack(lambda_rows),
        heights,
    )


PARTS = 8
LANES = 128


def ceil_to(count, step):
    return -(-count // step) * step


class Sizes:
    def __init__(self, mesh_shape, block_shape):
        self.n_mode, self.n_ex, self.n_ey = (mesh_shape[name] for name in ("mode", "ex", "ey"))
        self.nodes, _, self.elems, self.rows, self.planes = block_shape
        self.order = self.nodes - 1
        self.gauss = 3 * self.nodes // 2
        self.rows_total = self.rows * self.n_ey
        self.elems_total = self.elems * self.n_ex
        self.planes_total = self.planes * self.n_mode
        self.block_x = self.order * self.elems + 1
        full_y = self.order * self.rows + 1
        self.inner = [
            [j for j in range(full_y) if not (p == 0 and j == 0) and not (p == self.n_ey - 1 and j == full_y - 1)]
            for p in range(self.n_ey)
        ]
        self.block_y = max(len(found) for found in self.inner)
        self.cuts = 1
        self.cut_elems = self.elems // self.cuts
        self.cut_x = self.order * self.cut_elems + 1
        share = -(-self.cut_x * self.block_y // self.n_mode)
        self.share = ceil_to(share, LANES if share > 64 else 16)
        self.cut_nodes = self.share * self.n_mode
        self.lane_nodes = ceil_to(self.block_x * self.block_y + 2, LANES)
        self.columns = 2 * self.planes
        self.spots = self.n_ex * self.n_ey
        self.own = self.columns // self.spots
        self.folds = self.own // PARTS
        self.fold_width = LANES // self.folds
        self.points = self.nodes + 2
        self.x_cuts = self.n_ex * self.cuts * self.cut_x
        self.x_pad = ceil_to(max(self.x_cuts, self.n_ex * self.block_x), 16)
        self.x_eig = self.elems_total * self.points
        self.y_eig = self.rows_total * self.points
        self.fine = ceil_to(self.gauss * self.gauss, 16)
        assert self.own == PARTS * self.folds and self.x_eig % 16 == 0
        assert max(self.y_eig, self.n_ey * self.block_y) <= self.fold_width
        assert 2 * self.planes == LANES


def high_low(table):
    high = np.asarray(table, np.float32).astype(BF16)
    low = (np.asarray(table, np.float64) - high.astype(np.float64)).astype(BF16)
    return high, low


def beside(table):
    high, low = high_low(table)
    return np.concatenate([high, high, low], 1)


def host_tables(sz):
    derivative, interp, gauss_weights, weights, stiffness, basis_x, lam_x, basis_y, lam_y, heights = spectral_tables(
        sz.order, sz.rows_total
    )
    nodes, fine, points = sz.nodes, sz.fine, sz.points
    gauss_count = sz.gauss**2
    lift = np.zeros((3 * fine, nodes * nodes))
    lift[:gauss_count] = np.kron(interp, interp)
    lift[fine : fine + gauss_count] = np.kron(interp @ derivative, interp)
    lift[2 * fine : 2 * fine + gauss_count] = np.kron(interp, interp @ derivative)
    back = np.zeros((sz.n_ey, nodes * sz.block_y, sz.rows * fine))
    weighted = interp.T * gauss_weights[None, :]
    for place in range(sz.n_ey):
        for f in range(sz.rows):
            for jj, j in enumerate(sz.inner[place]):
                b = j - sz.order * f
                if 0 <= b < nodes:
                    back[place, jj :: sz.block_y, f * fine : f * fine + gauss_count] = -np.kron(
                        weighted, weighted[b : b + 1]
                    )
    grid_x, grid_y = sz.order * sz.elems_total, sz.order * sz.rows_total + 1
    to_x, stiff_x, mass_x = np.zeros((sz.x_eig, grid_x)), np.zeros((grid_x, grid_x)), np.zeros(grid_x)
    for e in range(sz.elems_total):
        for t in range(points):
            to_x[e * points : (e + 1) * points, (sz.order * e + t - 1) % grid_x] += basis_x[t]
        index = (sz.order * e + np.arange(nodes)) % grid_x
        stiff_x[np.ix_(index, index)] += stiffness * (2.0 / element_width)
        mass_x[index] += weights * (element_width / 2.0)
    to_y, stiff_y, mass_y = np.zeros((sz.y_eig, grid_y)), np.zeros((grid_y, grid_y)), np.zeros(grid_y)
    for f in range(sz.rows_total):
        for t in range(points):
            y = sz.order * f + t - 1
            if 0 < y < grid_y - 1:
                to_y[f * points : (f + 1) * points, y] = basis_y[f][t]
        index = sz.order * f + np.arange(nodes)
        stiff_y[np.ix_(index, index)] += stiffness * (2.0 / heights[f])
        mass_y[index] += weights * (heights[f] / 2.0)
    stiff_xx, mass_xx = to_x @ stiff_x @ to_x.T, (to_x * mass_x) @ to_x.T
    stiff_yy, mass_yy = to_y @ stiff_y @ to_y.T, (to_y * mass_y) @ to_y.T
    def block_x(blocks, elems):
        length = sz.order * elems + 1
        nodes_of = [(sz.order * elems * p + i) % grid_x for p in range(blocks) for i in range(length)]
        table = np.zeros((sz.x_eig, sz.x_pad))
        table[:, : len(nodes_of)] = to_x[:, nodes_of]
        return table

    width, folds = sz.fold_width, sz.folds
    block_y = np.zeros((width, width))
    for place in range(sz.n_ey):
        for jj, j in enumerate(sz.inner[place]):
            block_y[place * sz.block_y + jj, : sz.y_eig] = to_y[:, sz.order * sz.rows * place + j]

    def folded(table):
        padded = np.zeros((width, width))
        padded[: table.shape[0], : table.shape[1]] = table
        return np.kron(np.eye(folds), padded)

    def one_dot(table):
        high, low = high_low(folded(table))
        return np.block([[high, low], [high, np.zeros_like(low)]]).astype(BF16)

    mass_pair, stiff_pair = high_low(folded(mass_yy)), high_low(folded(stiff_yy))
    heads = np.concatenate([mass_pair[0], stiff_pair[0]], 1)
    tails = np.concatenate([mass_pair[1], stiff_pair[1]], 1)
    lam_lanes = np.ones((1, folds, width))
    lam_lanes[:, :, : sz.y_eig] = lam_y.reshape(-1)
    planes_total = sz.planes_total
    turns = np.arange(planes_total)[None, :] * np.arange(planes_total // 2)[:, None] % planes_total
    angles = turns * (2.0 * math.pi / planes_total)
    waves = np.stack([np.cos(angles), -np.sin(angles)], 1).reshape(planes_total, planes_total) / planes_total
    return dict(
        heights=np.asarray(heights, np.float32),
        lift=beside(lift),
        back=np.stack([beside(table) for table in back]),
        waves=np.stack(high_low(waves)),
        in_y=one_dot(block_y),
        in_x=stacked(block_x(sz.n_ex * sz.cuts, sz.cut_elems)),
        pair_y=np.concatenate([heads, heads, tails], 0),
        pair_x=stacked(np.concatenate([stiff_xx, mass_xx], 1)),
        out_y=one_dot(block_y.T),
        out_x=stacked(block_x(sz.n_ex, sz.elems).T),
        lam_x=np.asarray(np.tile(lam_x, sz.elems_total)[:, None] * np.ones((1, LANES)), np.float32),
        lam_y=np.asarray(lam_lanes.reshape(1, LANES), np.float32),
    )


def stacked(table):
    return np.concatenate(high_low(table), 0)


def split(value):
    high = value.astype(jnp.bfloat16)
    low = (value - high.astype(jnp.float32)).astype(jnp.bfloat16)
    return high, low


def dot(left, right):
    return lax.dot_general(left, right, (((1,), (0,)), ((), ())), preferred_element_type=jnp.float32)


def below(value):
    high, low = split(value)
    return jnp.concatenate([high, low, high], 0)


def left_dot(table_ref, value):
    rows = table_ref.shape[0] // 2
    high, low = split(value)
    both = dot(table_ref[...], high)
    return both[:rows] + both[rows:] + dot(table_ref[:rows, :], low)


def along(value):
    return jnp.concatenate(split(value), 1)


def partner(spot, step, count):
    if count & (count - 1) == 0:
        return spot ^ step
    return (spot + step) % count


def origin(spot, step, count):
    if count & (count - 1) == 0:
        return spot ^ step
    return (spot - step + count) % count


def lane_index(shape):
    return lax.broadcasted_iota(jnp.int32, shape, len(shape) - 1)


def advect_kernel(sz, heights, stream_hbm, normal_hbm, lift_hbm, back_hbm, *others):
    out_refs, (total_ref, stream_ref, normal_ref, lift_ref, back_ref, arrived) = others[:-6], others[-6:]
    place = lax.axis_index("ey")
    fetched = [
        pltpu.make_async_copy(source, target, arrived.at[i])
        for i, (source, target) in enumerate(
            (
                (stream_hbm, stream_ref),
                (normal_hbm, normal_ref),
                (lift_hbm, lift_ref),
                (back_hbm.at[place], back_ref),
            )
        )
    ]
    for copy in fetched:
        copy.start()
    count, fine, rows = sz.nodes * sz.nodes, sz.fine, sz.rows
    spots = sz.elems * rows
    half = lane_index((fine, LANES)) < sz.planes
    column, step = sz.nodes * sz.block_y, sz.order * sz.block_y
    factors = [
        sum(jnp.where(place == q, heights[q * rows + f] * 0.5, 0.0) for q in range(sz.n_ey)) for f in range(rows)
    ]
    full = sz.cut_x * sz.block_y // 8 * 8
    total_ref[pl.ds(full, sz.cut_nodes - full), :] = jnp.zeros((sz.cut_nodes - full, LANES), jnp.float32)
    spot = lax.axis_index("mode")
    for copy in fetched[:3]:
        copy.wait()
    for cut in range(sz.cuts):
        products = []
        for e in range(cut * sz.cut_elems, (cut + 1) * sz.cut_elems):
            speeds = jnp.concatenate(
                [
                    ref[pl.ds(e * rows + f, count, stride=spots), :]
                    for f in range(rows)
                    for ref in (stream_ref, normal_ref)
                ],
                1,
            )
            values = dot(lift_ref[...], below(speeds))
            highs, lows = [], []
            for f in range(rows):
                mine = values[:, f * LANES : (f + 1) * LANES]
                both, slope_x, slope_y = mine[:fine], mine[fine : 2 * fine], mine[2 * fine :]
                turned = pltpu.roll(both, sz.planes, 1)
                stream = jnp.where(half, both, turned)
                normal = jnp.where(half, turned, both)
                high, low = split((stream * factors[f]) * slope_x + (normal * (element_width * 0.5)) * slope_y)
                highs.append(high)
                lows.append(low)
            products.append(jnp.concatenate(highs + lows + highs, 0))
        if cut == 0:
            fetched[3].wait()
        weak = dot(back_ref[...], jnp.concatenate(products, 1))
        carry = None
        for e in range(sz.cut_elems):
            mine = weak[:, e * LANES : (e + 1) * LANES]
            if carry is not None:
                gap = jnp.zeros((column - carry.shape[0], LANES), jnp.float32)
                mine = mine + jnp.concatenate([carry, gap], 0)
            length = step if e < sz.cut_elems - 1 else column
            total_ref[pl.ds(e * step, length), :] = mine[:length]
            carry = mine[length:]
        for turn in range(sz.n_mode):
            goal = partner(spot, turn, sz.n_mode)
            out_refs[cut * sz.n_mode + turn][...] = total_ref[pl.ds(pl.multiple_of(goal * sz.share, 8), sz.share), :]


def transform_kernel(sz, *refs):
    weak_refs, (waves_ref, out_ref, mixed_ref, signal_ref) = refs[: sz.n_mode], refs[-4:]
    spot = lax.axis_index("mode")
    for step, weak_ref in enumerate(weak_refs):
        turned = weak_ref[...].T
        first = pl.multiple_of(origin(spot, step, sz.n_mode) * sz.planes, 8)
        for k in range(2):
            signal_ref[k, pl.ds(first, sz.planes), :] = turned[k * sz.planes : (k + 1) * sz.planes]
    modes = sz.planes_total
    for k in range(2):
        high, low = split(signal_ref[k])
        part = dot(waves_ref[0], high) + dot(waves_ref[0], low) + dot(waves_ref[1], high)
        for t in range(mixed_ref.shape[0]):
            tile = part[:, t * LANES : (t + 1) * LANES]
            mixed_ref[t, pl.ds(k, modes, stride=2), pl.ds(0, tile.shape[1])] = tile
    for t in range(mixed_ref.shape[0]):
        last = min(LANES, sz.share - t * LANES)
        out_ref[:, pl.ds(t * LANES, last)] = mixed_ref[t, :, pl.ds(0, last)]


def smooth_kernel(
    sz,
    *refs,
):
    terms_refs, out_refs = refs[: sz.cuts], refs[sz.cuts + 8 : -4]
    field_ref, first_ref, work_ref, stiff_ref = refs[-4:]
    in_y_ref, in_x_ref, pair_y_ref, pair_x_ref, out_y_ref, out_x_ref, lam_x_ref, lam_y_ref = refs[
        sz.cuts : sz.cuts + 8
    ]
    width, folds, strip = sz.fold_width, sz.folds, sz.block_y
    tiles = -(-sz.cut_nodes // LANES)
    lanes = lane_index((PARTS, LANES))
    x_pad, x_eig = sz.x_pad, sz.x_eig
    place, spot = lax.axis_index("ey"), lax.axis_index("ex")
    device = (lax.axis_index("mode") * sz.n_ex + spot) * sz.n_ey + place
    first_mode = device * (sz.own // 4)

    for c in range(PARTS):
        field_ref[pl.ds(c * x_pad + sz.x_cuts, x_pad - sz.x_cuts), :] = jnp.zeros(
            (x_pad - sz.x_cuts, LANES), jnp.float32
        )
    for p, cut in [(p, cut) for p in range(sz.n_ex) for cut in range(sz.cuts)]:
        block = (spot + p) % sz.n_ex
        held = {}
        for q in range(sz.n_ey):
            for fold in range(folds):
                whole = jnp.concatenate(
                    [
                        terms_refs[cut][(z * sz.n_ex + block) * sz.n_ey + q, pl.ds(fold * PARTS, PARTS), :]
                        for z in range(sz.n_mode)
                    ],
                    1,
                )
                held[q, fold] = [whole[:, t * LANES : (t + 1) * LANES] for t in range(tiles)]
        for i in range(sz.cut_x):
            start = i * strip
            t, r = start // LANES, start % LANES
            result = jnp.zeros((PARTS, LANES), jnp.float32)
            for fold in range(folds):
                for q in range(sz.n_ey):
                    source = held[q, fold][t]
                    if r + strip > LANES:
                        source = jnp.where(lanes >= r, source, held[q, fold][t + 1])
                    goal = fold * width + q * strip
                    moved = pltpu.roll(source, (goal - r) % LANES, 1) if goal != r else source
                    result = jnp.where((lanes >= goal) & (lanes < goal + strip), moved, result)
            field_ref[pl.ds((p * sz.cuts + cut) * sz.cut_x + i, PARTS, stride=x_pad), :] = result

    parts = dot(along(field_ref[...]), in_y_ref[...])
    field_ref[...] = parts[:, :LANES] + parts[:, LANES:]
    fold_of_lane = lane_index((1, LANES)) // width
    shifts, inverses = [], []
    for group in range(PARTS // 4):
        mode = (first_mode + fold_of_lane * (PARTS // 4) + group).astype(jnp.float32)
        shift = shift_base + (span_rate * mode) ** 2
        shifts.append(shift)
        inverses.append(1.0 / (lam_x_ref[...] + (lam_y_ref[...] + shift)))
    for c in range(0, PARTS, 2):
        pair = jnp.concatenate([field_ref[pl.ds((c + d) * x_pad, x_pad), :] for d in range(2)], 1)
        forced = left_dot(in_x_ref, pair)
        for d in range(2):
            mine = forced[:, d * LANES : (d + 1) * LANES]
            first_ref[pl.ds((c + d) * x_eig, x_eig), :] = mine
            work_ref[pl.ds((c + d) * x_eig, x_eig), :] = mine * inverses[(c + d) // 4]
    high, low = split(work_ref[...])
    both = dot(jnp.concatenate([high, low, high], 1), pair_y_ref[...])
    work_ref[...] = both[:, :LANES]
    stiff_ref[...] = both[:, LANES:]
    for c in range(0, PARTS, 2):
        masses, stiffs = [], []
        for d in range(2):
            rows = pl.ds((c + d) * x_eig, x_eig)
            masses.append(work_ref[rows, :])
            stiffs.append(stiff_ref[rows, :] + shifts[c // 4] * masses[d])
        stacked_pair = jnp.concatenate([jnp.concatenate(masses, 1), jnp.concatenate(stiffs, 1)], 0)
        applied = left_dot(pair_x_ref, stacked_pair)
        for d in range(2):
            rows = pl.ds((c + d) * x_eig, x_eig)
            mine = applied[:, d * LANES : (d + 1) * LANES]
            first_ref[rows, :] = (2.0 * first_ref[rows, :] - mine) * inverses[c // 4]
    parts = dot(along(first_ref[...]), out_y_ref[...])
    work_ref[...] = parts[:, :LANES] + parts[:, LANES:]
    for c in range(0, PARTS, 2):
        pair = jnp.concatenate([work_ref[pl.ds((c + d) * x_eig, x_eig), :] for d in range(2)], 1)
        solved = left_dot(out_x_ref, pair)
        for d in range(2):
            field_ref[pl.ds((c + d) * x_pad, x_pad), :] = solved[:, d * LANES : (d + 1) * LANES]

    for p in range(sz.n_ex):
        made = {}
        for i in range(sz.block_x):
            source = field_ref[pl.ds(p * sz.block_x + i, PARTS, stride=x_pad), :]
            for q in range(sz.n_ey):
                begin = i * strip + sz.inner[q][0]
                count = len(sz.inner[q])
                t, r = begin // LANES, begin % LANES
                for fold in range(folds):
                    origin = fold * width + q * strip
                    moved = pltpu.roll(source, (r - origin) % LANES, 1) if origin != r else source
                    for tile, low, high in ((t, r, r + count), (t + 1, 0, r + count - LANES)):
                        if high > 0:
                            old = made.get((q, fold, tile))
                            if old is None:
                                old = jnp.zeros((PARTS, LANES), jnp.float32)
                            made[q, fold, tile] = jnp.where((lanes >= low) & (lanes < high), moved, old)
        for fold in range(folds):
            for tile in range(sz.lane_nodes // LANES):
                for turn in range(sz.n_ey):
                    chosen = jnp.zeros((PARTS, LANES), jnp.float32)
                    for q in range(sz.n_ey):
                        if (q, fold, tile) in made:
                            chosen = jnp.where((place + turn) % sz.n_ey == q, made[q, fold, tile], chosen)
                    out_refs[p * sz.n_ey + turn][pl.ds(fold * PARTS, PARTS), pl.ds(tile * LANES, LANES)] = chosen


def spread_kernel(sz, *refs):
    solved_refs, (out_ref, stacked_ref, turned_ref) = refs[:-3], refs[-3:]
    place, spot = lax.axis_index("ey"), lax.axis_index("ex")
    for step, solved_ref in enumerate(solved_refs):
        shift, turn = step // sz.n_ey, step % sz.n_ey
        source = (spot - shift + sz.n_ex) % sz.n_ex * sz.n_ey + (place - turn + sz.n_ey) % sz.n_ey
        stacked_ref[pl.ds(pl.multiple_of(source * sz.own, PARTS), sz.own), :] = solved_ref[...]
    turned_ref[...] = stacked_ref[...].T
    spots = sz.elems * sz.rows
    for e in range(sz.elems):
        for f in range(sz.rows):
            for a in range(sz.nodes):
                start = sz.block_y * (sz.order * e + a) + sz.order * f
                out_ref[pl.ds(a * sz.nodes * spots + e * sz.rows + f, sz.nodes, stride=spots), :] = turned_ref[
                    pl.ds(start, sz.nodes), :
                ]
    blank = jnp.zeros((sz.elems, LANES), jnp.float32)

    @pl.when(place == 0)
    def _():
        for a in range(sz.nodes):
            out_ref[pl.ds(a * sz.nodes * spots, sz.elems, stride=sz.rows), :] = blank

    @pl.when(place == sz.n_ey - 1)
    def _():
        for a in range(sz.nodes):
            first = ((a + 1) * sz.nodes - 1) * spots + sz.rows - 1
            out_ref[pl.ds(first, sz.elems, stride=sz.rows), :] = blank


def call(kernel, shapes, operands, scratch=(), spaces=pltpu.VMEM, limit=16, flops=10**9):
    if not isinstance(spaces, list):
        spaces = [spaces] * len(operands)
    made = pl.pallas_call(
        kernel,
        out_shape=[jax.ShapeDtypeStruct(shape, jnp.float32) for shape in shapes],
        in_specs=[pl.BlockSpec(memory_space=space) for space in spaces],
        out_specs=[pl.BlockSpec(memory_space=pltpu.VMEM) for _ in shapes],
        scratch_shapes=[pltpu.VMEM(each, jnp.float32) if isinstance(each, tuple) else each for each in scratch],
        compiler_params=pltpu.CompilerParams(vmem_limit_bytes=limit * 2**20),
        cost_estimate=pl.CostEstimate(flops=flops, bytes_accessed=10**6, transcendentals=0),
    )(*operands)
    return list(made)


def on_device(sz, tables, stream_speed, normal_speed):
    flat = sz.nodes * sz.nodes * sz.elems * sz.rows
    table = {name: jnp.asarray(value) for name, value in tables.items() if name != "heights"}
    heights = [float(height) for height in tables["heights"]]
    pieces = call(
        functools.partial(advect_kernel, sz, heights),
        [(sz.share, LANES)] * (sz.n_mode * sz.cuts),
        [
            pltpu.with_memory_space_constraint(each, pltpu.HBM)
            for each in (
                stream_speed.reshape(flat, sz.planes),
                normal_speed.reshape(flat, sz.planes),
                table["lift"],
                table["back"],
            )
        ],
        [
            (sz.cut_nodes, LANES),
            (flat, sz.planes),
            (flat, sz.planes),
            pltpu.VMEM(tables["lift"].shape, jnp.bfloat16),
            pltpu.VMEM(tables["back"].shape[1:], jnp.bfloat16),
            pltpu.SemaphoreType.DMA((4,)),
        ],
        pltpu.HBM,
    )
    weak = [pieces[cut * sz.n_mode : (cut + 1) * sz.n_mode] for cut in range(sz.cuts)]
    for cut in range(sz.cuts):
        for step in sorted(range(1, sz.n_mode), key=lambda each: (each & -each, each), reverse=True):
            pairs = [(z, partner(z, step, sz.n_mode)) for z in range(sz.n_mode)]
            weak[cut][step] = lax.ppermute(weak[cut][step], "mode", pairs)
    terms, ahead = [], []
    for cut in range(sz.cuts):
        (spectra,) = call(
            functools.partial(transform_kernel, sz),
            [(2 * sz.planes_total, sz.share)],
            [*weak[cut], *ahead, table["waves"]],
            [(-(-sz.share // LANES), 2 * sz.planes_total, LANES), (2, sz.planes_total, sz.share)],
            [pltpu.VMEM] * sz.n_mode + [pl.ANY] * len(ahead) + [pltpu.VMEM],
            flops=10**11 if cut == sz.cuts - 1 else 10**8,
        )
        spectra = spectra.reshape(sz.n_mode * sz.spots, sz.own, sz.share)
        terms.append(lax.all_to_all(spectra, ("mode", "ex", "ey"), split_axis=0, concat_axis=0, tiled=True))
        ahead = [spectra]
    names = ("in_y", "in_x", "pair_y", "pair_x", "out_y", "out_x", "lam_x", "lam_y")
    solved = call(
        functools.partial(smooth_kernel, sz),
        [(sz.own, sz.lane_nodes)] * sz.spots,
        terms + [table[name] for name in names],
        [(PARTS * sz.x_pad, LANES)] + [(PARTS * sz.x_eig, LANES)] * 3,
    )
    for step in sorted(range(1, sz.spots), key=lambda each: each // sz.n_ey == 0):
        shift, turn = step // sz.n_ey, step % sz.n_ey
        pairs = [
            (p * sz.n_ey + q, (p + shift) % sz.n_ex * sz.n_ey + (q + turn) % sz.n_ey)
            for p in range(sz.n_ex)
            for q in range(sz.n_ey)
        ]
        solved[step] = lax.ppermute(solved[step], ("ex", "ey"), pairs)
    (out,) = call(
        functools.partial(spread_kernel, sz),
        [(flat, LANES)],
        solved,
        [(sz.columns, sz.lane_nodes), (sz.lane_nodes, LANES)],
    )
    return out.reshape(sz.nodes, sz.nodes, sz.elems, sz.rows, sz.columns)


def solution(mesh):
    spec = P(None, None, "ex", "ey", "mode")

    def whole(stream_speed, normal_speed):
        shape = stream_speed.shape
        counts = mesh.shape
        block = shape[:2] + (shape[2] // counts["ex"], shape[3] // counts["ey"], shape[4] // counts["mode"])
        sz = Sizes(counts, block)
        return jax.shard_map(
            functools.partial(on_device, sz, host_tables(sz)),
            mesh=mesh,
            in_specs=(spec, spec),
            out_specs=spec,
            check_vma=False,
        )(stream_speed, normal_speed)

    return whole
```

```python
import functools
import math

import jax
import jax.numpy as jnp
import ml_dtypes
import numpy as np
from jax import lax
from jax.experimental import pallas as pl
from jax.experimental.pallas import tpu as pltpu
from jax.sharding import PartitionSpec as P

BF16 = ml_dtypes.bfloat16

element_width = 2.0
shift_base = 10.0
span_rate = 0.0125


def legendre_pair(degree, points):
    before = points * 0.0 + 1.0
    current = points.copy()
    for step in range(1, degree):
        upcoming = ((2 * step + 1) * points * current - step * before) / (step + 1)
        before = current
        current = upcoming
    return (current, before)


def legendre_slope(degree, points):
    current, before = legendre_pair(degree, points)
    return (current, degree * (points * current - before) / (points * points - 1.0))


def lobatto_points(order):
    guesses = -np.cos(np.pi * np.arange(1, order) / order)
    for step in range(60):
        current, slope = legendre_slope(order, guesses)
        second = (2.0 * guesses * slope - order * (order + 1) * current) / (1.0 - guesses * guesses)
        guesses = guesses - slope / second
    return guesses


def gauss_rule(count):
    guesses = -np.cos(np.pi * (np.arange(count) + 0.75) / (count + 0.5))
    for step in range(60):
        current, slope = legendre_slope(count, guesses)
        guesses = guesses - current / slope
    current, slope = legendre_slope(count, guesses)
    return (guesses, 2.0 / ((1.0 - guesses * guesses) * slope * slope))


def jacobi_eigen(matrix):
    size_n = matrix.shape[0]
    work = matrix.copy()
    vectors = np.eye(size_n)
    for sweep_number in range(20):
        for first in range(size_n):
            for second in range(first + 1, size_n):
                coupling = work[first, second]
                if abs(coupling) > 1e-300:
                    theta = (work[second, second] - work[first, first]) / (2.0 * coupling)
                    direction = 1.0 if theta >= 0.0 else -1.0
                    tangent = direction / (abs(theta) + np.sqrt(theta * theta + 1.0))
                    cosine = 1.0 / np.sqrt(tangent * tangent + 1.0)
                    sine = tangent * cosine
                    rotation = np.eye(size_n)
                    rotation[first, first] = cosine
                    rotation[second, second] = cosine
                    rotation[first, second] = sine
                    rotation[second, first] = -sine
                    work = rotation.T @ work @ rotation
                    vectors = vectors @ rotation
    diagonal_index = np.arange(size_n)
    return (work[diagonal_index, diagonal_index], vectors)


def extended_basis(stiffness, weights, left_width, centre_width, right_width):
    node_count = weights.shape[0]
    full_count = 3 * node_count - 2
    stiff_full = np.zeros((full_count, full_count))
    mass_full = np.zeros(full_count)
    for position, span_width in enumerate((left_width, centre_width, right_width)):
        if span_width > 0.0:
            first_node = position * (node_count - 1)
            stiff_full[
                first_node : first_node + node_count, first_node : first_node + node_count
            ] += stiffness * (2.0 / span_width)
            mass_full[first_node : first_node + node_count] += weights * (span_width / 2.0)
    low_index = node_count - 2
    high_index = low_index + node_count + 2
    stiff_ext = stiff_full[low_index:high_index, low_index:high_index].copy()
    mass_ext = mass_full[low_index:high_index].copy()
    frozen_list = []
    if left_width <= 0.0:
        frozen_list += [0, 1]
    if right_width <= 0.0:
        frozen_list += [node_count, node_count + 1]
    for frozen_index in frozen_list:
        stiff_ext[frozen_index, :] = 0.0
        stiff_ext[:, frozen_index] = 0.0
        stiff_ext[frozen_index, frozen_index] = 1.0
        mass_ext[frozen_index] = 1.0
    inverse_root = 1.0 / np.sqrt(mass_ext)
    lambdas, vectors = jacobi_eigen(inverse_root[:, None] * stiff_ext * inverse_root[None, :])
    return (inverse_root[:, None] * vectors, lambdas)


def spectral_tables(order, rows_total):
    inner_points = lobatto_points(order)
    points = np.concatenate([[-1.0], inner_points, [1.0]])
    values, unused_before = legendre_pair(order, points)
    weights = 2.0 / (order * (order + 1) * values**2)
    identity = np.eye(order + 1)
    point_gaps = points[:, None] - points[None, :] + identity
    derivative = values[:, None] / (values[None, :] * point_gaps) * (1.0 - identity)
    derivative[0, 0] = -order * (order + 1) / 4.0
    derivative[order, order] = order * (order + 1) / 4.0
    stiffness = derivative.T @ (weights[:, None] * derivative)
    gauss_points, gauss_weights = gauss_rule(3 * (order + 1) // 2)
    offsets = gauss_points[:, None, None] - points[None, None, :]
    numerators = np.prod(np.where(identity[None, :, :] > 0.5, 1.0, offsets), axis=2)
    denominators = np.prod(np.where(identity > 0.5, 1.0, points[:, None] - points[None, :]), axis=1)
    interp = numerators / denominators[None, :]
    heights = 0.6 + 1.4 * np.sin(np.pi * (np.arange(rows_total) + 0.5) / rows_total)
    basis_x, lambdas_x = extended_basis(
        stiffness, weights, element_width, element_width, element_width
    )
    basis_rows = []
    lambda_rows = []
    for row_number in range(rows_total):
        below = heights[row_number - 1] if row_number > 0 else 0.0
        above = heights[row_number + 1] if row_number < rows_total - 1 else 0.0
        basis_one, lambda_one = extended_basis(
            stiffness, weights, below, heights[row_number], above
        )
        basis_rows.append(basis_one)
        lambda_rows.append(lambda_one)
    return (
        derivative,
        interp,
        gauss_weights,
        weights,
        stiffness,
        basis_x,
        lambdas_x,
        np.stack(basis_rows),
        np.stack(lambda_rows),
        heights,
    )


PARTS = 8
LANES = 128


def ceil_to(count, step):
    return -(-count // step) * step


class Sizes:
    def __init__(self, mesh_shape, block_shape):
        self.n_mode, self.n_ex, self.n_ey = (mesh_shape[name] for name in ("mode", "ex", "ey"))
        self.nodes, _, self.elems, self.rows, self.planes = block_shape
        self.order = self.nodes - 1
        self.gauss = 3 * self.nodes // 2
        self.rows_total = self.rows * self.n_ey
        self.elems_total = self.elems * self.n_ex
        self.planes_total = self.planes * self.n_mode
        self.block_x = self.order * self.elems + 1
        full_y = self.order * self.rows + 1
        self.inner = [
            [j for j in range(full_y) if not (p == 0 and j == 0) and not (p == self.n_ey - 1 and j == full_y - 1)]
            for p in range(self.n_ey)
        ]
        self.block_y = max(len(found) for found in self.inner)
        self.cuts = 1
        self.cut_elems = self.elems // self.cuts
        self.cut_x = self.order * self.cut_elems + 1
        share = -(-self.cut_x * self.block_y // self.n_mode)
        self.sent = ceil_to(share, 8)
        self.share = ceil_to(self.sent, LANES if share > 64 else 16)
        self.cut_nodes = self.sent * self.n_mode
        self.lane_nodes = ceil_to(self.block_x * self.block_y + 2, LANES)
        self.columns = 2 * self.planes
        self.spots = self.n_ex * self.n_ey
        self.own = self.columns // self.spots
        self.folds = self.own // PARTS
        self.fold_width = LANES // self.folds
        self.stripe = self.fold_width // self.n_ey
        self.points = self.nodes + 2
        self.x_cuts = self.n_ex * self.cuts * self.cut_x
        self.x_pad = ceil_to(max(self.x_cuts, self.n_ex * self.block_x), 16)
        self.x_eig = self.elems_total * self.points
        self.y_eig = self.rows_total * self.points
        self.fine = ceil_to(self.gauss * self.gauss, 16)
        assert self.own == PARTS * self.folds and self.x_eig % 16 == 0
        assert self.y_eig <= self.fold_width and self.block_y < self.stripe
        assert 2 * self.planes == LANES


def high_low(table):
    high = np.asarray(table, np.float32).astype(BF16)
    low = (np.asarray(table, np.float64) - high.astype(np.float64)).astype(BF16)
    return high, low


def beside(table):
    high, low = high_low(table)
    return np.concatenate([high, high, low], 1)


def host_tables(sz):
    derivative, interp, gauss_weights, weights, stiffness, basis_x, lam_x, basis_y, lam_y, heights = spectral_tables(
        sz.order, sz.rows_total
    )
    nodes, fine, points = sz.nodes, sz.fine, sz.points
    gauss_count = sz.gauss**2
    lift = np.zeros((3 * fine, nodes * nodes))
    lift[:gauss_count] = np.kron(interp, interp)
    lift[fine : fine + gauss_count] = np.kron(interp @ derivative, interp)
    lift[2 * fine : 2 * fine + gauss_count] = np.kron(interp, interp @ derivative)
    back = np.zeros((sz.n_ey, nodes * sz.block_y, sz.rows * fine))
    weighted = interp.T * gauss_weights[None, :]
    for place in range(sz.n_ey):
        for f in range(sz.rows):
            for jj, j in enumerate(sz.inner[place]):
                b = j - sz.order * f
                if 0 <= b < nodes:
                    back[place, jj :: sz.block_y, f * fine : f * fine + gauss_count] = -np.kron(
                        weighted, weighted[b : b + 1]
                    )
    grid_x, grid_y = sz.order * sz.elems_total, sz.order * sz.rows_total + 1
    to_x, stiff_x, mass_x = np.zeros((sz.x_eig, grid_x)), np.zeros((grid_x, grid_x)), np.zeros(grid_x)
    for e in range(sz.elems_total):
        for t in range(points):
            to_x[e * points : (e + 1) * points, (sz.order * e + t - 1) % grid_x] += basis_x[t]
        index = (sz.order * e + np.arange(nodes)) % grid_x
        stiff_x[np.ix_(index, index)] += stiffness * (2.0 / element_width)
        mass_x[index] += weights * (element_width / 2.0)
    to_y, stiff_y, mass_y = np.zeros((sz.y_eig, grid_y)), np.zeros((grid_y, grid_y)), np.zeros(grid_y)
    for f in range(sz.rows_total):
        for t in range(points):
            y = sz.order * f + t - 1
            if 0 < y < grid_y - 1:
                to_y[f * points : (f + 1) * points, y] = basis_y[f][t]
        index = sz.order * f + np.arange(nodes)
        stiff_y[np.ix_(index, index)] += stiffness * (2.0 / heights[f])
        mass_y[index] += weights * (heights[f] / 2.0)
    stiff_xx, mass_xx = to_x @ stiff_x @ to_x.T, (to_x * mass_x) @ to_x.T
    stiff_yy, mass_yy = to_y @ stiff_y @ to_y.T, (to_y * mass_y) @ to_y.T
    def block_x(blocks, elems):
        length = sz.order * elems + 1
        nodes_of = [(sz.order * elems * p + i) % grid_x for p in range(blocks) for i in range(length)]
        table = np.zeros((sz.x_eig, sz.x_pad))
        table[:, : len(nodes_of)] = to_x[:, nodes_of]
        return table

    width, folds = sz.fold_width, sz.folds
    enter_y, leave_y = np.zeros((width, width)), np.zeros((width, width))
    for place in range(sz.n_ey):
        for jj, j in enumerate(sz.inner[place]):
            enter_y[place * sz.stripe + jj, : sz.y_eig] = to_y[:, sz.order * sz.rows * place + j]
            leave_y[: sz.y_eig, place * sz.stripe + j] = to_y[:, sz.order * sz.rows * place + j]

    def folded(table):
        padded = np.zeros((width, width))
        padded[: table.shape[0], : table.shape[1]] = table
        return np.kron(np.eye(folds), padded)

    def one_dot(table):
        high, low = high_low(folded(table))
        return np.block([[high, low], [high, np.zeros_like(low)]]).astype(BF16)

    mass_pair, stiff_pair = high_low(folded(mass_yy)), high_low(folded(stiff_yy))
    heads = np.concatenate([mass_pair[0], stiff_pair[0]], 1)
    tails = np.concatenate([mass_pair[1], stiff_pair[1]], 1)
    lam_lanes = np.ones((1, folds, width))
    lam_lanes[:, :, : sz.y_eig] = lam_y.reshape(-1)
    planes_total = sz.planes_total
    turns = np.arange(planes_total)[None, :] * np.arange(planes_total // 2)[:, None] % planes_total
    angles = turns * (2.0 * math.pi / planes_total)
    waves = np.stack([np.cos(angles), -np.sin(angles)], 1).reshape(planes_total, planes_total) / planes_total
    return dict(
        heights=np.asarray(heights, np.float32),
        lift=beside(lift),
        back=np.stack([beside(table) for table in back]),
        waves=np.stack(high_low(waves)),
        in_y=one_dot(enter_y),
        in_x=stacked(block_x(sz.n_ex * sz.cuts, sz.cut_elems)),
        pair_y=np.concatenate([heads, heads, tails], 0),
        pair_x=stacked(np.concatenate([stiff_xx, mass_xx], 1)),
        out_y=one_dot(leave_y),
        out_x=stacked(block_x(sz.n_ex, sz.elems).T),
        lam_x=np.asarray(np.tile(lam_x, sz.elems_total)[:, None] * np.ones((1, LANES)), np.float32),
        lam_y=np.asarray(lam_lanes.reshape(1, LANES), np.float32),
    )


def stacked(table):
    return np.concatenate(high_low(table), 0)


def split(value):
    high = value.astype(jnp.bfloat16)
    low = (value - high.astype(jnp.float32)).astype(jnp.bfloat16)
    return high, low


def dot(left, right):
    return lax.dot_general(left, right, (((1,), (0,)), ((), ())), preferred_element_type=jnp.float32)


def below(value):
    high, low = split(value)
    return jnp.concatenate([high, low, high], 0)


def left_dot(table_ref, value):
    rows = table_ref.shape[0] // 2
    high, low = split(value)
    both = dot(table_ref[...], high)
    return both[:rows] + both[rows:] + dot(table_ref[:rows, :], low)


def along(value):
    return jnp.concatenate(split(value), 1)


def partner(spot, step, count):
    if count & (count - 1) == 0:
        return spot ^ step
    return (spot + step) % count


def origin(spot, step, count):
    if count & (count - 1) == 0:
        return spot ^ step
    return (spot - step + count) % count


def rotate(tiles, shift):
    width = tiles[0].shape[-1]
    whole, part = shift % (width * len(tiles)) // width, shift % width
    if part == 0:
        return [tiles[t - whole] for t in range(len(tiles))]
    moved = [pltpu.roll(tile, part, tile.ndim - 1) for tile in tiles]
    crossed = lane_index(tiles[0].shape) < part
    return [jnp.where(crossed, moved[t - whole - 1], moved[t - whole]) for t in range(len(tiles))]


def runs(sz, i, shift, start, count, size, share):
    found = []
    for j in range(start, start + count):
        n = i * sz.block_y + j
        part, lane = n // size, (n % size + shift) % share
        key = (part, lane // LANES)
        if found and found[-1][:2] == key and found[-1][2] + found[-1][4] == lane % LANES:
            found[-1][4] += 1
        else:
            found.append([*key, lane % LANES, shift + j, 1])
    return found


def lane_index(shape):
    return lax.broadcasted_iota(jnp.int32, shape, len(shape) - 1)


def advect_kernel(sz, heights, stream_hbm, normal_hbm, lift_hbm, back_hbm, *others):
    out_refs, (total_ref, stream_ref, normal_ref, lift_ref, back_ref, arrived) = others[:-6], others[-6:]
    place = lax.axis_index("ey")
    fetched = [
        pltpu.make_async_copy(source, target, arrived.at[i])
        for i, (source, target) in enumerate(
            (
                (stream_hbm, stream_ref),
                (normal_hbm, normal_ref),
                (lift_hbm, lift_ref),
                (back_hbm.at[place], back_ref),
            )
        )
    ]
    for copy in fetched:
        copy.start()
    count, fine, rows = sz.nodes * sz.nodes, sz.fine, sz.rows
    spots = sz.elems * rows
    half = lane_index((fine, LANES)) < sz.planes
    column, step = sz.nodes * sz.block_y, sz.order * sz.block_y
    factors = [
        sum(jnp.where(place == q, heights[q * rows + f] * 0.5, 0.0) for q in range(sz.n_ey)) for f in range(rows)
    ]
    full = sz.cut_x * sz.block_y // 8 * 8
    total_ref[pl.ds(full, sz.cut_nodes - full), :] = jnp.zeros((sz.cut_nodes - full, LANES), jnp.float32)
    spot = lax.axis_index("mode")
    for copy in fetched[:3]:
        copy.wait()
    for cut in range(sz.cuts):
        products = []
        for e in range(cut * sz.cut_elems, (cut + 1) * sz.cut_elems):
            speeds = jnp.concatenate(
                [
                    ref[pl.ds(e * rows + f, count, stride=spots), :]
                    for f in range(rows)
                    for ref in (stream_ref, normal_ref)
                ],
                1,
            )
            values = dot(lift_ref[...], below(speeds))
            highs, lows = [], []
            for f in range(rows):
                mine = values[:, f * LANES : (f + 1) * LANES]
                both, slope_x, slope_y = mine[:fine], mine[fine : 2 * fine], mine[2 * fine :]
                turned = pltpu.roll(both, sz.planes, 1)
                stream = jnp.where(half, both, turned)
                normal = jnp.where(half, turned, both)
                high, low = split((stream * factors[f]) * slope_x + (normal * (element_width * 0.5)) * slope_y)
                highs.append(high)
                lows.append(low)
            products.append(jnp.concatenate(highs + lows + highs, 0))
        if cut == 0:
            fetched[3].wait()
        weak = dot(back_ref[...], jnp.concatenate(products, 1))
        carry = None
        for e in range(sz.cut_elems):
            mine = weak[:, e * LANES : (e + 1) * LANES]
            if carry is not None:
                gap = jnp.zeros((column - carry.shape[0], LANES), jnp.float32)
                mine = mine + jnp.concatenate([carry, gap], 0)
            length = step if e < sz.cut_elems - 1 else column
            total_ref[pl.ds(e * step, length), :] = mine[:length]
            carry = mine[length:]
        for turn in range(sz.n_mode):
            goal = partner(spot, turn, sz.n_mode)
            out_refs[cut * sz.n_mode + turn][...] = total_ref[pl.ds(pl.multiple_of(goal * sz.sent, 8), sz.sent), :]


def transform_kernel(sz, *refs):
    weak_refs, (waves_ref, out_ref, mixed_ref, signal_ref, stage_ref) = refs[: sz.n_mode], refs[-5:]
    spot, place = lax.axis_index("mode"), lax.axis_index("ey")
    if sz.share > sz.sent:
        stage_ref[...] = jnp.zeros(stage_ref.shape, jnp.float32)
    for step, weak_ref in enumerate(weak_refs):
        for q in range(sz.n_ey):

            @pl.when(place == q)
            def _(begin=q * sz.stripe % sz.share, weak_ref=weak_ref):
                end = min(begin + sz.sent, sz.share)
                stage_ref[begin:end, :] = weak_ref[: end - begin, :]
                if end - begin < sz.sent:
                    stage_ref[: sz.sent - (end - begin), :] = weak_ref[end - begin :, :]

        turned = stage_ref[...].T
        first = pl.multiple_of(origin(spot, step, sz.n_mode) * sz.planes, 8)
        for k in range(2):
            signal_ref[k, pl.ds(first, sz.planes), :] = turned[k * sz.planes : (k + 1) * sz.planes]
    modes, tiles = sz.planes_total, mixed_ref.shape[0]
    last = min(LANES, sz.share)
    for k in range(2):
        high, low = split(signal_ref[k])
        part = dot(waves_ref[0], high) + dot(waves_ref[0], low) + dot(waves_ref[1], high)
        for t in range(tiles):
            mixed_ref[t, pl.ds(k, modes, stride=2), pl.ds(0, last)] = part[:, t * LANES : (t + 1) * LANES]
    shape = (sz.n_mode * sz.spots, sz.folds, PARTS, last)
    mixed = [mixed_ref[t, :, pl.ds(0, last)].reshape(shape) for t in range(tiles)]
    for fold in range(sz.folds):
        for t, tile in enumerate(rotate([each[:, fold] for each in mixed], fold * sz.fold_width % sz.share)):
            out_ref[:, fold, :, pl.ds(t * LANES, last)] = tile


def smooth_kernel(
    sz,
    *refs,
):
    terms_refs, out_refs = refs[: sz.cuts], refs[sz.cuts + 8 : -4]
    field_ref, first_ref, work_ref, stiff_ref = refs[-4:]
    in_y_ref, in_x_ref, pair_y_ref, pair_x_ref, out_y_ref, out_x_ref, lam_x_ref, lam_y_ref = refs[
        sz.cuts : sz.cuts + 8
    ]
    width, folds = sz.fold_width, sz.folds
    tiles = -(-sz.share // LANES)
    lanes = lane_index((PARTS, LANES))
    x_pad, x_eig = sz.x_pad, sz.x_eig
    place, spot = lax.axis_index("ey"), lax.axis_index("ex")
    device = (lax.axis_index("mode") * sz.n_ex + spot) * sz.n_ey + place
    first_mode = device * (sz.own // 4)
    masks = {}

    def within(low, length):
        if (low, length) not in masks:
            masks[low, length] = (lanes >= low) & (lanes < low + length)
        return masks[low, length]

    strips = [(q, fold, fold * width + q * sz.stripe) for q in range(sz.n_ey) for fold in range(folds)]

    for c in range(PARTS):
        field_ref[pl.ds(c * x_pad + sz.x_cuts, x_pad - sz.x_cuts), :] = jnp.zeros(
            (x_pad - sz.x_cuts, LANES), jnp.float32
        )
    for p, cut in [(p, cut) for p in range(sz.n_ex) for cut in range(sz.cuts)]:
        block = (spot + p) % sz.n_ex
        held = {}
        for q, fold, _ in strips:
            for z in range(sz.n_mode):
                whole = terms_refs[cut][(z * sz.n_ex + block) * sz.n_ey + q, pl.ds(fold * PARTS, PARTS), :]
                if sz.share < LANES:
                    whole = jnp.concatenate([whole] * (LANES // sz.share), 1)
                for t in range(tiles):
                    held[q, fold, z, t] = whole[:, t * LANES : (t + 1) * LANES]
        for i in range(sz.cut_x):
            groups = {}
            for q, fold, goal in strips:
                for z, t, lane, end, length in runs(sz, i, goal, 0, len(sz.inner[q]), sz.sent, sz.share):
                    source = held[q, fold, z, t]
                    shift = (end - lane) % LANES
                    old = groups.get(shift)
                    if old is not None:
                        source = jnp.where(within(lane, length), source, old[0])
                    groups[shift] = (source, (old[1] if old else []) + [(end, length)])
            result = None
            for shift, (source, spans) in groups.items():
                moved = pltpu.roll(source, shift, 1) if shift else source
                if result is None:
                    result = moved
                else:
                    for low, length in spans:
                        result = jnp.where(within(low, length), moved, result)
            field_ref[pl.ds((p * sz.cuts + cut) * sz.cut_x + i, PARTS, stride=x_pad), :] = result

    parts = dot(along(field_ref[...]), in_y_ref[...])
    field_ref[...] = parts[:, :LANES] + parts[:, LANES:]
    fold_of_lane = lane_index((1, LANES)) // width
    shifts, inverses = [], []
    for group in range(PARTS // 4):
        mode = (first_mode + fold_of_lane * (PARTS // 4) + group).astype(jnp.float32)
        shift = shift_base + (span_rate * mode) ** 2
        shifts.append(shift)
        inverses.append(1.0 / (lam_x_ref[...] + (lam_y_ref[...] + shift)))
    for c in range(0, PARTS, 2):
        pair = jnp.concatenate([field_ref[pl.ds((c + d) * x_pad, x_pad), :] for d in range(2)], 1)
        forced = left_dot(in_x_ref, pair)
        for d in range(2):
            mine = forced[:, d * LANES : (d + 1) * LANES]
            first_ref[pl.ds((c + d) * x_eig, x_eig), :] = mine
            work_ref[pl.ds((c + d) * x_eig, x_eig), :] = mine * inverses[(c + d) // 4]
    high, low = split(work_ref[...])
    both = dot(jnp.concatenate([high, low, high], 1), pair_y_ref[...])
    work_ref[...] = both[:, :LANES]
    stiff_ref[...] = both[:, LANES:]
    for c in range(0, PARTS, 2):
        masses, stiffs = [], []
        for d in range(2):
            rows = pl.ds((c + d) * x_eig, x_eig)
            masses.append(work_ref[rows, :])
            stiffs.append(stiff_ref[rows, :] + shifts[c // 4] * masses[d])
        stacked_pair = jnp.concatenate([jnp.concatenate(masses, 1), jnp.concatenate(stiffs, 1)], 0)
        applied = left_dot(pair_x_ref, stacked_pair)
        for d in range(2):
            rows = pl.ds((c + d) * x_eig, x_eig)
            mine = applied[:, d * LANES : (d + 1) * LANES]
            first_ref[rows, :] = (2.0 * first_ref[rows, :] - mine) * inverses[c // 4]
    parts = dot(along(first_ref[...]), out_y_ref[...])
    work_ref[...] = parts[:, :LANES] + parts[:, LANES:]
    for c in range(0, PARTS, 2):
        pair = jnp.concatenate([work_ref[pl.ds((c + d) * x_eig, x_eig), :] for d in range(2)], 1)
        solved = left_dot(out_x_ref, pair)
        for d in range(2):
            field_ref[pl.ds((c + d) * x_pad, x_pad), :] = solved[:, d * LANES : (d + 1) * LANES]

    for p in range(sz.n_ex):
        made = {}
        for i in range(sz.block_x):
            source = field_ref[pl.ds(p * sz.block_x + i, PARTS, stride=x_pad), :]
            shift = i * sz.block_y % LANES
            moved = pltpu.roll(source, shift, 1) if shift else source
            for q, fold, goal in strips:
                inner = sz.inner[q]
                for _, tile, lane, _, length in runs(
                    sz, i, goal, inner[0], len(inner), sz.lane_nodes, sz.lane_nodes
                ):
                    old = made.get((q, fold, tile), moved)
                    if old is not moved:
                        old = jnp.where(within(lane, length), moved, old)
                    made[q, fold, tile] = old
        for fold in range(folds):
            for tile in range(sz.lane_nodes // LANES):
                for turn in range(sz.n_ey):
                    chosen = jnp.zeros((PARTS, LANES), jnp.float32)
                    for q in range(sz.n_ey):
                        if (q, fold, tile) in made:
                            chosen = jnp.where((place + turn) % sz.n_ey == q, made[q, fold, tile], chosen)
                    out_refs[p * sz.n_ey + turn][pl.ds(fold * PARTS, PARTS), pl.ds(tile * LANES, LANES)] = chosen


def spread_kernel(sz, *refs):
    solved_refs, (out_ref, stacked_ref, turned_ref) = refs[:-3], refs[-3:]
    place, spot = lax.axis_index("ey"), lax.axis_index("ex")
    for step, solved_ref in enumerate(solved_refs):
        shift, turn = step // sz.n_ey, step % sz.n_ey
        source = (spot - shift + sz.n_ex) % sz.n_ex * sz.n_ey + (place - turn + sz.n_ey) % sz.n_ey
        for q in range(sz.n_ey):

            @pl.when(place == q)
            def _(q=q, solved_ref=solved_ref, source=source):
                for fold in range(sz.folds):
                    shift = -(fold * sz.fold_width + q * sz.stripe)
                    tiles = [
                        solved_ref[pl.ds(fold * PARTS, PARTS), pl.ds(t * LANES, LANES)]
                        for t in range(sz.lane_nodes // LANES)
                    ]
                    rows = pl.ds(pl.multiple_of(source * sz.own + fold * PARTS, PARTS), PARTS)
                    for t, tile in enumerate(rotate(tiles, shift)):
                        stacked_ref[rows, pl.ds(t * LANES, LANES)] = tile

    turned_ref[...] = stacked_ref[...].T
    spots = sz.elems * sz.rows
    for e in range(sz.elems):
        for f in range(sz.rows):
            for a in range(sz.nodes):
                start = sz.block_y * (sz.order * e + a) + sz.order * f
                out_ref[pl.ds(a * sz.nodes * spots + e * sz.rows + f, sz.nodes, stride=spots), :] = turned_ref[
                    pl.ds(start, sz.nodes), :
                ]
    blank = jnp.zeros((sz.elems, LANES), jnp.float32)

    @pl.when(place == 0)
    def _():
        for a in range(sz.nodes):
            out_ref[pl.ds(a * sz.nodes * spots, sz.elems, stride=sz.rows), :] = blank

    @pl.when(place == sz.n_ey - 1)
    def _():
        for a in range(sz.nodes):
            first = ((a + 1) * sz.nodes - 1) * spots + sz.rows - 1
            out_ref[pl.ds(first, sz.elems, stride=sz.rows), :] = blank


def call(kernel, shapes, operands, scratch=(), spaces=pltpu.VMEM, limit=16, flops=10**9):
    if not isinstance(spaces, list):
        spaces = [spaces] * len(operands)
    made = pl.pallas_call(
        kernel,
        out_shape=[jax.ShapeDtypeStruct(shape, jnp.float32) for shape in shapes],
        in_specs=[pl.BlockSpec(memory_space=space) for space in spaces],
        out_specs=[pl.BlockSpec(memory_space=pltpu.VMEM) for _ in shapes],
        scratch_shapes=[pltpu.VMEM(each, jnp.float32) if isinstance(each, tuple) else each for each in scratch],
        compiler_params=pltpu.CompilerParams(vmem_limit_bytes=limit * 2**20),
        cost_estimate=pl.CostEstimate(flops=flops, bytes_accessed=10**6, transcendentals=0),
    )(*operands)
    return list(made)


def on_device(sz, tables, stream_speed, normal_speed):
    flat = sz.nodes * sz.nodes * sz.elems * sz.rows
    table = {name: jnp.asarray(value) for name, value in tables.items() if name != "heights"}
    heights = [float(height) for height in tables["heights"]]
    pieces = call(
        functools.partial(advect_kernel, sz, heights),
        [(sz.sent, LANES)] * (sz.n_mode * sz.cuts),
        [
            pltpu.with_memory_space_constraint(each, pltpu.HBM)
            for each in (
                stream_speed.reshape(flat, sz.planes),
                normal_speed.reshape(flat, sz.planes),
                table["lift"],
                table["back"],
            )
        ],
        [
            (sz.cut_nodes, LANES),
            (flat, sz.planes),
            (flat, sz.planes),
            pltpu.VMEM(tables["lift"].shape, jnp.bfloat16),
            pltpu.VMEM(tables["back"].shape[1:], jnp.bfloat16),
            pltpu.SemaphoreType.DMA((4,)),
        ],
        pltpu.HBM,
    )
    weak = [pieces[cut * sz.n_mode : (cut + 1) * sz.n_mode] for cut in range(sz.cuts)]
    for cut in range(sz.cuts):
        for step in sorted(range(1, sz.n_mode), key=lambda each: (each & -each, each), reverse=True):
            pairs = [(z, partner(z, step, sz.n_mode)) for z in range(sz.n_mode)]
            weak[cut][step] = lax.ppermute(weak[cut][step], "mode", pairs)
    terms, ahead = [], []
    for cut in range(sz.cuts):
        (spectra,) = call(
            functools.partial(transform_kernel, sz),
            [(sz.n_mode * sz.spots, sz.folds, PARTS, sz.share)],
            [*weak[cut], *ahead, table["waves"]],
            [
                (-(-sz.share // LANES), 2 * sz.planes_total, LANES),
                (2, sz.planes_total, sz.share),
                (sz.share, LANES),
            ],
            [pltpu.VMEM] * sz.n_mode + [pl.ANY] * len(ahead) + [pltpu.VMEM],
            flops=10**11 if cut == sz.cuts - 1 else 10**8,
        )
        spectra = spectra.reshape(sz.n_mode * sz.spots, sz.own, sz.share)
        terms.append(lax.all_to_all(spectra, ("mode", "ex", "ey"), split_axis=0, concat_axis=0, tiled=True))
        ahead = [spectra]
    names = ("in_y", "in_x", "pair_y", "pair_x", "out_y", "out_x", "lam_x", "lam_y")
    solved = call(
        functools.partial(smooth_kernel, sz),
        [(sz.own, sz.lane_nodes)] * sz.spots,
        terms + [table[name] for name in names],
        [(PARTS * sz.x_pad, LANES)] + [(PARTS * sz.x_eig, LANES)] * 3,
    )
    for step in sorted(range(1, sz.spots), key=lambda each: each // sz.n_ey == 0):
        shift, turn = step // sz.n_ey, step % sz.n_ey
        pairs = [
            (p * sz.n_ey + q, (p + shift) % sz.n_ex * sz.n_ey + (q + turn) % sz.n_ey)
            for p in range(sz.n_ex)
            for q in range(sz.n_ey)
        ]
        solved[step] = lax.ppermute(solved[step], ("ex", "ey"), pairs)
    (out,) = call(
        functools.partial(spread_kernel, sz),
        [(flat, LANES)],
        solved,
        [(sz.columns, sz.lane_nodes), (sz.lane_nodes, LANES)],
    )
    return out.reshape(sz.nodes, sz.nodes, sz.elems, sz.rows, sz.columns)


def solution(mesh):
    spec = P(None, None, "ex", "ey", "mode")

    def whole(stream_speed, normal_speed):
        shape = stream_speed.shape
        counts = mesh.shape
        block = shape[:2] + (shape[2] // counts["ex"], shape[3] // counts["ey"], shape[4] // counts["mode"])
        sz = Sizes(counts, block)
        return jax.shard_map(
            functools.partial(on_device, sz, host_tables(sz)),
            mesh=mesh,
            in_specs=(spec, spec),
            out_specs=spec,
            check_vma=False,
        )(stream_speed, normal_speed)

    return whole
```

```python
import functools
import math

import jax
import jax.numpy as jnp
import ml_dtypes
import numpy as np
from jax import lax
from jax.experimental import pallas as pl
from jax.experimental.pallas import tpu as pltpu
from jax.sharding import PartitionSpec as P

BF16 = ml_dtypes.bfloat16

element_width = 2.0
shift_base = 10.0
span_rate = 0.0125


def legendre_pair(degree, points):
    before = points * 0.0 + 1.0
    current = points.copy()
    for step in range(1, degree):
        upcoming = ((2 * step + 1) * points * current - step * before) / (step + 1)
        before = current
        current = upcoming
    return (current, before)


def legendre_slope(degree, points):
    current, before = legendre_pair(degree, points)
    return (current, degree * (points * current - before) / (points * points - 1.0))


def lobatto_points(order):
    guesses = -np.cos(np.pi * np.arange(1, order) / order)
    for step in range(60):
        current, slope = legendre_slope(order, guesses)
        second = (2.0 * guesses * slope - order * (order + 1) * current) / (1.0 - guesses * guesses)
        guesses = guesses - slope / second
    return guesses


def gauss_rule(count):
    guesses = -np.cos(np.pi * (np.arange(count) + 0.75) / (count + 0.5))
    for step in range(60):
        current, slope = legendre_slope(count, guesses)
        guesses = guesses - current / slope
    current, slope = legendre_slope(count, guesses)
    return (guesses, 2.0 / ((1.0 - guesses * guesses) * slope * slope))


def jacobi_eigen(matrix):
    size_n = matrix.shape[0]
    work = matrix.copy()
    vectors = np.eye(size_n)
    for sweep_number in range(20):
        for first in range(size_n):
            for second in range(first + 1, size_n):
                coupling = work[first, second]
                if abs(coupling) > 1e-300:
                    theta = (work[second, second] - work[first, first]) / (2.0 * coupling)
                    direction = 1.0 if theta >= 0.0 else -1.0
                    tangent = direction / (abs(theta) + np.sqrt(theta * theta + 1.0))
                    cosine = 1.0 / np.sqrt(tangent * tangent + 1.0)
                    sine = tangent * cosine
                    rotation = np.eye(size_n)
                    rotation[first, first] = cosine
                    rotation[second, second] = cosine
                    rotation[first, second] = sine
                    rotation[second, first] = -sine
                    work = rotation.T @ work @ rotation
                    vectors = vectors @ rotation
    diagonal_index = np.arange(size_n)
    return (work[diagonal_index, diagonal_index], vectors)


def extended_basis(stiffness, weights, left_width, centre_width, right_width):
    node_count = weights.shape[0]
    full_count = 3 * node_count - 2
    stiff_full = np.zeros((full_count, full_count))
    mass_full = np.zeros(full_count)
    for position, span_width in enumerate((left_width, centre_width, right_width)):
        if span_width > 0.0:
            first_node = position * (node_count - 1)
            stiff_full[
                first_node : first_node + node_count, first_node : first_node + node_count
            ] += stiffness * (2.0 / span_width)
            mass_full[first_node : first_node + node_count] += weights * (span_width / 2.0)
    low_index = node_count - 2
    high_index = low_index + node_count + 2
    stiff_ext = stiff_full[low_index:high_index, low_index:high_index].copy()
    mass_ext = mass_full[low_index:high_index].copy()
    frozen_list = []
    if left_width <= 0.0:
        frozen_list += [0, 1]
    if right_width <= 0.0:
        frozen_list += [node_count, node_count + 1]
    for frozen_index in frozen_list:
        stiff_ext[frozen_index, :] = 0.0
        stiff_ext[:, frozen_index] = 0.0
        stiff_ext[frozen_index, frozen_index] = 1.0
        mass_ext[frozen_index] = 1.0
    inverse_root = 1.0 / np.sqrt(mass_ext)
    lambdas, vectors = jacobi_eigen(inverse_root[:, None] * stiff_ext * inverse_root[None, :])
    return (inverse_root[:, None] * vectors, lambdas)


def spectral_tables(order, rows_total):
    inner_points = lobatto_points(order)
    points = np.concatenate([[-1.0], inner_points, [1.0]])
    values, unused_before = legendre_pair(order, points)
    weights = 2.0 / (order * (order + 1) * values**2)
    identity = np.eye(order + 1)
    point_gaps = points[:, None] - points[None, :] + identity
    derivative = values[:, None] / (values[None, :] * point_gaps) * (1.0 - identity)
    derivative[0, 0] = -order * (order + 1) / 4.0
    derivative[order, order] = order * (order + 1) / 4.0
    stiffness = derivative.T @ (weights[:, None] * derivative)
    gauss_points, gauss_weights = gauss_rule(3 * (order + 1) // 2)
    offsets = gauss_points[:, None, None] - points[None, None, :]
    numerators = np.prod(np.where(identity[None, :, :] > 0.5, 1.0, offsets), axis=2)
    denominators = np.prod(np.where(identity > 0.5, 1.0, points[:, None] - points[None, :]), axis=1)
    interp = numerators / denominators[None, :]
    heights = 0.6 + 1.4 * np.sin(np.pi * (np.arange(rows_total) + 0.5) / rows_total)
    basis_x, lambdas_x = extended_basis(
        stiffness, weights, element_width, element_width, element_width
    )
    basis_rows = []
    lambda_rows = []
    for row_number in range(rows_total):
        below = heights[row_number - 1] if row_number > 0 else 0.0
        above = heights[row_number + 1] if row_number < rows_total - 1 else 0.0
        basis_one, lambda_one = extended_basis(
            stiffness, weights, below, heights[row_number], above
        )
        basis_rows.append(basis_one)
        lambda_rows.append(lambda_one)
    return (
        derivative,
        interp,
        gauss_weights,
        weights,
        stiffness,
        basis_x,
        lambdas_x,
        np.stack(basis_rows),
        np.stack(lambda_rows),
        heights,
    )


PARTS = 8
LANES = 128


def ceil_to(count, step):
    return -(-count // step) * step


class Sizes:
    def __init__(self, mesh_shape, block_shape):
        self.n_mode, self.n_ex, self.n_ey = (mesh_shape[name] for name in ("mode", "ex", "ey"))
        self.nodes, _, self.elems, self.rows, self.planes = block_shape
        self.order = self.nodes - 1
        self.gauss = 3 * self.nodes // 2
        self.rows_total = self.rows * self.n_ey
        self.elems_total = self.elems * self.n_ex
        self.planes_total = self.planes * self.n_mode
        self.block_x = self.order * self.elems + 1
        full_y = self.order * self.rows + 1
        self.inner = [
            [j for j in range(full_y) if not (p == 0 and j == 0) and not (p == self.n_ey - 1 and j == full_y - 1)]
            for p in range(self.n_ey)
        ]
        self.block_y = max(len(found) for found in self.inner)
        self.cuts = 2 if self.elems % 2 == 0 else 1
        self.cut_elems = self.elems // self.cuts
        self.cut_x = self.order * self.cut_elems + 1
        share = -(-self.cut_x * self.block_y // self.n_mode)
        self.share = ceil_to(share, LANES if share > 64 else 16)
        self.cut_nodes = self.share * self.n_mode
        self.lane_nodes = ceil_to(self.block_x * self.block_y + 2, LANES)
        self.columns = 2 * self.planes
        self.spots = self.n_ex * self.n_ey
        self.own = self.columns // self.spots
        self.folds = self.own // PARTS
        self.fold_width = LANES // self.folds
        self.points = self.nodes + 2
        self.x_cuts = self.n_ex * self.cuts * self.cut_x
        self.x_pad = ceil_to(max(self.x_cuts, self.n_ex * self.block_x), 16)
        self.x_eig = self.elems_total * self.points
        self.y_eig = self.rows_total * self.points
        self.fine = ceil_to(self.gauss * self.gauss, 16)
        assert self.own == PARTS * self.folds and self.x_eig % 16 == 0
        assert max(self.y_eig, self.n_ey * self.block_y) <= self.fold_width
        assert 2 * self.planes == LANES


def high_low(table):
    high = np.asarray(table, np.float32).astype(BF16)
    low = (np.asarray(table, np.float64) - high.astype(np.float64)).astype(BF16)
    return high, low


def beside(table):
    high, low = high_low(table)
    return np.concatenate([high, high, low], 1)


def host_tables(sz):
    derivative, interp, gauss_weights, weights, stiffness, basis_x, lam_x, basis_y, lam_y, heights = spectral_tables(
        sz.order, sz.rows_total
    )
    nodes, fine, points = sz.nodes, sz.fine, sz.points
    gauss_count = sz.gauss**2
    lift = np.zeros((3 * fine, nodes * nodes))
    lift[:gauss_count] = np.kron(interp, interp)
    lift[fine : fine + gauss_count] = np.kron(interp @ derivative, interp)
    lift[2 * fine : 2 * fine + gauss_count] = np.kron(interp, interp @ derivative)
    back = np.zeros((sz.n_ey, nodes * sz.block_y, sz.rows * fine))
    weighted = interp.T * gauss_weights[None, :]
    for place in range(sz.n_ey):
        for f in range(sz.rows):
            for jj, j in enumerate(sz.inner[place]):
                b = j - sz.order * f
                if 0 <= b < nodes:
                    back[place, jj :: sz.block_y, f * fine : f * fine + gauss_count] = -np.kron(
                        weighted, weighted[b : b + 1]
                    )
    grid_x, grid_y = sz.order * sz.elems_total, sz.order * sz.rows_total + 1
    to_x, stiff_x, mass_x = np.zeros((sz.x_eig, grid_x)), np.zeros((grid_x, grid_x)), np.zeros(grid_x)
    for e in range(sz.elems_total):
        for t in range(points):
            to_x[e * points : (e + 1) * points, (sz.order * e + t - 1) % grid_x] += basis_x[t]
        index = (sz.order * e + np.arange(nodes)) % grid_x
        stiff_x[np.ix_(index, index)] += stiffness * (2.0 / element_width)
        mass_x[index] += weights * (element_width / 2.0)
    to_y, stiff_y, mass_y = np.zeros((sz.y_eig, grid_y)), np.zeros((grid_y, grid_y)), np.zeros(grid_y)
    for f in range(sz.rows_total):
        for t in range(points):
            y = sz.order * f + t - 1
            if 0 < y < grid_y - 1:
                to_y[f * points : (f + 1) * points, y] = basis_y[f][t]
        index = sz.order * f + np.arange(nodes)
        stiff_y[np.ix_(index, index)] += stiffness * (2.0 / heights[f])
        mass_y[index] += weights * (heights[f] / 2.0)
    stiff_xx, mass_xx = to_x @ stiff_x @ to_x.T, (to_x * mass_x) @ to_x.T
    stiff_yy, mass_yy = to_y @ stiff_y @ to_y.T, (to_y * mass_y) @ to_y.T
    def block_x(blocks, elems):
        length = sz.order * elems + 1
        nodes_of = [(sz.order * elems * p + i) % grid_x for p in range(blocks) for i in range(length)]
        table = np.zeros((sz.x_eig, sz.x_pad))
        table[:, : len(nodes_of)] = to_x[:, nodes_of]
        return table

    width, folds = sz.fold_width, sz.folds
    block_y = np.zeros((width, width))
    for place in range(sz.n_ey):
        for jj, j in enumerate(sz.inner[place]):
            block_y[place * sz.block_y + jj, : sz.y_eig] = to_y[:, sz.order * sz.rows * place + j]

    def folded(table):
        padded = np.zeros((width, width))
        padded[: table.shape[0], : table.shape[1]] = table
        return np.kron(np.eye(folds), padded)

    def one_dot(table):
        high, low = high_low(folded(table))
        return np.block([[high, low], [high, np.zeros_like(low)]]).astype(BF16)

    mass_pair, stiff_pair = high_low(folded(mass_yy)), high_low(folded(stiff_yy))
    heads = np.concatenate([mass_pair[0], stiff_pair[0]], 1)
    tails = np.concatenate([mass_pair[1], stiff_pair[1]], 1)
    lam_lanes = np.ones((1, folds, width))
    lam_lanes[:, :, : sz.y_eig] = lam_y.reshape(-1)
    planes_total = sz.planes_total
    turns = np.arange(planes_total)[None, :] * np.arange(planes_total // 2)[:, None] % planes_total
    angles = turns * (2.0 * math.pi / planes_total)
    waves = np.stack([np.cos(angles), -np.sin(angles)], 1).reshape(planes_total, planes_total) / planes_total
    return dict(
        heights=np.asarray(heights, np.float32),
        lift=beside(lift),
        back=np.stack([beside(table) for table in back]),
        waves=np.stack(high_low(waves)),
        in_y=one_dot(block_y),
        in_x=stacked(block_x(sz.n_ex * sz.cuts, sz.cut_elems)),
        pair_y=np.concatenate([heads, heads, tails], 0),
        pair_x=stacked(np.concatenate([stiff_xx, mass_xx], 1)),
        out_y=one_dot(block_y.T),
        out_x=stacked(block_x(sz.n_ex, sz.elems).T),
        lam_x=np.asarray(np.tile(lam_x, sz.elems_total)[:, None] * np.ones((1, LANES)), np.float32),
        lam_y=np.asarray(lam_lanes.reshape(1, LANES), np.float32),
    )


def stacked(table):
    return np.concatenate(high_low(table), 0)


def split(value):
    high = value.astype(jnp.bfloat16)
    low = (value - high.astype(jnp.float32)).astype(jnp.bfloat16)
    return high, low


def dot(left, right):
    return lax.dot_general(left, right, (((1,), (0,)), ((), ())), preferred_element_type=jnp.float32)


def below(value):
    high, low = split(value)
    return jnp.concatenate([high, low, high], 0)


def left_dot(table_ref, value):
    rows = table_ref.shape[0] // 2
    high, low = split(value)
    both = dot(table_ref[...], high)
    return both[:rows] + both[rows:] + dot(table_ref[:rows, :], low)


def along(value):
    return jnp.concatenate(split(value), 1)


def partner(spot, step, count):
    if count & (count - 1) == 0:
        return spot ^ step
    return (spot + step) % count


def origin(spot, step, count):
    if count & (count - 1) == 0:
        return spot ^ step
    return (spot - step + count) % count


def lane_index(shape):
    return lax.broadcasted_iota(jnp.int32, shape, len(shape) - 1)


def advect_kernel(sz, heights, cut, stream_hbm, normal_hbm, lift_hbm, back_hbm, *others):
    out_refs, (total_ref, stream_ref, normal_ref, lift_ref, back_ref, arrived) = others[:-6], others[-6:]
    place = lax.axis_index("ey")
    fetched = [
        pltpu.make_async_copy(source, target, arrived.at[i])
        for i, (source, target) in enumerate(
            (
                (stream_hbm, stream_ref),
                (normal_hbm, normal_ref),
                (lift_hbm, lift_ref),
                (back_hbm.at[place], back_ref),
            )
        )
    ]
    for copy in fetched:
        copy.start()
    count, fine, rows = sz.nodes * sz.nodes, sz.fine, sz.rows
    spots = sz.elems * rows
    half = lane_index((fine, LANES)) < sz.planes
    column, step = sz.nodes * sz.block_y, sz.order * sz.block_y
    factors = [
        sum(jnp.where(place == q, heights[q * rows + f] * 0.5, 0.0) for q in range(sz.n_ey)) for f in range(rows)
    ]
    full = sz.cut_x * sz.block_y // 8 * 8
    total_ref[pl.ds(full, sz.cut_nodes - full), :] = jnp.zeros((sz.cut_nodes - full, LANES), jnp.float32)
    spot = lax.axis_index("mode")
    for copy in fetched[:3]:
        copy.wait()
    products = []
    for e in range(cut * sz.cut_elems, (cut + 1) * sz.cut_elems):
        speeds = jnp.concatenate(
            [
                ref[pl.ds(e * rows + f, count, stride=spots), :]
                for f in range(rows)
                for ref in (stream_ref, normal_ref)
            ],
            1,
        )
        values = dot(lift_ref[...], below(speeds))
        highs, lows = [], []
        for f in range(rows):
            mine = values[:, f * LANES : (f + 1) * LANES]
            both, slope_x, slope_y = mine[:fine], mine[fine : 2 * fine], mine[2 * fine :]
            turned = pltpu.roll(both, sz.planes, 1)
            stream = jnp.where(half, both, turned)
            normal = jnp.where(half, turned, both)
            high, low = split((stream * factors[f]) * slope_x + (normal * (element_width * 0.5)) * slope_y)
            highs.append(high)
            lows.append(low)
        products.append(jnp.concatenate(highs + lows + highs, 0))
    fetched[3].wait()
    weak = dot(back_ref[...], jnp.concatenate(products, 1))
    carry = None
    for e in range(sz.cut_elems):
        mine = weak[:, e * LANES : (e + 1) * LANES]
        if carry is not None:
            gap = jnp.zeros((column - carry.shape[0], LANES), jnp.float32)
            mine = mine + jnp.concatenate([carry, gap], 0)
        length = step if e < sz.cut_elems - 1 else column
        total_ref[pl.ds(e * step, length), :] = mine[:length]
        carry = mine[length:]
    for turn in range(sz.n_mode):
        goal = partner(spot, turn, sz.n_mode)
        out_refs[turn][...] = total_ref[pl.ds(pl.multiple_of(goal * sz.share, 8), sz.share), :]


def transform_kernel(sz, *refs):
    weak_refs, (waves_ref, out_ref, mixed_ref, signal_ref) = refs[:-4], refs[-4:]
    spot = lax.axis_index("mode")
    for number, weak_ref in enumerate(weak_refs):
        cut, step = number // sz.n_mode, number % sz.n_mode
        turned = weak_ref[...].T
        first = pl.multiple_of(origin(spot, step, sz.n_mode) * sz.planes, 8)
        for k in range(2):
            signal_ref[k, pl.ds(first, sz.planes), pl.ds(cut * sz.share, sz.share)] = turned[
                k * sz.planes : (k + 1) * sz.planes
            ]
    modes, width = sz.planes_total, sz.cuts * sz.share
    for k in range(2):
        high, low = split(signal_ref[k])
        part = dot(waves_ref[0], high) + dot(waves_ref[0], low) + dot(waves_ref[1], high)
        for t in range(mixed_ref.shape[0]):
            tile = part[:, t * LANES : (t + 1) * LANES]
            mixed_ref[t, pl.ds(k, modes, stride=2), pl.ds(0, tile.shape[1])] = tile
    for t in range(mixed_ref.shape[0]):
        last = min(LANES, width - t * LANES)
        out_ref[:, pl.ds(t * LANES, last)] = mixed_ref[t, :, pl.ds(0, last)]


def smooth_kernel(
    sz,
    *refs,
):
    terms_ref, out_refs = refs[0], refs[9:-4]
    field_ref, first_ref, work_ref, stiff_ref = refs[-4:]
    in_y_ref, in_x_ref, pair_y_ref, pair_x_ref, out_y_ref, out_x_ref, lam_x_ref, lam_y_ref = refs[1:9]
    width, folds, strip = sz.fold_width, sz.folds, sz.block_y
    tiles = -(-sz.cut_nodes // LANES)
    lanes = lane_index((PARTS, LANES))
    x_pad, x_eig = sz.x_pad, sz.x_eig
    place, spot = lax.axis_index("ey"), lax.axis_index("ex")
    device = (lax.axis_index("mode") * sz.n_ex + spot) * sz.n_ey + place
    first_mode = device * (sz.own // 4)

    for c in range(PARTS):
        field_ref[pl.ds(c * x_pad + sz.x_cuts, x_pad - sz.x_cuts), :] = jnp.zeros(
            (x_pad - sz.x_cuts, LANES), jnp.float32
        )
    for p, cut in [(p, cut) for p in range(sz.n_ex) for cut in range(sz.cuts)]:
        block = (spot + p) % sz.n_ex
        held = {}
        for q in range(sz.n_ey):
            for fold in range(folds):
                whole = jnp.concatenate(
                    [
                        terms_ref[
                            (z * sz.n_ex + block) * sz.n_ey + q,
                            pl.ds(fold * PARTS, PARTS),
                            pl.ds(cut * sz.share, sz.share),
                        ]
                        for z in range(sz.n_mode)
                    ],
                    1,
                )
                held[q, fold] = [whole[:, t * LANES : (t + 1) * LANES] for t in range(tiles)]
        for i in range(sz.cut_x):
            start = i * strip
            t, r = start // LANES, start % LANES
            result = jnp.zeros((PARTS, LANES), jnp.float32)
            for fold in range(folds):
                for q in range(sz.n_ey):
                    source = held[q, fold][t]
                    if r + strip > LANES:
                        source = jnp.where(lanes >= r, source, held[q, fold][t + 1])
                    goal = fold * width + q * strip
                    moved = pltpu.roll(source, (goal - r) % LANES, 1) if goal != r else source
                    result = jnp.where((lanes >= goal) & (lanes < goal + strip), moved, result)
            field_ref[pl.ds((p * sz.cuts + cut) * sz.cut_x + i, PARTS, stride=x_pad), :] = result

    parts = dot(along(field_ref[...]), in_y_ref[...])
    field_ref[...] = parts[:, :LANES] + parts[:, LANES:]
    fold_of_lane = lane_index((1, LANES)) // width
    shifts, inverses = [], []
    for group in range(PARTS // 4):
        mode = (first_mode + fold_of_lane * (PARTS // 4) + group).astype(jnp.float32)
        shift = shift_base + (span_rate * mode) ** 2
        shifts.append(shift)
        inverses.append(1.0 / (lam_x_ref[...] + (lam_y_ref[...] + shift)))
    for c in range(0, PARTS, 2):
        pair = jnp.concatenate([field_ref[pl.ds((c + d) * x_pad, x_pad), :] for d in range(2)], 1)
        forced = left_dot(in_x_ref, pair)
        for d in range(2):
            mine = forced[:, d * LANES : (d + 1) * LANES]
            first_ref[pl.ds((c + d) * x_eig, x_eig), :] = mine
            work_ref[pl.ds((c + d) * x_eig, x_eig), :] = mine * inverses[(c + d) // 4]
    high, low = split(work_ref[...])
    both = dot(jnp.concatenate([high, low, high], 1), pair_y_ref[...])
    work_ref[...] = both[:, :LANES]
    stiff_ref[...] = both[:, LANES:]
    for c in range(0, PARTS, 2):
        masses, stiffs = [], []
        for d in range(2):
            rows = pl.ds((c + d) * x_eig, x_eig)
            masses.append(work_ref[rows, :])
            stiffs.append(stiff_ref[rows, :] + shifts[c // 4] * masses[d])
        stacked_pair = jnp.concatenate([jnp.concatenate(masses, 1), jnp.concatenate(stiffs, 1)], 0)
        applied = left_dot(pair_x_ref, stacked_pair)
        for d in range(2):
            rows = pl.ds((c + d) * x_eig, x_eig)
            mine = applied[:, d * LANES : (d + 1) * LANES]
            first_ref[rows, :] = (2.0 * first_ref[rows, :] - mine) * inverses[c // 4]
    parts = dot(along(first_ref[...]), out_y_ref[...])
    work_ref[...] = parts[:, :LANES] + parts[:, LANES:]
    for c in range(0, PARTS, 2):
        pair = jnp.concatenate([work_ref[pl.ds((c + d) * x_eig, x_eig), :] for d in range(2)], 1)
        solved = left_dot(out_x_ref, pair)
        for d in range(2):
            field_ref[pl.ds((c + d) * x_pad, x_pad), :] = solved[:, d * LANES : (d + 1) * LANES]

    for p in range(sz.n_ex):
        made = {}
        for i in range(sz.block_x):
            source = field_ref[pl.ds(p * sz.block_x + i, PARTS, stride=x_pad), :]
            for q in range(sz.n_ey):
                begin = i * strip + sz.inner[q][0]
                count = len(sz.inner[q])
                t, r = begin // LANES, begin % LANES
                for fold in range(folds):
                    origin = fold * width + q * strip
                    moved = pltpu.roll(source, (r - origin) % LANES, 1) if origin != r else source
                    for tile, low, high in ((t, r, r + count), (t + 1, 0, r + count - LANES)):
                        if high > 0:
                            old = made.get((q, fold, tile))
                            if old is None:
                                old = jnp.zeros((PARTS, LANES), jnp.float32)
                            made[q, fold, tile] = jnp.where((lanes >= low) & (lanes < high), moved, old)
        for fold in range(folds):
            for tile in range(sz.lane_nodes // LANES):
                for turn in range(sz.n_ey):
                    chosen = jnp.zeros((PARTS, LANES), jnp.float32)
                    for q in range(sz.n_ey):
                        if (q, fold, tile) in made:
                            chosen = jnp.where((place + turn) % sz.n_ey == q, made[q, fold, tile], chosen)
                    out_refs[p * sz.n_ey + turn][pl.ds(fold * PARTS, PARTS), pl.ds(tile * LANES, LANES)] = chosen


def spread_kernel(sz, *refs):
    solved_refs, (out_ref, stacked_ref, turned_ref) = refs[:-3], refs[-3:]
    place, spot = lax.axis_index("ey"), lax.axis_index("ex")
    for step, solved_ref in enumerate(solved_refs):
        shift, turn = step // sz.n_ey, step % sz.n_ey
        source = (spot - shift + sz.n_ex) % sz.n_ex * sz.n_ey + (place - turn + sz.n_ey) % sz.n_ey
        stacked_ref[pl.ds(pl.multiple_of(source * sz.own, PARTS), sz.own), :] = solved_ref[...]
    turned_ref[...] = stacked_ref[...].T
    spots = sz.elems * sz.rows
    for e in range(sz.elems):
        for f in range(sz.rows):
            for a in range(sz.nodes):
                start = sz.block_y * (sz.order * e + a) + sz.order * f
                out_ref[pl.ds(a * sz.nodes * spots + e * sz.rows + f, sz.nodes, stride=spots), :] = turned_ref[
                    pl.ds(start, sz.nodes), :
                ]
    blank = jnp.zeros((sz.elems, LANES), jnp.float32)

    @pl.when(place == 0)
    def _():
        for a in range(sz.nodes):
            out_ref[pl.ds(a * sz.nodes * spots, sz.elems, stride=sz.rows), :] = blank

    @pl.when(place == sz.n_ey - 1)
    def _():
        for a in range(sz.nodes):
            first = ((a + 1) * sz.nodes - 1) * spots + sz.rows - 1
            out_ref[pl.ds(first, sz.elems, stride=sz.rows), :] = blank


def call(kernel, shapes, operands, scratch=(), spaces=pltpu.VMEM, limit=16, flops=10**9):
    if not isinstance(spaces, list):
        spaces = [spaces] * len(operands)
    made = pl.pallas_call(
        kernel,
        out_shape=[jax.ShapeDtypeStruct(shape, jnp.float32) for shape in shapes],
        in_specs=[pl.BlockSpec(memory_space=space) for space in spaces],
        out_specs=[pl.BlockSpec(memory_space=pltpu.VMEM) for _ in shapes],
        scratch_shapes=[pltpu.VMEM(each, jnp.float32) if isinstance(each, tuple) else each for each in scratch],
        compiler_params=pltpu.CompilerParams(vmem_limit_bytes=limit * 2**20),
        cost_estimate=pl.CostEstimate(flops=flops, bytes_accessed=10**6, transcendentals=0),
    )(*operands)
    return list(made)


def on_device(sz, tables, stream_speed, normal_speed):
    flat = sz.nodes * sz.nodes * sz.elems * sz.rows
    table = {name: jnp.asarray(value) for name, value in tables.items() if name != "heights"}
    heights = [float(height) for height in tables["heights"]]
    weak = []
    for cut in range(sz.cuts):
        pieces = call(
            functools.partial(advect_kernel, sz, heights, cut),
            [(sz.share, LANES)] * sz.n_mode,
            [
                pltpu.with_memory_space_constraint(each, pltpu.HBM)
                for each in (
                    stream_speed.reshape(flat, sz.planes),
                    normal_speed.reshape(flat, sz.planes),
                    table["lift"],
                    table["back"],
                )
            ],
            [
                (sz.cut_nodes, LANES),
                (flat, sz.planes),
                (flat, sz.planes),
                pltpu.VMEM(tables["lift"].shape, jnp.bfloat16),
                pltpu.VMEM(tables["back"].shape[1:], jnp.bfloat16),
                pltpu.SemaphoreType.DMA((4,)),
            ],
            pltpu.HBM,
        )
        for step in sorted(range(1, sz.n_mode), key=lambda each: (each & -each, each), reverse=True):
            pairs = [(z, partner(z, step, sz.n_mode)) for z in range(sz.n_mode)]
            pieces[step] = lax.ppermute(pieces[step], "mode", pairs)
        weak += pieces
    width = sz.cuts * sz.share
    (spectra,) = call(
        functools.partial(transform_kernel, sz),
        [(2 * sz.planes_total, width)],
        [*weak, table["waves"]],
        [(-(-width // LANES), 2 * sz.planes_total, LANES), (2, sz.planes_total, width)],
    )
    spectra = spectra.reshape(sz.n_mode * sz.spots, sz.own, width)
    terms = lax.all_to_all(spectra, ("mode", "ex", "ey"), split_axis=0, concat_axis=0, tiled=True)
    names = ("in_y", "in_x", "pair_y", "pair_x", "out_y", "out_x", "lam_x", "lam_y")
    solved = call(
        functools.partial(smooth_kernel, sz),
        [(sz.own, sz.lane_nodes)] * sz.spots,
        [terms] + [table[name] for name in names],
        [(PARTS * sz.x_pad, LANES)] + [(PARTS * sz.x_eig, LANES)] * 3,
    )
    for step in sorted(range(1, sz.spots), key=lambda each: each // sz.n_ey == 0):
        shift, turn = step // sz.n_ey, step % sz.n_ey
        pairs = [
            (p * sz.n_ey + q, (p + shift) % sz.n_ex * sz.n_ey + (q + turn) % sz.n_ey)
            for p in range(sz.n_ex)
            for q in range(sz.n_ey)
        ]
        solved[step] = lax.ppermute(solved[step], ("ex", "ey"), pairs)
    (out,) = call(
        functools.partial(spread_kernel, sz),
        [(flat, LANES)],
        solved,
        [(sz.columns, sz.lane_nodes), (sz.lane_nodes, LANES)],
    )
    return out.reshape(sz.nodes, sz.nodes, sz.elems, sz.rows, sz.columns)


def solution(mesh):
    spec = P(None, None, "ex", "ey", "mode")

    def whole(stream_speed, normal_speed):
        shape = stream_speed.shape
        counts = mesh.shape
        block = shape[:2] + (shape[2] // counts["ex"], shape[3] // counts["ey"], shape[4] // counts["mode"])
        sz = Sizes(counts, block)
        return jax.shard_map(
            functools.partial(on_device, sz, host_tables(sz)),
            mesh=mesh,
            in_specs=(spec, spec),
            out_specs=spec,
            check_vma=False,
        )(stream_speed, normal_speed)

    return whole
```

```python
import functools
import math

import jax
import jax.numpy as jnp
import ml_dtypes
import numpy as np
from jax import lax
from jax.experimental import pallas as pl
from jax.experimental.pallas import tpu as pltpu
from jax.sharding import PartitionSpec as P

BF16 = ml_dtypes.bfloat16

element_width = 2.0
shift_base = 10.0
span_rate = 0.0125


def legendre_pair(degree, points):
    before = points * 0.0 + 1.0
    current = points.copy()
    for step in range(1, degree):
        upcoming = ((2 * step + 1) * points * current - step * before) / (step + 1)
        before = current
        current = upcoming
    return (current, before)


def legendre_slope(degree, points):
    current, before = legendre_pair(degree, points)
    return (current, degree * (points * current - before) / (points * points - 1.0))


def lobatto_points(order):
    guesses = -np.cos(np.pi * np.arange(1, order) / order)
    for step in range(60):
        current, slope = legendre_slope(order, guesses)
        second = (2.0 * guesses * slope - order * (order + 1) * current) / (1.0 - guesses * guesses)
        guesses = guesses - slope / second
    return guesses


def gauss_rule(count):
    guesses = -np.cos(np.pi * (np.arange(count) + 0.75) / (count + 0.5))
    for step in range(60):
        current, slope = legendre_slope(count, guesses)
        guesses = guesses - current / slope
    current, slope = legendre_slope(count, guesses)
    return (guesses, 2.0 / ((1.0 - guesses * guesses) * slope * slope))


def jacobi_eigen(matrix):
    size_n = matrix.shape[0]
    work = matrix.copy()
    vectors = np.eye(size_n)
    for sweep_number in range(20):
        for first in range(size_n):
            for second in range(first + 1, size_n):
                coupling = work[first, second]
                if abs(coupling) > 1e-300:
                    theta = (work[second, second] - work[first, first]) / (2.0 * coupling)
                    direction = 1.0 if theta >= 0.0 else -1.0
                    tangent = direction / (abs(theta) + np.sqrt(theta * theta + 1.0))
                    cosine = 1.0 / np.sqrt(tangent * tangent + 1.0)
                    sine = tangent * cosine
                    rotation = np.eye(size_n)
                    rotation[first, first] = cosine
                    rotation[second, second] = cosine
                    rotation[first, second] = sine
                    rotation[second, first] = -sine
                    work = rotation.T @ work @ rotation
                    vectors = vectors @ rotation
    diagonal_index = np.arange(size_n)
    return (work[diagonal_index, diagonal_index], vectors)


def extended_basis(stiffness, weights, left_width, centre_width, right_width):
    node_count = weights.shape[0]
    full_count = 3 * node_count - 2
    stiff_full = np.zeros((full_count, full_count))
    mass_full = np.zeros(full_count)
    for position, span_width in enumerate((left_width, centre_width, right_width)):
        if span_width > 0.0:
            first_node = position * (node_count - 1)
            stiff_full[
                first_node : first_node + node_count, first_node : first_node + node_count
            ] += stiffness * (2.0 / span_width)
            mass_full[first_node : first_node + node_count] += weights * (span_width / 2.0)
    low_index = node_count - 2
    high_index = low_index + node_count + 2
    stiff_ext = stiff_full[low_index:high_index, low_index:high_index].copy()
    mass_ext = mass_full[low_index:high_index].copy()
    frozen_list = []
    if left_width <= 0.0:
        frozen_list += [0, 1]
    if right_width <= 0.0:
        frozen_list += [node_count, node_count + 1]
    for frozen_index in frozen_list:
        stiff_ext[frozen_index, :] = 0.0
        stiff_ext[:, frozen_index] = 0.0
        stiff_ext[frozen_index, frozen_index] = 1.0
        mass_ext[frozen_index] = 1.0
    inverse_root = 1.0 / np.sqrt(mass_ext)
    lambdas, vectors = jacobi_eigen(inverse_root[:, None] * stiff_ext * inverse_root[None, :])
    return (inverse_root[:, None] * vectors, lambdas)


def spectral_tables(order, rows_total):
    inner_points = lobatto_points(order)
    points = np.concatenate([[-1.0], inner_points, [1.0]])
    values, unused_before = legendre_pair(order, points)
    weights = 2.0 / (order * (order + 1) * values**2)
    identity = np.eye(order + 1)
    point_gaps = points[:, None] - points[None, :] + identity
    derivative = values[:, None] / (values[None, :] * point_gaps) * (1.0 - identity)
    derivative[0, 0] = -order * (order + 1) / 4.0
    derivative[order, order] = order * (order + 1) / 4.0
    stiffness = derivative.T @ (weights[:, None] * derivative)
    gauss_points, gauss_weights = gauss_rule(3 * (order + 1) // 2)
    offsets = gauss_points[:, None, None] - points[None, None, :]
    numerators = np.prod(np.where(identity[None, :, :] > 0.5, 1.0, offsets), axis=2)
    denominators = np.prod(np.where(identity > 0.5, 1.0, points[:, None] - points[None, :]), axis=1)
    interp = numerators / denominators[None, :]
    heights = 0.6 + 1.4 * np.sin(np.pi * (np.arange(rows_total) + 0.5) / rows_total)
    basis_x, lambdas_x = extended_basis(
        stiffness, weights, element_width, element_width, element_width
    )
    basis_rows = []
    lambda_rows = []
    for row_number in range(rows_total):
        below = heights[row_number - 1] if row_number > 0 else 0.0
        above = heights[row_number + 1] if row_number < rows_total - 1 else 0.0
        basis_one, lambda_one = extended_basis(
            stiffness, weights, below, heights[row_number], above
        )
        basis_rows.append(basis_one)
        lambda_rows.append(lambda_one)
    return (
        derivative,
        interp,
        gauss_weights,
        weights,
        stiffness,
        basis_x,
        lambdas_x,
        np.stack(basis_rows),
        np.stack(lambda_rows),
        heights,
    )


PARTS = 8
LANES = 128


def ceil_to(count, step):
    return -(-count // step) * step


class Sizes:
    def __init__(self, mesh_shape, block_shape):
        self.n_mode, self.n_ex, self.n_ey = (mesh_shape[name] for name in ("mode", "ex", "ey"))
        self.nodes, _, self.elems, self.rows, self.planes = block_shape
        self.order = self.nodes - 1
        self.gauss = 3 * self.nodes // 2
        self.rows_total = self.rows * self.n_ey
        self.elems_total = self.elems * self.n_ex
        self.planes_total = self.planes * self.n_mode
        self.block_x = self.order * self.elems + 1
        full_y = self.order * self.rows + 1
        self.inner = [
            [j for j in range(full_y) if not (p == 0 and j == 0) and not (p == self.n_ey - 1 and j == full_y - 1)]
            for p in range(self.n_ey)
        ]
        self.block_y = max(len(found) for found in self.inner)
        self.cuts = 1
        self.cut_elems = self.elems // self.cuts
        self.cut_x = self.order * self.cut_elems + 1
        share = -(-self.cut_x * self.block_y // self.n_mode)
        self.sent = ceil_to(share, 8)
        self.share = ceil_to(self.sent, LANES if share > 64 else 16)
        self.cut_nodes = self.sent * self.n_mode
        self.lane_nodes = ceil_to(self.block_x * self.block_y + 2, LANES)
        self.columns = 2 * self.planes
        self.spots = self.n_ex * self.n_ey
        self.own = self.columns // self.spots
        self.folds = self.own // PARTS
        self.fold_width = LANES // self.folds
        self.points = self.nodes + 2
        self.x_cuts = self.n_ex * self.cuts * self.cut_x
        self.x_pad = ceil_to(max(self.x_cuts, self.n_ex * self.block_x), 16)
        self.x_eig = self.elems_total * self.points
        self.y_eig = self.rows_total * self.points
        self.fine = ceil_to(self.gauss * self.gauss, 16)
        assert self.own == PARTS * self.folds and self.x_eig % 16 == 0
        assert max(self.y_eig, self.n_ey * self.block_y) <= self.fold_width
        assert 2 * self.planes == LANES


def high_low(table):
    high = np.asarray(table, np.float32).astype(BF16)
    low = (np.asarray(table, np.float64) - high.astype(np.float64)).astype(BF16)
    return high, low


def beside(table):
    high, low = high_low(table)
    return np.concatenate([high, high, low], 1)


def host_tables(sz):
    derivative, interp, gauss_weights, weights, stiffness, basis_x, lam_x, basis_y, lam_y, heights = spectral_tables(
        sz.order, sz.rows_total
    )
    nodes, fine, points = sz.nodes, sz.fine, sz.points
    gauss_count = sz.gauss**2
    lift = np.zeros((3 * fine, nodes * nodes))
    lift[:gauss_count] = np.kron(interp, interp)
    lift[fine : fine + gauss_count] = np.kron(interp @ derivative, interp)
    lift[2 * fine : 2 * fine + gauss_count] = np.kron(interp, interp @ derivative)
    back = np.zeros((sz.n_ey, nodes * sz.block_y, sz.rows * fine))
    weighted = interp.T * gauss_weights[None, :]
    for place in range(sz.n_ey):
        for f in range(sz.rows):
            for jj, j in enumerate(sz.inner[place]):
                b = j - sz.order * f
                if 0 <= b < nodes:
                    back[place, jj :: sz.block_y, f * fine : f * fine + gauss_count] = -np.kron(
                        weighted, weighted[b : b + 1]
                    )
    grid_x, grid_y = sz.order * sz.elems_total, sz.order * sz.rows_total + 1
    to_x, stiff_x, mass_x = np.zeros((sz.x_eig, grid_x)), np.zeros((grid_x, grid_x)), np.zeros(grid_x)
    for e in range(sz.elems_total):
        for t in range(points):
            to_x[e * points : (e + 1) * points, (sz.order * e + t - 1) % grid_x] += basis_x[t]
        index = (sz.order * e + np.arange(nodes)) % grid_x
        stiff_x[np.ix_(index, index)] += stiffness * (2.0 / element_width)
        mass_x[index] += weights * (element_width / 2.0)
    to_y, stiff_y, mass_y = np.zeros((sz.y_eig, grid_y)), np.zeros((grid_y, grid_y)), np.zeros(grid_y)
    for f in range(sz.rows_total):
        for t in range(points):
            y = sz.order * f + t - 1
            if 0 < y < grid_y - 1:
                to_y[f * points : (f + 1) * points, y] = basis_y[f][t]
        index = sz.order * f + np.arange(nodes)
        stiff_y[np.ix_(index, index)] += stiffness * (2.0 / heights[f])
        mass_y[index] += weights * (heights[f] / 2.0)
    stiff_xx, mass_xx = to_x @ stiff_x @ to_x.T, (to_x * mass_x) @ to_x.T
    stiff_yy, mass_yy = to_y @ stiff_y @ to_y.T, (to_y * mass_y) @ to_y.T
    def block_x(blocks, elems):
        length = sz.order * elems + 1
        nodes_of = [(sz.order * elems * p + i) % grid_x for p in range(blocks) for i in range(length)]
        table = np.zeros((sz.x_eig, sz.x_pad))
        table[:, : len(nodes_of)] = to_x[:, nodes_of]
        return table

    width, folds = sz.fold_width, sz.folds
    block_y = np.zeros((width, width))
    for place in range(sz.n_ey):
        for jj, j in enumerate(sz.inner[place]):
            block_y[place * sz.block_y + jj, : sz.y_eig] = to_y[:, sz.order * sz.rows * place + j]

    def folded(table):
        padded = np.zeros((width, width))
        padded[: table.shape[0], : table.shape[1]] = table
        return np.kron(np.eye(folds), padded)

    def one_dot(table):
        high, low = high_low(folded(table))
        return np.block([[high, low], [high, np.zeros_like(low)]]).astype(BF16)

    mass_pair, stiff_pair = high_low(folded(mass_yy)), high_low(folded(stiff_yy))
    heads = np.concatenate([mass_pair[0], stiff_pair[0]], 1)
    tails = np.concatenate([mass_pair[1], stiff_pair[1]], 1)
    lam_lanes = np.ones((1, folds, width))
    lam_lanes[:, :, : sz.y_eig] = lam_y.reshape(-1)
    planes_total = sz.planes_total
    turns = np.arange(planes_total)[None, :] * np.arange(planes_total // 2)[:, None] % planes_total
    angles = turns * (2.0 * math.pi / planes_total)
    waves = np.stack([np.cos(angles), -np.sin(angles)], 1).reshape(planes_total, planes_total) / planes_total
    return dict(
        heights=np.asarray(heights, np.float32),
        lift=beside(lift),
        back=np.stack([stacked(table) for table in back]),
        waves=np.stack(high_low(waves)),
        in_y=one_dot(block_y),
        in_x=stacked(block_x(sz.n_ex * sz.cuts, sz.cut_elems)),
        pair_y=np.concatenate([heads, heads, tails], 0),
        pair_x=stacked(np.concatenate([stiff_xx, mass_xx], 1)),
        out_y=one_dot(block_y.T),
        out_x=stacked(block_x(sz.n_ex, sz.elems).T),
        lam_x=np.asarray(np.tile(lam_x, sz.elems_total)[:, None] * np.ones((1, LANES)), np.float32),
        lam_y=np.asarray(lam_lanes.reshape(1, LANES), np.float32),
    )


def stacked(table):
    return np.concatenate(high_low(table), 0)


def split(value):
    high = value.astype(jnp.bfloat16)
    low = (value - high.astype(jnp.float32)).astype(jnp.bfloat16)
    return high, low


def dot(left, right):
    return lax.dot_general(left, right, (((1,), (0,)), ((), ())), preferred_element_type=jnp.float32)


def below(value):
    high, low = split(value)
    return jnp.concatenate([high, low, high], 0)


def left_dot(table_ref, value):
    rows = table_ref.shape[0] // 2
    high, low = split(value)
    both = dot(table_ref[...], high)
    return both[:rows] + both[rows:] + dot(table_ref[:rows, :], low)


def along(value):
    return jnp.concatenate(split(value), 1)


def partner(spot, step, count):
    if count & (count - 1) == 0:
        return spot ^ step
    return (spot + step) % count


def origin(spot, step, count):
    if count & (count - 1) == 0:
        return spot ^ step
    return (spot - step + count) % count


def lane_index(shape):
    return lax.broadcasted_iota(jnp.int32, shape, len(shape) - 1)


def advect_kernel(sz, heights, stream_hbm, normal_hbm, lift_hbm, back_hbm, *others):
    out_refs, (total_ref, stream_ref, normal_ref, lift_ref, back_ref, arrived) = others[:-6], others[-6:]
    place = lax.axis_index("ey")
    fetched = [
        pltpu.make_async_copy(source, target, arrived.at[i])
        for i, (source, target) in enumerate(
            (
                (stream_hbm, stream_ref),
                (normal_hbm, normal_ref),
                (lift_hbm, lift_ref),
                (back_hbm.at[place], back_ref),
            )
        )
    ]
    for copy in fetched[:3]:
        copy.start()
    count, fine, rows = sz.nodes * sz.nodes, sz.fine, sz.rows
    spots = sz.elems * rows
    half = lane_index((fine, LANES)) < sz.planes
    column, step = sz.nodes * sz.block_y, sz.order * sz.block_y
    factors = [
        sum(jnp.where(place == q, heights[q * rows + f] * 0.5, 0.0) for q in range(sz.n_ey)) for f in range(rows)
    ]
    full = sz.cut_x * sz.block_y // 8 * 8
    total_ref[pl.ds(full, sz.cut_nodes - full), :] = jnp.zeros((sz.cut_nodes - full, LANES), jnp.float32)
    spot = lax.axis_index("mode")
    for copy in fetched[:3]:
        copy.wait()
    fetched[3].start()
    for cut in range(sz.cuts):
        high_parts, low_parts = [], []
        for e in range(cut * sz.cut_elems, (cut + 1) * sz.cut_elems):
            speeds = jnp.concatenate(
                [
                    ref[pl.ds(e * rows + f, count, stride=spots), :]
                    for f in range(rows)
                    for ref in (stream_ref, normal_ref)
                ],
                1,
            )
            values = dot(lift_ref[...], below(speeds))
            highs, lows = [], []
            for f in range(rows):
                mine = values[:, f * LANES : (f + 1) * LANES]
                both, slope_x, slope_y = mine[:fine], mine[fine : 2 * fine], mine[2 * fine :]
                turned = pltpu.roll(both, sz.planes, 1)
                stream = jnp.where(half, both, turned)
                normal = jnp.where(half, turned, both)
                high, low = split((stream * factors[f]) * slope_x + (normal * (element_width * 0.5)) * slope_y)
                highs.append(high)
                lows.append(low)
            high_parts.append(jnp.concatenate(highs, 0))
            low_parts.append(jnp.concatenate(lows, 0))
        if cut == 0:
            fetched[3].wait()
        both = dot(back_ref[...], jnp.concatenate(high_parts, 1))
        weak = both[:column] + both[column:] + dot(back_ref[:column, :], jnp.concatenate(low_parts, 1))
        carry = None
        for e in range(sz.cut_elems):
            mine = weak[:, e * LANES : (e + 1) * LANES]
            if carry is not None:
                gap = jnp.zeros((column - carry.shape[0], LANES), jnp.float32)
                mine = mine + jnp.concatenate([carry, gap], 0)
            length = step if e < sz.cut_elems - 1 else column
            total_ref[pl.ds(e * step, length), :] = mine[:length]
            carry = mine[length:]
        for turn in range(sz.n_mode):
            goal = partner(spot, turn, sz.n_mode)
            out_refs[cut * sz.n_mode + turn][...] = total_ref[pl.ds(pl.multiple_of(goal * sz.sent, 8), sz.sent), :]


def transform_kernel(sz, *refs):
    weak_refs, (waves_ref, out_ref, mixed_ref, signal_ref) = refs[: sz.n_mode], refs[-4:]
    spot = lax.axis_index("mode")
    if sz.share > sz.sent:
        signal_ref[...] = jnp.zeros(signal_ref.shape, jnp.float32)
    for step, weak_ref in enumerate(weak_refs):
        turned = weak_ref[...].T
        first = pl.multiple_of(origin(spot, step, sz.n_mode) * sz.planes, 8)
        for k in range(2):
            signal_ref[k, pl.ds(first, sz.planes), pl.ds(0, sz.sent)] = turned[k * sz.planes : (k + 1) * sz.planes]
    modes = sz.planes_total
    for k in range(2):
        high, low = split(signal_ref[k])
        part = dot(waves_ref[0], high) + dot(waves_ref[0], low) + dot(waves_ref[1], high)
        for t in range(mixed_ref.shape[0]):
            tile = part[:, t * LANES : (t + 1) * LANES]
            mixed_ref[t, pl.ds(k, modes, stride=2), pl.ds(0, tile.shape[1])] = tile
    for t in range(mixed_ref.shape[0]):
        last = min(LANES, sz.share - t * LANES)
        out_ref[:, pl.ds(t * LANES, last)] = mixed_ref[t, :, pl.ds(0, last)]


def smooth_kernel(
    sz,
    *refs,
):
    terms_refs, out_refs = refs[: sz.cuts], refs[sz.cuts + 8 : -4]
    field_ref, first_ref, work_ref, stiff_ref = refs[-4:]
    in_y_ref, in_x_ref, pair_y_ref, pair_x_ref, out_y_ref, out_x_ref, lam_x_ref, lam_y_ref = refs[
        sz.cuts : sz.cuts + 8
    ]
    width, folds, strip = sz.fold_width, sz.folds, sz.block_y
    tiles = -(-(sz.share * sz.n_mode) // LANES)
    lanes = lane_index((PARTS, LANES))
    x_pad, x_eig = sz.x_pad, sz.x_eig
    place, spot = lax.axis_index("ey"), lax.axis_index("ex")
    device = (lax.axis_index("mode") * sz.n_ex + spot) * sz.n_ey + place
    first_mode = device * (sz.own // 4)

    for c in range(PARTS):
        field_ref[pl.ds(c * x_pad + sz.x_cuts, x_pad - sz.x_cuts), :] = jnp.zeros(
            (x_pad - sz.x_cuts, LANES), jnp.float32
        )
    for p, cut in [(p, cut) for p in range(sz.n_ex) for cut in range(sz.cuts)]:
        block = (spot + p) % sz.n_ex
        held = {}
        for q in range(sz.n_ey):
            for fold in range(folds):
                whole = jnp.concatenate(
                    [
                        terms_refs[cut][(z * sz.n_ex + block) * sz.n_ey + q, pl.ds(fold * PARTS, PARTS), :]
                        for z in range(sz.n_mode)
                    ],
                    1,
                )
                held[q, fold] = [whole[:, t * LANES : (t + 1) * LANES] for t in range(tiles)]
        for i in range(sz.cut_x):
            cutting = sorted({0, strip} | {n - i * strip for n in range(0, sz.cut_nodes, sz.sent)} & set(range(strip)))
            cutting = [0] + [n for n in cutting if n > 0]
            result = jnp.zeros((PARTS, LANES), jnp.float32)
            for begin, end in zip(cutting[:-1], cutting[1:]):
                piece, row = (i * strip + begin) // sz.sent, (i * strip + begin) % sz.sent
                t, r = (piece * sz.share + row) // LANES, (piece * sz.share + row) % LANES
                for fold in range(folds):
                    for q in range(sz.n_ey):
                        source = held[q, fold][t]
                        if r + end - begin > LANES:
                            source = jnp.where(lanes >= r, source, held[q, fold][t + 1])
                        goal = fold * width + q * strip + begin
                        moved = pltpu.roll(source, (goal - r) % LANES, 1) if goal != r else source
                        result = jnp.where((lanes >= goal) & (lanes < goal + end - begin), moved, result)
            field_ref[pl.ds((p * sz.cuts + cut) * sz.cut_x + i, PARTS, stride=x_pad), :] = result

    parts = dot(along(field_ref[...]), in_y_ref[...])
    field_ref[...] = parts[:, :LANES] + parts[:, LANES:]
    fold_of_lane = lane_index((1, LANES)) // width
    shifts, inverses = [], []
    for group in range(PARTS // 4):
        mode = (first_mode + fold_of_lane * (PARTS // 4) + group).astype(jnp.float32)
        shift = shift_base + (span_rate * mode) ** 2
        shifts.append(shift)
        inverses.append(1.0 / (lam_x_ref[...] + (lam_y_ref[...] + shift)))
    for c in range(0, PARTS, 2):
        pair = jnp.concatenate([field_ref[pl.ds((c + d) * x_pad, x_pad), :] for d in range(2)], 1)
        forced = left_dot(in_x_ref, pair)
        for d in range(2):
            mine = forced[:, d * LANES : (d + 1) * LANES]
            first_ref[pl.ds((c + d) * x_eig, x_eig), :] = mine
            work_ref[pl.ds((c + d) * x_eig, x_eig), :] = mine * inverses[(c + d) // 4]
    high, low = split(work_ref[...])
    both = dot(jnp.concatenate([high, low, high], 1), pair_y_ref[...])
    work_ref[...] = both[:, :LANES]
    stiff_ref[...] = both[:, LANES:]
    for c in range(0, PARTS, 2):
        masses, stiffs = [], []
        for d in range(2):
            rows = pl.ds((c + d) * x_eig, x_eig)
            masses.append(work_ref[rows, :])
            stiffs.append(stiff_ref[rows, :] + shifts[c // 4] * masses[d])
        stacked_pair = jnp.concatenate([jnp.concatenate(masses, 1), jnp.concatenate(stiffs, 1)], 0)
        applied = left_dot(pair_x_ref, stacked_pair)
        for d in range(2):
            rows = pl.ds((c + d) * x_eig, x_eig)
            mine = applied[:, d * LANES : (d + 1) * LANES]
            first_ref[rows, :] = (2.0 * first_ref[rows, :] - mine) * inverses[c // 4]
    parts = dot(along(first_ref[...]), out_y_ref[...])
    work_ref[...] = parts[:, :LANES] + parts[:, LANES:]
    for c in range(0, PARTS, 2):
        pair = jnp.concatenate([work_ref[pl.ds((c + d) * x_eig, x_eig), :] for d in range(2)], 1)
        solved = left_dot(out_x_ref, pair)
        for d in range(2):
            field_ref[pl.ds((c + d) * x_pad, x_pad), :] = solved[:, d * LANES : (d + 1) * LANES]

    for p in range(sz.n_ex):
        made = {}
        for i in range(sz.block_x):
            source = field_ref[pl.ds(p * sz.block_x + i, PARTS, stride=x_pad), :]
            for q in range(sz.n_ey):
                begin = i * strip + sz.inner[q][0]
                count = len(sz.inner[q])
                t, r = begin // LANES, begin % LANES
                for fold in range(folds):
                    origin = fold * width + q * strip
                    moved = pltpu.roll(source, (r - origin) % LANES, 1) if origin != r else source
                    for tile, low, high in ((t, r, r + count), (t + 1, 0, r + count - LANES)):
                        if high > 0:
                            old = made.get((q, fold, tile))
                            if old is None:
                                old = jnp.zeros((PARTS, LANES), jnp.float32)
                            made[q, fold, tile] = jnp.where((lanes >= low) & (lanes < high), moved, old)
        for fold in range(folds):
            for tile in range(sz.lane_nodes // LANES):
                for turn in range(sz.n_ey):
                    chosen = jnp.zeros((PARTS, LANES), jnp.float32)
                    for q in range(sz.n_ey):
                        if (q, fold, tile) in made:
                            chosen = jnp.where((place + turn) % sz.n_ey == q, made[q, fold, tile], chosen)
                    out_refs[p * sz.n_ey + turn][pl.ds(fold * PARTS, PARTS), pl.ds(tile * LANES, LANES)] = chosen


def spread_kernel(sz, *refs):
    solved_refs, (out_ref, stacked_ref, turned_ref) = refs[:-3], refs[-3:]
    place, spot = lax.axis_index("ey"), lax.axis_index("ex")
    for step, solved_ref in enumerate(solved_refs):
        shift, turn = step // sz.n_ey, step % sz.n_ey
        source = (spot - shift + sz.n_ex) % sz.n_ex * sz.n_ey + (place - turn + sz.n_ey) % sz.n_ey
        stacked_ref[pl.ds(pl.multiple_of(source * sz.own, PARTS), sz.own), :] = solved_ref[...]
    turned_ref[...] = stacked_ref[...].T
    spots = sz.elems * sz.rows
    for e in range(sz.elems):
        for f in range(sz.rows):
            for a in range(sz.nodes):
                start = sz.block_y * (sz.order * e + a) + sz.order * f
                out_ref[pl.ds(a * sz.nodes * spots + e * sz.rows + f, sz.nodes, stride=spots), :] = turned_ref[
                    pl.ds(start, sz.nodes), :
                ]
    blank = jnp.zeros((sz.elems, LANES), jnp.float32)

    @pl.when(place == 0)
    def _():
        for a in range(sz.nodes):
            out_ref[pl.ds(a * sz.nodes * spots, sz.elems, stride=sz.rows), :] = blank

    @pl.when(place == sz.n_ey - 1)
    def _():
        for a in range(sz.nodes):
            first = ((a + 1) * sz.nodes - 1) * spots + sz.rows - 1
            out_ref[pl.ds(first, sz.elems, stride=sz.rows), :] = blank


def call(kernel, shapes, operands, scratch=(), spaces=pltpu.VMEM, limit=16, flops=10**9):
    if not isinstance(spaces, list):
        spaces = [spaces] * len(operands)
    made = pl.pallas_call(
        kernel,
        out_shape=[jax.ShapeDtypeStruct(shape, jnp.float32) for shape in shapes],
        in_specs=[pl.BlockSpec(memory_space=space) for space in spaces],
        out_specs=[pl.BlockSpec(memory_space=pltpu.VMEM) for _ in shapes],
        scratch_shapes=[pltpu.VMEM(each, jnp.float32) if isinstance(each, tuple) else each for each in scratch],
        compiler_params=pltpu.CompilerParams(vmem_limit_bytes=limit * 2**20),
        cost_estimate=pl.CostEstimate(flops=flops, bytes_accessed=10**6, transcendentals=0),
    )(*operands)
    return list(made)


def on_device(sz, tables, stream_speed, normal_speed):
    flat = sz.nodes * sz.nodes * sz.elems * sz.rows
    table = {name: jnp.asarray(value) for name, value in tables.items() if name != "heights"}
    heights = [float(height) for height in tables["heights"]]
    pieces = call(
        functools.partial(advect_kernel, sz, heights),
        [(sz.sent, LANES)] * (sz.n_mode * sz.cuts),
        [
            pltpu.with_memory_space_constraint(each, pltpu.HBM)
            for each in (
                stream_speed.reshape(flat, sz.planes),
                normal_speed.reshape(flat, sz.planes),
                table["lift"],
                table["back"],
            )
        ],
        [
            (sz.cut_nodes, LANES),
            (flat, sz.planes),
            (flat, sz.planes),
            pltpu.VMEM(tables["lift"].shape, jnp.bfloat16),
            pltpu.VMEM(tables["back"].shape[1:], jnp.bfloat16),
            pltpu.SemaphoreType.DMA((4,)),
        ],
        pltpu.HBM,
    )
    weak = [pieces[cut * sz.n_mode : (cut + 1) * sz.n_mode] for cut in range(sz.cuts)]
    for cut in range(sz.cuts):
        for step in sorted(range(1, sz.n_mode), key=lambda each: (each & -each, each), reverse=True):
            pairs = [(z, partner(z, step, sz.n_mode)) for z in range(sz.n_mode)]
            weak[cut][step] = lax.ppermute(weak[cut][step], "mode", pairs)
    terms, ahead = [], []
    for cut in range(sz.cuts):
        (spectra,) = call(
            functools.partial(transform_kernel, sz),
            [(2 * sz.planes_total, sz.share)],
            [*weak[cut], *ahead, table["waves"]],
            [(-(-sz.share // LANES), 2 * sz.planes_total, LANES), (2, sz.planes_total, sz.share)],
            [pltpu.VMEM] * sz.n_mode + [pl.ANY] * len(ahead) + [pltpu.VMEM],
            flops=10**11 if cut == sz.cuts - 1 else 10**8,
        )
        spectra = spectra.reshape(sz.n_mode * sz.spots, sz.own, sz.share)
        terms.append(lax.all_to_all(spectra, ("mode", "ex", "ey"), split_axis=0, concat_axis=0, tiled=True))
        ahead = [spectra]
    names = ("in_y", "in_x", "pair_y", "pair_x", "out_y", "out_x", "lam_x", "lam_y")
    solved = call(
        functools.partial(smooth_kernel, sz),
        [(sz.own, sz.lane_nodes)] * sz.spots,
        terms + [table[name] for name in names],
        [(PARTS * sz.x_pad, LANES)] + [(PARTS * sz.x_eig, LANES)] * 3,
    )
    for step in sorted(range(1, sz.spots), key=lambda each: each // sz.n_ey == 0):
        shift, turn = step // sz.n_ey, step % sz.n_ey
        pairs = [
            (p * sz.n_ey + q, (p + shift) % sz.n_ex * sz.n_ey + (q + turn) % sz.n_ey)
            for p in range(sz.n_ex)
            for q in range(sz.n_ey)
        ]
        solved[step] = lax.ppermute(solved[step], ("ex", "ey"), pairs)
    (out,) = call(
        functools.partial(spread_kernel, sz),
        [(flat, LANES)],
        solved,
        [(sz.columns, sz.lane_nodes), (sz.lane_nodes, LANES)],
    )
    return out.reshape(sz.nodes, sz.nodes, sz.elems, sz.rows, sz.columns)


def solution(mesh):
    spec = P(None, None, "ex", "ey", "mode")

    def whole(stream_speed, normal_speed):
        shape = stream_speed.shape
        counts = mesh.shape
        block = shape[:2] + (shape[2] // counts["ex"], shape[3] // counts["ey"], shape[4] // counts["mode"])
        sz = Sizes(counts, block)
        return jax.shard_map(
            functools.partial(on_device, sz, host_tables(sz)),
            mesh=mesh,
            in_specs=(spec, spec),
            out_specs=spec,
            check_vma=False,
        )(stream_speed, normal_speed)

    return whole
```

```python
import functools
import math

import jax
import jax.numpy as jnp
import ml_dtypes
import numpy as np
from jax import lax
from jax.experimental import pallas as pl
from jax.experimental.pallas import tpu as pltpu
from jax.sharding import PartitionSpec as P

BF16 = ml_dtypes.bfloat16

element_width = 2.0
shift_base = 10.0
span_rate = 0.0125


def legendre_pair(degree, points):
    before = points * 0.0 + 1.0
    current = points.copy()
    for step in range(1, degree):
        upcoming = ((2 * step + 1) * points * current - step * before) / (step + 1)
        before = current
        current = upcoming
    return (current, before)


def legendre_slope(degree, points):
    current, before = legendre_pair(degree, points)
    return (current, degree * (points * current - before) / (points * points - 1.0))


def lobatto_points(order):
    guesses = -np.cos(np.pi * np.arange(1, order) / order)
    for step in range(60):
        current, slope = legendre_slope(order, guesses)
        second = (2.0 * guesses * slope - order * (order + 1) * current) / (1.0 - guesses * guesses)
        guesses = guesses - slope / second
    return guesses


def gauss_rule(count):
    guesses = -np.cos(np.pi * (np.arange(count) + 0.75) / (count + 0.5))
    for step in range(60):
        current, slope = legendre_slope(count, guesses)
        guesses = guesses - current / slope
    current, slope = legendre_slope(count, guesses)
    return (guesses, 2.0 / ((1.0 - guesses * guesses) * slope * slope))


def jacobi_eigen(matrix):
    size_n = matrix.shape[0]
    work = matrix.copy()
    vectors = np.eye(size_n)
    for sweep_number in range(20):
        for first in range(size_n):
            for second in range(first + 1, size_n):
                coupling = work[first, second]
                if abs(coupling) > 1e-300:
                    theta = (work[second, second] - work[first, first]) / (2.0 * coupling)
                    direction = 1.0 if theta >= 0.0 else -1.0
                    tangent = direction / (abs(theta) + np.sqrt(theta * theta + 1.0))
                    cosine = 1.0 / np.sqrt(tangent * tangent + 1.0)
                    sine = tangent * cosine
                    rotation = np.eye(size_n)
                    rotation[first, first] = cosine
                    rotation[second, second] = cosine
                    rotation[first, second] = sine
                    rotation[second, first] = -sine
                    work = rotation.T @ work @ rotation
                    vectors = vectors @ rotation
    diagonal_index = np.arange(size_n)
    return (work[diagonal_index, diagonal_index], vectors)


def extended_basis(stiffness, weights, left_width, centre_width, right_width):
    node_count = weights.shape[0]
    full_count = 3 * node_count - 2
    stiff_full = np.zeros((full_count, full_count))
    mass_full = np.zeros(full_count)
    for position, span_width in enumerate((left_width, centre_width, right_width)):
        if span_width > 0.0:
            first_node = position * (node_count - 1)
            stiff_full[
                first_node : first_node + node_count, first_node : first_node + node_count
            ] += stiffness * (2.0 / span_width)
            mass_full[first_node : first_node + node_count] += weights * (span_width / 2.0)
    low_index = node_count - 2
    high_index = low_index + node_count + 2
    stiff_ext = stiff_full[low_index:high_index, low_index:high_index].copy()
    mass_ext = mass_full[low_index:high_index].copy()
    frozen_list = []
    if left_width <= 0.0:
        frozen_list += [0, 1]
    if right_width <= 0.0:
        frozen_list += [node_count, node_count + 1]
    for frozen_index in frozen_list:
        stiff_ext[frozen_index, :] = 0.0
        stiff_ext[:, frozen_index] = 0.0
        stiff_ext[frozen_index, frozen_index] = 1.0
        mass_ext[frozen_index] = 1.0
    inverse_root = 1.0 / np.sqrt(mass_ext)
    lambdas, vectors = jacobi_eigen(inverse_root[:, None] * stiff_ext * inverse_root[None, :])
    return (inverse_root[:, None] * vectors, lambdas)


def spectral_tables(order, rows_total):
    inner_points = lobatto_points(order)
    points = np.concatenate([[-1.0], inner_points, [1.0]])
    values, unused_before = legendre_pair(order, points)
    weights = 2.0 / (order * (order + 1) * values**2)
    identity = np.eye(order + 1)
    point_gaps = points[:, None] - points[None, :] + identity
    derivative = values[:, None] / (values[None, :] * point_gaps) * (1.0 - identity)
    derivative[0, 0] = -order * (order + 1) / 4.0
    derivative[order, order] = order * (order + 1) / 4.0
    stiffness = derivative.T @ (weights[:, None] * derivative)
    gauss_points, gauss_weights = gauss_rule(3 * (order + 1) // 2)
    offsets = gauss_points[:, None, None] - points[None, None, :]
    numerators = np.prod(np.where(identity[None, :, :] > 0.5, 1.0, offsets), axis=2)
    denominators = np.prod(np.where(identity > 0.5, 1.0, points[:, None] - points[None, :]), axis=1)
    interp = numerators / denominators[None, :]
    heights = 0.6 + 1.4 * np.sin(np.pi * (np.arange(rows_total) + 0.5) / rows_total)
    basis_x, lambdas_x = extended_basis(
        stiffness, weights, element_width, element_width, element_width
    )
    basis_rows = []
    lambda_rows = []
    for row_number in range(rows_total):
        below = heights[row_number - 1] if row_number > 0 else 0.0
        above = heights[row_number + 1] if row_number < rows_total - 1 else 0.0
        basis_one, lambda_one = extended_basis(
            stiffness, weights, below, heights[row_number], above
        )
        basis_rows.append(basis_one)
        lambda_rows.append(lambda_one)
    return (
        derivative,
        interp,
        gauss_weights,
        weights,
        stiffness,
        basis_x,
        lambdas_x,
        np.stack(basis_rows),
        np.stack(lambda_rows),
        heights,
    )


PARTS = 8
LANES = 128


def ceil_to(count, step):
    return -(-count // step) * step


class Sizes:
    def __init__(self, mesh_shape, block_shape):
        self.n_mode, self.n_ex, self.n_ey = (mesh_shape[name] for name in ("mode", "ex", "ey"))
        self.nodes, _, self.elems, self.rows, self.planes = block_shape
        self.order = self.nodes - 1
        self.gauss = 3 * self.nodes // 2
        self.rows_total = self.rows * self.n_ey
        self.elems_total = self.elems * self.n_ex
        self.planes_total = self.planes * self.n_mode
        self.block_x = self.order * self.elems + 1
        full_y = self.order * self.rows + 1
        self.inner = [
            [j for j in range(full_y) if not (p == 0 and j == 0) and not (p == self.n_ey - 1 and j == full_y - 1)]
            for p in range(self.n_ey)
        ]
        self.block_y = max(len(found) for found in self.inner)
        self.cuts = 1
        self.cut_elems = self.elems // self.cuts
        self.cut_x = self.order * self.cut_elems + 1
        share = -(-self.cut_x * self.block_y // self.n_mode)
        self.sent = ceil_to(share, 8)
        self.share = ceil_to(self.sent, LANES if share > 64 else 16)
        self.cut_nodes = self.sent * self.n_mode
        self.lane_nodes = ceil_to(self.block_x * self.block_y + 2, LANES)
        self.columns = 2 * self.planes
        self.spots = self.n_ex * self.n_ey
        self.own = self.columns // self.spots
        self.folds = self.own // PARTS
        self.fold_width = LANES // self.folds
        self.points = self.nodes + 2
        self.x_cuts = self.n_ex * self.cuts * self.cut_x
        self.x_pad = ceil_to(max(self.x_cuts, self.n_ex * self.block_x), 16)
        self.x_eig = self.elems_total * self.points
        self.y_eig = self.rows_total * self.points
        self.fine = ceil_to(self.gauss * self.gauss, 16)
        assert self.own == PARTS * self.folds and self.x_eig % 16 == 0
        assert max(self.y_eig, self.n_ey * self.block_y) <= self.fold_width
        assert 2 * self.planes == LANES


def high_low(table):
    high = np.asarray(table, np.float32).astype(BF16)
    low = (np.asarray(table, np.float64) - high.astype(np.float64)).astype(BF16)
    return high, low


def beside(table):
    high, low = high_low(table)
    return np.concatenate([high, high, low], 1)


def host_tables(sz):
    derivative, interp, gauss_weights, weights, stiffness, basis_x, lam_x, basis_y, lam_y, heights = spectral_tables(
        sz.order, sz.rows_total
    )
    nodes, fine, points = sz.nodes, sz.fine, sz.points
    gauss_count = sz.gauss**2
    lift = np.zeros((3 * fine, nodes * nodes))
    lift[:gauss_count] = np.kron(interp, interp)
    lift[fine : fine + gauss_count] = np.kron(interp @ derivative, interp)
    lift[2 * fine : 2 * fine + gauss_count] = np.kron(interp, interp @ derivative)
    back = np.zeros((sz.n_ey, nodes * sz.block_y, sz.rows * fine))
    weighted = interp.T * gauss_weights[None, :]
    for place in range(sz.n_ey):
        for f in range(sz.rows):
            for jj, j in enumerate(sz.inner[place]):
                b = j - sz.order * f
                if 0 <= b < nodes:
                    back[place, jj :: sz.block_y, f * fine : f * fine + gauss_count] = -np.kron(
                        weighted, weighted[b : b + 1]
                    )
    grid_x, grid_y = sz.order * sz.elems_total, sz.order * sz.rows_total + 1
    to_x, stiff_x, mass_x = np.zeros((sz.x_eig, grid_x)), np.zeros((grid_x, grid_x)), np.zeros(grid_x)
    for e in range(sz.elems_total):
        for t in range(points):
            to_x[e * points : (e + 1) * points, (sz.order * e + t - 1) % grid_x] += basis_x[t]
        index = (sz.order * e + np.arange(nodes)) % grid_x
        stiff_x[np.ix_(index, index)] += stiffness * (2.0 / element_width)
        mass_x[index] += weights * (element_width / 2.0)
    to_y, stiff_y, mass_y = np.zeros((sz.y_eig, grid_y)), np.zeros((grid_y, grid_y)), np.zeros(grid_y)
    for f in range(sz.rows_total):
        for t in range(points):
            y = sz.order * f + t - 1
            if 0 < y < grid_y - 1:
                to_y[f * points : (f + 1) * points, y] = basis_y[f][t]
        index = sz.order * f + np.arange(nodes)
        stiff_y[np.ix_(index, index)] += stiffness * (2.0 / heights[f])
        mass_y[index] += weights * (heights[f] / 2.0)
    stiff_xx, mass_xx = to_x @ stiff_x @ to_x.T, (to_x * mass_x) @ to_x.T
    stiff_yy, mass_yy = to_y @ stiff_y @ to_y.T, (to_y * mass_y) @ to_y.T
    def block_x(blocks, elems):
        length = sz.order * elems + 1
        nodes_of = [(sz.order * elems * p + i) % grid_x for p in range(blocks) for i in range(length)]
        table = np.zeros((sz.x_eig, sz.x_pad))
        table[:, : len(nodes_of)] = to_x[:, nodes_of]
        return table

    width, folds = sz.fold_width, sz.folds
    block_y = np.zeros((width, width))
    for place in range(sz.n_ey):
        for jj, j in enumerate(sz.inner[place]):
            block_y[place * sz.block_y + jj, : sz.y_eig] = to_y[:, sz.order * sz.rows * place + j]

    def folded(table):
        padded = np.zeros((width, width))
        padded[: table.shape[0], : table.shape[1]] = table
        return np.kron(np.eye(folds), padded)

    def one_dot(table):
        high, low = high_low(folded(table))
        return np.block([[high, low], [high, np.zeros_like(low)]]).astype(BF16)

    mass_pair, stiff_pair = high_low(folded(mass_yy)), high_low(folded(stiff_yy))
    heads = np.concatenate([mass_pair[0], stiff_pair[0]], 1)
    tails = np.concatenate([mass_pair[1], stiff_pair[1]], 1)
    lam_lanes = np.ones((1, folds, width))
    lam_lanes[:, :, : sz.y_eig] = lam_y.reshape(-1)
    planes_total = sz.planes_total
    turns = np.arange(planes_total)[None, :] * np.arange(planes_total // 2)[:, None] % planes_total
    angles = turns * (2.0 * math.pi / planes_total)
    waves = np.stack([np.cos(angles), -np.sin(angles)], 1).reshape(planes_total, planes_total) / planes_total
    return dict(
        heights=np.asarray(heights, np.float32),
        lift=beside(lift),
        back=np.stack([stacked(table) for table in back]),
        waves=np.stack(high_low(waves)),
        in_y=one_dot(block_y),
        in_x=stacked(block_x(sz.n_ex * sz.cuts, sz.cut_elems)),
        pair_y=np.concatenate([heads, heads, tails], 0),
        pair_x=stacked(np.concatenate([stiff_xx, mass_xx], 1)),
        out_y=one_dot(block_y.T),
        out_x=stacked(block_x(sz.n_ex, sz.elems).T),
        lam_x=np.asarray(np.tile(lam_x, sz.elems_total)[:, None] * np.ones((1, LANES)), np.float32),
        lam_y=np.asarray(lam_lanes.reshape(1, LANES), np.float32),
    )


def stacked(table):
    return np.concatenate(high_low(table), 0)


def split(value):
    high = value.astype(jnp.bfloat16)
    low = (value - high.astype(jnp.float32)).astype(jnp.bfloat16)
    return high, low


def dot(left, right):
    return lax.dot_general(left, right, (((1,), (0,)), ((), ())), preferred_element_type=jnp.float32)


def below(value):
    high, low = split(value)
    return jnp.concatenate([high, low, high], 0)


def left_dot(table_ref, value):
    rows = table_ref.shape[0] // 2
    high, low = split(value)
    both = dot(table_ref[...], high)
    return both[:rows] + both[rows:] + dot(table_ref[:rows, :], low)


def along(value):
    return jnp.concatenate(split(value), 1)


def partner(spot, step, count):
    if count & (count - 1) == 0:
        return spot ^ step
    return (spot + step) % count


def origin(spot, step, count):
    if count & (count - 1) == 0:
        return spot ^ step
    return (spot - step + count) % count


def lane_index(shape):
    return lax.broadcasted_iota(jnp.int32, shape, len(shape) - 1)


def advect_kernel(sz, heights, stream_hbm, normal_hbm, lift_hbm, back_hbm, *others):
    out_refs, (total_ref, stream_ref, normal_ref, lift_ref, back_ref, arrived) = others[:-6], others[-6:]
    place = lax.axis_index("ey")
    fetched = [
        pltpu.make_async_copy(source, target, arrived.at[i])
        for i, (source, target) in enumerate(
            (
                (stream_hbm, stream_ref),
                (normal_hbm, normal_ref),
                (lift_hbm, lift_ref),
                (back_hbm.at[place], back_ref),
            )
        )
    ]
    for copy in fetched:
        copy.start()
    count, fine, rows = sz.nodes * sz.nodes, sz.fine, sz.rows
    spots = sz.elems * rows
    half = lane_index((fine, LANES)) < sz.planes
    column, step = sz.nodes * sz.block_y, sz.order * sz.block_y
    factors = [
        sum(jnp.where(place == q, heights[q * rows + f] * 0.5, 0.0) for q in range(sz.n_ey)) for f in range(rows)
    ]
    full = sz.cut_x * sz.block_y // 8 * 8
    total_ref[pl.ds(full, sz.cut_nodes - full), :] = jnp.zeros((sz.cut_nodes - full, LANES), jnp.float32)
    spot = lax.axis_index("mode")
    for copy in fetched[:3]:
        copy.wait()
    for cut in range(sz.cuts):
        high_parts, low_parts = [], []
        for e in range(cut * sz.cut_elems, (cut + 1) * sz.cut_elems):
            speeds = jnp.concatenate(
                [
                    ref[pl.ds(e * rows + f, count, stride=spots), :]
                    for f in range(rows)
                    for ref in (stream_ref, normal_ref)
                ],
                1,
            )
            values = dot(lift_ref[...], below(speeds))
            highs, lows = [], []
            for f in range(rows):
                mine = values[:, f * LANES : (f + 1) * LANES]
                both, slope_x, slope_y = mine[:fine], mine[fine : 2 * fine], mine[2 * fine :]
                turned = pltpu.roll(both, sz.planes, 1)
                stream = jnp.where(half, both, turned)
                normal = jnp.where(half, turned, both)
                high, low = split((stream * factors[f]) * slope_x + (normal * (element_width * 0.5)) * slope_y)
                highs.append(high)
                lows.append(low)
            high_parts.append(jnp.concatenate(highs, 0))
            low_parts.append(jnp.concatenate(lows, 0))
        if cut == 0:
            fetched[3].wait()
        both = dot(back_ref[...], jnp.concatenate(high_parts, 1))
        weak = both[:column] + both[column:] + dot(back_ref[:column, :], jnp.concatenate(low_parts, 1))
        carry = None
        for e in range(sz.cut_elems):
            mine = weak[:, e * LANES : (e + 1) * LANES]
            if carry is not None:
                gap = jnp.zeros((column - carry.shape[0], LANES), jnp.float32)
                mine = mine + jnp.concatenate([carry, gap], 0)
            length = step if e < sz.cut_elems - 1 else column
            total_ref[pl.ds(e * step, length), :] = mine[:length]
            carry = mine[length:]
        for turn in range(sz.n_mode):
            goal = partner(spot, turn, sz.n_mode)
            out_refs[cut * sz.n_mode + turn][...] = total_ref[pl.ds(pl.multiple_of(goal * sz.sent, 8), sz.sent), :]


def transform_kernel(sz, *refs):
    weak_refs, (waves_ref, out_ref, mixed_ref, signal_ref) = refs[: sz.n_mode], refs[-4:]
    spot = lax.axis_index("mode")
    if sz.share > sz.sent:
        signal_ref[...] = jnp.zeros(signal_ref.shape, jnp.float32)
    for step, weak_ref in enumerate(weak_refs):
        turned = weak_ref[...].T
        first = pl.multiple_of(origin(spot, step, sz.n_mode) * sz.planes, 8)
        for k in range(2):
            signal_ref[k, pl.ds(first, sz.planes), pl.ds(0, sz.sent)] = turned[k * sz.planes : (k + 1) * sz.planes]
    modes = sz.planes_total
    for k in range(2):
        high, low = split(signal_ref[k])
        part = dot(waves_ref[0], high) + dot(waves_ref[0], low) + dot(waves_ref[1], high)
        for t in range(mixed_ref.shape[0]):
            tile = part[:, t * LANES : (t + 1) * LANES]
            mixed_ref[t, pl.ds(k, modes, stride=2), pl.ds(0, tile.shape[1])] = tile
    for t in range(mixed_ref.shape[0]):
        last = min(LANES, sz.share - t * LANES)
        out_ref[:, pl.ds(t * LANES, last)] = mixed_ref[t, :, pl.ds(0, last)]


def smooth_kernel(
    sz,
    *refs,
):
    terms_refs, out_refs = refs[: sz.cuts], refs[sz.cuts + 8 : -4]
    field_ref, first_ref, work_ref, stiff_ref = refs[-4:]
    in_y_ref, in_x_ref, pair_y_ref, pair_x_ref, out_y_ref, out_x_ref, lam_x_ref, lam_y_ref = refs[
        sz.cuts : sz.cuts + 8
    ]
    width, folds, strip = sz.fold_width, sz.folds, sz.block_y
    tiles = -(-(sz.share * sz.n_mode) // LANES)
    lanes = lane_index((PARTS, LANES))
    x_pad, x_eig = sz.x_pad, sz.x_eig
    place, spot = lax.axis_index("ey"), lax.axis_index("ex")
    device = (lax.axis_index("mode") * sz.n_ex + spot) * sz.n_ey + place
    first_mode = device * (sz.own // 4)

    for c in range(PARTS):
        field_ref[pl.ds(c * x_pad + sz.x_cuts, x_pad - sz.x_cuts), :] = jnp.zeros(
            (x_pad - sz.x_cuts, LANES), jnp.float32
        )
    for p, cut in [(p, cut) for p in range(sz.n_ex) for cut in range(sz.cuts)]:
        block = (spot + p) % sz.n_ex
        held = {}
        for q in range(sz.n_ey):
            for fold in range(folds):
                whole = jnp.concatenate(
                    [
                        terms_refs[cut][(z * sz.n_ex + block) * sz.n_ey + q, pl.ds(fold * PARTS, PARTS), :]
                        for z in range(sz.n_mode)
                    ],
                    1,
                )
                held[q, fold] = [whole[:, t * LANES : (t + 1) * LANES] for t in range(tiles)]
        for i in range(sz.cut_x):
            cutting = sorted({0, strip} | {n - i * strip for n in range(0, sz.cut_nodes, sz.sent)} & set(range(strip)))
            cutting = [0] + [n for n in cutting if n > 0]
            result = jnp.zeros((PARTS, LANES), jnp.float32)
            for begin, end in zip(cutting[:-1], cutting[1:]):
                piece, row = (i * strip + begin) // sz.sent, (i * strip + begin) % sz.sent
                t, r = (piece * sz.share + row) // LANES, (piece * sz.share + row) % LANES
                for fold in range(folds):
                    for q in range(sz.n_ey):
                        source = held[q, fold][t]
                        if r + end - begin > LANES:
                            source = jnp.where(lanes >= r, source, held[q, fold][t + 1])
                        goal = fold * width + q * strip + begin
                        moved = pltpu.roll(source, (goal - r) % LANES, 1) if goal != r else source
                        result = jnp.where((lanes >= goal) & (lanes < goal + end - begin), moved, result)
            field_ref[pl.ds((p * sz.cuts + cut) * sz.cut_x + i, PARTS, stride=x_pad), :] = result

    parts = dot(along(field_ref[...]), in_y_ref[...])
    field_ref[...] = parts[:, :LANES] + parts[:, LANES:]
    fold_of_lane = lane_index((1, LANES)) // width
    shifts, inverses = [], []
    for group in range(PARTS // 4):
        mode = (first_mode + fold_of_lane * (PARTS // 4) + group).astype(jnp.float32)
        shift = shift_base + (span_rate * mode) ** 2
        shifts.append(shift)
        inverses.append(1.0 / (lam_x_ref[...] + (lam_y_ref[...] + shift)))
    for c in range(0, PARTS, 2):
        pair = jnp.concatenate([field_ref[pl.ds((c + d) * x_pad, x_pad), :] for d in range(2)], 1)
        forced = left_dot(in_x_ref, pair)
        for d in range(2):
            mine = forced[:, d * LANES : (d + 1) * LANES]
            first_ref[pl.ds((c + d) * x_eig, x_eig), :] = mine
            work_ref[pl.ds((c + d) * x_eig, x_eig), :] = mine * inverses[(c + d) // 4]
    high, low = split(work_ref[...])
    both = dot(jnp.concatenate([high, low, high], 1), pair_y_ref[...])
    work_ref[...] = both[:, :LANES]
    stiff_ref[...] = both[:, LANES:]
    for c in range(0, PARTS, 2):
        masses, stiffs = [], []
        for d in range(2):
            rows = pl.ds((c + d) * x_eig, x_eig)
            masses.append(work_ref[rows, :])
            stiffs.append(stiff_ref[rows, :] + shifts[c // 4] * masses[d])
        stacked_pair = jnp.concatenate([jnp.concatenate(masses, 1), jnp.concatenate(stiffs, 1)], 0)
        applied = left_dot(pair_x_ref, stacked_pair)
        for d in range(2):
            rows = pl.ds((c + d) * x_eig, x_eig)
            mine = applied[:, d * LANES : (d + 1) * LANES]
            first_ref[rows, :] = (2.0 * first_ref[rows, :] - mine) * inverses[c // 4]
    parts = dot(along(first_ref[...]), out_y_ref[...])
    work_ref[...] = parts[:, :LANES] + parts[:, LANES:]
    for c in range(0, PARTS, 2):
        pair = jnp.concatenate([work_ref[pl.ds((c + d) * x_eig, x_eig), :] for d in range(2)], 1)
        solved = left_dot(out_x_ref, pair)
        for d in range(2):
            field_ref[pl.ds((c + d) * x_pad, x_pad), :] = solved[:, d * LANES : (d + 1) * LANES]

    for p in range(sz.n_ex):
        made = {}
        for i in range(sz.block_x):
            source = field_ref[pl.ds(p * sz.block_x + i, PARTS, stride=x_pad), :]
            for q in range(sz.n_ey):
                begin = i * strip + sz.inner[q][0]
                count = len(sz.inner[q])
                t, r = begin // LANES, begin % LANES
                for fold in range(folds):
                    origin = fold * width + q * strip
                    moved = pltpu.roll(source, (r - origin) % LANES, 1) if origin != r else source
                    for tile, low, high in ((t, r, r + count), (t + 1, 0, r + count - LANES)):
                        if high > 0:
                            old = made.get((q, fold, tile))
                            if old is None:
                                old = jnp.zeros((PARTS, LANES), jnp.float32)
                            made[q, fold, tile] = jnp.where((lanes >= low) & (lanes < high), moved, old)
        for fold in range(folds):
            for tile in range(sz.lane_nodes // LANES):
                for turn in range(sz.n_ey):
                    chosen = jnp.zeros((PARTS, LANES), jnp.float32)
                    for q in range(sz.n_ey):
                        if (q, fold, tile) in made:
                            chosen = jnp.where((place + turn) % sz.n_ey == q, made[q, fold, tile], chosen)
                    out_refs[p][pl.ds(turn * sz.own + fold * PARTS, PARTS), pl.ds(tile * LANES, LANES)] = chosen


def spread_kernel(sz, *refs):
    solved_refs, (out_ref, stacked_ref, turned_ref) = refs[:-3], refs[-3:]
    place, spot = lax.axis_index("ey"), lax.axis_index("ex")
    for step, solved_ref in enumerate(solved_refs):
        shift, turn = step // sz.n_ey, step % sz.n_ey
        source = (spot - shift + sz.n_ex) % sz.n_ex * sz.n_ey + (place - turn + sz.n_ey) % sz.n_ey
        rows = pl.ds(pl.multiple_of(source * sz.own, PARTS), sz.own)
        stacked_ref[rows, :] = solved_ref[pl.ds(turn * sz.own, sz.own), :]
    turned_ref[...] = stacked_ref[...].T
    spots = sz.elems * sz.rows
    for e in range(sz.elems):
        for f in range(sz.rows):
            for a in range(sz.nodes):
                start = sz.block_y * (sz.order * e + a) + sz.order * f
                out_ref[pl.ds(a * sz.nodes * spots + e * sz.rows + f, sz.nodes, stride=spots), :] = turned_ref[
                    pl.ds(start, sz.nodes), :
                ]
    blank = jnp.zeros((sz.elems, LANES), jnp.float32)

    @pl.when(place == 0)
    def _():
        for a in range(sz.nodes):
            out_ref[pl.ds(a * sz.nodes * spots, sz.elems, stride=sz.rows), :] = blank

    @pl.when(place == sz.n_ey - 1)
    def _():
        for a in range(sz.nodes):
            first = ((a + 1) * sz.nodes - 1) * spots + sz.rows - 1
            out_ref[pl.ds(first, sz.elems, stride=sz.rows), :] = blank


def call(kernel, shapes, operands, scratch=(), spaces=pltpu.VMEM, limit=16, flops=10**9):
    if not isinstance(spaces, list):
        spaces = [spaces] * len(operands)
    made = pl.pallas_call(
        kernel,
        out_shape=[jax.ShapeDtypeStruct(shape, jnp.float32) for shape in shapes],
        in_specs=[pl.BlockSpec(memory_space=space) for space in spaces],
        out_specs=[pl.BlockSpec(memory_space=pltpu.VMEM) for _ in shapes],
        scratch_shapes=[pltpu.VMEM(each, jnp.float32) if isinstance(each, tuple) else each for each in scratch],
        compiler_params=pltpu.CompilerParams(vmem_limit_bytes=limit * 2**20),
        cost_estimate=pl.CostEstimate(flops=flops, bytes_accessed=10**6, transcendentals=0),
    )(*operands)
    return list(made)


def on_device(sz, tables, stream_speed, normal_speed):
    flat = sz.nodes * sz.nodes * sz.elems * sz.rows
    table = {name: jnp.asarray(value) for name, value in tables.items() if name != "heights"}
    heights = [float(height) for height in tables["heights"]]
    pieces = call(
        functools.partial(advect_kernel, sz, heights),
        [(sz.sent, LANES)] * (sz.n_mode * sz.cuts),
        [
            pltpu.with_memory_space_constraint(each, pltpu.HBM)
            for each in (
                stream_speed.reshape(flat, sz.planes),
                normal_speed.reshape(flat, sz.planes),
                table["lift"],
                table["back"],
            )
        ],
        [
            (sz.cut_nodes, LANES),
            (flat, sz.planes),
            (flat, sz.planes),
            pltpu.VMEM(tables["lift"].shape, jnp.bfloat16),
            pltpu.VMEM(tables["back"].shape[1:], jnp.bfloat16),
            pltpu.SemaphoreType.DMA((4,)),
        ],
        pltpu.HBM,
    )
    weak = [pieces[cut * sz.n_mode : (cut + 1) * sz.n_mode] for cut in range(sz.cuts)]
    for cut in range(sz.cuts):
        for step in sorted(range(1, sz.n_mode), key=lambda each: (each & -each, each), reverse=True):
            pairs = [(z, partner(z, step, sz.n_mode)) for z in range(sz.n_mode)]
            weak[cut][step] = lax.ppermute(weak[cut][step], "mode", pairs)
    terms, ahead = [], []
    for cut in range(sz.cuts):
        (spectra,) = call(
            functools.partial(transform_kernel, sz),
            [(2 * sz.planes_total, sz.share)],
            [*weak[cut], *ahead, table["waves"]],
            [(-(-sz.share // LANES), 2 * sz.planes_total, LANES), (2, sz.planes_total, sz.share)],
            [pltpu.VMEM] * sz.n_mode + [pl.ANY] * len(ahead) + [pltpu.VMEM],
            flops=10**11 if cut == sz.cuts - 1 else 10**8,
        )
        spectra = spectra.reshape(sz.n_mode * sz.spots, sz.own, sz.share)
        terms.append(lax.all_to_all(spectra, ("mode", "ex", "ey"), split_axis=0, concat_axis=0, tiled=True))
        ahead = [spectra]
    names = ("in_y", "in_x", "pair_y", "pair_x", "out_y", "out_x", "lam_x", "lam_y")
    solved = call(
        functools.partial(smooth_kernel, sz),
        [(sz.n_ey * sz.own, sz.lane_nodes)] * sz.n_ex,
        terms + [table[name] for name in names],
        [(PARTS * sz.x_pad, LANES)] + [(PARTS * sz.x_eig, LANES)] * 3,
    )
    for shift in sorted(range(1, sz.n_ex), key=lambda each: (each & -each, each), reverse=True):
        pairs = [(p, (p + shift) % sz.n_ex) for p in range(sz.n_ex)]
        solved[shift] = lax.ppermute(solved[shift], "ex", pairs)
    arrived = []
    for shift in range(sz.n_ex):
        for turn in range(sz.n_ey):
            pairs = [(q, (q + turn) % sz.n_ey) for q in range(sz.n_ey)]
            arrived.append(lax.ppermute(solved[shift], "ey", pairs) if turn else solved[shift])
    (out,) = call(
        functools.partial(spread_kernel, sz),
        [(flat, LANES)],
        arrived,
        [(sz.columns, sz.lane_nodes), (sz.lane_nodes, LANES)],
    )
    return out.reshape(sz.nodes, sz.nodes, sz.elems, sz.rows, sz.columns)


def solution(mesh):
    spec = P(None, None, "ex", "ey", "mode")

    def whole(stream_speed, normal_speed):
        shape = stream_speed.shape
        counts = mesh.shape
        block = shape[:2] + (shape[2] // counts["ex"], shape[3] // counts["ey"], shape[4] // counts["mode"])
        sz = Sizes(counts, block)
        return jax.shard_map(
            functools.partial(on_device, sz, host_tables(sz)),
            mesh=mesh,
            in_specs=(spec, spec),
            out_specs=spec,
            check_vma=False,
        )(stream_speed, normal_speed)

    return whole
```

```python
import functools
import math

import jax
import jax.numpy as jnp
import ml_dtypes
import numpy as np
from jax import lax
from jax.experimental import pallas as pl
from jax.experimental.pallas import tpu as pltpu
from jax.sharding import PartitionSpec as P

BF16 = ml_dtypes.bfloat16

element_width = 2.0
shift_base = 10.0
span_rate = 0.0125


def legendre_pair(degree, points):
    before = points * 0.0 + 1.0
    current = points.copy()
    for step in range(1, degree):
        upcoming = ((2 * step + 1) * points * current - step * before) / (step + 1)
        before = current
        current = upcoming
    return (current, before)


def legendre_slope(degree, points):
    current, before = legendre_pair(degree, points)
    return (current, degree * (points * current - before) / (points * points - 1.0))


def lobatto_points(order):
    guesses = -np.cos(np.pi * np.arange(1, order) / order)
    for step in range(60):
        current, slope = legendre_slope(order, guesses)
        second = (2.0 * guesses * slope - order * (order + 1) * current) / (1.0 - guesses * guesses)
        guesses = guesses - slope / second
    return guesses


def gauss_rule(count):
    guesses = -np.cos(np.pi * (np.arange(count) + 0.75) / (count + 0.5))
    for step in range(60):
        current, slope = legendre_slope(count, guesses)
        guesses = guesses - current / slope
    current, slope = legendre_slope(count, guesses)
    return (guesses, 2.0 / ((1.0 - guesses * guesses) * slope * slope))


def jacobi_eigen(matrix):
    size_n = matrix.shape[0]
    work = matrix.copy()
    vectors = np.eye(size_n)
    for sweep_number in range(20):
        for first in range(size_n):
            for second in range(first + 1, size_n):
                coupling = work[first, second]
                if abs(coupling) > 1e-300:
                    theta = (work[second, second] - work[first, first]) / (2.0 * coupling)
                    direction = 1.0 if theta >= 0.0 else -1.0
                    tangent = direction / (abs(theta) + np.sqrt(theta * theta + 1.0))
                    cosine = 1.0 / np.sqrt(tangent * tangent + 1.0)
                    sine = tangent * cosine
                    rotation = np.eye(size_n)
                    rotation[first, first] = cosine
                    rotation[second, second] = cosine
                    rotation[first, second] = sine
                    rotation[second, first] = -sine
                    work = rotation.T @ work @ rotation
                    vectors = vectors @ rotation
    diagonal_index = np.arange(size_n)
    return (work[diagonal_index, diagonal_index], vectors)


def extended_basis(stiffness, weights, left_width, centre_width, right_width):
    node_count = weights.shape[0]
    full_count = 3 * node_count - 2
    stiff_full = np.zeros((full_count, full_count))
    mass_full = np.zeros(full_count)
    for position, span_width in enumerate((left_width, centre_width, right_width)):
        if span_width > 0.0:
            first_node = position * (node_count - 1)
            stiff_full[
                first_node : first_node + node_count, first_node : first_node + node_count
            ] += stiffness * (2.0 / span_width)
            mass_full[first_node : first_node + node_count] += weights * (span_width / 2.0)
    low_index = node_count - 2
    high_index = low_index + node_count + 2
    stiff_ext = stiff_full[low_index:high_index, low_index:high_index].copy()
    mass_ext = mass_full[low_index:high_index].copy()
    frozen_list = []
    if left_width <= 0.0:
        frozen_list += [0, 1]
    if right_width <= 0.0:
        frozen_list += [node_count, node_count + 1]
    for frozen_index in frozen_list:
        stiff_ext[frozen_index, :] = 0.0
        stiff_ext[:, frozen_index] = 0.0
        stiff_ext[frozen_index, frozen_index] = 1.0
        mass_ext[frozen_index] = 1.0
    inverse_root = 1.0 / np.sqrt(mass_ext)
    lambdas, vectors = jacobi_eigen(inverse_root[:, None] * stiff_ext * inverse_root[None, :])
    return (inverse_root[:, None] * vectors, lambdas)


def spectral_tables(order, rows_total):
    inner_points = lobatto_points(order)
    points = np.concatenate([[-1.0], inner_points, [1.0]])
    values, unused_before = legendre_pair(order, points)
    weights = 2.0 / (order * (order + 1) * values**2)
    identity = np.eye(order + 1)
    point_gaps = points[:, None] - points[None, :] + identity
    derivative = values[:, None] / (values[None, :] * point_gaps) * (1.0 - identity)
    derivative[0, 0] = -order * (order + 1) / 4.0
    derivative[order, order] = order * (order + 1) / 4.0
    stiffness = derivative.T @ (weights[:, None] * derivative)
    gauss_points, gauss_weights = gauss_rule(3 * (order + 1) // 2)
    offsets = gauss_points[:, None, None] - points[None, None, :]
    numerators = np.prod(np.where(identity[None, :, :] > 0.5, 1.0, offsets), axis=2)
    denominators = np.prod(np.where(identity > 0.5, 1.0, points[:, None] - points[None, :]), axis=1)
    interp = numerators / denominators[None, :]
    heights = 0.6 + 1.4 * np.sin(np.pi * (np.arange(rows_total) + 0.5) / rows_total)
    basis_x, lambdas_x = extended_basis(
        stiffness, weights, element_width, element_width, element_width
    )
    basis_rows = []
    lambda_rows = []
    for row_number in range(rows_total):
        below = heights[row_number - 1] if row_number > 0 else 0.0
        above = heights[row_number + 1] if row_number < rows_total - 1 else 0.0
        basis_one, lambda_one = extended_basis(
            stiffness, weights, below, heights[row_number], above
        )
        basis_rows.append(basis_one)
        lambda_rows.append(lambda_one)
    return (
        derivative,
        interp,
        gauss_weights,
        weights,
        stiffness,
        basis_x,
        lambdas_x,
        np.stack(basis_rows),
        np.stack(lambda_rows),
        heights,
    )


PARTS = 8
LANES = 128


def ceil_to(count, step):
    return -(-count // step) * step


class Sizes:
    def __init__(self, mesh_shape, block_shape):
        self.n_mode, self.n_ex, self.n_ey = (mesh_shape[name] for name in ("mode", "ex", "ey"))
        self.nodes, _, self.elems, self.rows, self.planes = block_shape
        self.order = self.nodes - 1
        self.gauss = 3 * self.nodes // 2
        self.rows_total = self.rows * self.n_ey
        self.elems_total = self.elems * self.n_ex
        self.planes_total = self.planes * self.n_mode
        self.block_x = self.order * self.elems + 1
        full_y = self.order * self.rows + 1
        self.inner = [
            [j for j in range(full_y) if not (p == 0 and j == 0) and not (p == self.n_ey - 1 and j == full_y - 1)]
            for p in range(self.n_ey)
        ]
        self.block_y = max(len(found) for found in self.inner)
        self.cuts = 1
        self.cut_elems = self.elems // self.cuts
        self.cut_x = self.order * self.cut_elems + 1
        share = -(-self.cut_x * self.block_y // self.n_mode)
        self.sent = ceil_to(share, 8)
        self.share = ceil_to(self.sent, LANES if share > 64 else 16)
        self.cut_nodes = self.sent * self.n_mode
        self.lane_nodes = ceil_to(self.block_x * self.block_y + 2, LANES)
        self.columns = 2 * self.planes
        self.spots = self.n_ex * self.n_ey
        self.own = self.columns // self.spots
        self.folds = self.own // PARTS
        self.fold_width = LANES // self.folds
        self.points = self.nodes + 2
        self.x_cuts = self.n_ex * self.cuts * self.cut_x
        self.x_pad = ceil_to(max(self.x_cuts, self.n_ex * self.block_x), 16)
        self.x_eig = self.elems_total * self.points
        self.y_eig = self.rows_total * self.points
        self.fine = ceil_to(self.gauss * self.gauss, 16)
        assert self.own == PARTS * self.folds and self.x_eig % 16 == 0
        assert max(self.y_eig, self.n_ey * self.block_y) <= self.fold_width
        assert 2 * self.planes == LANES


def high_low(table):
    high = np.asarray(table, np.float32).astype(BF16)
    low = (np.asarray(table, np.float64) - high.astype(np.float64)).astype(BF16)
    return high, low


def beside(table):
    high, low = high_low(table)
    return np.concatenate([high, high, low], 1)


def host_tables(sz):
    derivative, interp, gauss_weights, weights, stiffness, basis_x, lam_x, basis_y, lam_y, heights = spectral_tables(
        sz.order, sz.rows_total
    )
    nodes, fine, points = sz.nodes, sz.fine, sz.points
    gauss_count = sz.gauss**2
    lift = np.zeros((3 * fine, nodes * nodes))
    lift[:gauss_count] = np.kron(interp, interp)
    lift[fine : fine + gauss_count] = np.kron(interp @ derivative, interp)
    lift[2 * fine : 2 * fine + gauss_count] = np.kron(interp, interp @ derivative)
    back = np.zeros((sz.n_ey, nodes * sz.block_y, sz.rows * fine))
    weighted = interp.T * gauss_weights[None, :]
    for place in range(sz.n_ey):
        for f in range(sz.rows):
            for jj, j in enumerate(sz.inner[place]):
                b = j - sz.order * f
                if 0 <= b < nodes:
                    back[place, jj :: sz.block_y, f * fine : f * fine + gauss_count] = -np.kron(
                        weighted, weighted[b : b + 1]
                    )
    grid_x, grid_y = sz.order * sz.elems_total, sz.order * sz.rows_total + 1
    to_x, stiff_x, mass_x = np.zeros((sz.x_eig, grid_x)), np.zeros((grid_x, grid_x)), np.zeros(grid_x)
    for e in range(sz.elems_total):
        for t in range(points):
            to_x[e * points : (e + 1) * points, (sz.order * e + t - 1) % grid_x] += basis_x[t]
        index = (sz.order * e + np.arange(nodes)) % grid_x
        stiff_x[np.ix_(index, index)] += stiffness * (2.0 / element_width)
        mass_x[index] += weights * (element_width / 2.0)
    to_y, stiff_y, mass_y = np.zeros((sz.y_eig, grid_y)), np.zeros((grid_y, grid_y)), np.zeros(grid_y)
    for f in range(sz.rows_total):
        for t in range(points):
            y = sz.order * f + t - 1
            if 0 < y < grid_y - 1:
                to_y[f * points : (f + 1) * points, y] = basis_y[f][t]
        index = sz.order * f + np.arange(nodes)
        stiff_y[np.ix_(index, index)] += stiffness * (2.0 / heights[f])
        mass_y[index] += weights * (heights[f] / 2.0)
    stiff_xx, mass_xx = to_x @ stiff_x @ to_x.T, (to_x * mass_x) @ to_x.T
    stiff_yy, mass_yy = to_y @ stiff_y @ to_y.T, (to_y * mass_y) @ to_y.T
    def block_x(blocks, elems):
        length = sz.order * elems + 1
        nodes_of = [(sz.order * elems * p + i) % grid_x for p in range(blocks) for i in range(length)]
        table = np.zeros((sz.x_eig, sz.x_pad))
        table[:, : len(nodes_of)] = to_x[:, nodes_of]
        return table

    width, folds = sz.fold_width, sz.folds
    block_y = np.zeros((width, width))
    for place in range(sz.n_ey):
        for jj, j in enumerate(sz.inner[place]):
            block_y[place * sz.block_y + jj, : sz.y_eig] = to_y[:, sz.order * sz.rows * place + j]

    def folded(table):
        padded = np.zeros((width, width))
        padded[: table.shape[0], : table.shape[1]] = table
        return np.kron(np.eye(folds), padded)

    def one_dot(table):
        high, low = high_low(folded(table))
        return np.block([[high, low], [high, np.zeros_like(low)]]).astype(BF16)

    mass_pair, stiff_pair = high_low(folded(mass_yy)), high_low(folded(stiff_yy))
    heads = np.concatenate([mass_pair[0], stiff_pair[0]], 1)
    tails = np.concatenate([mass_pair[1], stiff_pair[1]], 1)
    lam_lanes = np.ones((1, folds, width))
    lam_lanes[:, :, : sz.y_eig] = lam_y.reshape(-1)
    planes_total = sz.planes_total
    turns = np.arange(planes_total)[None, :] * np.arange(planes_total // 2)[:, None] % planes_total
    angles = turns * (2.0 * math.pi / planes_total)
    waves = np.stack([np.cos(angles), -np.sin(angles)], 1).reshape(planes_total, planes_total) / planes_total
    return dict(
        heights=np.asarray(heights, np.float32),
        lift=beside(lift),
        back=np.stack([beside(table) for table in back]),
        waves=np.stack(high_low(waves)),
        in_y=one_dot(block_y),
        in_x=stacked(block_x(sz.n_ex * sz.cuts, sz.cut_elems)),
        pair_y=np.concatenate([heads, heads, tails], 0),
        pair_x=stacked(np.concatenate([stiff_xx, mass_xx], 1)),
        out_y=one_dot(block_y.T),
        out_x=stacked(block_x(sz.n_ex, sz.elems).T),
        lam_x=np.asarray(np.tile(lam_x, sz.elems_total)[:, None] * np.ones((1, LANES)), np.float32),
        lam_y=np.asarray(lam_lanes.reshape(1, LANES), np.float32),
    )


def stacked(table):
    return np.concatenate(high_low(table), 0)


def split(value):
    high = value.astype(jnp.bfloat16)
    low = (value - high.astype(jnp.float32)).astype(jnp.bfloat16)
    return high, low


def dot(left, right):
    return lax.dot_general(left, right, (((1,), (0,)), ((), ())), preferred_element_type=jnp.float32)


def below(value):
    high, low = split(value)
    return jnp.concatenate([high, low, high], 0)


def left_dot(table_ref, value):
    rows = table_ref.shape[0] // 2
    high, low = split(value)
    both = dot(table_ref[...], high)
    return both[:rows] + both[rows:] + dot(table_ref[:rows, :], low)


def along(value):
    return jnp.concatenate(split(value), 1)


def partner(spot, step, count):
    if count & (count - 1) == 0:
        return spot ^ step
    return (spot + step) % count


def origin(spot, step, count):
    if count & (count - 1) == 0:
        return spot ^ step
    return (spot - step + count) % count


def lane_index(shape):
    return lax.broadcasted_iota(jnp.int32, shape, len(shape) - 1)


def advect_kernel(sz, heights, stream_hbm, normal_hbm, lift_hbm, back_hbm, *others):
    out_refs, (total_ref, stream_ref, normal_ref, lift_ref, back_ref, arrived) = others[:-6], others[-6:]
    place = lax.axis_index("ey")
    fetched = [
        pltpu.make_async_copy(source, target, arrived.at[i])
        for i, (source, target) in enumerate(
            (
                (stream_hbm, stream_ref),
                (normal_hbm, normal_ref),
                (lift_hbm, lift_ref),
                (back_hbm.at[place], back_ref),
            )
        )
    ]
    for copy in fetched:
        copy.start()
    count, fine, rows = sz.nodes * sz.nodes, sz.fine, sz.rows
    spots = sz.elems * rows
    half = lane_index((fine, LANES)) < sz.planes
    column, step = sz.nodes * sz.block_y, sz.order * sz.block_y
    factors = [
        sum(jnp.where(place == q, heights[q * rows + f] * 0.5, 0.0) for q in range(sz.n_ey)) for f in range(rows)
    ]
    full = sz.cut_x * sz.block_y // 8 * 8
    total_ref[pl.ds(full, sz.cut_nodes - full), :] = jnp.zeros((sz.cut_nodes - full, LANES), jnp.float32)
    spot = lax.axis_index("mode")
    for copy in fetched[:3]:
        copy.wait()
    for cut in range(sz.cuts):
        products = []
        for e in range(cut * sz.cut_elems, (cut + 1) * sz.cut_elems):
            speeds = jnp.concatenate(
                [
                    ref[pl.ds(e * rows + f, count, stride=spots), :]
                    for f in range(rows)
                    for ref in (stream_ref, normal_ref)
                ],
                1,
            )
            values = dot(lift_ref[...], below(speeds))
            highs, lows = [], []
            for f in range(rows):
                mine = values[:, f * LANES : (f + 1) * LANES]
                both, slope_x, slope_y = mine[:fine], mine[fine : 2 * fine], mine[2 * fine :]
                turned = pltpu.roll(both, sz.planes, 1)
                stream = jnp.where(half, both, turned)
                normal = jnp.where(half, turned, both)
                high, low = split((stream * factors[f]) * slope_x + (normal * (element_width * 0.5)) * slope_y)
                highs.append(high)
                lows.append(low)
            products.append(jnp.concatenate(highs + lows + highs, 0))
        if cut == 0:
            fetched[3].wait()
        weak = dot(back_ref[...], jnp.concatenate(products, 1))
        carry = None
        for e in range(sz.cut_elems):
            mine = weak[:, e * LANES : (e + 1) * LANES]
            if carry is not None:
                gap = jnp.zeros((column - carry.shape[0], LANES), jnp.float32)
                mine = mine + jnp.concatenate([carry, gap], 0)
            length = step if e < sz.cut_elems - 1 else column
            total_ref[pl.ds(e * step, length), :] = mine[:length]
            carry = mine[length:]
        for turn in range(sz.n_mode):
            goal = partner(spot, turn, sz.n_mode)
            out_refs[cut * sz.n_mode + turn][...] = total_ref[pl.ds(pl.multiple_of(goal * sz.sent, 8), sz.sent), :]


def transform_kernel(sz, *refs):
    weak_refs, (waves_ref, out_ref, mixed_ref, signal_ref) = refs[: sz.n_mode], refs[-4:]
    spot = lax.axis_index("mode")
    if sz.share > sz.sent:
        signal_ref[...] = jnp.zeros(signal_ref.shape, jnp.float32)
    for step, weak_ref in enumerate(weak_refs):
        turned = weak_ref[...].T
        first = pl.multiple_of(origin(spot, step, sz.n_mode) * sz.planes, 8)
        for k in range(2):
            signal_ref[k, pl.ds(first, sz.planes), pl.ds(0, sz.sent)] = turned[k * sz.planes : (k + 1) * sz.planes]
    modes = sz.planes_total
    for k in range(2):
        high, low = split(signal_ref[k])
        part = dot(waves_ref[0], high) + dot(waves_ref[0], low) + dot(waves_ref[1], high)
        for t in range(mixed_ref.shape[0]):
            tile = part[:, t * LANES : (t + 1) * LANES]
            mixed_ref[t, pl.ds(k, modes, stride=2), pl.ds(0, tile.shape[1])] = tile
    for t in range(mixed_ref.shape[0]):
        last = min(LANES, sz.share - t * LANES)
        out_ref[:, pl.ds(t * LANES, last)] = mixed_ref[t, :, pl.ds(0, last)]


def smooth_kernel(
    sz,
    *refs,
):
    terms_refs, out_refs = refs[: sz.cuts], refs[sz.cuts + 8 : -4]
    field_ref, first_ref, work_ref, stiff_ref = refs[-4:]
    in_y_ref, in_x_ref, pair_y_ref, pair_x_ref, out_y_ref, out_x_ref, lam_x_ref, lam_y_ref = refs[
        sz.cuts : sz.cuts + 8
    ]
    width, folds, strip = sz.fold_width, sz.folds, sz.block_y
    tiles = -(-(sz.share * sz.n_mode) // LANES)
    lanes = lane_index((PARTS, LANES))
    x_pad, x_eig = sz.x_pad, sz.x_eig
    place, spot = lax.axis_index("ey"), lax.axis_index("ex")
    device = (lax.axis_index("mode") * sz.n_ex + spot) * sz.n_ey + place
    first_mode = device * (sz.own // 4)

    for c in range(PARTS):
        field_ref[pl.ds(c * x_pad + sz.x_cuts, x_pad - sz.x_cuts), :] = jnp.zeros(
            (x_pad - sz.x_cuts, LANES), jnp.float32
        )
    for p, cut in [(p, cut) for p in range(sz.n_ex) for cut in range(sz.cuts)]:
        block = (spot + p) % sz.n_ex
        held = {}
        for q in range(sz.n_ey):
            for fold in range(folds):
                whole = jnp.concatenate(
                    [
                        terms_refs[cut][(z * sz.n_ex + block) * sz.n_ey + q, pl.ds(fold * PARTS, PARTS), :]
                        for z in range(sz.n_mode)
                    ],
                    1,
                )
                held[q, fold] = [whole[:, t * LANES : (t + 1) * LANES] for t in range(tiles)]
        for i in range(sz.cut_x):
            cutting = sorted({0, strip} | {n - i * strip for n in range(0, sz.cut_nodes, sz.sent)} & set(range(strip)))
            cutting = [0] + [n for n in cutting if n > 0]
            result = jnp.zeros((PARTS, LANES), jnp.float32)
            for begin, end in zip(cutting[:-1], cutting[1:]):
                piece, row = (i * strip + begin) // sz.sent, (i * strip + begin) % sz.sent
                t, r = (piece * sz.share + row) // LANES, (piece * sz.share + row) % LANES
                for fold in range(folds):
                    for q in range(sz.n_ey):
                        source = held[q, fold][t]
                        if r + end - begin > LANES:
                            source = jnp.where(lanes >= r, source, held[q, fold][t + 1])
                        goal = fold * width + q * strip + begin
                        moved = pltpu.roll(source, (goal - r) % LANES, 1) if goal != r else source
                        result = jnp.where((lanes >= goal) & (lanes < goal + end - begin), moved, result)
            field_ref[pl.ds((p * sz.cuts + cut) * sz.cut_x + i, PARTS, stride=x_pad), :] = result

    parts = dot(along(field_ref[...]), in_y_ref[...])
    field_ref[...] = parts[:, :LANES] + parts[:, LANES:]
    fold_of_lane = lane_index((1, LANES)) // width
    shifts, inverses = [], []
    for group in range(PARTS // 4):
        mode = (first_mode + fold_of_lane * (PARTS // 4) + group).astype(jnp.float32)
        shift = shift_base + (span_rate * mode) ** 2
        shifts.append(shift)
        inverses.append(1.0 / (lam_x_ref[...] + (lam_y_ref[...] + shift)))
    for c in range(0, PARTS, 2):
        pair = jnp.concatenate([field_ref[pl.ds((c + d) * x_pad, x_pad), :] for d in range(2)], 1)
        forced = left_dot(in_x_ref, pair)
        for d in range(2):
            mine = forced[:, d * LANES : (d + 1) * LANES]
            first_ref[pl.ds((c + d) * x_eig, x_eig), :] = mine
            work_ref[pl.ds((c + d) * x_eig, x_eig), :] = mine * inverses[(c + d) // 4]
    high, low = split(work_ref[...])
    both = dot(jnp.concatenate([high, low, high], 1), pair_y_ref[...])
    work_ref[...] = both[:, :LANES]
    stiff_ref[...] = both[:, LANES:]
    for c in range(0, PARTS, 2):
        masses, stiffs = [], []
        for d in range(2):
            rows = pl.ds((c + d) * x_eig, x_eig)
            masses.append(work_ref[rows, :])
            stiffs.append(stiff_ref[rows, :] + shifts[c // 4] * masses[d])
        stacked_pair = jnp.concatenate([jnp.concatenate(masses, 1), jnp.concatenate(stiffs, 1)], 0)
        applied = left_dot(pair_x_ref, stacked_pair)
        for d in range(2):
            rows = pl.ds((c + d) * x_eig, x_eig)
            mine = applied[:, d * LANES : (d + 1) * LANES]
            first_ref[rows, :] = (2.0 * first_ref[rows, :] - mine) * inverses[c // 4]
    parts = dot(along(first_ref[...]), out_y_ref[...])
    work_ref[...] = parts[:, :LANES] + parts[:, LANES:]
    for c in range(0, PARTS, 2):
        pair = jnp.concatenate([work_ref[pl.ds((c + d) * x_eig, x_eig), :] for d in range(2)], 1)
        solved = left_dot(out_x_ref, pair)
        for d in range(2):
            field_ref[pl.ds((c + d) * x_pad, x_pad), :] = solved[:, d * LANES : (d + 1) * LANES]

    for p in range(sz.n_ex):
        made = {}
        for i in range(sz.block_x):
            source = field_ref[pl.ds(p * sz.block_x + i, PARTS, stride=x_pad), :]
            for q in range(sz.n_ey):
                begin = i * strip + sz.inner[q][0]
                count = len(sz.inner[q])
                t, r = begin // LANES, begin % LANES
                for fold in range(folds):
                    origin = fold * width + q * strip
                    moved = pltpu.roll(source, (r - origin) % LANES, 1) if origin != r else source
                    for tile, low, high in ((t, r, r + count), (t + 1, 0, r + count - LANES)):
                        if high > 0:
                            old = made.get((q, fold, tile))
                            if old is None:
                                old = jnp.zeros((PARTS, LANES), jnp.float32)
                            made[q, fold, tile] = jnp.where((lanes >= low) & (lanes < high), moved, old)
        for fold in range(folds):
            for tile in range(sz.lane_nodes // LANES):
                for turn in range(sz.n_ey):
                    chosen = jnp.zeros((PARTS, LANES), jnp.float32)
                    for q in range(sz.n_ey):
                        if (q, fold, tile) in made:
                            chosen = jnp.where((place + turn) % sz.n_ey == q, made[q, fold, tile], chosen)
                    out_refs[p * sz.n_ey + turn][pl.ds(fold * PARTS, PARTS), pl.ds(tile * LANES, LANES)] = chosen


def spread_kernel(sz, *refs):
    solved_refs, (out_ref, stacked_ref, turned_ref) = refs[:-3], refs[-3:]
    place, spot = lax.axis_index("ey"), lax.axis_index("ex")
    for step, solved_ref in enumerate(solved_refs):
        shift, turn = step // sz.n_ey, step % sz.n_ey
        source = (spot - shift + sz.n_ex) % sz.n_ex * sz.n_ey + (place - turn + sz.n_ey) % sz.n_ey
        stacked_ref[pl.ds(pl.multiple_of(source * sz.own, PARTS), sz.own), :] = solved_ref[...]
    turned_ref[...] = stacked_ref[...].T
    spots = sz.elems * sz.rows
    for e in range(sz.elems):
        for f in range(sz.rows):
            for a in range(sz.nodes):
                start = sz.block_y * (sz.order * e + a) + sz.order * f
                out_ref[pl.ds(a * sz.nodes * spots + e * sz.rows + f, sz.nodes, stride=spots), :] = turned_ref[
                    pl.ds(start, sz.nodes), :
                ]
    blank = jnp.zeros((sz.elems, LANES), jnp.float32)

    @pl.when(place == 0)
    def _():
        for a in range(sz.nodes):
            out_ref[pl.ds(a * sz.nodes * spots, sz.elems, stride=sz.rows), :] = blank

    @pl.when(place == sz.n_ey - 1)
    def _():
        for a in range(sz.nodes):
            first = ((a + 1) * sz.nodes - 1) * spots + sz.rows - 1
            out_ref[pl.ds(first, sz.elems, stride=sz.rows), :] = blank


def call(kernel, shapes, operands, scratch=(), spaces=pltpu.VMEM, limit=16, flops=10**9):
    if not isinstance(spaces, list):
        spaces = [spaces] * len(operands)
    made = pl.pallas_call(
        kernel,
        out_shape=[jax.ShapeDtypeStruct(shape, jnp.float32) for shape in shapes],
        in_specs=[pl.BlockSpec(memory_space=space) for space in spaces],
        out_specs=[pl.BlockSpec(memory_space=pltpu.VMEM) for _ in shapes],
        scratch_shapes=[pltpu.VMEM(each, jnp.float32) if isinstance(each, tuple) else each for each in scratch],
        compiler_params=pltpu.CompilerParams(vmem_limit_bytes=limit * 2**20),
        cost_estimate=pl.CostEstimate(flops=flops, bytes_accessed=10**6, transcendentals=0),
    )(*operands)
    return list(made)


def on_device(sz, tables, stream_speed, normal_speed):
    flat = sz.nodes * sz.nodes * sz.elems * sz.rows
    table = {name: jnp.asarray(value) for name, value in tables.items() if name != "heights"}
    heights = [float(height) for height in tables["heights"]]
    pieces = call(
        functools.partial(advect_kernel, sz, heights),
        [(sz.sent, LANES)] * (sz.n_mode * sz.cuts),
        [
            pltpu.with_memory_space_constraint(each, pltpu.HBM)
            for each in (
                stream_speed.reshape(flat, sz.planes),
                normal_speed.reshape(flat, sz.planes),
                table["lift"],
                table["back"],
            )
        ],
        [
            (sz.cut_nodes, LANES),
            (flat, sz.planes),
            (flat, sz.planes),
            pltpu.VMEM(tables["lift"].shape, jnp.bfloat16),
            pltpu.VMEM(tables["back"].shape[1:], jnp.bfloat16),
            pltpu.SemaphoreType.DMA((4,)),
        ],
        pltpu.HBM,
    )
    weak = [pieces[cut * sz.n_mode : (cut + 1) * sz.n_mode] for cut in range(sz.cuts)]
    for cut in range(sz.cuts):
        for step in range(sz.n_mode - 1, 0, -1):
            pairs = [(z, partner(z, step, sz.n_mode)) for z in range(sz.n_mode)]
            weak[cut][step] = lax.ppermute(weak[cut][step], "mode", pairs)
    terms, ahead = [], []
    for cut in range(sz.cuts):
        (spectra,) = call(
            functools.partial(transform_kernel, sz),
            [(2 * sz.planes_total, sz.share)],
            [*weak[cut], *ahead, table["waves"]],
            [(-(-sz.share // LANES), 2 * sz.planes_total, LANES), (2, sz.planes_total, sz.share)],
            [pltpu.VMEM] * sz.n_mode + [pl.ANY] * len(ahead) + [pltpu.VMEM],
            flops=10**11 if cut == sz.cuts - 1 else 10**8,
        )
        spectra = spectra.reshape(sz.n_mode * sz.spots, sz.own, sz.share)
        terms.append(lax.all_to_all(spectra, ("mode", "ex", "ey"), split_axis=0, concat_axis=0, tiled=True))
        ahead = [spectra]
    names = ("in_y", "in_x", "pair_y", "pair_x", "out_y", "out_x", "lam_x", "lam_y")
    solved = call(
        functools.partial(smooth_kernel, sz),
        [(sz.own, sz.lane_nodes)] * sz.spots,
        terms + [table[name] for name in names],
        [(PARTS * sz.x_pad, LANES)] + [(PARTS * sz.x_eig, LANES)] * 3,
    )
    for step in sorted(range(1, sz.spots), key=lambda each: each // sz.n_ey == 0):
        shift, turn = step // sz.n_ey, step % sz.n_ey
        pairs = [
            (p * sz.n_ey + q, (p + shift) % sz.n_ex * sz.n_ey + (q + turn) % sz.n_ey)
            for p in range(sz.n_ex)
            for q in range(sz.n_ey)
        ]
        solved[step] = lax.ppermute(solved[step], ("ex", "ey"), pairs)
    (out,) = call(
        functools.partial(spread_kernel, sz),
        [(flat, LANES)],
        solved,
        [(sz.columns, sz.lane_nodes), (sz.lane_nodes, LANES)],
    )
    return out.reshape(sz.nodes, sz.nodes, sz.elems, sz.rows, sz.columns)


def solution(mesh):
    spec = P(None, None, "ex", "ey", "mode")

    def whole(stream_speed, normal_speed):
        shape = stream_speed.shape
        counts = mesh.shape
        block = shape[:2] + (shape[2] // counts["ex"], shape[3] // counts["ey"], shape[4] // counts["mode"])
        sz = Sizes(counts, block)
        return jax.shard_map(
            functools.partial(on_device, sz, host_tables(sz)),
            mesh=mesh,
            in_specs=(spec, spec),
            out_specs=spec,
            check_vma=False,
        )(stream_speed, normal_speed)

    return whole
```

```python
import functools
import math

import jax
import jax.numpy as jnp
import ml_dtypes
import numpy as np
from jax import lax
from jax.experimental import pallas as pl
from jax.experimental.pallas import tpu as pltpu
from jax.sharding import PartitionSpec as P

BF16 = ml_dtypes.bfloat16

element_width = 2.0
shift_base = 10.0
span_rate = 0.0125


def legendre_pair(degree, points):
    before = points * 0.0 + 1.0
    current = points.copy()
    for step in range(1, degree):
        upcoming = ((2 * step + 1) * points * current - step * before) / (step + 1)
        before = current
        current = upcoming
    return (current, before)


def legendre_slope(degree, points):
    current, before = legendre_pair(degree, points)
    return (current, degree * (points * current - before) / (points * points - 1.0))


def lobatto_points(order):
    guesses = -np.cos(np.pi * np.arange(1, order) / order)
    for step in range(60):
        current, slope = legendre_slope(order, guesses)
        second = (2.0 * guesses * slope - order * (order + 1) * current) / (1.0 - guesses * guesses)
        guesses = guesses - slope / second
    return guesses


def gauss_rule(count):
    guesses = -np.cos(np.pi * (np.arange(count) + 0.75) / (count + 0.5))
    for step in range(60):
        current, slope = legendre_slope(count, guesses)
        guesses = guesses - current / slope
    current, slope = legendre_slope(count, guesses)
    return (guesses, 2.0 / ((1.0 - guesses * guesses) * slope * slope))


def jacobi_eigen(matrix):
    size_n = matrix.shape[0]
    work = matrix.copy()
    vectors = np.eye(size_n)
    for sweep_number in range(20):
        for first in range(size_n):
            for second in range(first + 1, size_n):
                coupling = work[first, second]
                if abs(coupling) > 1e-300:
                    theta = (work[second, second] - work[first, first]) / (2.0 * coupling)
                    direction = 1.0 if theta >= 0.0 else -1.0
                    tangent = direction / (abs(theta) + np.sqrt(theta * theta + 1.0))
                    cosine = 1.0 / np.sqrt(tangent * tangent + 1.0)
                    sine = tangent * cosine
                    rotation = np.eye(size_n)
                    rotation[first, first] = cosine
                    rotation[second, second] = cosine
                    rotation[first, second] = sine
                    rotation[second, first] = -sine
                    work = rotation.T @ work @ rotation
                    vectors = vectors @ rotation
    diagonal_index = np.arange(size_n)
    return (work[diagonal_index, diagonal_index], vectors)


def extended_basis(stiffness, weights, left_width, centre_width, right_width):
    node_count = weights.shape[0]
    full_count = 3 * node_count - 2
    stiff_full = np.zeros((full_count, full_count))
    mass_full = np.zeros(full_count)
    for position, span_width in enumerate((left_width, centre_width, right_width)):
        if span_width > 0.0:
            first_node = position * (node_count - 1)
            stiff_full[
                first_node : first_node + node_count, first_node : first_node + node_count
            ] += stiffness * (2.0 / span_width)
            mass_full[first_node : first_node + node_count] += weights * (span_width / 2.0)
    low_index = node_count - 2
    high_index = low_index + node_count + 2
    stiff_ext = stiff_full[low_index:high_index, low_index:high_index].copy()
    mass_ext = mass_full[low_index:high_index].copy()
    frozen_list = []
    if left_width <= 0.0:
        frozen_list += [0, 1]
    if right_width <= 0.0:
        frozen_list += [node_count, node_count + 1]
    for frozen_index in frozen_list:
        stiff_ext[frozen_index, :] = 0.0
        stiff_ext[:, frozen_index] = 0.0
        stiff_ext[frozen_index, frozen_index] = 1.0
        mass_ext[frozen_index] = 1.0
    inverse_root = 1.0 / np.sqrt(mass_ext)
    lambdas, vectors = jacobi_eigen(inverse_root[:, None] * stiff_ext * inverse_root[None, :])
    return (inverse_root[:, None] * vectors, lambdas)


def spectral_tables(order, rows_total):
    inner_points = lobatto_points(order)
    points = np.concatenate([[-1.0], inner_points, [1.0]])
    values, unused_before = legendre_pair(order, points)
    weights = 2.0 / (order * (order + 1) * values**2)
    identity = np.eye(order + 1)
    point_gaps = points[:, None] - points[None, :] + identity
    derivative = values[:, None] / (values[None, :] * point_gaps) * (1.0 - identity)
    derivative[0, 0] = -order * (order + 1) / 4.0
    derivative[order, order] = order * (order + 1) / 4.0
    stiffness = derivative.T @ (weights[:, None] * derivative)
    gauss_points, gauss_weights = gauss_rule(3 * (order + 1) // 2)
    offsets = gauss_points[:, None, None] - points[None, None, :]
    numerators = np.prod(np.where(identity[None, :, :] > 0.5, 1.0, offsets), axis=2)
    denominators = np.prod(np.where(identity > 0.5, 1.0, points[:, None] - points[None, :]), axis=1)
    interp = numerators / denominators[None, :]
    heights = 0.6 + 1.4 * np.sin(np.pi * (np.arange(rows_total) + 0.5) / rows_total)
    basis_x, lambdas_x = extended_basis(
        stiffness, weights, element_width, element_width, element_width
    )
    basis_rows = []
    lambda_rows = []
    for row_number in range(rows_total):
        below = heights[row_number - 1] if row_number > 0 else 0.0
        above = heights[row_number + 1] if row_number < rows_total - 1 else 0.0
        basis_one, lambda_one = extended_basis(
            stiffness, weights, below, heights[row_number], above
        )
        basis_rows.append(basis_one)
        lambda_rows.append(lambda_one)
    return (
        derivative,
        interp,
        gauss_weights,
        weights,
        stiffness,
        basis_x,
        lambdas_x,
        np.stack(basis_rows),
        np.stack(lambda_rows),
        heights,
    )


PARTS = 8
LANES = 128


def ceil_to(count, step):
    return -(-count // step) * step


class Sizes:
    def __init__(self, mesh_shape, block_shape):
        self.n_mode, self.n_ex, self.n_ey = (mesh_shape[name] for name in ("mode", "ex", "ey"))
        self.nodes, _, self.elems, self.rows, self.planes = block_shape
        self.order = self.nodes - 1
        self.gauss = 3 * self.nodes // 2
        self.rows_total = self.rows * self.n_ey
        self.elems_total = self.elems * self.n_ex
        self.planes_total = self.planes * self.n_mode
        self.block_x = self.order * self.elems + 1
        full_y = self.order * self.rows + 1
        self.inner = [
            [j for j in range(full_y) if not (p == 0 and j == 0) and not (p == self.n_ey - 1 and j == full_y - 1)]
            for p in range(self.n_ey)
        ]
        self.block_y = max(len(found) for found in self.inner)
        self.cuts = 1
        self.cut_elems = self.elems // self.cuts
        self.cut_x = self.order * self.cut_elems + 1
        share = -(-self.cut_x * self.block_y // self.n_mode)
        self.sent = ceil_to(share, 8)
        self.share = ceil_to(self.sent, LANES if share > 64 else 16)
        self.cut_nodes = self.sent * self.n_mode
        self.lane_nodes = ceil_to(self.block_x * self.block_y + 2, LANES)
        self.columns = 2 * self.planes
        self.spots = self.n_ex * self.n_ey
        self.own = self.columns // self.spots
        self.folds = self.own // PARTS
        self.fold_width = LANES // self.folds
        self.points = self.nodes + 2
        self.x_cuts = self.n_ex * self.cuts * self.cut_x
        self.x_pad = ceil_to(max(self.x_cuts, self.n_ex * self.block_x), 16)
        self.x_eig = self.elems_total * self.points
        self.y_eig = self.rows_total * self.points
        self.fine = ceil_to(self.gauss * self.gauss, 16)
        assert self.own == PARTS * self.folds and self.x_eig % 16 == 0
        assert max(self.y_eig, self.n_ey * self.block_y) <= self.fold_width
        assert 2 * self.planes == LANES


def high_low(table):
    high = np.asarray(table, np.float32).astype(BF16)
    low = (np.asarray(table, np.float64) - high.astype(np.float64)).astype(BF16)
    return high, low


def beside(table):
    high, low = high_low(table)
    return np.concatenate([high, high, low], 1)


def host_tables(sz):
    derivative, interp, gauss_weights, weights, stiffness, basis_x, lam_x, basis_y, lam_y, heights = spectral_tables(
        sz.order, sz.rows_total
    )
    nodes, fine, points = sz.nodes, sz.fine, sz.points
    gauss_count = sz.gauss**2
    lift = np.zeros((3 * fine, nodes * nodes))
    lift[:gauss_count] = np.kron(interp, interp)
    lift[fine : fine + gauss_count] = np.kron(interp @ derivative, interp)
    lift[2 * fine : 2 * fine + gauss_count] = np.kron(interp, interp @ derivative)
    back = np.zeros((sz.n_ey, nodes * sz.block_y, sz.rows * fine))
    weighted = interp.T * gauss_weights[None, :]
    for place in range(sz.n_ey):
        for f in range(sz.rows):
            for jj, j in enumerate(sz.inner[place]):
                b = j - sz.order * f
                if 0 <= b < nodes:
                    back[place, jj :: sz.block_y, f * fine : f * fine + gauss_count] = -np.kron(
                        weighted, weighted[b : b + 1]
                    )
    grid_x, grid_y = sz.order * sz.elems_total, sz.order * sz.rows_total + 1
    to_x, stiff_x, mass_x = np.zeros((sz.x_eig, grid_x)), np.zeros((grid_x, grid_x)), np.zeros(grid_x)
    for e in range(sz.elems_total):
        for t in range(points):
            to_x[e * points : (e + 1) * points, (sz.order * e + t - 1) % grid_x] += basis_x[t]
        index = (sz.order * e + np.arange(nodes)) % grid_x
        stiff_x[np.ix_(index, index)] += stiffness * (2.0 / element_width)
        mass_x[index] += weights * (element_width / 2.0)
    to_y, stiff_y, mass_y = np.zeros((sz.y_eig, grid_y)), np.zeros((grid_y, grid_y)), np.zeros(grid_y)
    for f in range(sz.rows_total):
        for t in range(points):
            y = sz.order * f + t - 1
            if 0 < y < grid_y - 1:
                to_y[f * points : (f + 1) * points, y] = basis_y[f][t]
        index = sz.order * f + np.arange(nodes)
        stiff_y[np.ix_(index, index)] += stiffness * (2.0 / heights[f])
        mass_y[index] += weights * (heights[f] / 2.0)
    stiff_xx, mass_xx = to_x @ stiff_x @ to_x.T, (to_x * mass_x) @ to_x.T
    stiff_yy, mass_yy = to_y @ stiff_y @ to_y.T, (to_y * mass_y) @ to_y.T
    def block_x(blocks, elems):
        length = sz.order * elems + 1
        nodes_of = [(sz.order * elems * p + i) % grid_x for p in range(blocks) for i in range(length)]
        table = np.zeros((sz.x_eig, sz.x_pad))
        table[:, : len(nodes_of)] = to_x[:, nodes_of]
        return table

    width, folds = sz.fold_width, sz.folds
    block_y = np.zeros((width, width))
    for place in range(sz.n_ey):
        for jj, j in enumerate(sz.inner[place]):
            block_y[place * sz.block_y + jj, : sz.y_eig] = to_y[:, sz.order * sz.rows * place + j]

    def folded(table):
        padded = np.zeros((width, width))
        padded[: table.shape[0], : table.shape[1]] = table
        return np.kron(np.eye(folds), padded)

    def one_dot(table):
        high, low = high_low(folded(table))
        return np.block([[high, low], [high, np.zeros_like(low)]]).astype(BF16)

    mass_pair, stiff_pair = high_low(folded(mass_yy)), high_low(folded(stiff_yy))
    heads = np.concatenate([mass_pair[0], stiff_pair[0]], 1)
    tails = np.concatenate([mass_pair[1], stiff_pair[1]], 1)
    lam_lanes = np.ones((1, folds, width))
    lam_lanes[:, :, : sz.y_eig] = lam_y.reshape(-1)
    planes_total = sz.planes_total
    turns = np.arange(planes_total)[None, :] * np.arange(planes_total // 2)[:, None] % planes_total
    angles = turns * (2.0 * math.pi / planes_total)
    waves = np.stack([np.cos(angles), -np.sin(angles)], 1).reshape(planes_total, planes_total) / planes_total
    return dict(
        heights=np.asarray(heights, np.float32),
        lift=beside(lift),
        back=np.stack([beside(table) for table in back]),
        waves=np.stack(high_low(waves)),
        in_y=one_dot(block_y),
        in_x=stacked(block_x(sz.n_ex * sz.cuts, sz.cut_elems)),
        pair_y=np.concatenate([heads, heads, tails], 0),
        pair_x=stacked(np.concatenate([stiff_xx, mass_xx], 1)),
        out_y=one_dot(block_y.T),
        out_x=stacked(block_x(sz.n_ex, sz.elems).T),
        lam_x=np.asarray(np.tile(lam_x, sz.elems_total)[:, None] * np.ones((1, LANES)), np.float32),
        lam_y=np.asarray(lam_lanes.reshape(1, LANES), np.float32),
    )


def stacked(table):
    return np.concatenate(high_low(table), 0)


def split(value):
    high = value.astype(jnp.bfloat16)
    low = (value - high.astype(jnp.float32)).astype(jnp.bfloat16)
    return high, low


def dot(left, right):
    return lax.dot_general(left, right, (((1,), (0,)), ((), ())), preferred_element_type=jnp.float32)


def below(value):
    high, low = split(value)
    return jnp.concatenate([high, low, high], 0)


def left_dot(table_ref, value):
    rows = table_ref.shape[0] // 2
    high, low = split(value)
    both = dot(table_ref[...], high)
    return both[:rows] + both[rows:] + dot(table_ref[:rows, :], low)


def along(value):
    return jnp.concatenate(split(value), 1)


def partner(spot, step, count):
    if count & (count - 1) == 0:
        return spot ^ step
    return (spot + step) % count


def origin(spot, step, count):
    if count & (count - 1) == 0:
        return spot ^ step
    return (spot - step + count) % count


def lane_index(shape):
    return lax.broadcasted_iota(jnp.int32, shape, len(shape) - 1)


def advect_kernel(sz, heights, stream_hbm, normal_hbm, lift_hbm, back_hbm, *others):
    out_refs, (total_ref, stream_ref, normal_ref, lift_ref, back_ref, arrived) = others[:-6], others[-6:]
    place = lax.axis_index("ey")
    fetched = [
        pltpu.make_async_copy(source, target, arrived.at[i])
        for i, (source, target) in enumerate(
            (
                (stream_hbm, stream_ref),
                (normal_hbm, normal_ref),
                *(
                    (lift_hbm.at[pl.ds(part * sz.fine, sz.fine)], lift_ref.at[pl.ds(part * sz.fine, sz.fine)])
                    for part in range(3)
                ),
                (back_hbm.at[place], back_ref),
            )
        )
    ]
    for copy in fetched:
        copy.start()
    count, fine, rows = sz.nodes * sz.nodes, sz.fine, sz.rows
    spots = sz.elems * rows
    half = lane_index((fine, LANES)) < sz.planes
    column, step = sz.nodes * sz.block_y, sz.order * sz.block_y
    factors = [
        sum(jnp.where(place == q, heights[q * rows + f] * 0.5, 0.0) for q in range(sz.n_ey)) for f in range(rows)
    ]
    full = sz.cut_x * sz.block_y // 8 * 8
    total_ref[pl.ds(full, sz.cut_nodes - full), :] = jnp.zeros((sz.cut_nodes - full, LANES), jnp.float32)
    spot = lax.axis_index("mode")
    for copy in fetched[:2]:
        copy.wait()
    waiting = fetched[2:5]
    for cut in range(sz.cuts):
        products = []
        for e in range(cut * sz.cut_elems, (cut + 1) * sz.cut_elems):
            speeds = jnp.concatenate(
                [
                    ref[pl.ds(e * rows + f, count, stride=spots), :]
                    for f in range(rows)
                    for ref in (stream_ref, normal_ref)
                ],
                1,
            )
            spread = below(speeds)
            values = []
            for part in range(3):
                if waiting:
                    waiting.pop(0).wait()
                values.append(dot(lift_ref[pl.ds(part * fine, fine), :], spread))
            highs, lows = [], []
            for f in range(rows):
                both, slope_x, slope_y = (part[:, f * LANES : (f + 1) * LANES] for part in values)
                turned = pltpu.roll(both, sz.planes, 1)
                stream = jnp.where(half, both, turned)
                normal = jnp.where(half, turned, both)
                high, low = split((stream * factors[f]) * slope_x + (normal * (element_width * 0.5)) * slope_y)
                highs.append(high)
                lows.append(low)
            products.append(jnp.concatenate(highs + lows + highs, 0))
        if cut == 0:
            fetched[5].wait()
        weak = dot(back_ref[...], jnp.concatenate(products, 1))
        carry = None
        for e in range(sz.cut_elems):
            mine = weak[:, e * LANES : (e + 1) * LANES]
            if carry is not None:
                gap = jnp.zeros((column - carry.shape[0], LANES), jnp.float32)
                mine = mine + jnp.concatenate([carry, gap], 0)
            length = step if e < sz.cut_elems - 1 else column
            total_ref[pl.ds(e * step, length), :] = mine[:length]
            carry = mine[length:]
        for turn in range(sz.n_mode):
            goal = partner(spot, turn, sz.n_mode)
            out_refs[cut * sz.n_mode + turn][...] = total_ref[pl.ds(pl.multiple_of(goal * sz.sent, 8), sz.sent), :]


def transform_kernel(sz, *refs):
    weak_refs, (waves_ref, out_ref, mixed_ref, signal_ref) = refs[: sz.n_mode], refs[-4:]
    spot = lax.axis_index("mode")
    if sz.share > sz.sent:
        signal_ref[...] = jnp.zeros(signal_ref.shape, jnp.float32)
    for step, weak_ref in enumerate(weak_refs):
        turned = weak_ref[...].T
        first = pl.multiple_of(origin(spot, step, sz.n_mode) * sz.planes, 8)
        for k in range(2):
            signal_ref[k, pl.ds(first, sz.planes), pl.ds(0, sz.sent)] = turned[k * sz.planes : (k + 1) * sz.planes]
    modes = sz.planes_total
    for k in range(2):
        high, low = split(signal_ref[k])
        part = dot(waves_ref[0], high) + dot(waves_ref[0], low) + dot(waves_ref[1], high)
        for t in range(mixed_ref.shape[0]):
            tile = part[:, t * LANES : (t + 1) * LANES]
            mixed_ref[t, pl.ds(k, modes, stride=2), pl.ds(0, tile.shape[1])] = tile
    for t in range(mixed_ref.shape[0]):
        last = min(LANES, sz.share - t * LANES)
        out_ref[:, pl.ds(t * LANES, last)] = mixed_ref[t, :, pl.ds(0, last)]


def smooth_kernel(
    sz,
    *refs,
):
    terms_refs, out_refs = refs[: sz.cuts], refs[sz.cuts + 8 : -4]
    field_ref, first_ref, work_ref, stiff_ref = refs[-4:]
    in_y_ref, in_x_ref, pair_y_ref, pair_x_ref, out_y_ref, out_x_ref, lam_x_ref, lam_y_ref = refs[
        sz.cuts : sz.cuts + 8
    ]
    width, folds, strip = sz.fold_width, sz.folds, sz.block_y
    tiles = -(-(sz.share * sz.n_mode) // LANES)
    lanes = lane_index((PARTS, LANES))
    x_pad, x_eig = sz.x_pad, sz.x_eig
    place, spot = lax.axis_index("ey"), lax.axis_index("ex")
    device = (lax.axis_index("mode") * sz.n_ex + spot) * sz.n_ey + place
    first_mode = device * (sz.own // 4)

    for c in range(PARTS):
        field_ref[pl.ds(c * x_pad + sz.x_cuts, x_pad - sz.x_cuts), :] = jnp.zeros(
            (x_pad - sz.x_cuts, LANES), jnp.float32
        )
    for p, cut in [(p, cut) for p in range(sz.n_ex) for cut in range(sz.cuts)]:
        block = (spot + p) % sz.n_ex
        held = {}
        for q in range(sz.n_ey):
            for fold in range(folds):
                whole = jnp.concatenate(
                    [
                        terms_refs[cut][(z * sz.n_ex + block) * sz.n_ey + q, pl.ds(fold * PARTS, PARTS), :]
                        for z in range(sz.n_mode)
                    ],
                    1,
                )
                held[q, fold] = [whole[:, t * LANES : (t + 1) * LANES] for t in range(tiles)]
        for i in range(sz.cut_x):
            cutting = sorted({0, strip} | {n - i * strip for n in range(0, sz.cut_nodes, sz.sent)} & set(range(strip)))
            cutting = [0] + [n for n in cutting if n > 0]
            result = jnp.zeros((PARTS, LANES), jnp.float32)
            for begin, end in zip(cutting[:-1], cutting[1:]):
                piece, row = (i * strip + begin) // sz.sent, (i * strip + begin) % sz.sent
                t, r = (piece * sz.share + row) // LANES, (piece * sz.share + row) % LANES
                for fold in range(folds):
                    for q in range(sz.n_ey):
                        source = held[q, fold][t]
                        if r + end - begin > LANES:
                            source = jnp.where(lanes >= r, source, held[q, fold][t + 1])
                        goal = fold * width + q * strip + begin
                        moved = pltpu.roll(source, (goal - r) % LANES, 1) if goal != r else source
                        result = jnp.where((lanes >= goal) & (lanes < goal + end - begin), moved, result)
            field_ref[pl.ds((p * sz.cuts + cut) * sz.cut_x + i, PARTS, stride=x_pad), :] = result

    parts = dot(along(field_ref[...]), in_y_ref[...])
    field_ref[...] = parts[:, :LANES] + parts[:, LANES:]
    fold_of_lane = lane_index((1, LANES)) // width
    shifts, inverses = [], []
    for group in range(PARTS // 4):
        mode = (first_mode + fold_of_lane * (PARTS // 4) + group).astype(jnp.float32)
        shift = shift_base + (span_rate * mode) ** 2
        shifts.append(shift)
        inverses.append(1.0 / (lam_x_ref[...] + (lam_y_ref[...] + shift)))
    for c in range(0, PARTS, 2):
        pair = jnp.concatenate([field_ref[pl.ds((c + d) * x_pad, x_pad), :] for d in range(2)], 1)
        forced = left_dot(in_x_ref, pair)
        for d in range(2):
            mine = forced[:, d * LANES : (d + 1) * LANES]
            first_ref[pl.ds((c + d) * x_eig, x_eig), :] = mine
            work_ref[pl.ds((c + d) * x_eig, x_eig), :] = mine * inverses[(c + d) // 4]
    high, low = split(work_ref[...])
    both = dot(jnp.concatenate([high, low, high], 1), pair_y_ref[...])
    work_ref[...] = both[:, :LANES]
    stiff_ref[...] = both[:, LANES:]
    for c in range(0, PARTS, 2):
        masses, stiffs = [], []
        for d in range(2):
            rows = pl.ds((c + d) * x_eig, x_eig)
            masses.append(work_ref[rows, :])
            stiffs.append(stiff_ref[rows, :] + shifts[c // 4] * masses[d])
        stacked_pair = jnp.concatenate([jnp.concatenate(masses, 1), jnp.concatenate(stiffs, 1)], 0)
        applied = left_dot(pair_x_ref, stacked_pair)
        for d in range(2):
            rows = pl.ds((c + d) * x_eig, x_eig)
            mine = applied[:, d * LANES : (d + 1) * LANES]
            first_ref[rows, :] = (2.0 * first_ref[rows, :] - mine) * inverses[c // 4]
    parts = dot(along(first_ref[...]), out_y_ref[...])
    work_ref[...] = parts[:, :LANES] + parts[:, LANES:]
    for c in range(0, PARTS, 2):
        pair = jnp.concatenate([work_ref[pl.ds((c + d) * x_eig, x_eig), :] for d in range(2)], 1)
        solved = left_dot(out_x_ref, pair)
        for d in range(2):
            field_ref[pl.ds((c + d) * x_pad, x_pad), :] = solved[:, d * LANES : (d + 1) * LANES]

    for p in range(sz.n_ex):
        made = {}
        for i in range(sz.block_x):
            source = field_ref[pl.ds(p * sz.block_x + i, PARTS, stride=x_pad), :]
            for q in range(sz.n_ey):
                begin = i * strip + sz.inner[q][0]
                count = len(sz.inner[q])
                t, r = begin // LANES, begin % LANES
                for fold in range(folds):
                    origin = fold * width + q * strip
                    moved = pltpu.roll(source, (r - origin) % LANES, 1) if origin != r else source
                    for tile, low, high in ((t, r, r + count), (t + 1, 0, r + count - LANES)):
                        if high > 0:
                            old = made.get((q, fold, tile))
                            if old is None:
                                old = jnp.zeros((PARTS, LANES), jnp.float32)
                            made[q, fold, tile] = jnp.where((lanes >= low) & (lanes < high), moved, old)
        for fold in range(folds):
            for tile in range(sz.lane_nodes // LANES):
                for turn in range(sz.n_ey):
                    chosen = jnp.zeros((PARTS, LANES), jnp.float32)
                    for q in range(sz.n_ey):
                        if (q, fold, tile) in made:
                            chosen = jnp.where((place + turn) % sz.n_ey == q, made[q, fold, tile], chosen)
                    out_refs[p * sz.n_ey + turn][pl.ds(fold * PARTS, PARTS), pl.ds(tile * LANES, LANES)] = chosen


def spread_kernel(sz, *refs):
    solved_refs, (out_ref, stacked_ref, turned_ref) = refs[:-3], refs[-3:]
    place, spot = lax.axis_index("ey"), lax.axis_index("ex")
    for step, solved_ref in enumerate(solved_refs):
        shift, turn = step // sz.n_ey, step % sz.n_ey
        source = (spot - shift + sz.n_ex) % sz.n_ex * sz.n_ey + (place - turn + sz.n_ey) % sz.n_ey
        stacked_ref[pl.ds(pl.multiple_of(source * sz.own, PARTS), sz.own), :] = solved_ref[...]
    turned_ref[...] = stacked_ref[...].T
    spots = sz.elems * sz.rows
    for e in range(sz.elems):
        for f in range(sz.rows):
            for a in range(sz.nodes):
                start = sz.block_y * (sz.order * e + a) + sz.order * f
                out_ref[pl.ds(a * sz.nodes * spots + e * sz.rows + f, sz.nodes, stride=spots), :] = turned_ref[
                    pl.ds(start, sz.nodes), :
                ]
    blank = jnp.zeros((sz.elems, LANES), jnp.float32)

    @pl.when(place == 0)
    def _():
        for a in range(sz.nodes):
            out_ref[pl.ds(a * sz.nodes * spots, sz.elems, stride=sz.rows), :] = blank

    @pl.when(place == sz.n_ey - 1)
    def _():
        for a in range(sz.nodes):
            first = ((a + 1) * sz.nodes - 1) * spots + sz.rows - 1
            out_ref[pl.ds(first, sz.elems, stride=sz.rows), :] = blank


def call(kernel, shapes, operands, scratch=(), spaces=pltpu.VMEM, limit=16, flops=10**9):
    if not isinstance(spaces, list):
        spaces = [spaces] * len(operands)
    made = pl.pallas_call(
        kernel,
        out_shape=[jax.ShapeDtypeStruct(shape, jnp.float32) for shape in shapes],
        in_specs=[pl.BlockSpec(memory_space=space) for space in spaces],
        out_specs=[pl.BlockSpec(memory_space=pltpu.VMEM) for _ in shapes],
        scratch_shapes=[pltpu.VMEM(each, jnp.float32) if isinstance(each, tuple) else each for each in scratch],
        compiler_params=pltpu.CompilerParams(vmem_limit_bytes=limit * 2**20),
        cost_estimate=pl.CostEstimate(flops=flops, bytes_accessed=10**6, transcendentals=0),
    )(*operands)
    return list(made)


def on_device(sz, tables, stream_speed, normal_speed):
    flat = sz.nodes * sz.nodes * sz.elems * sz.rows
    table = {name: jnp.asarray(value) for name, value in tables.items() if name != "heights"}
    heights = [float(height) for height in tables["heights"]]
    pieces = call(
        functools.partial(advect_kernel, sz, heights),
        [(sz.sent, LANES)] * (sz.n_mode * sz.cuts),
        [
            pltpu.with_memory_space_constraint(each, pltpu.HBM)
            for each in (
                stream_speed.reshape(flat, sz.planes),
                normal_speed.reshape(flat, sz.planes),
                table["lift"],
                table["back"],
            )
        ],
        [
            (sz.cut_nodes, LANES),
            (flat, sz.planes),
            (flat, sz.planes),
            pltpu.VMEM(tables["lift"].shape, jnp.bfloat16),
            pltpu.VMEM(tables["back"].shape[1:], jnp.bfloat16),
            pltpu.SemaphoreType.DMA((6,)),
        ],
        pltpu.HBM,
    )
    weak = [pieces[cut * sz.n_mode : (cut + 1) * sz.n_mode] for cut in range(sz.cuts)]
    for cut in range(sz.cuts):
        for step in range(sz.n_mode - 1, 0, -1):
            pairs = [(z, partner(z, step, sz.n_mode)) for z in range(sz.n_mode)]
            weak[cut][step] = lax.ppermute(weak[cut][step], "mode", pairs)
    terms, ahead = [], []
    for cut in range(sz.cuts):
        (spectra,) = call(
            functools.partial(transform_kernel, sz),
            [(2 * sz.planes_total, sz.share)],
            [*weak[cut], *ahead, table["waves"]],
            [(-(-sz.share // LANES), 2 * sz.planes_total, LANES), (2, sz.planes_total, sz.share)],
            [pltpu.VMEM] * sz.n_mode + [pl.ANY] * len(ahead) + [pltpu.VMEM],
            flops=10**11 if cut == sz.cuts - 1 else 10**8,
        )
        spectra = spectra.reshape(sz.n_mode * sz.spots, sz.own, sz.share)
        terms.append(lax.all_to_all(spectra, ("mode", "ex", "ey"), split_axis=0, concat_axis=0, tiled=True))
        ahead = [spectra]
    names = ("in_y", "in_x", "pair_y", "pair_x", "out_y", "out_x", "lam_x", "lam_y")
    solved = call(
        functools.partial(smooth_kernel, sz),
        [(sz.own, sz.lane_nodes)] * sz.spots,
        terms + [table[name] for name in names],
        [(PARTS * sz.x_pad, LANES)] + [(PARTS * sz.x_eig, LANES)] * 3,
    )
    for step in sorted(range(1, sz.spots), key=lambda each: each // sz.n_ey == 0):
        shift, turn = step // sz.n_ey, step % sz.n_ey
        pairs = [
            (p * sz.n_ey + q, (p + shift) % sz.n_ex * sz.n_ey + (q + turn) % sz.n_ey)
            for p in range(sz.n_ex)
            for q in range(sz.n_ey)
        ]
        solved[step] = lax.ppermute(solved[step], ("ex", "ey"), pairs)
    (out,) = call(
        functools.partial(spread_kernel, sz),
        [(flat, LANES)],
        solved,
        [(sz.columns, sz.lane_nodes), (sz.lane_nodes, LANES)],
    )
    return out.reshape(sz.nodes, sz.nodes, sz.elems, sz.rows, sz.columns)


def solution(mesh):
    spec = P(None, None, "ex", "ey", "mode")

    def whole(stream_speed, normal_speed):
        shape = stream_speed.shape
        counts = mesh.shape
        block = shape[:2] + (shape[2] // counts["ex"], shape[3] // counts["ey"], shape[4] // counts["mode"])
        sz = Sizes(counts, block)
        return jax.shard_map(
            functools.partial(on_device, sz, host_tables(sz)),
            mesh=mesh,
            in_specs=(spec, spec),
            out_specs=spec,
            check_vma=False,
        )(stream_speed, normal_speed)

    return whole
```

```python
import functools
import math

import jax
import jax.numpy as jnp
import ml_dtypes
import numpy as np
from jax import lax
from jax.experimental import pallas as pl
from jax.experimental.pallas import tpu as pltpu
from jax.sharding import PartitionSpec as P

BF16 = ml_dtypes.bfloat16

element_width = 2.0
shift_base = 10.0
span_rate = 0.0125


def legendre_pair(degree, points):
    before = points * 0.0 + 1.0
    current = points.copy()
    for step in range(1, degree):
        upcoming = ((2 * step + 1) * points * current - step * before) / (step + 1)
        before = current
        current = upcoming
    return (current, before)


def legendre_slope(degree, points):
    current, before = legendre_pair(degree, points)
    return (current, degree * (points * current - before) / (points * points - 1.0))


def lobatto_points(order):
    guesses = -np.cos(np.pi * np.arange(1, order) / order)
    for step in range(60):
        current, slope = legendre_slope(order, guesses)
        second = (2.0 * guesses * slope - order * (order + 1) * current) / (1.0 - guesses * guesses)
        guesses = guesses - slope / second
    return guesses


def gauss_rule(count):
    guesses = -np.cos(np.pi * (np.arange(count) + 0.75) / (count + 0.5))
    for step in range(60):
        current, slope = legendre_slope(count, guesses)
        guesses = guesses - current / slope
    current, slope = legendre_slope(count, guesses)
    return (guesses, 2.0 / ((1.0 - guesses * guesses) * slope * slope))


def jacobi_eigen(matrix):
    size_n = matrix.shape[0]
    work = matrix.copy()
    vectors = np.eye(size_n)
    for sweep_number in range(20):
        for first in range(size_n):
            for second in range(first + 1, size_n):
                coupling = work[first, second]
                if abs(coupling) > 1e-300:
                    theta = (work[second, second] - work[first, first]) / (2.0 * coupling)
                    direction = 1.0 if theta >= 0.0 else -1.0
                    tangent = direction / (abs(theta) + np.sqrt(theta * theta + 1.0))
                    cosine = 1.0 / np.sqrt(tangent * tangent + 1.0)
                    sine = tangent * cosine
                    rotation = np.eye(size_n)
                    rotation[first, first] = cosine
                    rotation[second, second] = cosine
                    rotation[first, second] = sine
                    rotation[second, first] = -sine
                    work = rotation.T @ work @ rotation
                    vectors = vectors @ rotation
    diagonal_index = np.arange(size_n)
    return (work[diagonal_index, diagonal_index], vectors)


def extended_basis(stiffness, weights, left_width, centre_width, right_width):
    node_count = weights.shape[0]
    full_count = 3 * node_count - 2
    stiff_full = np.zeros((full_count, full_count))
    mass_full = np.zeros(full_count)
    for position, span_width in enumerate((left_width, centre_width, right_width)):
        if span_width > 0.0:
            first_node = position * (node_count - 1)
            stiff_full[
                first_node : first_node + node_count, first_node : first_node + node_count
            ] += stiffness * (2.0 / span_width)
            mass_full[first_node : first_node + node_count] += weights * (span_width / 2.0)
    low_index = node_count - 2
    high_index = low_index + node_count + 2
    stiff_ext = stiff_full[low_index:high_index, low_index:high_index].copy()
    mass_ext = mass_full[low_index:high_index].copy()
    frozen_list = []
    if left_width <= 0.0:
        frozen_list += [0, 1]
    if right_width <= 0.0:
        frozen_list += [node_count, node_count + 1]
    for frozen_index in frozen_list:
        stiff_ext[frozen_index, :] = 0.0
        stiff_ext[:, frozen_index] = 0.0
        stiff_ext[frozen_index, frozen_index] = 1.0
        mass_ext[frozen_index] = 1.0
    inverse_root = 1.0 / np.sqrt(mass_ext)
    lambdas, vectors = jacobi_eigen(inverse_root[:, None] * stiff_ext * inverse_root[None, :])
    return (inverse_root[:, None] * vectors, lambdas)


def spectral_tables(order, rows_total):
    inner_points = lobatto_points(order)
    points = np.concatenate([[-1.0], inner_points, [1.0]])
    values, unused_before = legendre_pair(order, points)
    weights = 2.0 / (order * (order + 1) * values**2)
    identity = np.eye(order + 1)
    point_gaps = points[:, None] - points[None, :] + identity
    derivative = values[:, None] / (values[None, :] * point_gaps) * (1.0 - identity)
    derivative[0, 0] = -order * (order + 1) / 4.0
    derivative[order, order] = order * (order + 1) / 4.0
    stiffness = derivative.T @ (weights[:, None] * derivative)
    gauss_points, gauss_weights = gauss_rule(3 * (order + 1) // 2)
    offsets = gauss_points[:, None, None] - points[None, None, :]
    numerators = np.prod(np.where(identity[None, :, :] > 0.5, 1.0, offsets), axis=2)
    denominators = np.prod(np.where(identity > 0.5, 1.0, points[:, None] - points[None, :]), axis=1)
    interp = numerators / denominators[None, :]
    heights = 0.6 + 1.4 * np.sin(np.pi * (np.arange(rows_total) + 0.5) / rows_total)
    basis_x, lambdas_x = extended_basis(
        stiffness, weights, element_width, element_width, element_width
    )
    basis_rows = []
    lambda_rows = []
    for row_number in range(rows_total):
        below = heights[row_number - 1] if row_number > 0 else 0.0
        above = heights[row_number + 1] if row_number < rows_total - 1 else 0.0
        basis_one, lambda_one = extended_basis(
            stiffness, weights, below, heights[row_number], above
        )
        basis_rows.append(basis_one)
        lambda_rows.append(lambda_one)
    return (
        derivative,
        interp,
        gauss_weights,
        weights,
        stiffness,
        basis_x,
        lambdas_x,
        np.stack(basis_rows),
        np.stack(lambda_rows),
        heights,
    )


PARTS = 8
LANES = 128


def ceil_to(count, step):
    return -(-count // step) * step


class Sizes:
    def __init__(self, mesh_shape, block_shape):
        self.n_mode, self.n_ex, self.n_ey = (mesh_shape[name] for name in ("mode", "ex", "ey"))
        self.nodes, _, self.elems, self.rows, self.planes = block_shape
        self.order = self.nodes - 1
        self.gauss = 3 * self.nodes // 2
        self.rows_total = self.rows * self.n_ey
        self.elems_total = self.elems * self.n_ex
        self.planes_total = self.planes * self.n_mode
        self.block_x = self.order * self.elems + 1
        full_y = self.order * self.rows + 1
        self.inner = [
            [j for j in range(full_y) if not (p == 0 and j == 0) and not (p == self.n_ey - 1 and j == full_y - 1)]
            for p in range(self.n_ey)
        ]
        self.block_y = max(len(found) for found in self.inner)
        self.cuts = 1
        self.cut_elems = self.elems // self.cuts
        self.cut_x = self.order * self.cut_elems + 1
        share = -(-self.cut_x * self.block_y // self.n_mode)
        self.sent = ceil_to(share, 8)
        self.share = ceil_to(self.sent, LANES if share > 64 else 16)
        self.cut_nodes = self.sent * self.n_mode
        self.lane_nodes = ceil_to(self.block_x * self.block_y + 2, LANES)
        self.columns = 2 * self.planes
        self.spots = self.n_ex * self.n_ey
        self.own = self.columns // self.spots
        self.folds = self.own // PARTS
        self.fold_width = LANES // self.folds
        self.points = self.nodes + 2
        self.x_cuts = self.n_ex * self.cuts * self.cut_x
        self.x_pad = ceil_to(max(self.x_cuts, self.n_ex * self.block_x), 16)
        self.x_eig = self.elems_total * self.points
        self.y_eig = self.rows_total * self.points
        self.fine = ceil_to(self.gauss * self.gauss, 16)
        assert self.own == PARTS * self.folds and self.x_eig % 16 == 0
        assert max(self.y_eig, self.n_ey * self.block_y) <= self.fold_width
        assert 2 * self.planes == LANES


def high_low(table):
    high = np.asarray(table, np.float32).astype(BF16)
    low = (np.asarray(table, np.float64) - high.astype(np.float64)).astype(BF16)
    return high, low


def beside(table):
    high, low = high_low(table)
    return np.concatenate([high, high, low], 1)


def host_tables(sz):
    derivative, interp, gauss_weights, weights, stiffness, basis_x, lam_x, basis_y, lam_y, heights = spectral_tables(
        sz.order, sz.rows_total
    )
    nodes, fine, points = sz.nodes, sz.fine, sz.points
    gauss_count = sz.gauss**2
    lift = np.zeros((3 * fine, nodes * nodes))
    lift[:gauss_count] = np.kron(interp, interp)
    lift[fine : fine + gauss_count] = np.kron(interp @ derivative, interp)
    lift[2 * fine : 2 * fine + gauss_count] = np.kron(interp, interp @ derivative)
    back = np.zeros((sz.n_ey, nodes * sz.block_y, sz.rows * fine))
    weighted = interp.T * gauss_weights[None, :]
    for place in range(sz.n_ey):
        for f in range(sz.rows):
            for jj, j in enumerate(sz.inner[place]):
                b = j - sz.order * f
                if 0 <= b < nodes:
                    back[place, jj :: sz.block_y, f * fine : f * fine + gauss_count] = -np.kron(
                        weighted, weighted[b : b + 1]
                    )
    grid_x, grid_y = sz.order * sz.elems_total, sz.order * sz.rows_total + 1
    to_x, stiff_x, mass_x = np.zeros((sz.x_eig, grid_x)), np.zeros((grid_x, grid_x)), np.zeros(grid_x)
    for e in range(sz.elems_total):
        for t in range(points):
            to_x[e * points : (e + 1) * points, (sz.order * e + t - 1) % grid_x] += basis_x[t]
        index = (sz.order * e + np.arange(nodes)) % grid_x
        stiff_x[np.ix_(index, index)] += stiffness * (2.0 / element_width)
        mass_x[index] += weights * (element_width / 2.0)
    to_y, stiff_y, mass_y = np.zeros((sz.y_eig, grid_y)), np.zeros((grid_y, grid_y)), np.zeros(grid_y)
    for f in range(sz.rows_total):
        for t in range(points):
            y = sz.order * f + t - 1
            if 0 < y < grid_y - 1:
                to_y[f * points : (f + 1) * points, y] = basis_y[f][t]
        index = sz.order * f + np.arange(nodes)
        stiff_y[np.ix_(index, index)] += stiffness * (2.0 / heights[f])
        mass_y[index] += weights * (heights[f] / 2.0)
    stiff_xx, mass_xx = to_x @ stiff_x @ to_x.T, (to_x * mass_x) @ to_x.T
    stiff_yy, mass_yy = to_y @ stiff_y @ to_y.T, (to_y * mass_y) @ to_y.T
    def block_x(blocks, elems):
        length = sz.order * elems + 1
        nodes_of = [(sz.order * elems * p + i) % grid_x for p in range(blocks) for i in range(length)]
        table = np.zeros((sz.x_eig, sz.x_pad))
        table[:, : len(nodes_of)] = to_x[:, nodes_of]
        return table

    width, folds = sz.fold_width, sz.folds
    block_y = np.zeros((width, width))
    for place in range(sz.n_ey):
        for jj, j in enumerate(sz.inner[place]):
            block_y[place * sz.block_y + jj, : sz.y_eig] = to_y[:, sz.order * sz.rows * place + j]

    def folded(table):
        padded = np.zeros((width, width))
        padded[: table.shape[0], : table.shape[1]] = table
        return np.kron(np.eye(folds), padded)

    def one_dot(table):
        high, low = high_low(folded(table))
        return np.block([[high, low], [high, np.zeros_like(low)]]).astype(BF16)

    mass_pair, stiff_pair = high_low(folded(mass_yy)), high_low(folded(stiff_yy))
    heads = np.concatenate([mass_pair[0], stiff_pair[0]], 1)
    tails = np.concatenate([mass_pair[1], stiff_pair[1]], 1)
    lam_lanes = np.ones((1, folds, width))
    lam_lanes[:, :, : sz.y_eig] = lam_y.reshape(-1)
    planes_total = sz.planes_total
    turns = np.arange(planes_total)[None, :] * np.arange(planes_total // 2)[:, None] % planes_total
    angles = turns * (2.0 * math.pi / planes_total)
    waves = np.stack([np.cos(angles), -np.sin(angles)], 1).reshape(planes_total, planes_total) / planes_total
    return dict(
        heights=np.asarray(heights, np.float32),
        lift=beside(lift),
        back=np.stack([stacked(table) for table in back]),
        waves=np.stack(high_low(waves)),
        in_y=one_dot(block_y),
        in_x=stacked(block_x(sz.n_ex * sz.cuts, sz.cut_elems)),
        pair_y=np.concatenate([heads, heads, tails], 0),
        pair_x=stacked(np.concatenate([stiff_xx, mass_xx], 1)),
        out_y=one_dot(block_y.T),
        out_x=stacked(block_x(sz.n_ex, sz.elems).T),
        lam_x=np.asarray(np.tile(lam_x, sz.elems_total)[:, None] * np.ones((1, LANES)), np.float32),
        lam_y=np.asarray(lam_lanes.reshape(1, LANES), np.float32),
    )


def stacked(table):
    return np.concatenate(high_low(table), 0)


def split(value):
    high = value.astype(jnp.bfloat16)
    low = (value - high.astype(jnp.float32)).astype(jnp.bfloat16)
    return high, low


def dot(left, right):
    return lax.dot_general(left, right, (((1,), (0,)), ((), ())), preferred_element_type=jnp.float32)


def below(value):
    high, low = split(value)
    return jnp.concatenate([high, low, high], 0)


def left_dot(table_ref, value):
    rows = table_ref.shape[0] // 2
    high, low = split(value)
    both = dot(table_ref[...], high)
    return both[:rows] + both[rows:] + dot(table_ref[:rows, :], low)


def along(value):
    return jnp.concatenate(split(value), 1)


def partner(spot, step, count):
    if count & (count - 1) == 0:
        return spot ^ step
    return (spot + step) % count


def origin(spot, step, count):
    if count & (count - 1) == 0:
        return spot ^ step
    return (spot - step + count) % count


def lane_index(shape):
    return lax.broadcasted_iota(jnp.int32, shape, len(shape) - 1)


def advect_kernel(sz, heights, stream_hbm, normal_hbm, lift_hbm, back_hbm, *others):
    out_refs, (total_ref, stream_ref, normal_ref, lift_ref, back_ref, arrived) = others[:-6], others[-6:]
    place = lax.axis_index("ey")
    fetched = [
        pltpu.make_async_copy(source, target, arrived.at[i])
        for i, (source, target) in enumerate(
            (
                (stream_hbm, stream_ref),
                (normal_hbm, normal_ref),
                (lift_hbm, lift_ref),
                (back_hbm.at[place], back_ref),
            )
        )
    ]
    for copy in fetched[:3]:
        copy.start()
    count, fine, rows = sz.nodes * sz.nodes, sz.fine, sz.rows
    spots = sz.elems * rows
    half = lane_index((fine, LANES)) < sz.planes
    column, step = sz.nodes * sz.block_y, sz.order * sz.block_y
    factors = [
        sum(jnp.where(place == q, heights[q * rows + f] * 0.5, 0.0) for q in range(sz.n_ey)) for f in range(rows)
    ]
    full = sz.cut_x * sz.block_y // 8 * 8
    total_ref[pl.ds(full, sz.cut_nodes - full), :] = jnp.zeros((sz.cut_nodes - full, LANES), jnp.float32)
    spot = lax.axis_index("mode")
    for copy in fetched[:3]:
        copy.wait()
    fetched[3].start()
    for cut in range(sz.cuts):
        high_parts, low_parts = [], []
        for e in range(cut * sz.cut_elems, (cut + 1) * sz.cut_elems):
            speeds = jnp.concatenate(
                [
                    ref[pl.ds(e * rows + f, count, stride=spots), :]
                    for f in range(rows)
                    for ref in (stream_ref, normal_ref)
                ],
                1,
            )
            values = dot(lift_ref[...], below(speeds))
            highs, lows = [], []
            for f in range(rows):
                mine = values[:, f * LANES : (f + 1) * LANES]
                both, slope_x, slope_y = mine[:fine], mine[fine : 2 * fine], mine[2 * fine :]
                turned = pltpu.roll(both, sz.planes, 1)
                stream = jnp.where(half, both, turned)
                normal = jnp.where(half, turned, both)
                high, low = split((stream * factors[f]) * slope_x + (normal * (element_width * 0.5)) * slope_y)
                highs.append(high)
                lows.append(low)
            high_parts.append(jnp.concatenate(highs, 0))
            low_parts.append(jnp.concatenate(lows, 0))
        if cut == 0:
            fetched[3].wait()
        both = dot(back_ref[...], jnp.concatenate(high_parts, 1))
        weak = both[:column] + both[column:] + dot(back_ref[:column, :], jnp.concatenate(low_parts, 1))
        carry = None
        for e in range(sz.cut_elems):
            mine = weak[:, e * LANES : (e + 1) * LANES]
            if carry is not None:
                gap = jnp.zeros((column - carry.shape[0], LANES), jnp.float32)
                mine = mine + jnp.concatenate([carry, gap], 0)
            length = step if e < sz.cut_elems - 1 else column
            total_ref[pl.ds(e * step, length), :] = mine[:length]
            carry = mine[length:]
        for turn in range(sz.n_mode):
            goal = partner(spot, turn, sz.n_mode)
            out_refs[cut * sz.n_mode + turn][...] = total_ref[pl.ds(pl.multiple_of(goal * sz.sent, 8), sz.sent), :]


def transform_kernel(sz, *refs):
    weak_refs, (waves_ref, out_ref, mixed_ref, signal_ref) = refs[: sz.n_mode], refs[-4:]
    spot = lax.axis_index("mode")
    if sz.share > sz.sent:
        signal_ref[...] = jnp.zeros(signal_ref.shape, jnp.float32)
    for step, weak_ref in enumerate(weak_refs):
        turned = weak_ref[...].T
        first = pl.multiple_of(origin(spot, step, sz.n_mode) * sz.planes, 8)
        for k in range(2):
            signal_ref[k, pl.ds(first, sz.planes), pl.ds(0, sz.sent)] = turned[k * sz.planes : (k + 1) * sz.planes]
    modes = sz.planes_total
    for k in range(2):
        high, low = split(signal_ref[k])
        part = dot(waves_ref[0], high) + dot(waves_ref[0], low) + dot(waves_ref[1], high)
        for t in range(mixed_ref.shape[0]):
            tile = part[:, t * LANES : (t + 1) * LANES]
            mixed_ref[t, pl.ds(k, modes, stride=2), pl.ds(0, tile.shape[1])] = tile
    for t in range(mixed_ref.shape[0]):
        last = min(LANES, sz.share - t * LANES)
        out_ref[:, pl.ds(t * LANES, last)] = mixed_ref[t, :, pl.ds(0, last)]


def smooth_kernel(
    sz,
    *refs,
):
    terms_refs, out_refs = refs[: sz.cuts], refs[sz.cuts + 8 : -4]
    field_ref, first_ref, work_ref, stiff_ref = refs[-4:]
    in_y_ref, in_x_ref, pair_y_ref, pair_x_ref, out_y_ref, out_x_ref, lam_x_ref, lam_y_ref = refs[
        sz.cuts : sz.cuts + 8
    ]
    width, folds, strip = sz.fold_width, sz.folds, sz.block_y
    tiles = -(-(sz.share * sz.n_mode) // LANES)
    lanes = lane_index((PARTS, LANES))
    x_pad, x_eig = sz.x_pad, sz.x_eig
    place, spot = lax.axis_index("ey"), lax.axis_index("ex")
    device = (lax.axis_index("mode") * sz.n_ex + spot) * sz.n_ey + place
    first_mode = device * (sz.own // 4)

    for c in range(PARTS):
        field_ref[pl.ds(c * x_pad + sz.x_cuts, x_pad - sz.x_cuts), :] = jnp.zeros(
            (x_pad - sz.x_cuts, LANES), jnp.float32
        )
    for p, cut in [(p, cut) for p in range(sz.n_ex) for cut in range(sz.cuts)]:
        block = (spot + p) % sz.n_ex
        held = {}
        for q in range(sz.n_ey):
            for fold in range(folds):
                whole = jnp.concatenate(
                    [
                        terms_refs[cut][(z * sz.n_ex + block) * sz.n_ey + q, pl.ds(fold * PARTS, PARTS), :]
                        for z in range(sz.n_mode)
                    ],
                    1,
                )
                held[q, fold] = [whole[:, t * LANES : (t + 1) * LANES] for t in range(tiles)]
        for i in range(sz.cut_x):
            cutting = sorted({0, strip} | {n - i * strip for n in range(0, sz.cut_nodes, sz.sent)} & set(range(strip)))
            cutting = [0] + [n for n in cutting if n > 0]
            result = jnp.zeros((PARTS, LANES), jnp.float32)
            for begin, end in zip(cutting[:-1], cutting[1:]):
                piece, row = (i * strip + begin) // sz.sent, (i * strip + begin) % sz.sent
                t, r = (piece * sz.share + row) // LANES, (piece * sz.share + row) % LANES
                for fold in range(folds):
                    for q in range(sz.n_ey):
                        source = held[q, fold][t]
                        if r + end - begin > LANES:
                            source = jnp.where(lanes >= r, source, held[q, fold][t + 1])
                        goal = fold * width + q * strip + begin
                        moved = pltpu.roll(source, (goal - r) % LANES, 1) if goal != r else source
                        result = jnp.where((lanes >= goal) & (lanes < goal + end - begin), moved, result)
            field_ref[pl.ds((p * sz.cuts + cut) * sz.cut_x + i, PARTS, stride=x_pad), :] = result

    parts = dot(along(field_ref[...]), in_y_ref[...])
    field_ref[...] = parts[:, :LANES] + parts[:, LANES:]
    fold_of_lane = lane_index((1, LANES)) // width
    shifts, inverses = [], []
    for group in range(PARTS // 4):
        mode = (first_mode + fold_of_lane * (PARTS // 4) + group).astype(jnp.float32)
        shift = shift_base + (span_rate * mode) ** 2
        shifts.append(shift)
        inverses.append(1.0 / (lam_x_ref[...] + (lam_y_ref[...] + shift)))
    for c in range(0, PARTS, 2):
        pair = jnp.concatenate([field_ref[pl.ds((c + d) * x_pad, x_pad), :] for d in range(2)], 1)
        forced = left_dot(in_x_ref, pair)
        for d in range(2):
            mine = forced[:, d * LANES : (d + 1) * LANES]
            first_ref[pl.ds((c + d) * x_eig, x_eig), :] = mine
            work_ref[pl.ds((c + d) * x_eig, x_eig), :] = mine * inverses[(c + d) // 4]
    high, low = split(work_ref[...])
    both = dot(jnp.concatenate([high, low, high], 1), pair_y_ref[...])
    work_ref[...] = both[:, :LANES]
    stiff_ref[...] = both[:, LANES:]
    for c in range(0, PARTS, 2):
        masses, stiffs = [], []
        for d in range(2):
            rows = pl.ds((c + d) * x_eig, x_eig)
            masses.append(work_ref[rows, :])
            stiffs.append(stiff_ref[rows, :] + shifts[c // 4] * masses[d])
        stacked_pair = jnp.concatenate([jnp.concatenate(masses, 1), jnp.concatenate(stiffs, 1)], 0)
        applied = left_dot(pair_x_ref, stacked_pair)
        for d in range(2):
            rows = pl.ds((c + d) * x_eig, x_eig)
            mine = applied[:, d * LANES : (d + 1) * LANES]
            first_ref[rows, :] = (2.0 * first_ref[rows, :] - mine) * inverses[c // 4]
    parts = dot(along(first_ref[...]), out_y_ref[...])
    work_ref[...] = parts[:, :LANES] + parts[:, LANES:]
    for c in range(0, PARTS, 2):
        pair = jnp.concatenate([work_ref[pl.ds((c + d) * x_eig, x_eig), :] for d in range(2)], 1)
        solved = left_dot(out_x_ref, pair)
        for d in range(2):
            field_ref[pl.ds((c + d) * x_pad, x_pad), :] = solved[:, d * LANES : (d + 1) * LANES]

    for p in range(sz.n_ex):
        made = {}
        for i in range(sz.block_x):
            source = field_ref[pl.ds(p * sz.block_x + i, PARTS, stride=x_pad), :]
            for q in range(sz.n_ey):
                begin = i * strip + sz.inner[q][0]
                count = len(sz.inner[q])
                t, r = begin // LANES, begin % LANES
                for fold in range(folds):
                    origin = fold * width + q * strip
                    moved = pltpu.roll(source, (r - origin) % LANES, 1) if origin != r else source
                    for tile, low, high in ((t, r, r + count), (t + 1, 0, r + count - LANES)):
                        if high > 0:
                            old = made.get((q, fold, tile))
                            if old is None:
                                old = jnp.zeros((PARTS, LANES), jnp.float32)
                            made[q, fold, tile] = jnp.where((lanes >= low) & (lanes < high), moved, old)
        for fold in range(folds):
            for tile in range(sz.lane_nodes // LANES):
                for turn in range(sz.n_ey):
                    chosen = jnp.zeros((PARTS, LANES), jnp.float32)
                    for q in range(sz.n_ey):
                        if (q, fold, tile) in made:
                            chosen = jnp.where((place + turn) % sz.n_ey == q, made[q, fold, tile], chosen)
                    out_refs[p * sz.n_ey + turn][pl.ds(fold * PARTS, PARTS), pl.ds(tile * LANES, LANES)] = chosen


def spread_kernel(sz, *refs):
    solved_refs, (out_ref, stacked_ref, turned_ref, made_ref, left) = refs[:-5], refs[-5:]
    place, spot = lax.axis_index("ey"), lax.axis_index("ex")
    for step, solved_ref in enumerate(solved_refs):
        shift, turn = step // sz.n_ey, step % sz.n_ey
        source = (spot - shift + sz.n_ex) % sz.n_ex * sz.n_ey + (place - turn + sz.n_ey) % sz.n_ey
        stacked_ref[pl.ds(pl.multiple_of(source * sz.own, PARTS), sz.own), :] = solved_ref[...]
    turned_ref[...] = stacked_ref[...].T
    spots = sz.elems * sz.rows
    slab = sz.nodes * spots
    blank = jnp.zeros((sz.elems, LANES), jnp.float32)
    group = 3 if sz.nodes % 3 == 0 else 1
    copies = []
    for a in range(sz.nodes):
        for e in range(sz.elems):
            for f in range(sz.rows):
                start = sz.block_y * (sz.order * e + a) + sz.order * f
                made_ref[pl.ds(a * slab + e * sz.rows + f, sz.nodes, stride=spots), :] = turned_ref[
                    pl.ds(start, sz.nodes), :
                ]

        @pl.when(place == 0)
        def _(a=a):
            made_ref[pl.ds(a * slab, sz.elems, stride=sz.rows), :] = blank

        @pl.when(place == sz.n_ey - 1)
        def _(a=a):
            made_ref[pl.ds((a + 1) * slab - spots + sz.rows - 1, sz.elems, stride=sz.rows), :] = blank

        if a % group == group - 1:
            rows = pl.ds((a + 1 - group) * slab, group * slab)
            copies.append(pltpu.make_async_copy(made_ref.at[rows], out_ref.at[rows], left.at[len(copies)]))
            copies[-1].start()
    for copy in copies:
        copy.wait()


def call(kernel, shapes, operands, scratch=(), spaces=pltpu.VMEM, limit=16, flops=10**9, out_space=pltpu.VMEM):
    if not isinstance(spaces, list):
        spaces = [spaces] * len(operands)
    made = pl.pallas_call(
        kernel,
        out_shape=[jax.ShapeDtypeStruct(shape, jnp.float32) for shape in shapes],
        in_specs=[pl.BlockSpec(memory_space=space) for space in spaces],
        out_specs=[pl.BlockSpec(memory_space=out_space) for _ in shapes],
        scratch_shapes=[pltpu.VMEM(each, jnp.float32) if isinstance(each, tuple) else each for each in scratch],
        compiler_params=pltpu.CompilerParams(vmem_limit_bytes=limit * 2**20),
        cost_estimate=pl.CostEstimate(flops=flops, bytes_accessed=10**6, transcendentals=0),
    )(*operands)
    return list(made)


def on_device(sz, tables, stream_speed, normal_speed):
    flat = sz.nodes * sz.nodes * sz.elems * sz.rows
    table = {name: jnp.asarray(value) for name, value in tables.items() if name != "heights"}
    heights = [float(height) for height in tables["heights"]]
    pieces = call(
        functools.partial(advect_kernel, sz, heights),
        [(sz.sent, LANES)] * (sz.n_mode * sz.cuts),
        [
            pltpu.with_memory_space_constraint(each, pltpu.HBM)
            for each in (
                stream_speed.reshape(flat, sz.planes),
                normal_speed.reshape(flat, sz.planes),
                table["lift"],
                table["back"],
            )
        ],
        [
            (sz.cut_nodes, LANES),
            (flat, sz.planes),
            (flat, sz.planes),
            pltpu.VMEM(tables["lift"].shape, jnp.bfloat16),
            pltpu.VMEM(tables["back"].shape[1:], jnp.bfloat16),
            pltpu.SemaphoreType.DMA((4,)),
        ],
        pltpu.HBM,
    )
    weak = [pieces[cut * sz.n_mode : (cut + 1) * sz.n_mode] for cut in range(sz.cuts)]
    for cut in range(sz.cuts):
        for step in sorted(range(1, sz.n_mode), key=lambda each: (each & -each, each), reverse=True):
            pairs = [(z, partner(z, step, sz.n_mode)) for z in range(sz.n_mode)]
            weak[cut][step] = lax.ppermute(weak[cut][step], "mode", pairs)
    terms, ahead = [], []
    for cut in range(sz.cuts):
        (spectra,) = call(
            functools.partial(transform_kernel, sz),
            [(2 * sz.planes_total, sz.share)],
            [*weak[cut], *ahead, table["waves"]],
            [(-(-sz.share // LANES), 2 * sz.planes_total, LANES), (2, sz.planes_total, sz.share)],
            [pltpu.VMEM] * sz.n_mode + [pl.ANY] * len(ahead) + [pltpu.VMEM],
            flops=10**11 if cut == sz.cuts - 1 else 10**8,
        )
        spectra = spectra.reshape(sz.n_mode * sz.spots, sz.own, sz.share)
        terms.append(lax.all_to_all(spectra, ("mode", "ex", "ey"), split_axis=0, concat_axis=0, tiled=True))
        ahead = [spectra]
    names = ("in_y", "in_x", "pair_y", "pair_x", "out_y", "out_x", "lam_x", "lam_y")
    solved = call(
        functools.partial(smooth_kernel, sz),
        [(sz.own, sz.lane_nodes)] * sz.spots,
        terms + [table[name] for name in names],
        [(PARTS * sz.x_pad, LANES)] + [(PARTS * sz.x_eig, LANES)] * 3,
    )
    for step in sorted(range(1, sz.spots), key=lambda each: each // sz.n_ey == 0):
        shift, turn = step // sz.n_ey, step % sz.n_ey
        pairs = [
            (p * sz.n_ey + q, (p + shift) % sz.n_ex * sz.n_ey + (q + turn) % sz.n_ey)
            for p in range(sz.n_ex)
            for q in range(sz.n_ey)
        ]
        solved[step] = lax.ppermute(solved[step], ("ex", "ey"), pairs)
    (out,) = call(
        functools.partial(spread_kernel, sz),
        [(flat, LANES)],
        solved,
        [(sz.columns, sz.lane_nodes), (sz.lane_nodes, LANES), (flat, LANES), pltpu.SemaphoreType.DMA((sz.nodes,))],
        out_space=pltpu.HBM,
    )
    return out.reshape(sz.nodes, sz.nodes, sz.elems, sz.rows, sz.columns)


def solution(mesh):
    spec = P(None, None, "ex", "ey", "mode")

    def whole(stream_speed, normal_speed):
        shape = stream_speed.shape
        counts = mesh.shape
        block = shape[:2] + (shape[2] // counts["ex"], shape[3] // counts["ey"], shape[4] // counts["mode"])
        sz = Sizes(counts, block)
        return jax.shard_map(
            functools.partial(on_device, sz, host_tables(sz)),
            mesh=mesh,
            in_specs=(spec, spec),
            out_specs=spec,
            check_vma=False,
        )(stream_speed, normal_speed)

    return whole
```
